128 devices in a mesh: dp: 16 (over z, y), row: 2 (over x_lo), col: 4 (over x_hi, core).
Axes of the slice: x: 4 (x_hi: 2, x_lo: 2; x = x_hi * 2 + x_lo), y: 4, z: 4, core: 2. Of those that a mesh axis runs over, the one named last changes fastest.
Arguments:
- layer_input: bfloat16 [16384, 1536], P(('dp', 'row'), 'col'), may hold values from -6 to 6
- gain_attn: bfloat16 [1536], P('col'), may hold values from 0.099609375 to 1.8984375
- w_query: bfloat16 [1536, 1536], P('col', 'row'), may hold values from -0.15625 to 0.15625
- w_key: bfloat16 [1536, 256], P('col', 'row'), may hold values from -0.15625 to 0.15625
- w_value: bfloat16 [1536, 256], P('col', 'row'), may hold values from -0.15625 to 0.15625
- b_query: bfloat16 [1536], P('row'), may hold values from -3 to 3
- b_key: bfloat16 [256], P('row'), may hold values from -3 to 3
- b_value: bfloat16 [256], P('row'), may hold values from -0.3125 to 0.3125
- w_out: bfloat16 [1536, 1536], P('row', 'col'), may hold values from -1.25 to 1.25
- gain_ffn: bfloat16 [1536], P('col'), may hold values from 0.099609375 to 1.8984375
- w_gate: bfloat16 [1536, 8960], P('col', 'row'), may hold values from -0.15625 to 0.15625
- w_up: bfloat16 [1536, 8960], P('col', 'row'), may hold values from -0.15625 to 0.15625
- w_down: bfloat16 [8960, 1536], P('row', 'col'), may hold values from -0.0625 to 0.0625
- out_grad: bfloat16 [16384, 1536], P(('dp', 'row'), 'col'), may hold values from -6 to 6
Outputs:
- layer_output: float32 [16384, 1536], P(('dp', 'row'), 'col')
- grad_input: float32 [16384, 1536], P(('dp', 'row'), 'col')
- grad_gain_attn: float32 [1536], P('col')
- grad_w_query: float32 [1536, 1536], P('col', 'row')
- grad_w_key: float32 [1536, 256], P('col', 'row')
- grad_w_value: float32 [1536, 256], P('col', 'row')
- grad_b_query: float32 [1536], P('row')
- grad_b_key: float32 [256], P('row')
- grad_b_value: float32 [256], P('row')
- grad_w_out: float32 [1536, 1536], P('row', 'col')
- grad_gain_ffn: float32 [1536], P('col')
- grad_w_gate: float32 [1536, 8960], P('col', 'row')
- grad_w_up: float32 [1536, 8960], P('col', 'row')
- grad_w_down: float32 [8960, 1536], P('row', 'col')
The draws below stay inside these ranges and needn't reach their ends.
All inputs are finite; a program needn't handle non-finite values.
Results may differ from the reference program's by a relative error of at most 0.023.
Values may be sent and summed in bfloat16 or wider, within the bound.
A program may use at most 256 MiB of HBM per device.

```python
import jax
import jax.numpy as jnp
from jax import lax

D = 1536
FF = 8960
QH = 12
KVH = 2
HEAD = 128
LEN = 1024
TOKENS = 16384
N_DP = 16


def level_of(stream_key, shape, cuts, least, high):
    def one(position, parts):
        heights = jax.random.uniform(jax.random.fold_in(jax.random.fold_in(stream_key, 6), position), (parts,), jnp.float32, least / len(cuts), high / len(cuts))
        return jnp.repeat(jnp.exp(heights), shape[position] // parts).reshape((-1,) + (1,) * (len(shape) - position - 1))

    level = one(*cuts[0])
    for cut in cuts[1:]:
        level = level * one(*cut)
    return level


def bell_draw(key, dims, spread, reach, pieces=(), held_as=jnp.bfloat16):
    values = spread * jax.random.normal(key, dims, jnp.float32)
    if pieces:
        values = values * level_of(key, dims, pieces, -0.22, 0.18)
    return jnp.clip(values, -reach, reach).astype(held_as)


def setup_inputs(seed: int = 0) -> dict:
    splits = jax.random.split(jax.random.key(seed), 15)
    return {
        "layer_input": bell_draw(splits[0], (TOKENS, D), 1.0, 6.0, ((0, 32), (1, 4))),
        "gain_attn": jnp.clip(1.0 + 0.18 * jax.random.normal(splits[1], (D,), jnp.float32), 0.099609375, 1.8984375).astype(jnp.bfloat16),
        "w_query": bell_draw(splits[2], (D, QH * HEAD), D ** -0.5, 0.15625, ((0, 4), (1, 2))),
        "w_key": bell_draw(splits[3], (D, KVH * HEAD), D ** -0.5, 0.15625, ((0, 4), (1, 2))),
        "w_value": bell_draw(splits[4], (D, KVH * HEAD), D ** -0.5, 0.15625, ((0, 4), (1, 2))),
        "b_query": bell_draw(splits[5], (QH * HEAD,), 0.5, 3.0, ((0, 2),)),
        "b_key": bell_draw(splits[6], (KVH * HEAD,), 0.5, 3.0, ((0, 2),)),
        "b_value": bell_draw(splits[7], (KVH * HEAD,), 0.05, 0.3125, ((0, 2),)),
        "w_out": bell_draw(splits[8], (QH * HEAD, D), (QH * HEAD // 64) ** -0.5, 1.25, ((0, 2), (1, 4))),
        "gain_ffn": jnp.clip(1.0 + 0.18 * jax.random.normal(splits[9], (D,), jnp.float32), 0.099609375, 1.8984375).astype(jnp.bfloat16),
        "w_gate": bell_draw(splits[10], (D, FF), D ** -0.5, 0.15625, ((0, 4), (1, 2))),
        "w_up": bell_draw(splits[11], (D, FF), D ** -0.5, 0.15625, ((0, 4), (1, 2))),
        "w_down": bell_draw(splits[12], (FF, D), FF ** -0.5, 0.0625, ((0, 2), (1, 4))),
        "out_grad": bell_draw(splits[13], (TOKENS, D), 1.0, 6.0, ((0, 32), (1, 4))),
    }


@jax.custom_vjp
def low(v):
    return lax.optimization_barrier(v.astype(jnp.bfloat16)).astype(jnp.float32)

@jax.custom_vjp
def low_back(v):
    return v

def low_keep(v):
    return (low(v), None)

def low_pass(kept, grad):
    return (grad,)

def back_keep(v):
    return (v, None)

def back_low(kept, grad):
    return (low(grad),)
low.defvjp(low_keep, low_pass)
low_back.defvjp(back_keep, back_low)
EPS = 1e-06
THETA = 1000000.0
NEG = -1e+30

def matmul(left, right):
    return jnp.dot(left, right, precision=lax.Precision.HIGHEST, preferred_element_type=jnp.float32)

def normalize(values, gain):
    return values * lax.rsqrt(lax.optimization_barrier(jnp.mean(values * values, axis=-1, keepdims=True)) + EPS) * gain

def rope_tables(count):
    places = (jnp.arange(count) % LEN).astype(jnp.float32)
    inverse = 1.0 / THETA ** (jnp.arange(0, HEAD, 2).astype(jnp.float32) / HEAD)
    angles = places[:, None] * inverse[None, :]
    cosine = jnp.concatenate([jnp.cos(angles), jnp.cos(angles)], axis=-1)
    sine = jnp.concatenate([jnp.sin(angles), jnp.sin(angles)], axis=-1)
    return (cosine, sine)

def rotate(values, cosine, sine):
    half = values.shape[-1] // 2
    turned = jnp.concatenate([-values[..., half:], values[..., :half]], axis=-1)
    return values * cosine + turned * sine

def attend_one(item):
    query, key, value = item
    group = QH // KVH
    key = jnp.repeat(key, group, axis=1)
    value = jnp.repeat(value, group, axis=1)
    raw = low_back(jnp.einsum('thd,shd->hts', query, key, precision=lax.Precision.HIGHEST))
    scores = raw * HEAD ** (-0.5)
    places = jnp.arange(LEN)
    keep = places[None, :] <= places[:, None]
    scores = jnp.where(keep[None], scores, NEG)
    probs = low(jax.nn.softmax(scores, axis=-1))
    return jnp.einsum('hts,shd->thd', probs, value, precision=lax.Precision.HIGHEST)

def forward(layer_input, gain_attn, w_query, w_key, w_value, b_query, b_key, b_value, w_out, gain_ffn, w_gate, w_up, w_down):
    normed1 = low(normalize(layer_input, gain_attn))
    weights = jnp.concatenate([w_query, w_key, w_value], axis=1)
    biases = jnp.concatenate([b_query, b_key, b_value])
    qkv = low_back(matmul(normed1, weights) + biases)
    query_cols = QH * HEAD
    key_cols = KVH * HEAD
    cosine, sine = rope_tables(TOKENS)
    cosine = cosine[:, None, :]
    sine = sine[:, None, :]
    query = low(rotate(qkv[:, :query_cols].reshape(TOKENS, QH, HEAD), cosine, sine))
    key = low(rotate(qkv[:, query_cols:query_cols + key_cols].reshape(TOKENS, KVH, HEAD), cosine, sine))
    value = low(qkv[:, query_cols + key_cols:].reshape(TOKENS, KVH, HEAD))

    def by_sequence(array):
        return array.reshape(N_DP, LEN, array.shape[1], HEAD)
    attn = lax.map(jax.checkpoint(attend_one), (by_sequence(query), by_sequence(key), by_sequence(value)))
    attn = low(low_back(attn.reshape(TOKENS, query_cols)))
    mid = layer_input + low_back(matmul(attn, w_out))
    normed2 = low(normalize(mid, gain_ffn))
    gate = low_back(matmul(normed2, w_gate))
    up = low_back(matmul(normed2, w_up))
    hidden = low(jax.nn.silu(gate) * up)
    return mid + low_back(matmul(hidden, w_down))

def reference(layer_input, gain_attn, w_query, w_key, w_value, b_query, b_key, b_value, w_out, gain_ffn, w_gate, w_up, w_down, out_grad):
    params = [array.astype(jnp.float32) for array in (layer_input, gain_attn, w_query, w_key, w_value, b_query, b_key, b_value, w_out, gain_ffn, w_gate, w_up, w_down)]
    output, pullback = jax.vjp(forward, *params)
    grads = pullback(out_grad.astype(jnp.float32))
    return (output, grads[0], grads[1], grads[2], grads[3], grads[4], grads[5], grads[6], grads[7], grads[8], grads[9], grads[10], grads[11], grads[12])
```

```python
import jax
import jax.numpy as jnp
from jax import lax
from jax.sharding import PartitionSpec as P

EPS = 1e-06
THETA = 1000000.0
NEG = -1e30
BF = jnp.bfloat16
F32 = jnp.float32
HEAD = 128
LANES = 128


def dot(left, right, left_dim, right_dim):
    return lax.dot_general(
        left, right, (((left_dim,), (right_dim,)), ((), ())), preferred_element_type=F32
    )


def flip(values, bit):
    count = lax.axis_size("col")
    return lax.ppermute(values, "col", [(i, i ^ bit) for i in range(count)])


def by_source(blocks, me):
    stacked = jnp.stack(blocks)
    return jnp.take(stacked, me ^ jnp.arange(4), axis=0)


def rope_tables(count):
    places = jnp.arange(count, dtype=jnp.int32).astype(F32)
    inverse = 1.0 / THETA ** (jnp.arange(0, HEAD, 2).astype(F32) / HEAD)
    angles = places[:, None] * inverse[None, :]
    cosine = jnp.concatenate([jnp.cos(angles), jnp.cos(angles)], axis=-1)
    sine = jnp.concatenate([jnp.sin(angles), jnp.sin(angles)], axis=-1)
    return (cosine, sine)


def rotate(values, cosine, sine):
    half = values.shape[-1] // 2
    turned = jnp.concatenate([-values[..., half:], values[..., :half]], axis=-1)
    return values * cosine + turned * sine


def unrotate(grads, cosine, sine):
    half = grads.shape[-1] // 2
    weighted = grads * sine
    return grads * cosine + jnp.concatenate([weighted[..., half:], -weighted[..., :half]], axis=-1)


def gather_dp(block):
    n_dp = lax.axis_size("dp")
    rows = block.shape[0] // n_dp
    mine = lax.dynamic_slice_in_dim(block, lax.axis_index("dp") * rows, rows, 0)
    return lax.all_gather(flip(mine, 2), "dp", axis=0, tiled=True)


def body(
    layer_input,
    gain_attn,
    w_query,
    w_key,
    w_value,
    b_query,
    b_key,
    b_value,
    w_out,
    gain_ffn,
    w_gate,
    w_up,
    w_down,
    out_grad,
):
    n_dp = lax.axis_size("dp")
    dp, row, col = lax.axis_index("dp"), lax.axis_index("row"), lax.axis_index("col")
    half, feat = layer_input.shape
    seq, model = 2 * half, 4 * feat
    block = seq // 8
    units = w_gate.shape[1]
    part = -(-units // (4 * LANES)) * LANES
    padded = 4 * part
    query_cols = w_query.shape[1]
    heads = query_cols // HEAD

    w_qkv = jnp.concatenate([w_query, w_key, w_value], axis=1)
    gate_pad = jnp.pad(w_gate, ((0, 0), (0, padded - units)))
    up_pad = jnp.pad(w_up, ((0, 0), (0, padded - units)))
    down_pad = jnp.pad(w_down, ((0, padded - units), (0, 0)))
    mine_half, other_half = (col // 2) * 2 * part, (1 - col // 2) * 2 * part

    def cols_of(array, start, width):
        return lax.dynamic_slice_in_dim(array, start, width, 1)

    def rows_of(array, start, width):
        return lax.dynamic_slice_in_dim(array, start, width, 0)

    qkv_far = gather_dp(w_qkv)
    out_far = gather_dp(w_out)
    gate_far = gather_dp(cols_of(gate_pad, other_half, 2 * part))
    up_far = gather_dp(cols_of(up_pad, other_half, 2 * part))
    down_far = gather_dp(rows_of(down_pad, other_half, 2 * part))
    gate_own = cols_of(gate_pad, mine_half, 2 * part)
    up_own = cols_of(up_pad, mine_half, 2 * part)
    down_own = rows_of(down_pad, mine_half, 2 * part)
    mine, theirs = (col % 2) * part, (1 - col % 2) * part
    qkv_w = by_source([w_qkv, flip(w_qkv, 1), qkv_far, flip(qkv_far, 1)], col).reshape(model, -1)
    out_w = by_source([w_out, flip(w_out, 1), out_far, flip(out_far, 1)], col)
    out_w = out_w.transpose(1, 0, 2).reshape(-1, model)

    def quarter(own, far, pick):
        return by_source(
            [
                pick(own, mine, part),
                flip(pick(own, theirs, part), 1),
                pick(far, mine, part),
                flip(pick(far, theirs, part), 1),
            ],
            col,
        )

    gate_w = quarter(gate_own, gate_far, cols_of).reshape(model, part)
    up_w = quarter(up_own, up_far, cols_of).reshape(model, part)
    down_w = quarter(down_own, down_far, rows_of).transpose(1, 0, 2).reshape(part, model)

    def whole(array):
        stacked = lax.all_gather(array, ("row", "col"))
        return stacked.reshape(2, 4, half, feat).transpose(0, 2, 1, 3).reshape(seq, model)

    def mirror(array):
        return jnp.concatenate(
            [array[:half], array[half:].reshape(4, block, -1)[::-1].reshape(half, -1)]
        )

    inputs_all = whole(layer_input)
    grads_all = mirror(whole(out_grad))
    gain1 = lax.all_gather(gain_attn, "col", tiled=True).astype(F32)
    gain2 = lax.all_gather(gain_ffn, "col", tiled=True).astype(F32)
    low, high = col * block, (7 - col) * block
    shard = jnp.where(row == 0, low, high)

    def pair(array):
        return jnp.concatenate([rows_of(array, low, block), rows_of(array, high, block)])

    def normalize(values, gain):
        scale = lax.rsqrt(jnp.mean(values * values, axis=1, keepdims=True) + EPS)
        unit = values * scale
        return scale, unit, (unit * gain).astype(BF)

    def norm_back(d_normed, gain, scale, unit):
        bent = d_normed * gain
        mean_term = jnp.mean(bent * unit, axis=1, keepdims=True)
        return scale * (bent - unit * mean_term), jnp.sum(d_normed * unit, axis=0)

    _, _, normed1 = normalize(inputs_all.astype(F32), gain1)
    input_shard = rows_of(inputs_all, shard, block).astype(F32)
    scale1, unit1, _ = normalize(input_shard, gain1)

    cosine, sine = rope_tables(seq)
    cos_pair, sin_pair = pair(cosine), pair(sine)
    kv = dot(normed1, qkv_w[:, query_cols:], 1, 0)
    kv = kv + jnp.concatenate([b_key, b_value]).astype(F32)
    key = rotate(kv[:, :HEAD], cosine, sine).astype(BF)
    value = kv[:, HEAD:].astype(BF)
    queries = dot(pair(normed1), qkv_w[:, :query_cols], 1, 0) + b_query.astype(F32)
    queries = rotate(
        queries.reshape(2 * block, heads, HEAD), cos_pair[:, None, :], sin_pair[:, None, :]
    ).astype(BF)
    places = jnp.concatenate([low + jnp.arange(block), high + jnp.arange(block)])
    keep = jnp.arange(seq)[None, :] <= places[:, None]
    scaling = HEAD ** (-0.5)

    def scores_of():
        raw = jnp.einsum("thd,sd->hts", queries, key, preferred_element_type=F32)
        return jnp.where(keep[None], raw * scaling, NEG)

    scores = scores_of()
    top = jnp.max(scores, axis=-1)
    lse = top + jnp.log(jnp.sum(jnp.exp(scores - top[..., None]), axis=-1))
    probs = jnp.exp(scores - lse[..., None]).astype(BF)
    attn = jnp.einsum("hts,sd->thd", probs, value, preferred_element_type=F32)
    attn = attn.reshape(2 * block, query_cols).astype(BF)
    proj = lax.psum_scatter(
        dot(attn, out_w, 1, 0), "row", scatter_dimension=0, tiled=True
    )
    mid = input_shard + proj
    scale2, unit2, normed2 = normalize(mid, gain2)
    normed2_all = lax.all_gather(normed2, ("row", "col"), tiled=True)

    gate = dot(normed2_all, gate_w, 1, 0)
    up = dot(normed2_all, up_w, 1, 0)
    d_hidden = dot(grads_all, down_w, 1, 1)
    sig = jax.nn.sigmoid(gate)
    act = gate * sig
    hidden = (act * up).astype(BF)
    d_gate = (d_hidden * up * sig * (1.0 + gate * (1.0 - sig))).astype(BF)
    d_up = (d_hidden * act).astype(BF)
    d_normed2_part = dot(d_gate, gate_w, 1, 1) + dot(d_up, up_w, 1, 1)

    def shards_sum(partial):
        return lax.psum_scatter(
            partial.astype(BF), ("row", "col"), scatter_dimension=0, tiled=True
        ).astype(F32)

    d_normed2 = shards_sum(d_normed2_part)
    start = (row * 4 + col) * block
    ffn = dot(hidden, down_w, 1, 0)
    ffn = lax.dynamic_update_slice_in_dim(ffn, rows_of(ffn, start, block) + mid, start, 0)
    ffn = mirror(ffn).reshape(2, half, 4, feat).transpose(0, 2, 1, 3).reshape(8 * half, feat)
    layer_output = shards_sum(ffn)

    def sum_dp(grad):
        rows = grad.shape[1] // n_dp
        sliced = grad.astype(BF).reshape(4, n_dp, rows, -1).transpose(1, 0, 2, 3)
        mine = lax.psum_scatter(sliced, "dp", scatter_dimension=0, tiled=True)[0]
        return lax.all_to_all(mine, "col", 0, 0, tiled=True)

    def spread(grad):
        return lax.all_gather(grad, "dp", axis=0, tiled=True).astype(F32)

    def down_order(grad):
        return grad.reshape(part, 4, feat).transpose(1, 0, 2)

    grad_down = sum_dp(down_order(dot(hidden, grads_all, 0, 0)))
    grad_gate = sum_dp(dot(normed2_all, d_gate, 0, 0).reshape(4, feat, part))
    grad_up = sum_dp(dot(normed2_all, d_up, 0, 0).reshape(4, feat, part))

    d_mid_norm, grad_gain_ffn = norm_back(d_normed2, gain2, scale2, unit2)
    d_mid = rows_of(grads_all, start, block).astype(F32) + d_mid_norm
    d_mid_low = d_mid.astype(BF)
    d_mid_all = lax.all_gather(d_mid_low, ("row", "col"))
    d_mid_cols = cols_of(d_mid_all.reshape(seq, model), col * feat, feat)
    d_mid_cols = d_mid_cols.reshape(2, 4, block, feat).transpose(1, 0, 2, 3).reshape(seq, feat)
    d_mid_pair = lax.dynamic_slice_in_dim(d_mid_all, col, 1, 0)
    d_mid_pair = jnp.concatenate([d_mid_pair, lax.dynamic_slice_in_dim(d_mid_all, col + 4, 1, 0)])
    d_mid_pair = d_mid_pair.reshape(2 * block, model)
    attn_all = lax.all_gather(attn, "col", tiled=True)
    grad_out = dot(attn_all, d_mid_cols, 0, 0)
    d_attn = dot(d_mid_pair, out_w, 1, 1).astype(BF).reshape(2 * block, heads, HEAD)

    exact = jnp.exp(scores_of() - lse[..., None])
    d_probs = jnp.einsum("thd,sd->hts", d_attn, value, preferred_element_type=F32)
    inner = jnp.sum(exact * d_probs, axis=-1)
    d_scores = (exact * (d_probs - inner[..., None]) * scaling).astype(BF)
    d_query = jnp.einsum("hts,sd->thd", d_scores, key, preferred_element_type=F32)
    d_key = jnp.einsum("hts,thd->sd", d_scores, queries, preferred_element_type=F32)
    d_value = jnp.einsum("hts,thd->sd", exact.astype(BF), d_attn, preferred_element_type=F32)
    d_kv = jnp.concatenate([d_key, d_value], axis=1)
    d_kv = jnp.stack([d_kv[:half].reshape(4, block, -1), d_kv[half:].reshape(4, block, -1)[::-1]], 1)
    d_kv = lax.psum_scatter(
        d_kv.reshape(seq, 2 * HEAD), "col", scatter_dimension=0, tiled=True
    )
    d_query = unrotate(d_query, cos_pair[:, None, :], sin_pair[:, None, :])
    d_key = unrotate(d_kv[:, :HEAD], cos_pair, sin_pair)
    d_qkv = jnp.concatenate(
        [d_query.reshape(2 * block, query_cols), d_key, d_kv[:, HEAD:]], axis=1
    ).astype(BF)
    d_normed1 = lax.psum_scatter(dot(d_qkv, qkv_w, 1, 1), "row", scatter_dimension=0, tiled=True)
    d_qkv_all = lax.all_gather(d_qkv, "col", tiled=True)
    normed1_cols = cols_of(normed1, col * feat, feat)
    normed1_cols = jnp.stack(
        [normed1_cols[:half].reshape(4, block, -1), normed1_cols[half:].reshape(4, block, -1)[::-1]],
        1,
    ).reshape(seq, feat)
    grad_qkv = dot(normed1_cols, d_qkv_all, 0, 0)
    grad_bias = jnp.sum(d_qkv_all.astype(F32), axis=0)
    d_in_norm, grad_gain_attn = norm_back(d_normed1, gain1, scale1, unit1)
    grad_input = (d_mid + d_in_norm).astype(BF)
    grad_input = lax.all_to_all(
        grad_input.reshape(block, 4, feat).transpose(1, 0, 2), "col", 0, 0, tiled=True
    )
    grad_input = jnp.where(row == 0, grad_input, grad_input[::-1]).reshape(half, feat).astype(F32)

    def sum_all(grad):
        mine = lax.psum_scatter(grad.astype(BF), "dp", scatter_dimension=0, tiled=True)
        return spread(mine)

    grad_qkv = sum_all(grad_qkv)
    grad_out = sum_all(grad_out)
    gains = lax.psum(jnp.stack([grad_gain_attn, grad_gain_ffn]), ("dp", "row", "col"))
    gains = cols_of(gains, col * feat, feat)
    grad_bias = lax.psum(grad_bias, "dp")

    def join(grad):
        return spread(grad.transpose(1, 0, 2).reshape(grad.shape[1], padded)[:, :units])

    def join_down(grad):
        joined = grad.reshape(4, grad.shape[1], feat)
        gathered = lax.all_gather(joined, "dp", axis=1, tiled=True)
        return gathered.reshape(padded, feat)[:units].astype(F32)

    return (
        layer_output,
        grad_input,
        gains[0],
        grad_qkv[:, :query_cols],
        grad_qkv[:, query_cols : query_cols + HEAD],
        grad_qkv[:, query_cols + HEAD :],
        grad_bias[:query_cols],
        grad_bias[query_cols : query_cols + HEAD],
        grad_bias[query_cols + HEAD :],
        grad_out,
        gains[1],
        join(grad_gate),
        join(grad_up),
        join_down(grad_down),
    )


def solution(mesh):
    in_specs = (
        P(("dp", "row"), "col"),
        P("col"),
        P("col", "row"),
        P("col", "row"),
        P("col", "row"),
        P("row"),
        P("row"),
        P("row"),
        P("row", "col"),
        P("col"),
        P("col", "row"),
        P("col", "row"),
        P("row", "col"),
        P(("dp", "row"), "col"),
    )
    out_specs = (
        P(("dp", "row"), "col"),
        P(("dp", "row"), "col"),
        P("col"),
        P("col", "row"),
        P("col", "row"),
        P("col", "row"),
        P("row"),
        P("row"),
        P("row"),
        P("row", "col"),
        P("col"),
        P("col", "row"),
        P("col", "row"),
        P("row", "col"),
    )
    return jax.shard_map(body, mesh=mesh, in_specs=in_specs, out_specs=out_specs, check_vma=False)
```

```python
import functools

import jax
import jax.numpy as jnp
from jax import lax
from jax.experimental import pallas as pl
from jax.experimental.pallas import tpu as pltpu
from jax.sharding import PartitionSpec as P

EPS = 1e-06
THETA = 1000000.0
NEG = -1e30
BF = jnp.bfloat16
F32 = jnp.float32
MESH = pl.DeviceIdType.MESH
HEAD = 128
HEADS = 6
SEQ = 1024
MODEL = 1536
FEAT = 384
BLOCK = 128
UNITS = 4480
PART = 1152
QCOLS = 768
QKV = 1024
VMEM_LIMIT = 62 * 2**20
SCALE = HEAD ** (-0.5)


def dot(left, right, left_dim=1, right_dim=0):
    return lax.dot_general(
        left, right, (((left_dim,), (right_dim,)), ((), ())), preferred_element_type=F32
    )


def aligned(index, step):
    return pl.multiple_of(index * step, step)


def block_of(row, col):
    return col + row * (7 - 2 * col)


def quarter_start(col):
    return pl.multiple_of(col * PART - (col // 3) * HEAD, HEAD)


class Place:
    def __init__(self):
        self.dp, self.row, self.col = (lax.axis_index(a) for a in ("dp", "row", "col"))
        self.hi, self.core = self.col // 2, self.col % 2
        self.z, self.y = self.dp // 4, self.dp % 4
        self.sib = 2 * self.hi + 1 - self.core
        self.far = 2 * (1 - self.hi) + self.core
        self.sibfar = 2 * (1 - self.hi) + 1 - self.core
        self.block = block_of(self.row, self.col)
        self.S = {"col": self.sib}
        self.O = {"col": self.far}
        self.OS = {"col": self.sibfar}
        self.N1 = {"row": 1 - self.row}
        self.N2 = {"row": 1 - self.row, "col": self.far}
        self.N1S = {"row": 1 - self.row, "col": self.sib}
        self.N2S = {"row": 1 - self.row, "col": self.sibfar}

        def dp_at(z, y):
            return {"dp": lax.rem(z + 4, 4) * 4 + lax.rem(y + 4, 4)}

        self.YP, self.YM = dp_at(self.z, self.y + 1), dp_at(self.z, self.y - 1)
        self.ZP, self.ZM = dp_at(self.z + 1, self.y), dp_at(self.z - 1, self.y)

    def meet(self, partners):
        barrier = pltpu.get_barrier_semaphore()
        for device in partners:
            pl.semaphore_signal(barrier, inc=1, device_id=device, device_id_type=MESH)
        pl.semaphore_wait(barrier, len(partners))


class Net:
    def __init__(self, send_sems, recv_sems, at):
        self.ss, self.rs, self.at, self.count, self.sent = send_sems, recv_sems, at, 0, []

    def key(self):
        self.count += 1
        return self.count - 1

    def copy(self, key, src, dst, device):
        return pltpu.make_async_remote_copy(
            src_ref=src,
            dst_ref=dst,
            send_sem=self.ss.at[key],
            recv_sem=self.rs.at[key],
            device_id=device,
            device_id_type=MESH,
        )

    def send(self, src, dst, device):
        key = self.key()
        copy = self.copy(key, src, dst, device)
        copy.start()
        self.sent.append(copy)
        return key

    def take(self, key, dst):
        self.copy(key, dst, dst, self.at.S).wait_recv()

    def finish(self):
        for copy in self.sent:
            copy.wait_send()


class Gather8:
    def __init__(self, net, at, place):
        self.net, self.at, self.place = net, at, place

    def start(self, src):
        net, at = self.net, self.at
        mine = self.place(at.row, at.col, None)
        self.k1 = net.send(src, mine, at.N1)
        self.k2 = net.send(src, mine, at.N2)
        self.k0 = net.send(src, mine, at.S)

    def middle(self):
        net, at, place = self.net, self.at, self.place
        near, away = place(1 - at.row, at.col, None), place(1 - at.row, at.far, None)
        first, last = place(1 - at.row, at.col, 0), place(1 - at.row, at.far, 1)
        net.take(self.k1, near)
        self.ka = net.send(first, first, at.N2)
        self.f1 = net.send(near, near, at.S)
        net.take(self.k2, away)
        self.kb = net.send(last, last, at.N1)
        self.f2 = net.send(away, away, at.S)

    def late(self):
        net, at, place = self.net, self.at, self.place
        first, last = place(at.row, at.far, 0), place(at.row, at.far, 1)
        net.take(self.ka, first)
        self.f3 = net.send(first, first, at.S)
        net.take(self.kb, last)
        self.f4 = net.send(last, last, at.S)

    def end(self):
        net, at, place = self.net, self.at, self.place
        net.take(self.k0, place(at.row, at.sib, None))
        net.take(self.f1, place(1 - at.row, at.sib, None))
        net.take(self.f2, place(1 - at.row, at.sibfar, None))
        net.take(self.f3, place(at.row, at.sibfar, 0))
        net.take(self.f4, place(at.row, at.sibfar, 1))


def ring_dp(net, at, halves):
    def wrap(index):
        return lax.rem(index + 4, 4)

    sides = (((at.YP, at.YM), (at.ZP, at.ZM)), ((at.ZP, at.ZM), (at.YP, at.YM)))
    firsts, seconds = (at.y, at.z), (at.z, at.y)

    def refs(i, a, b):
        return halves[i](b, a) if i == 0 else halves[i](a, b)

    def send(i, a, b, device):
        return [net.send(ref, ref, device) for ref in refs(i, a, b)]

    def take(i, a, b, keys):
        for key, ref in zip(keys, refs(i, a, b), strict=True):
            net.take(key, ref)

    one, two, onward = {}, {}, {}
    for i in (0, 1):
        one[i] = [send(i, firsts[i], seconds[i], side) for side in sides[i][0]]
    for i in (0, 1):
        two[i, 0] = [send(i, firsts[i], seconds[i], side) for side in sides[i][1]]
    yield
    for i in (0, 1):
        minus = wrap(firsts[i] - 1)
        take(i, minus, seconds[i], one[i][0])
        one[i].append(send(i, minus, seconds[i], sides[i][0][0]))
        two[i, 1] = [send(i, minus, seconds[i], side) for side in sides[i][1]]
    yield
    for i in (0, 1):
        plus = wrap(firsts[i] + 1)
        take(i, plus, seconds[i], one[i][1])
        two[i, 2] = [send(i, plus, seconds[i], side) for side in sides[i][1]]
    offsets = (0, -1, 1, 2)
    for q in (0, 1, 2, 3):
        yield
        for i in (0, 1):
            if q == 1:
                across = wrap(firsts[i] + 2)
                take(i, across, seconds[i], one[i][2])
                two[i, 3] = [send(i, across, seconds[i], side) for side in sides[i][1]]
            slot = wrap(firsts[i] + offsets[q])
            minus, plus = wrap(seconds[i] - 1), wrap(seconds[i] + 1)
            take(i, slot, minus, two[i, q][0])
            if q < 2:
                onward[i, q] = send(i, slot, minus, sides[i][1][0])
            take(i, slot, plus, two[i, q][1])
            if q >= 2:
                onward[i, q] = send(i, slot, plus, sides[i][1][1])
    for q in (0, 1, 2, 3):
        yield
        for i in (0, 1):
            slot = wrap(firsts[i] + offsets[q])
            take(i, slot, wrap(seconds[i] + 2), onward[i, q])


def drain(steps):
    for _ in steps:
        pass


def rms(values):
    return lax.rsqrt(jnp.mean(values * values, axis=1, keepdims=True) + EPS)


def turn(values):
    return pltpu.roll(values, HEAD // 2, 1)


def causal(scores, start):
    places = start + lax.broadcasted_iota(jnp.int32, scores.shape, 0)
    keys = lax.broadcasted_iota(jnp.int32, scores.shape, 1)
    return jnp.where(keys <= places, scores, NEG)


def forward_kernel(
    x_ref,
    og_ref,
    wqkv_ref,
    wout_ref,
    wg_ref,
    wu_ref,
    wd_ref,
    gains_ref,
    bias_ref,
    cos_ref,
    sin_ref,
    xs_ref,
    n1c_ref,
    og_all,
    n2_all,
    qw,
    ow,
    gw,
    uw,
    dw,
    q_ref,
    k_ref,
    v_ref,
    lse_ref,
    attn_ref,
    mid_ref,
    gains_all,
    x_all,
    n1,
    part_out,
    part_in,
    send_sems,
    recv_sems,
    local_sems,
):
    at = Place()
    net = Net(send_sems, recv_sems, at)
    at.meet((at.S, at.N1, at.N2, at.O, at.OS, at.YP, at.YM, at.ZP, at.ZM))
    local = []

    def move(src, dst):
        copy = pltpu.make_async_copy(src, dst, local_sems.at[len(local)])
        copy.start()
        local.append(copy)

    def tokens_of(array):
        def place(row, col, part):
            if part is None:
                rows = pl.ds(aligned(row, SEQ // 2), SEQ // 2)
            else:
                rows = pl.ds(aligned(row * 2 + part, SEQ // 4), SEQ // 4)
            return array.at[rows, pl.ds(aligned(col, FEAT), FEAT)]

        return place

    mine, mine_far = aligned(at.col, FEAT), aligned(1 - at.hi, 2 * FEAT)
    move(x_ref, tokens_of(x_all)(at.row, at.col, None))
    move(wqkv_ref, qw.at[pl.ds(mine, FEAT), :])
    move(wout_ref, ow.at[:, pl.ds(mine, FEAT)])
    move(gains_ref, gains_all.at[:, pl.ds(mine, FEAT)])
    start = quarter_start(at.col)
    move(wg_ref.at[:, pl.ds(start, PART)], gw.at[pl.ds(mine, FEAT), :])
    move(wu_ref.at[:, pl.ds(start, PART)], uw.at[pl.ds(mine, FEAT), :])
    move(wd_ref.at[pl.ds(start, PART), :], dw.at[:, pl.ds(mine, FEAT)])
    move(og_ref, tokens_of(og_all)(at.row, at.col, None))

    eighth = at.dp % 8
    across = [net.key() for _ in range(5)]

    def slice_copies(core, first, last):
        device = {"col": 2 * (1 - at.hi) + core}
        rows = pl.ds(aligned(eighth, 48), 48)
        target = pl.ds(pl.multiple_of(mine + eighth * 48, 16), 48)
        columns = pl.ds(core * 512, 512)
        out_rows = pl.ds(pl.multiple_of(core * FEAT + eighth * 48, 16), 48)
        theirs = quarter_start(2 * (1 - at.hi) + core)
        down_rows = pl.ds(pl.multiple_of(theirs + eighth * 144, 16), 144)
        down_target = pl.ds(aligned(eighth, 144), 144)
        pairs = (
            (wqkv_ref.at[rows, columns], qw.at[target, columns]),
            (wout_ref.at[out_rows, :], ow.at[out_rows, pl.ds(mine, FEAT)]),
            (wg_ref.at[rows, pl.ds(theirs, PART)], gw.at[target, :]),
            (wu_ref.at[rows, pl.ds(theirs, PART)], uw.at[target, :]),
            (wd_ref.at[down_rows, :], dw.at[down_target, pl.ds(mine, FEAT)]),
        )
        return [
            pltpu.make_async_remote_copy(
                src_ref=pairs[i][0],
                dst_ref=pairs[i][1],
                send_sem=net.ss.at[spare[core][i]],
                recv_sem=net.rs.at[across[i]],
                device_id=device,
                device_id_type=MESH,
            )
            for i in range(first, last)
        ]

    spare = ([net.key() for _ in range(5)], [net.key() for _ in range(5)])
    chosen = at.core == at.dp // 8

    @pl.when(chosen)
    def _():
        for core in (0, 1):
            for copy in slice_copies(core, 0, 2):
                copy.start()

    gather_x = Gather8(net, at, tokens_of(x_all))
    gather_x.start(x_ref)
    gain_far = net.send(gains_ref, gains_all.at[:, pl.ds(mine, FEAT)], at.N2)
    gain_sib = net.send(gains_ref, gains_all.at[:, pl.ds(mine, FEAT)], at.S)
    near_qw = net.send(wqkv_ref, qw.at[pl.ds(mine, FEAT), :], at.S)
    near_ow = net.send(wout_ref, ow.at[:, pl.ds(mine, FEAT)], at.S)

    @pl.when(chosen)
    def _():
        for core in (0, 1):
            for copy in slice_copies(core, 2, 5):
                copy.start()

    far_half = pl.ds(mine_far, 2 * FEAT)

    def qkv_slices(z, y):
        rows = pl.ds(pl.multiple_of(mine_far + (z * 4 + y) * 48, 16), 48)
        return [qw.at[rows, pl.ds(aligned(at.core, 512), 512)]]

    def out_slices(z, y):
        index = z * 4 + y
        rows = pl.ds(pl.multiple_of(at.core * FEAT + (index % 8) * 48, 16), 48)
        return [ow.at[rows, pl.ds(pl.multiple_of(mine_far + (index // 8) * FEAT, HEAD), FEAT)]]

    def ffn_slices(weights, first, count):
        def slices(z, y):
            index = z * 4 + y
            rows = pl.ds(pl.multiple_of(mine_far + index * 48, 16), 48)
            down_rows = pl.ds(pl.multiple_of((index % 8) * 144 + first, 16), count)
            lanes = pl.ds(pl.multiple_of(mine_far + (index // 8) * FEAT, HEAD), FEAT)
            return [weights.at[rows, :], dw.at[down_rows, lanes]]

        return slices

    net.take(across[0], qkv_slices(at.z, at.y)[0])
    net.take(across[1], out_slices(at.z, at.y)[0])
    ring = ring_dp(net, at, (qkv_slices, out_slices))
    next(ring)
    near = [
        net.send(wg_ref.at[:, pl.ds(quarter_start(at.sib), PART)], gw.at[pl.ds(mine, FEAT), :], at.S),
        net.send(wu_ref.at[:, pl.ds(quarter_start(at.sib), PART)], uw.at[pl.ds(mine, FEAT), :], at.S),
        net.send(wd_ref.at[pl.ds(quarter_start(at.sib), PART), :], dw.at[:, pl.ds(mine, FEAT)], at.S),
    ]
    next(ring)
    next(ring)
    gather_x.middle()
    gains_far = gains_all.at[:, pl.ds(aligned(at.far, FEAT), FEAT)]
    net.take(gain_far, gains_far)
    gain_sibfar = net.send(gains_far, gains_far, at.S)
    next(ring)
    gather_og = Gather8(net, at, tokens_of(og_all))
    gather_x.late()
    gather_og.start(og_ref)
    drain(ring)
    cols_half, rows_half = pl.ds(aligned(at.core, 512), 512), pl.ds(aligned(at.core, FEAT), FEAT)
    far_qw = net.send(qw.at[far_half, cols_half], qw.at[far_half, cols_half], at.S)
    far_ow = net.send(ow.at[rows_half, far_half], ow.at[rows_half, far_half], at.S)
    net.take(across[2], ffn_slices(gw, 0, 80)(at.z, at.y)[0])
    net.take(across[3], ffn_slices(uw, 80, 64)(at.z, at.y)[0])
    net.take(across[4], ffn_slices(uw, 0, 144)(at.z, at.y)[1])
    ring = ring_dp(net, at, (ffn_slices(gw, 0, 80), ffn_slices(uw, 80, 64)))
    next(ring)
    gather_x.end()
    net.take(gain_sib, gains_all.at[:, pl.ds(aligned(at.sib, FEAT), FEAT)])
    net.take(gain_sibfar, gains_all.at[:, pl.ds(aligned(at.sibfar, FEAT), FEAT)])
    for copy in local:
        copy.wait()

    gain1, gain2 = gains_all[0:1, :], gains_all[1:2, :]

    def norm_block(i, carry):
        rows = pl.ds(aligned(i, BLOCK), BLOCK)
        values = x_all[rows, :].astype(F32)
        n1[rows, :] = (values * rms(values) * gain1).astype(BF)
        return carry

    lax.fori_loop(0, SEQ // BLOCK, norm_block, 0)
    next(ring)
    gather_og.middle()
    my_rows = pl.ds(aligned(at.block, BLOCK), BLOCK)
    xs_ref[...] = x_all[my_rows, :]
    n1c_ref[...] = n1[:, pl.ds(mine, FEAT)]
    net.take(near_qw, qw.at[pl.ds(aligned(at.sib, FEAT), FEAT), :])
    other_cols = pl.ds(aligned(1 - at.core, 512), 512)
    net.take(far_qw, qw.at[far_half, other_cols])

    def kv_block(i, carry):
        rows = pl.ds(aligned(i, 256), 256)
        both = dot(n1[rows, :], qw[:, QCOLS:]) + bias_ref[:, QCOLS:]
        key = both[:, :HEAD]
        k_ref[rows, :] = (key * cos_ref[rows, :] + turn(key) * sin_ref[rows, :]).astype(BF)
        v_ref[rows, :] = both[:, HEAD:].astype(BF)
        return carry

    lax.fori_loop(0, SEQ // 256, kv_block, 0)
    next(ring)
    pair = (at.col, 7 - at.col)
    for j in (0, 1):
        rows = pl.ds(aligned(pair[j], BLOCK), BLOCK)
        queries = dot(n1[rows, :], qw[:, :QCOLS]) + bias_ref[:, :QCOLS]
        cosine, sine = cos_ref[rows, :], sin_ref[rows, :]
        for h in range(HEADS):
            one = queries[:, h * HEAD : (h + 1) * HEAD]
            q_ref[pl.ds(j * BLOCK, BLOCK), pl.ds(h * HEAD, HEAD)] = (
                one * cosine + turn(one) * sine
            ).astype(BF)
    next(ring)
    gather_og.late()

    for j in (0, 1):
        keys = SEQ // 2 * (j + 1)
        rows = pl.ds(j * BLOCK, BLOCK)

        def attend(h, carry):
            lanes = pl.ds(aligned(h, HEAD), HEAD)
            scores = dot(q_ref[rows, lanes], k_ref[:keys, :], 1, 1) * SCALE
            scores = causal(scores, pair[j] * BLOCK)
            top = jnp.max(scores, axis=1, keepdims=True)
            weights = jnp.exp(scores - top)
            total = jnp.sum(weights, axis=1, keepdims=True)
            lse_ref[j * HEADS + h] = top + jnp.log(total)
            probs = (weights * (1.0 / total)).astype(BF)
            attn_ref[rows, lanes] = dot(probs, v_ref[:keys, :]).astype(BF)
            return carry

        lax.fori_loop(0, HEADS, attend, 0)
        next(ring)

    net.take(near_ow, ow.at[:, pl.ds(aligned(at.sib, FEAT), FEAT)])
    other_rows = pl.ds(aligned(1 - at.core, FEAT), FEAT)
    net.take(far_ow, ow.at[other_rows, far_half])
    part_out[...] = dot(attn_ref[pl.ds(aligned(1 - at.row, BLOCK), BLOCK), :], ow[...]).astype(BF)
    part = net.send(part_out, part_in, at.N1)
    own = dot(attn_ref[pl.ds(aligned(at.row, BLOCK), BLOCK), :], ow[...])
    next(ring)
    net.take(part, part_in)
    mid = xs_ref[...].astype(F32) + own + part_in[...].astype(F32)
    mid_ref[...] = mid

    def place_n2(row, col, part):
        first = block_of(row, col) * BLOCK
        if part is None:
            return n2_all.at[pl.ds(pl.multiple_of(first, BLOCK), BLOCK), :]
        return n2_all.at[pl.ds(pl.multiple_of(first + part * 64, 64), 64), :]

    n2_all[my_rows, :] = (mid * rms(mid) * gain2).astype(BF)
    gather_n2 = Gather8(net, at, place_n2)
    gather_n2.start(place_n2(at.row, at.col, None))
    gather_og.end()
    next(ring)
    gather_n2.middle()
    drain(ring)
    gather_n2.late()
    net.take(near[0], gw.at[pl.ds(aligned(at.sib, FEAT), FEAT), :])
    net.take(near[1], uw.at[pl.ds(aligned(at.sib, FEAT), FEAT), :])
    net.take(near[2], dw.at[:, pl.ds(aligned(at.sib, FEAT), FEAT)])
    gather_n2.end()
    net.finish()

    @pl.when(chosen)
    def _():
        for core in (0, 1):
            for copy in slice_copies(core, 0, 5):
                copy.wait_send()


def vmem():
    return pl.BlockSpec(memory_space=pltpu.VMEM)


def anywhere():
    return pl.BlockSpec(memory_space=pl.ANY)


def run_forward(x, og, wqkv, wout, wg, wu, wd, gains, bias, cosine, sine):
    def out(shape, dtype):
        return jax.ShapeDtypeStruct(shape, dtype)

    outs = (
        out((BLOCK, MODEL), BF),
        out((SEQ, FEAT), BF),
        out((SEQ, MODEL), BF),
        out((SEQ, MODEL), BF),
        out((MODEL, QKV), BF),
        out((QCOLS, MODEL), BF),
        out((MODEL, PART), BF),
        out((MODEL, PART), BF),
        out((PART, MODEL), BF),
        out((2 * BLOCK, QCOLS), BF),
        out((SEQ, HEAD), BF),
        out((SEQ, HEAD), BF),
        out((2 * HEADS, BLOCK, 1), F32),
        out((2 * BLOCK, QCOLS), BF),
        out((BLOCK, MODEL), F32),
        out((8, MODEL), F32),
    )
    return pl.pallas_call(
        forward_kernel,
        out_shape=outs,
        in_specs=[vmem()] * 4 + [anywhere()] * 3 + [vmem()] * 4,
        out_specs=[vmem()] * len(outs),
        scratch_shapes=[
            pltpu.VMEM((SEQ, MODEL), BF),
            pltpu.VMEM((SEQ, MODEL), BF),
            pltpu.VMEM((BLOCK, MODEL), BF),
            pltpu.VMEM((BLOCK, MODEL), BF),
            pltpu.SemaphoreType.DMA((160,)),
            pltpu.SemaphoreType.DMA((160,)),
            pltpu.SemaphoreType.DMA((8,)),
        ],
        compiler_params=pltpu.CompilerParams(
            collective_id=0, has_side_effects=True, vmem_limit_bytes=VMEM_LIMIT
        ),
        cost_estimate=pl.CostEstimate(
            flops=8 * 10**9, bytes_accessed=60 * 10**6, transcendentals=2 * 10**6
        ),
        name="attention_forward",
    )(x, og, wqkv, wout, wg, wu, wd, gains, bias, cosine, sine)


class Reduce8:
    def __init__(self, net, at, own, other, sib_in, first_in, last_in, near_in, away_in):
        self.net, self.at, self.own, self.other, self.sib_in = net, at, own, other, sib_in
        self.first_in, self.last_in, self.near_in, self.away_in = first_in, last_in, near_in, away_in
        self.half = own.shape[1] // 2
        self.keys = {}

    def put(self, j, mine, theirs):
        self.own[j] = mine
        self.other[j] = theirs
        self.keys[j] = self.net.send(self.other.at[j], self.sib_in.at[j], self.at.S)

    def step(self, j):
        net, at, half = self.net, self.at, self.half
        net.take(self.keys[j], self.sib_in.at[j])
        total = self.own[j].astype(F32) + self.sib_in[j].astype(F32)
        if j == 0:
            self.own[j] = total.astype(BF)
            self.first = net.send(self.own.at[j, pl.ds(0, half)], self.first_in, at.N1)
            self.last = net.send(self.own.at[j, pl.ds(half, half)], self.last_in, at.N2)
        elif j == 1:
            net.take(self.last, self.last_in)
            self.own[j, :half] = total[:half].astype(BF)
            self.own[j, half:] = (total[half:] + self.last_in[...].astype(F32)).astype(BF)
            self.near = net.send(self.own.at[j], self.near_in, at.N1)
        elif j == 2:
            net.take(self.first, self.first_in)
            self.own[j, :half] = (total[:half] + self.first_in[...].astype(F32)).astype(BF)
            self.own[j, half:] = total[half:].astype(BF)
            self.away = net.send(self.own.at[j], self.away_in, at.N2)
        else:
            net.take(self.near, self.near_in)
            net.take(self.away, self.away_in)
            return total + self.near_in[...].astype(F32) + self.away_in[...].astype(F32)
        return None


def reduce8_scratch(rows, columns):
    return [
        pltpu.VMEM((4, rows, columns), BF),
        pltpu.VMEM((4, rows, columns), BF),
        pltpu.VMEM((4, rows, columns), BF),
        pltpu.VMEM((rows // 2, columns), BF),
        pltpu.VMEM((rows // 2, columns), BF),
        pltpu.VMEM((rows, columns), BF),
        pltpu.VMEM((rows, columns), BF),
    ]


def tiles_of(width, step):
    return [(first, min(step, width - first)) for first in range(0, width, step)]


def outer_sum(left, right, out):
    width = right.shape[1]
    height = left.shape[1] // 2

    def tile(lanes):
        for i in (0, 1):
            rows = pl.ds(i * height, height)
            out[rows, lanes] = dot(left[:, rows], right[:, lanes], 0, 0).astype(BF)

    def step(n, carry):
        tile(pl.ds(aligned(n, 256), 256))
        return carry

    lax.fori_loop(0, width // 256, step, 0)
    if width % 256:
        tile(pl.ds(width // 256 * 256, width % 256))


def ffn_kernel(
    n2,
    og,
    gw,
    uw,
    dw,
    mid_ref,
    dn2_ref,
    out_ref,
    grad_gate,
    grad_up,
    grad_down,
    hidden,
    d_gate,
    d_up,
    ffn,
    *rest,
):
    red_a, red_b, (send_sems, recv_sems) = rest[:7], rest[7:14], rest[14:]
    at = Place()
    net = Net(send_sems, recv_sems, at)
    at.meet((at.S, at.N1, at.N2))
    norms = Reduce8(net, at, *red_a)
    outs = Reduce8(net, at, *red_b)
    chips = ((at.row, 1 - at.hi), (1 - at.row, at.hi), (1 - at.row, 1 - at.hi), (at.row, at.hi))
    last_part = at.col == 3

    def tokens(j):
        row, hi = chips[j]
        first = 2 * hi + row * (6 - 4 * hi)
        return pl.ds(aligned(first, BLOCK), 256), at.core + row * (1 - 2 * at.core)

    for j in range(4):
        rows, place = tokens(j)
        for first, width in tiles_of(PART, 512):
            lanes = pl.ds(first, width)
            gate = dot(n2[rows, :], gw[:, lanes])
            up = dot(n2[rows, :], uw[:, lanes])
            d_hidden = dot(og[rows, :], dw[lanes, :], 1, 1)
            sig = jax.nn.sigmoid(gate)
            act = gate * sig
            d_act = d_hidden * up * sig * (1.0 + gate * (1.0 - sig))
            values = [act * up, d_act, d_hidden * act]
            if first == 0:
                lane = lax.broadcasted_iota(jnp.int32, (1, width), 1)
                fresh = jnp.logical_or(lane >= HEAD, jnp.logical_not(last_part))
                values = [jnp.where(fresh, value, 0.0) for value in values]
            for ref, value in zip((hidden, d_gate, d_up), values, strict=True):
                ref[rows, lanes] = value.astype(BF)
        own_rows = pl.ds(pl.multiple_of(rows.start + place * BLOCK, BLOCK), BLOCK)
        other_rows = pl.ds(pl.multiple_of(rows.start + (1 - place) * BLOCK, BLOCK), BLOCK)
        parts = [
            (dot(d_gate[r, :], gw[...], 1, 1) + dot(d_up[r, :], uw[...], 1, 1)).astype(BF)
            for r in (other_rows, own_rows)
        ]
        norms.put(j, parts[1], parts[0])
        if j:
            norms.step(j - 1)

    outer_sum(hidden, og, grad_down)

    for j in range(4):
        row, hi = chips[j]
        rows = pl.ds(aligned(row, SEQ // 2), SEQ // 2)
        lanes = pl.ds(aligned(hi, QCOLS), QCOLS)
        ffn[...] = dot(hidden[rows, :], dw[:, lanes])
        if j in (0, 3):
            mine = pl.ds(pl.multiple_of((at.block - 4 * at.row) * BLOCK, BLOCK), BLOCK)
            ffn[mine, :] += mid_ref[:, lanes]
        own = ffn[:, pl.ds(aligned(at.core, FEAT), FEAT)].astype(BF)
        outs.put(j, own, ffn[:, pl.ds(aligned(1 - at.core, FEAT), FEAT)].astype(BF))
        if j:
            outs.step(j - 1)
        if j == 1:
            dn2_ref[...] = norms.step(3)

    outer_sum(n2, d_gate, grad_gate)
    outer_sum(n2, d_up, grad_up)
    out_ref[...] = outs.step(3)
    net.finish()


def run_ffn(n2, og, gw, uw, dw, mid):
    def out(shape, dtype):
        return jax.ShapeDtypeStruct(shape, dtype)

    outs = (
        out((BLOCK, MODEL), F32),
        out((SEQ // 2, FEAT), F32),
        out((MODEL, PART), BF),
        out((MODEL, PART), BF),
        out((PART, MODEL), BF),
    )
    return pl.pallas_call(
        ffn_kernel,
        out_shape=outs,
        in_specs=[vmem()] * 6,
        out_specs=[vmem()] * len(outs),
        scratch_shapes=[pltpu.VMEM((SEQ, PART), BF)] * 3
        + [pltpu.VMEM((SEQ // 2, QCOLS), F32)]
        + reduce8_scratch(BLOCK, MODEL)
        + reduce8_scratch(SEQ // 2, FEAT)
        + [pltpu.SemaphoreType.DMA((32,)), pltpu.SemaphoreType.DMA((32,))],
        compiler_params=pltpu.CompilerParams(
            collective_id=1, has_side_effects=True, vmem_limit_bytes=VMEM_LIMIT
        ),
        cost_estimate=pl.CostEstimate(
            flops=29 * 10**9, bytes_accessed=60 * 10**6, transcendentals=2 * 10**6
        ),
        name="feed_forward",
    )(n2, og, gw, uw, dw, mid)


def backward_kernel(
    dn2_ref,
    mid_ref,
    og_ref,
    gains_all,
    xs_ref,
    n1c,
    attn_ref,
    q_ref,
    k_ref,
    v_ref,
    lse_ref,
    ow,
    qw,
    cos_ref,
    sin_ref,
    grad_in,
    grad_out,
    grad_qkv,
    sums_ref,
    bias_ref,
    attn_all,
    mid_cols,
    mid_pair,
    d_mid,
    d_attn,
    d_q,
    d_kv,
    kv_out,
    kv_in,
    d_qkv_all,
    part_out,
    part_in,
    gi_out,
    gi_in,
    send_sems,
    recv_sems,
):
    at = Place()
    net = Net(send_sems, recv_sems, at)
    at.meet((at.S, at.O, at.OS, at.N1, at.N2, at.N1S, at.N2S))
    peers = ((at.S, at.sib), (at.O, at.far), (at.OS, at.sibfar))
    pair = (at.col, 7 - at.col)

    def rows_at(block):
        return pl.ds(aligned(block, BLOCK), BLOCK)

    def cols_at(col):
        return pl.ds(aligned(col, FEAT), FEAT)

    class GatherCol:
        def __init__(self, array):
            self.array = array

        def rows(self, col, j):
            return self.array.at[rows_at(col + j * (7 - 2 * col)), :]

        def start(self):
            self.far = [net.send(self.rows(at.col, j), self.rows(at.col, j), at.O) for j in (0, 1)]
            self.sib = [net.send(self.rows(at.col, j), self.rows(at.col, j), at.S) for j in (0, 1)]

        def middle(self):
            self.onward = []
            for j in (0, 1):
                net.take(self.far[j], self.rows(at.far, j))
                self.onward.append(net.send(self.rows(at.far, j), self.rows(at.far, j), at.S))

        def end(self):
            for j in (0, 1):
                net.take(self.sib[j], self.rows(at.sib, j))
                net.take(self.onward[j], self.rows(at.sibfar, j))

    gather_attn = GatherCol(attn_all)
    for j in (0, 1):
        attn_all[rows_at(pair[j]), :] = attn_ref[pl.ds(j * BLOCK, BLOCK), :]

    gain1, gain2 = gains_all[0:1, :], gains_all[1:2, :]
    mid = mid_ref[...]
    scale = rms(mid)
    unit = mid * scale
    d_normed = dn2_ref[...]
    sums_ref[...] = jnp.zeros_like(sums_ref)
    sums_ref[1:2, :] = jnp.sum(d_normed * unit, axis=0, keepdims=True)
    bent = d_normed * gain2
    d_mid[...] = og_ref[rows_at(at.block), :].astype(F32) + scale * (
        bent - unit * jnp.mean(bent * unit, axis=1, keepdims=True)
    )
    mid_pair[at.row] = d_mid[...].astype(BF)
    to_pair = net.send(mid_pair.at[at.row], mid_pair.at[at.row], at.N1)
    mid_cols[rows_at(at.block), :] = d_mid[:, cols_at(at.col)].astype(BF)
    spread = []
    others = (
        (at.S, at.row, at.sib),
        (at.N1, 1 - at.row, at.col),
        (at.N1S, 1 - at.row, at.sib),
        (at.O, at.row, at.far),
        (at.OS, at.row, at.sibfar),
        (at.N2, 1 - at.row, at.far),
        (at.N2S, 1 - at.row, at.sibfar),
    )
    for device, row, col in others:
        spread.append(
            net.send(
                mid_pair.at[at.row, :, cols_at(col)], mid_cols.at[rows_at(at.block), :], device
            )
        )
    gather_attn.start()
    net.take(to_pair, mid_pair.at[1 - at.row])
    for j in (0, 1):
        d_attn[pl.ds(j * BLOCK, BLOCK), :] = dot(mid_pair[j], ow[...], 1, 1).astype(BF)
    d_kv[...] = jnp.zeros_like(d_kv)

    for j in (0, 1):
        keys = SEQ // 2 * (j + 1)
        rows = pl.ds(j * BLOCK, BLOCK)

        def back(h, carry):
            lanes = pl.ds(aligned(h, HEAD), HEAD)
            queries, d_out = q_ref[rows, lanes], d_attn[rows, lanes]
            scores = dot(queries, k_ref[:keys, :], 1, 1) * SCALE
            scores = causal(scores, pair[j] * BLOCK)
            probs = jnp.exp(scores - lse_ref[j * HEADS + h])
            d_probs = dot(d_out, v_ref[:keys, :], 1, 1)
            inner = jnp.sum(probs * d_probs, axis=1, keepdims=True)
            d_scores = (probs * (d_probs - inner) * SCALE).astype(BF)
            d_q[rows, lanes] = dot(d_scores, k_ref[:keys, :])
            d_kv[:keys, :HEAD] += dot(d_scores, queries, 0, 0)
            d_kv[:keys, HEAD:] += dot(probs.astype(BF), d_out, 0, 0)
            return carry

        lax.fori_loop(0, HEADS, back, 0)
    gather_attn.middle()

    kv_out[...] = d_kv[...].astype(BF)
    kv_keys = [
        [
            net.send(kv_out.at[rows_at(col + j * (7 - 2 * col)), :], kv_in.at[i, j], device)
            for j in (0, 1)
        ]
        for i, (device, col) in enumerate(peers)
    ]
    cosines = [cos_ref[rows_at(pair[j]), :] for j in (0, 1)]
    sines = [sin_ref[rows_at(pair[j]), :] for j in (0, 1)]
    for j in (0, 1):
        for h in range(HEADS):
            one = d_q[pl.ds(j * BLOCK, BLOCK), pl.ds(h * HEAD, HEAD)]
            d_qkv_all[rows_at(pair[j]), pl.ds(h * HEAD, HEAD)] = (
                one * cosines[j] - turn(one) * sines[j]
            ).astype(BF)
    gather_attn.end()
    for key, (_, row, col) in zip(spread, others, strict=True):
        net.take(key, mid_cols.at[rows_at(block_of(row, col)), :])
    grad_out[...] = dot(attn_all[...], mid_cols[...], 0, 0).astype(BF)
    for j in (0, 1):
        total = d_kv[rows_at(pair[j]), :]
        for i in range(3):
            net.take(kv_keys[i][j], kv_in.at[i, j])
            total = total + kv_in[i, j].astype(F32)
        key = total[:, :HEAD]
        d_qkv_all[rows_at(pair[j]), pl.ds(QCOLS, HEAD)] = (
            key * cosines[j] - turn(key) * sines[j]
        ).astype(BF)
        d_qkv_all[rows_at(pair[j]), pl.ds(QCOLS + HEAD, HEAD)] = total[:, HEAD:].astype(BF)
    gather_qkv = GatherCol(d_qkv_all)
    gather_qkv.start()

    part_out[...] = dot(d_qkv_all[rows_at(block_of(1 - at.row, at.col)), :], qw[...], 1, 1).astype(BF)
    part = net.send(part_out, part_in, at.N1)
    d_normed = dot(d_qkv_all[rows_at(at.block), :], qw[...], 1, 1)
    net.take(part, part_in)
    d_normed = d_normed + part_in[...].astype(F32)
    values = xs_ref[...].astype(F32)
    scale = rms(values)
    unit = values * scale
    sums_ref[0:1, :] = jnp.sum(d_normed * unit, axis=0, keepdims=True)
    bent = d_normed * gain1
    total = d_mid[...] + scale * (bent - unit * jnp.mean(bent * unit, axis=1, keepdims=True))
    gi_out[...] = total.astype(BF)
    half_rows = pl.ds(pl.multiple_of((at.block - 4 * at.row) * BLOCK, BLOCK), BLOCK)
    gi_keys = [
        net.send(gi_out.at[:, cols_at(col)], gi_in.at[half_rows, :], device)
        for device, col in peers
    ]
    gi_in[half_rows, :] = gi_out[:, cols_at(at.col)]
    gather_qkv.middle()
    gather_qkv.end()
    grad_qkv[...] = dot(n1c[...], d_qkv_all[...], 0, 0).astype(BF)
    ones = jnp.ones((8, SEQ), BF)
    bias_ref[...] = dot(ones, d_qkv_all[...])
    for key, (_, col) in zip(gi_keys, peers, strict=True):
        offset = block_of(at.row, col) - 4 * at.row
        net.take(key, gi_in.at[pl.ds(pl.multiple_of(offset * BLOCK, BLOCK), BLOCK), :])
    grad_in[...] = gi_in[...].astype(F32)
    net.finish()


def run_backward(*args):
    def out(shape, dtype):
        return jax.ShapeDtypeStruct(shape, dtype)

    outs = (
        out((SEQ // 2, FEAT), F32),
        out((QCOLS, FEAT), BF),
        out((FEAT, QKV), BF),
        out((8, MODEL), F32),
        out((8, QKV), F32),
    )
    return pl.pallas_call(
        backward_kernel,
        out_shape=outs,
        in_specs=[vmem()] * len(args),
        out_specs=[vmem()] * len(outs),
        scratch_shapes=[
            pltpu.VMEM((SEQ, QCOLS), BF),
            pltpu.VMEM((SEQ, FEAT), BF),
            pltpu.VMEM((2, BLOCK, MODEL), BF),
            pltpu.VMEM((BLOCK, MODEL), F32),
            pltpu.VMEM((2 * BLOCK, QCOLS), BF),
            pltpu.VMEM((2 * BLOCK, QCOLS), F32),
            pltpu.VMEM((SEQ, 2 * HEAD), F32),
            pltpu.VMEM((SEQ, 2 * HEAD), BF),
            pltpu.VMEM((3, 2, BLOCK, 2 * HEAD), BF),
            pltpu.VMEM((SEQ, QKV), BF),
            pltpu.VMEM((BLOCK, MODEL), BF),
            pltpu.VMEM((BLOCK, MODEL), BF),
            pltpu.VMEM((BLOCK, MODEL), BF),
            pltpu.VMEM((SEQ // 2, FEAT), BF),
            pltpu.SemaphoreType.DMA((40,)),
            pltpu.SemaphoreType.DMA((40,)),
        ],
        compiler_params=pltpu.CompilerParams(
            collective_id=2, has_side_effects=True, vmem_limit_bytes=VMEM_LIMIT
        ),
        cost_estimate=pl.CostEstimate(
            flops=10 * 10**9, bytes_accessed=40 * 10**6, transcendentals=2 * 10**6
        ),
        name="attention_backward",
    )(*args)


def rope_tables(count):
    places = jnp.arange(count, dtype=jnp.int32).astype(F32)
    inverse = 1.0 / THETA ** (jnp.arange(0, HEAD, 2).astype(F32) / HEAD)
    angles = places[:, None] * inverse[None, :]
    cosine, sine = jnp.cos(angles), jnp.sin(angles)
    return jnp.concatenate([cosine, cosine], axis=-1), jnp.concatenate([-sine, sine], axis=-1)


def body(
    layer_input,
    gain_attn,
    w_query,
    w_key,
    w_value,
    b_query,
    b_key,
    b_value,
    w_out,
    gain_ffn,
    w_gate,
    w_up,
    w_down,
    out_grad,
):
    n_dp = lax.axis_size("dp")
    feat, part, units, query_cols = FEAT, PART, UNITS, QCOLS

    cosine, sine = rope_tables(SEQ)
    w_qkv = jnp.concatenate([w_query, w_key, w_value], axis=1)
    bias = jnp.concatenate([b_query, b_key, b_value]).astype(F32)[None]
    gains = jnp.zeros((8, FEAT), F32).at[0].set(gain_attn.astype(F32)).at[1].set(gain_ffn.astype(F32))
    (
        xs,
        normed1_cols,
        grads_all,
        normed2_all,
        qkv_w,
        out_w,
        gate_w,
        up_w,
        down_w,
        queries,
        key,
        value,
        lse,
        attn,
        mid,
        gains_all,
    ) = run_forward(
        layer_input, out_grad, w_qkv, w_out, w_gate, w_up, w_down, gains, bias, cosine, sine
    )
    dn2, layer_output, grad_gate, grad_up, grad_down = run_ffn(
        normed2_all, grads_all, gate_w, up_w, down_w, mid
    )
    grad_input, grad_out, grad_qkv, sums, grad_bias = run_backward(
        dn2,
        mid,
        grads_all,
        gains_all,
        xs,
        normed1_cols,
        attn,
        queries,
        key,
        value,
        lse,
        out_w,
        qkv_w,
        cosine,
        sine,
    )

    def sum_dp(grad):
        rows = grad.shape[1] // n_dp
        sliced = grad.reshape(4, n_dp, rows, -1).transpose(1, 0, 2, 3)
        mine = lax.psum_scatter(sliced, "dp", scatter_dimension=0, tiled=True)[0]
        return lax.all_to_all(mine, "col", 0, 0, tiled=True)

    def spread(grad):
        return lax.all_gather(grad, "dp", axis=0, tiled=True).astype(F32)

    grad_down = sum_dp(grad_down.reshape(part, 4, feat).transpose(1, 0, 2))
    grad_gate = sum_dp(grad_gate.reshape(4, feat, part))
    grad_up = sum_dp(grad_up.reshape(4, feat, part))

    def sum_all(grad):
        mine = lax.psum_scatter(grad.astype(BF), "dp", scatter_dimension=0, tiled=True)
        return spread(mine)

    grad_qkv = sum_all(grad_qkv)
    grad_out = sum_all(grad_out)
    gains = lax.psum(sums[:2], ("dp", "row", "col"))
    gains = lax.dynamic_slice_in_dim(gains, lax.axis_index("col") * feat, feat, 1)
    grad_bias = lax.psum(grad_bias[0], "dp")

    def join(grad):
        joined = jnp.concatenate([grad[0], grad[1], grad[2], grad[3][:, HEAD:]], axis=1)
        return spread(joined)

    def join_down(grad):
        gathered = lax.all_gather(grad, "dp", axis=1, tiled=True)
        joined = jnp.concatenate([gathered[0], gathered[1], gathered[2], gathered[3][HEAD:]])
        return joined.astype(F32)

    return (
        layer_output,
        grad_input,
        gains[0],
        grad_qkv[:, :query_cols],
        grad_qkv[:, query_cols : query_cols + HEAD],
        grad_qkv[:, query_cols + HEAD :],
        grad_bias[:query_cols],
        grad_bias[query_cols : query_cols + HEAD],
        grad_bias[query_cols + HEAD :],
        grad_out,
        gains[1],
        join(grad_gate),
        join(grad_up),
        join_down(grad_down),
    )


def solution(mesh):
    in_specs = (
        P(("dp", "row"), "col"),
        P("col"),
        P("col", "row"),
        P("col", "row"),
        P("col", "row"),
        P("row"),
        P("row"),
        P("row"),
        P("row", "col"),
        P("col"),
        P("col", "row"),
        P("col", "row"),
        P("row", "col"),
        P(("dp", "row"), "col"),
    )
    out_specs = (
        P(("dp", "row"), "col"),
        P(("dp", "row"), "col"),
        P("col"),
        P("col", "row"),
        P("col", "row"),
        P("col", "row"),
        P("row"),
        P("row"),
        P("row"),
        P("row", "col"),
        P("col"),
        P("col", "row"),
        P("col", "row"),
        P("row", "col"),
    )
    return jax.shard_map(body, mesh=mesh, in_specs=in_specs, out_specs=out_specs, check_vma=False)
```

```python
import functools

import jax
import jax.numpy as jnp
from jax import lax
from jax.experimental import pallas as pl
from jax.experimental.pallas import tpu as pltpu
from jax.sharding import PartitionSpec as P

EPS = 1e-06
THETA = 1000000.0
NEG = -1e30
BF = jnp.bfloat16
F32 = jnp.float32
MESH = pl.DeviceIdType.MESH
HEAD = 128
HEADS = 6
SEQ = 1024
MODEL = 1536
FEAT = 384
BLOCK = 128
UNITS = 4480
PART = 1152
QCOLS = 768
QKV = 1024
VMEM_LIMIT = 62 * 2**20
SCALE = HEAD ** (-0.5)


def dot(left, right, left_dim=1, right_dim=0):
    return lax.dot_general(
        left, right, (((left_dim,), (right_dim,)), ((), ())), preferred_element_type=F32
    )


def aligned(index, step):
    return pl.multiple_of(index * step, step)


def block_of(row, col):
    return col + row * (7 - 2 * col)


def quarter_start(col):
    return pl.multiple_of(col * PART - (col // 3) * HEAD, HEAD)


class Place:
    def __init__(self):
        self.dp, self.row, self.col = (lax.axis_index(a) for a in ("dp", "row", "col"))
        self.hi, self.core = self.col // 2, self.col % 2
        self.z, self.y = self.dp // 4, self.dp % 4
        self.sib = 2 * self.hi + 1 - self.core
        self.far = 2 * (1 - self.hi) + self.core
        self.sibfar = 2 * (1 - self.hi) + 1 - self.core
        self.block = block_of(self.row, self.col)
        self.S = {"col": self.sib}
        self.O = {"col": self.far}
        self.OS = {"col": self.sibfar}
        self.N1 = {"row": 1 - self.row}
        self.N2 = {"row": 1 - self.row, "col": self.far}
        self.N1S = {"row": 1 - self.row, "col": self.sib}
        self.N2S = {"row": 1 - self.row, "col": self.sibfar}

        def dp_at(z, y):
            return {"dp": lax.rem(z + 4, 4) * 4 + lax.rem(y + 4, 4)}

        self.YP, self.YM = dp_at(self.z, self.y + 1), dp_at(self.z, self.y - 1)
        self.Y2, self.Z2 = dp_at(self.z, self.y + 2), dp_at(self.z + 2, self.y)
        self.ZP, self.ZM = dp_at(self.z + 1, self.y), dp_at(self.z - 1, self.y)

    def meet(self, partners):
        barrier = pltpu.get_barrier_semaphore()
        for device in partners:
            pl.semaphore_signal(barrier, inc=1, device_id=device, device_id_type=MESH)
        pl.semaphore_wait(barrier, len(partners))


class Net:
    def __init__(self, send_sems, recv_sems, at):
        self.ss, self.rs, self.at, self.count, self.sent = send_sems, recv_sems, at, 0, []

    def key(self):
        self.count += 1
        return self.count - 1

    def copy(self, key, src, dst, device):
        return pltpu.make_async_remote_copy(
            src_ref=src,
            dst_ref=dst,
            send_sem=self.ss.at[key],
            recv_sem=self.rs.at[key],
            device_id=device,
            device_id_type=MESH,
        )

    def send(self, src, dst, device):
        key = self.key()
        copy = self.copy(key, src, dst, device)
        copy.start()
        self.sent.append(copy)
        return key

    def take(self, key, dst):
        self.copy(key, dst, dst, self.at.S).wait_recv()

    def finish(self):
        for copy in self.sent:
            copy.wait_send()


class Gather8:
    def __init__(self, net, at, place):
        self.net, self.at, self.place = net, at, place

    def start(self, src):
        net, at = self.net, self.at
        mine = self.place(at.row, at.col, None)
        self.k1 = net.send(src, mine, at.N1)
        self.k2 = net.send(src, mine, at.N2)
        self.k0 = net.send(src, mine, at.S)

    def middle(self):
        net, at, place = self.net, self.at, self.place
        near, away = place(1 - at.row, at.col, None), place(1 - at.row, at.far, None)
        first, last = place(1 - at.row, at.col, 0), place(1 - at.row, at.far, 1)
        net.take(self.k1, near)
        self.ka = net.send(first, first, at.N2)
        self.f1 = net.send(near, near, at.S)
        net.take(self.k2, away)
        self.kb = net.send(last, last, at.N1)
        self.f2 = net.send(away, away, at.S)

    def late(self):
        net, at, place = self.net, self.at, self.place
        first, last = place(at.row, at.far, 0), place(at.row, at.far, 1)
        net.take(self.ka, first)
        self.f3 = net.send(first, first, at.S)
        net.take(self.kb, last)
        self.f4 = net.send(last, last, at.S)

    def end(self):
        net, at, place = self.net, self.at, self.place
        net.take(self.k0, place(at.row, at.sib, None))
        net.take(self.f1, place(1 - at.row, at.sib, None))
        net.take(self.f2, place(1 - at.row, at.sibfar, None))
        net.take(self.f3, place(at.row, at.sibfar, 0))
        net.take(self.f4, place(at.row, at.sibfar, 1))


def ring_dp(net, at, halves):
    def wrap(index):
        return lax.rem(index + 4, 4)

    sides = (((at.YP, at.YM), (at.ZP, at.ZM)), ((at.ZP, at.ZM), (at.YP, at.YM)))
    firsts, seconds = (at.y, at.z), (at.z, at.y)

    def refs(i, a, b):
        return halves[i](b, a) if i == 0 else halves[i](a, b)

    def send(i, a, b, device):
        return [net.send(ref, ref, device) for ref in refs(i, a, b)]

    def take(i, a, b, keys):
        for key, ref in zip(keys, refs(i, a, b), strict=True):
            net.take(key, ref)

    one, two, onward = {}, {}, {}
    for i in (0, 1):
        one[i] = [send(i, firsts[i], seconds[i], side) for side in sides[i][0]]
    for i in (0, 1):
        two[i, 0] = [send(i, firsts[i], seconds[i], side) for side in sides[i][1]]
    yield
    for i in (0, 1):
        minus = wrap(firsts[i] - 1)
        take(i, minus, seconds[i], one[i][0])
        one[i].append(send(i, minus, seconds[i], sides[i][0][0]))
        two[i, 1] = [send(i, minus, seconds[i], side) for side in sides[i][1]]
    yield
    for i in (0, 1):
        plus = wrap(firsts[i] + 1)
        take(i, plus, seconds[i], one[i][1])
        two[i, 2] = [send(i, plus, seconds[i], side) for side in sides[i][1]]
    offsets = (0, -1, 1, 2)
    for q in (0, 1, 2, 3):
        yield
        for i in (0, 1):
            if q == 1:
                across = wrap(firsts[i] + 2)
                take(i, across, seconds[i], one[i][2])
                two[i, 3] = [send(i, across, seconds[i], side) for side in sides[i][1]]
            slot = wrap(firsts[i] + offsets[q])
            minus, plus = wrap(seconds[i] - 1), wrap(seconds[i] + 1)
            take(i, slot, minus, two[i, q][0])
            if q < 2:
                onward[i, q] = send(i, slot, minus, sides[i][1][0])
            take(i, slot, plus, two[i, q][1])
            if q >= 2:
                onward[i, q] = send(i, slot, plus, sides[i][1][1])
    for q in (0, 1, 2, 3):
        yield
        for i in (0, 1):
            slot = wrap(firsts[i] + offsets[q])
            take(i, slot, wrap(seconds[i] + 2), onward[i, q])


def drain(steps):
    for _ in steps:
        pass


def rms(values):
    return lax.rsqrt(jnp.mean(values * values, axis=1, keepdims=True) + EPS)


def turn(values):
    return pltpu.roll(values, HEAD // 2, 1)


def causal(scores, start):
    places = start + lax.broadcasted_iota(jnp.int32, scores.shape, 0)
    keys = lax.broadcasted_iota(jnp.int32, scores.shape, 1)
    return jnp.where(keys <= places, scores, NEG)


def forward_kernel(
    x_ref,
    og_ref,
    wqkv_ref,
    wout_ref,
    wg_ref,
    wu_ref,
    wd_ref,
    gains_ref,
    bias_ref,
    cos_ref,
    sin_ref,
    xs_ref,
    n1c_ref,
    og_all,
    n2_all,
    qw,
    ow,
    gw,
    uw,
    dw,
    q_ref,
    k_ref,
    v_ref,
    lse_ref,
    attn_ref,
    mid_ref,
    gains_all,
    x_all,
    n1,
    part_out,
    part_in,
    send_sems,
    recv_sems,
    local_sems,
):
    at = Place()
    net = Net(send_sems, recv_sems, at)
    at.meet((at.S, at.N1, at.N2, at.O, at.OS, at.YP, at.YM, at.ZP, at.ZM))
    local = []

    def move(src, dst):
        copy = pltpu.make_async_copy(src, dst, local_sems.at[len(local)])
        copy.start()
        local.append(copy)

    def tokens_of(array):
        def place(row, col, part):
            if part is None:
                rows = pl.ds(aligned(row, SEQ // 2), SEQ // 2)
            else:
                rows = pl.ds(aligned(row * 2 + part, SEQ // 4), SEQ // 4)
            return array.at[rows, pl.ds(aligned(col, FEAT), FEAT)]

        return place

    mine, mine_far = aligned(at.col, FEAT), aligned(1 - at.hi, 2 * FEAT)
    move(x_ref, tokens_of(x_all)(at.row, at.col, None))
    move(wqkv_ref, qw.at[pl.ds(mine, FEAT), :])
    move(wout_ref, ow.at[:, pl.ds(mine, FEAT)])
    move(gains_ref, gains_all.at[:, pl.ds(mine, FEAT)])
    start = quarter_start(at.col)
    move(wg_ref.at[:, pl.ds(start, PART)], gw.at[pl.ds(mine, FEAT), :])
    move(wu_ref.at[:, pl.ds(start, PART)], uw.at[pl.ds(mine, FEAT), :])
    move(wd_ref.at[pl.ds(start, PART), :], dw.at[:, pl.ds(mine, FEAT)])
    move(og_ref, tokens_of(og_all)(at.row, at.col, None))

    eighth = at.dp % 8
    across = [net.key() for _ in range(5)]

    def slice_copies(core, first, last):
        device = {"col": 2 * (1 - at.hi) + core}
        rows = pl.ds(aligned(eighth, 48), 48)
        target = pl.ds(pl.multiple_of(mine + eighth * 48, 16), 48)
        columns = pl.ds(core * 512, 512)
        out_rows = pl.ds(pl.multiple_of(core * FEAT + eighth * 48, 16), 48)
        theirs = quarter_start(2 * (1 - at.hi) + core)
        down_rows = pl.ds(pl.multiple_of(theirs + eighth * 144, 16), 144)
        down_target = pl.ds(aligned(eighth, 144), 144)
        pairs = (
            (wqkv_ref.at[rows, columns], qw.at[target, columns]),
            (wout_ref.at[out_rows, :], ow.at[out_rows, pl.ds(mine, FEAT)]),
            (wg_ref.at[rows, pl.ds(theirs, PART)], gw.at[target, :]),
            (wu_ref.at[rows, pl.ds(theirs, PART)], uw.at[target, :]),
            (wd_ref.at[down_rows, :], dw.at[down_target, pl.ds(mine, FEAT)]),
        )
        return [
            pltpu.make_async_remote_copy(
                src_ref=pairs[i][0],
                dst_ref=pairs[i][1],
                send_sem=net.ss.at[spare[core][i]],
                recv_sem=net.rs.at[across[i]],
                device_id=device,
                device_id_type=MESH,
            )
            for i in range(first, last)
        ]

    spare = ([net.key() for _ in range(5)], [net.key() for _ in range(5)])
    chosen = at.core == at.dp // 8

    @pl.when(chosen)
    def _():
        for core in (0, 1):
            for copy in slice_copies(core, 0, 2):
                copy.start()

    gather_x = Gather8(net, at, tokens_of(x_all))
    gather_x.start(x_ref)
    gain_far = net.send(gains_ref, gains_all.at[:, pl.ds(mine, FEAT)], at.N2)
    gain_sib = net.send(gains_ref, gains_all.at[:, pl.ds(mine, FEAT)], at.S)
    near_qw = net.send(wqkv_ref, qw.at[pl.ds(mine, FEAT), :], at.S)
    near_ow = net.send(wout_ref, ow.at[:, pl.ds(mine, FEAT)], at.S)

    @pl.when(chosen)
    def _():
        for core in (0, 1):
            for copy in slice_copies(core, 2, 5):
                copy.start()

    far_half = pl.ds(mine_far, 2 * FEAT)

    def qkv_slices(z, y):
        rows = pl.ds(pl.multiple_of(mine_far + (z * 4 + y) * 48, 16), 48)
        return [qw.at[rows, pl.ds(aligned(at.core, 512), 512)]]

    def out_slices(z, y):
        index = z * 4 + y
        rows = pl.ds(pl.multiple_of(at.core * FEAT + (index % 8) * 48, 16), 48)
        return [ow.at[rows, pl.ds(pl.multiple_of(mine_far + (index // 8) * FEAT, HEAD), FEAT)]]

    def ffn_slices(weights, first, count):
        def slices(z, y):
            index = z * 4 + y
            rows = pl.ds(pl.multiple_of(mine_far + index * 48, 16), 48)
            down_rows = pl.ds(pl.multiple_of((index % 8) * 144 + first, 16), count)
            lanes = pl.ds(pl.multiple_of(mine_far + (index // 8) * FEAT, HEAD), FEAT)
            return [weights.at[rows, :], dw.at[down_rows, lanes]]

        return slices

    net.take(across[0], qkv_slices(at.z, at.y)[0])
    net.take(across[1], out_slices(at.z, at.y)[0])
    ring = ring_dp(net, at, (qkv_slices, out_slices))
    next(ring)
    near = [
        net.send(wg_ref.at[:, pl.ds(quarter_start(at.sib), PART)], gw.at[pl.ds(mine, FEAT), :], at.S),
        net.send(wu_ref.at[:, pl.ds(quarter_start(at.sib), PART)], uw.at[pl.ds(mine, FEAT), :], at.S),
        net.send(wd_ref.at[pl.ds(quarter_start(at.sib), PART), :], dw.at[:, pl.ds(mine, FEAT)], at.S),
    ]
    next(ring)
    next(ring)
    gather_x.middle()
    gains_far = gains_all.at[:, pl.ds(aligned(at.far, FEAT), FEAT)]
    net.take(gain_far, gains_far)
    gain_sibfar = net.send(gains_far, gains_far, at.S)
    next(ring)
    gather_og = Gather8(net, at, tokens_of(og_all))
    gather_x.late()
    gather_og.start(og_ref)
    drain(ring)
    cols_half, rows_half = pl.ds(aligned(at.core, 512), 512), pl.ds(aligned(at.core, FEAT), FEAT)
    far_qw = net.send(qw.at[far_half, cols_half], qw.at[far_half, cols_half], at.S)
    far_ow = net.send(ow.at[rows_half, far_half], ow.at[rows_half, far_half], at.S)
    net.take(across[2], ffn_slices(gw, 0, 80)(at.z, at.y)[0])
    net.take(across[3], ffn_slices(uw, 80, 64)(at.z, at.y)[0])
    net.take(across[4], ffn_slices(uw, 0, 144)(at.z, at.y)[1])
    ring = ring_dp(net, at, (ffn_slices(gw, 0, 80), ffn_slices(uw, 80, 64)))
    next(ring)
    gather_x.end()
    net.take(gain_sib, gains_all.at[:, pl.ds(aligned(at.sib, FEAT), FEAT)])
    net.take(gain_sibfar, gains_all.at[:, pl.ds(aligned(at.sibfar, FEAT), FEAT)])
    for copy in local:
        copy.wait()

    gain1, gain2 = gains_all[0:1, :], gains_all[1:2, :]

    def norm_block(i, carry):
        rows = pl.ds(aligned(i, BLOCK), BLOCK)
        values = x_all[rows, :].astype(F32)
        n1[rows, :] = (values * rms(values) * gain1).astype(BF)
        return carry

    lax.fori_loop(0, SEQ // BLOCK, norm_block, 0)
    next(ring)
    gather_og.middle()
    my_rows = pl.ds(aligned(at.block, BLOCK), BLOCK)
    xs_ref[...] = x_all[my_rows, :]
    n1c_ref[...] = n1[:, pl.ds(mine, FEAT)]
    net.take(near_qw, qw.at[pl.ds(aligned(at.sib, FEAT), FEAT), :])
    other_cols = pl.ds(aligned(1 - at.core, 512), 512)
    net.take(far_qw, qw.at[far_half, other_cols])

    def kv_block(i, carry):
        rows = pl.ds(aligned(i, 256), 256)
        both = dot(n1[rows, :], qw[:, QCOLS:]) + bias_ref[:, QCOLS:]
        key = both[:, :HEAD]
        k_ref[rows, :] = (key * cos_ref[rows, :] + turn(key) * sin_ref[rows, :]).astype(BF)
        v_ref[rows, :] = both[:, HEAD:].astype(BF)
        return carry

    lax.fori_loop(0, SEQ // 256, kv_block, 0)
    next(ring)
    pair = (at.col, 7 - at.col)
    for j in (0, 1):
        rows = pl.ds(aligned(pair[j], BLOCK), BLOCK)
        queries = dot(n1[rows, :], qw[:, :QCOLS]) + bias_ref[:, :QCOLS]
        cosine, sine = cos_ref[rows, :], sin_ref[rows, :]
        for h in range(HEADS):
            one = queries[:, h * HEAD : (h + 1) * HEAD]
            q_ref[pl.ds(j * BLOCK, BLOCK), pl.ds(h * HEAD, HEAD)] = (
                one * cosine + turn(one) * sine
            ).astype(BF)
    next(ring)
    gather_og.late()

    for j in (0, 1):
        keys = SEQ // 2 * (j + 1)
        rows = pl.ds(j * BLOCK, BLOCK)

        def attend(h, carry):
            lanes = pl.ds(aligned(h, HEAD), HEAD)
            scores = dot(q_ref[rows, lanes], k_ref[:keys, :], 1, 1) * SCALE
            scores = causal(scores, pair[j] * BLOCK)
            top = jnp.max(scores, axis=1, keepdims=True)
            weights = jnp.exp(scores - top)
            total = jnp.sum(weights, axis=1, keepdims=True)
            lse_ref[j * HEADS + h] = top + jnp.log(total)
            probs = (weights * (1.0 / total)).astype(BF)
            attn_ref[rows, lanes] = dot(probs, v_ref[:keys, :]).astype(BF)
            return carry

        lax.fori_loop(0, HEADS, attend, 0)
        next(ring)

    net.take(near_ow, ow.at[:, pl.ds(aligned(at.sib, FEAT), FEAT)])
    other_rows = pl.ds(aligned(1 - at.core, FEAT), FEAT)
    net.take(far_ow, ow.at[other_rows, far_half])
    part_out[...] = dot(attn_ref[pl.ds(aligned(1 - at.row, BLOCK), BLOCK), :], ow[...]).astype(BF)
    part = net.send(part_out, part_in, at.N1)
    own = dot(attn_ref[pl.ds(aligned(at.row, BLOCK), BLOCK), :], ow[...])
    next(ring)
    net.take(part, part_in)
    mid = xs_ref[...].astype(F32) + own + part_in[...].astype(F32)
    mid_ref[...] = mid

    def place_n2(row, col, part):
        first = block_of(row, col) * BLOCK
        if part is None:
            return n2_all.at[pl.ds(pl.multiple_of(first, BLOCK), BLOCK), :]
        return n2_all.at[pl.ds(pl.multiple_of(first + part * 64, 64), 64), :]

    n2_all[my_rows, :] = (mid * rms(mid) * gain2).astype(BF)
    gather_n2 = Gather8(net, at, place_n2)
    gather_n2.start(place_n2(at.row, at.col, None))
    gather_og.end()
    next(ring)
    gather_n2.middle()
    drain(ring)
    gather_n2.late()
    net.take(near[0], gw.at[pl.ds(aligned(at.sib, FEAT), FEAT), :])
    net.take(near[1], uw.at[pl.ds(aligned(at.sib, FEAT), FEAT), :])
    net.take(near[2], dw.at[:, pl.ds(aligned(at.sib, FEAT), FEAT)])
    gather_n2.end()
    net.finish()

    @pl.when(chosen)
    def _():
        for core in (0, 1):
            for copy in slice_copies(core, 0, 5):
                copy.wait_send()


def vmem():
    return pl.BlockSpec(memory_space=pltpu.VMEM)


def anywhere():
    return pl.BlockSpec(memory_space=pl.ANY)


def run_forward(x, og, wqkv, wout, wg, wu, wd, gains, bias, cosine, sine):
    def out(shape, dtype):
        return jax.ShapeDtypeStruct(shape, dtype)

    outs = (
        out((BLOCK, MODEL), BF),
        out((SEQ, FEAT), BF),
        out((SEQ, MODEL), BF),
        out((SEQ, MODEL), BF),
        out((MODEL, QKV), BF),
        out((QCOLS, MODEL), BF),
        out((MODEL, PART), BF),
        out((MODEL, PART), BF),
        out((PART, MODEL), BF),
        out((2 * BLOCK, QCOLS), BF),
        out((SEQ, HEAD), BF),
        out((SEQ, HEAD), BF),
        out((2 * HEADS, BLOCK, 1), F32),
        out((2 * BLOCK, QCOLS), BF),
        out((BLOCK, MODEL), F32),
        out((8, MODEL), F32),
    )
    return pl.pallas_call(
        forward_kernel,
        out_shape=outs,
        in_specs=[vmem()] * 4 + [anywhere()] * 3 + [vmem()] * 4,
        out_specs=[vmem()] * len(outs),
        scratch_shapes=[
            pltpu.VMEM((SEQ, MODEL), BF),
            pltpu.VMEM((SEQ, MODEL), BF),
            pltpu.VMEM((BLOCK, MODEL), BF),
            pltpu.VMEM((BLOCK, MODEL), BF),
            pltpu.SemaphoreType.DMA((160,)),
            pltpu.SemaphoreType.DMA((160,)),
            pltpu.SemaphoreType.DMA((8,)),
        ],
        compiler_params=pltpu.CompilerParams(
            collective_id=0, has_side_effects=True, vmem_limit_bytes=VMEM_LIMIT
        ),
        cost_estimate=pl.CostEstimate(
            flops=8 * 10**9, bytes_accessed=60 * 10**6, transcendentals=2 * 10**6
        ),
        name="attention_forward",
    )(x, og, wqkv, wout, wg, wu, wd, gains, bias, cosine, sine)


class Reduce8:
    def __init__(self, net, at, own, other, sib_in, first_in, last_in, near_in, away_in):
        self.net, self.at, self.own, self.other, self.sib_in = net, at, own, other, sib_in
        self.first_in, self.last_in, self.near_in, self.away_in = first_in, last_in, near_in, away_in
        self.half = own.shape[1] // 2
        self.keys = {}

    def put(self, j, mine, theirs):
        self.own[j] = mine
        self.other[j] = theirs
        self.keys[j] = self.net.send(self.other.at[j], self.sib_in.at[j], self.at.S)

    def step(self, j):
        net, at, half = self.net, self.at, self.half
        net.take(self.keys[j], self.sib_in.at[j])
        total = self.own[j].astype(F32) + self.sib_in[j].astype(F32)
        if j == 0:
            self.own[j] = total.astype(BF)
            self.first = net.send(self.own.at[j, pl.ds(0, half)], self.first_in, at.N1)
            self.last = net.send(self.own.at[j, pl.ds(half, half)], self.last_in, at.N2)
        elif j == 1:
            net.take(self.last, self.last_in)
            self.own[j, :half] = total[:half].astype(BF)
            self.own[j, half:] = (total[half:] + self.last_in[...].astype(F32)).astype(BF)
            self.near = net.send(self.own.at[j], self.near_in, at.N1)
        elif j == 2:
            net.take(self.first, self.first_in)
            self.own[j, :half] = (total[:half] + self.first_in[...].astype(F32)).astype(BF)
            self.own[j, half:] = total[half:].astype(BF)
            self.away = net.send(self.own.at[j], self.away_in, at.N2)
        else:
            net.take(self.near, self.near_in)
            net.take(self.away, self.away_in)
            return total + self.near_in[...].astype(F32) + self.away_in[...].astype(F32)
        return None


def reduce8_scratch(rows, columns):
    return [
        pltpu.VMEM((4, rows, columns), BF),
        pltpu.VMEM((4, rows, columns), BF),
        pltpu.VMEM((4, rows, columns), BF),
        pltpu.VMEM((rows // 2, columns), BF),
        pltpu.VMEM((rows // 2, columns), BF),
        pltpu.VMEM((rows, columns), BF),
        pltpu.VMEM((rows, columns), BF),
    ]


def tiles_of(width, step):
    return [(first, min(step, width - first)) for first in range(0, width, step)]


def outer_sum(left, right, out):
    width = right.shape[1]
    height = left.shape[1] // 2

    def tile(lanes):
        for i in (0, 1):
            rows = pl.ds(i * height, height)
            out[rows, lanes] = dot(left[:, rows], right[:, lanes], 0, 0).astype(BF)

    def step(n, carry):
        tile(pl.ds(aligned(n, 256), 256))
        return carry

    lax.fori_loop(0, width // 256, step, 0)
    if width % 256:
        tile(pl.ds(width // 256 * 256, width % 256))


def ffn_kernel(
    n2,
    og,
    gw,
    uw,
    dw,
    mid_ref,
    dn2_ref,
    out_ref,
    grad_gu,
    grad_down,
    hidden,
    d_gate,
    d_up,
    ffn,
    *rest,
):
    red_a, red_b, (send_sems, recv_sems) = rest[:7], rest[7:14], rest[14:]
    at = Place()
    net = Net(send_sems, recv_sems, at)
    at.meet((at.S, at.N1, at.N2))
    norms = Reduce8(net, at, *red_a)
    outs = Reduce8(net, at, *red_b)
    chips = ((at.row, 1 - at.hi), (1 - at.row, at.hi), (1 - at.row, 1 - at.hi), (at.row, at.hi))
    last_part = at.col == 3

    def tokens(j):
        row, hi = chips[j]
        first = 2 * hi + row * (6 - 4 * hi)
        return pl.ds(aligned(first, BLOCK), 256), at.core + row * (1 - 2 * at.core)

    for j in range(4):
        rows, place = tokens(j)
        for first, width in tiles_of(PART, 512):
            lanes = pl.ds(first, width)
            gate = dot(n2[rows, :], gw[:, lanes])
            up = dot(n2[rows, :], uw[:, lanes])
            d_hidden = dot(og[rows, :], dw[lanes, :], 1, 1)
            sig = jax.nn.sigmoid(gate)
            act = gate * sig
            d_act = d_hidden * up * sig * (1.0 + gate * (1.0 - sig))
            values = [act * up, d_act, d_hidden * act]
            if first == 0:
                lane = lax.broadcasted_iota(jnp.int32, (1, width), 1)
                fresh = jnp.logical_or(lane >= HEAD, jnp.logical_not(last_part))
                values = [jnp.where(fresh, value, 0.0) for value in values]
            for ref, value in zip((hidden, d_gate, d_up), values, strict=True):
                ref[rows, lanes] = value.astype(BF)
        own_rows = pl.ds(pl.multiple_of(rows.start + place * BLOCK, BLOCK), BLOCK)
        other_rows = pl.ds(pl.multiple_of(rows.start + (1 - place) * BLOCK, BLOCK), BLOCK)
        parts = [
            (dot(d_gate[r, :], gw[...], 1, 1) + dot(d_up[r, :], uw[...], 1, 1)).astype(BF)
            for r in (other_rows, own_rows)
        ]
        norms.put(j, parts[1], parts[0])
        if j:
            norms.step(j - 1)

    outer_sum(hidden, og, grad_down)

    for j in range(4):
        row, hi = chips[j]
        rows = pl.ds(aligned(row, SEQ // 2), SEQ // 2)
        lanes = pl.ds(aligned(hi, QCOLS), QCOLS)
        ffn[...] = dot(hidden[rows, :], dw[:, lanes])
        if j in (0, 3):
            mine = pl.ds(pl.multiple_of((at.block - 4 * at.row) * BLOCK, BLOCK), BLOCK)
            ffn[mine, :] += mid_ref[:, lanes]
        own = ffn[:, pl.ds(aligned(at.core, FEAT), FEAT)].astype(BF)
        outs.put(j, own, ffn[:, pl.ds(aligned(1 - at.core, FEAT), FEAT)].astype(BF))
        if j:
            outs.step(j - 1)
        if j == 1:
            dn2_ref[...] = norms.step(3)

    outer_sum(n2, d_gate, grad_gu.at[0])
    outer_sum(n2, d_up, grad_gu.at[1])
    out_ref[...] = outs.step(3)
    net.finish()


def run_ffn(n2, og, gw, uw, dw, mid):
    def out(shape, dtype):
        return jax.ShapeDtypeStruct(shape, dtype)

    outs = (
        out((BLOCK, MODEL), F32),
        out((SEQ // 2, FEAT), F32),
        out((2, MODEL, PART), BF),
        out((PART, MODEL), BF),
    )
    return pl.pallas_call(
        ffn_kernel,
        out_shape=outs,
        in_specs=[vmem()] * 6,
        out_specs=[vmem()] * len(outs),
        scratch_shapes=[pltpu.VMEM((SEQ, PART), BF)] * 3
        + [pltpu.VMEM((SEQ // 2, QCOLS), F32)]
        + reduce8_scratch(BLOCK, MODEL)
        + reduce8_scratch(SEQ // 2, FEAT)
        + [pltpu.SemaphoreType.DMA((32,)), pltpu.SemaphoreType.DMA((32,))],
        compiler_params=pltpu.CompilerParams(
            collective_id=1, has_side_effects=True, vmem_limit_bytes=VMEM_LIMIT
        ),
        cost_estimate=pl.CostEstimate(
            flops=29 * 10**9, bytes_accessed=60 * 10**6, transcendentals=2 * 10**6
        ),
        name="feed_forward",
    )(n2, og, gw, uw, dw, mid)


def add_up(out, terms):
    lead = out.shape[:-2]
    if not lead:
        total = terms[0][...].astype(F32)
        for term in terms[1:]:
            total = total + term[...].astype(F32)
        out[...] = total.astype(out.dtype)
        return
    count = 1
    for size in lead:
        count *= size

    def step(i, carry):
        index = []
        for size in reversed(lead):
            index.insert(0, i % size)
            i = i // size
        index = tuple(index)
        total = terms[0].at[index][...].astype(F32)
        for term in terms[1:]:
            total = total + term.at[index][...].astype(F32)
        out.at[index][...] = total.astype(out.dtype)
        return carry

    lax.fori_loop(0, count, step, 0)


class RingItem:
    def __init__(self, net, sides, place, part, way, bufs, own):
        self.net, self.part, self.own = net, part, own
        self.relay, self.staged, self.from_last, self.from_next = bufs
        self.onward, self.back = (sides[0], sides[1]) if way == 0 else (sides[1], sides[0])
        step = 1 - 2 * way
        self.here, self.next, self.across, self.last = (
            lax.rem(place + 4 + step * i, 4) for i in (0, 1, 2, 3)
        )

    def start(self):
        self.k_relay = self.net.send(self.part(self.across), self.relay, self.onward)

    def direct(self):
        self.k_next = self.net.send(self.part(self.last), self.from_next, self.back)

    def middle(self):
        self.net.take(self.k_relay, self.relay)
        add_up(self.staged, [self.part(self.next), self.relay])
        self.k_last = self.net.send(self.staged, self.from_last, self.onward)

    def end(self):
        self.net.take(self.k_next, self.from_next)
        self.net.take(self.k_last, self.from_last)
        add_up(self.own, [self.part(self.here), self.from_next, self.from_last])


def begin(items):
    for item in items:
        item.start()
    for item in items:
        item.direct()


LEFT, RIGHT = pl.ds(0, QCOLS), pl.ds(QCOLS, QCOLS)
FFN_FIRST = (((2, 2, 48, PART), (2, 80, QCOLS)), ((2, 2, 48, PART), (144, QCOLS)))
FFN_LAST = (((2, 48, PART), (80, QCOLS)), ((2, 48, PART), (80, QCOLS)))
SMALL_FIRST = (((2, 48, 512),), ((2, 48, FEAT),))
SMALL_LAST = (((48, 512),), ((48, FEAT),))


def down_rows(k):
    return pl.ds(pl.multiple_of(72 * k - 8 * (k % 2), 16), 80)


def ring_scratch(first, last):
    scratch = []
    for i in (0, 1):
        for dims in first[i]:
            scratch += [pltpu.VMEM(dims, BF)] * 8
            scratch.append(pltpu.VMEM((2,) + dims, BF))
        for dims in last[i]:
            scratch += [pltpu.VMEM(dims, BF)] * 4
    return scratch


def ring_items(net, at, first, last, parts, seconds, finals, bufs):
    sides = (((at.YP, at.YM), (at.ZP, at.ZM)), ((at.ZP, at.ZM), (at.YP, at.YM)))
    places = ((at.y, at.z), (at.z, at.y))
    bufs = list(bufs)
    one, two = ([], []), ([], [])
    for i in (0, 1):
        owns = []
        for n in range(len(first[i])):
            own = bufs[8]
            for way in (0, 1):
                part = functools.partial(lambda k, f, w: f(k, w), f=parts[i][n], w=way)
                four = bufs[4 * way : 4 * way + 4]
                one[i].append(
                    RingItem(net, sides[i][0], places[i][0], part, way, four, own.at[way])
                )
            owns.append(own)
            bufs = bufs[9:]
        for n in range(len(last[i])):
            part = functools.partial(lambda k, f, o: f(o, k), f=seconds[i][n], o=owns[n])
            two[i].append(
                RingItem(net, sides[i][1], places[i][1], part, n % 2, bufs[:4], finals[i][n])
            )
            bufs = bufs[4:]

    def mix(pair):
        return [item for items in zip(*pair, strict=True) for item in items]

    return mix(one), mix(two)


def ffn_items(net, at, gu, down, gu_own, down_own, bufs):
    parts = (
        (
            lambda k, way: gu.at[way, pl.ds(0, 2), :, k],
            lambda k, way: down.at[way, :, down_rows(k), LEFT],
        ),
        (
            lambda k, way: gu.at[k // 2, pl.ds(2, 2), k % 2, pl.ds(2 * way, 2)],
            lambda k, way: down.at[k // 2, k % 2, pl.ds(144 * way, 144), RIGHT],
        ),
    )
    seconds = (
        (lambda own, k: own.at[k // 2, :, k % 2], lambda own, k: own.at[k // 2, k % 2]),
        (
            lambda own, k: own.at[k // 2, :, k % 2],
            lambda own, k: own.at[k // 2, pl.ds(pl.multiple_of((k % 2) * 64, 64), 80)],
        ),
    )
    finals = (
        (gu_own.at[pl.ds(0, 2)], down_own.at[:, LEFT]),
        (gu_own.at[pl.ds(2, 2)], down_own.at[:, RIGHT]),
    )
    return ring_items(net, at, FFN_FIRST, FFN_LAST, parts, seconds, finals, bufs)


def small_items(net, at, qkv, out, qkv_own, out_own, bufs):
    parts = (
        (lambda k, way: qkv.at[:, k, :, pl.ds(512 * way, 512)],),
        (lambda k, way: out.at[k // 2, k % 2, pl.ds(2 * way, 2)],),
    )
    seconds = ((lambda own, k: own.at[k // 2, k % 2],), (lambda own, k: own.at[k // 2, k % 2],))
    finals = ((qkv_own,), (out_own,))
    return ring_items(net, at, SMALL_FIRST, SMALL_LAST, parts, seconds, finals, bufs)


def backward_kernel(
    dn2_ref,
    mid_ref,
    og_ref,
    gains_all,
    xs_ref,
    n1c,
    attn_ref,
    q_ref,
    k_ref,
    v_ref,
    lse_ref,
    ow,
    qw,
    cos_ref,
    sin_ref,
    gu,
    down,
    grad_in,
    grad_out,
    grad_qkv,
    small_ref,
    gu_own,
    down_own,
    sums_ref,
    sums_in,
    attn_all,
    mid_cols,
    mid_pair,
    d_mid,
    d_attn,
    d_q,
    d_kv,
    kv_out,
    kv_in,
    d_qkv_all,
    part_out,
    part_in,
    gi_out,
    gi_in,
    *rest,
):
    bufs, (send_sems, recv_sems) = rest[:-2], rest[-2:]
    at = Place()
    net = Net(send_sems, recv_sems, at)
    at.meet(
        (at.S, at.O, at.OS, at.N1, at.N2, at.N1S, at.N2S, at.YP, at.YM, at.ZP, at.ZM)
    )
    first, last = ffn_items(net, at, gu, down, gu_own, down_own, bufs)
    begin(first)
    peers = ((at.S, at.sib), (at.O, at.far), (at.OS, at.sibfar))
    pair = (at.col, 7 - at.col)

    def rows_at(block):
        return pl.ds(aligned(block, BLOCK), BLOCK)

    def cols_at(col):
        return pl.ds(aligned(col, FEAT), FEAT)

    class GatherCol:
        def __init__(self, array):
            self.array = array

        def rows(self, col, j):
            return self.array.at[rows_at(col + j * (7 - 2 * col)), :]

        def start(self):
            self.far = [net.send(self.rows(at.col, j), self.rows(at.col, j), at.O) for j in (0, 1)]
            self.sib = [net.send(self.rows(at.col, j), self.rows(at.col, j), at.S) for j in (0, 1)]

        def middle(self):
            self.onward = []
            for j in (0, 1):
                net.take(self.far[j], self.rows(at.far, j))
                self.onward.append(net.send(self.rows(at.far, j), self.rows(at.far, j), at.S))

        def end(self):
            for j in (0, 1):
                net.take(self.sib[j], self.rows(at.sib, j))
                net.take(self.onward[j], self.rows(at.sibfar, j))

    gather_attn = GatherCol(attn_all)
    for j in (0, 1):
        attn_all[rows_at(pair[j]), :] = attn_ref[pl.ds(j * BLOCK, BLOCK), :]

    gain1, gain2 = gains_all[0:1, :], gains_all[1:2, :]
    mid = mid_ref[...]
    scale = rms(mid)
    unit = mid * scale
    d_normed = dn2_ref[...]
    sums_ref[...] = jnp.zeros_like(sums_ref)
    sums_ref[1:2, :] = jnp.sum(d_normed * unit, axis=0, keepdims=True)
    bent = d_normed * gain2
    d_mid[...] = og_ref[rows_at(at.block), :].astype(F32) + scale * (
        bent - unit * jnp.mean(bent * unit, axis=1, keepdims=True)
    )
    mid_pair[at.row] = d_mid[...].astype(BF)
    to_pair = net.send(mid_pair.at[at.row], mid_pair.at[at.row], at.N1)
    mid_cols[rows_at(at.block), :] = d_mid[:, cols_at(at.col)].astype(BF)
    spread = []
    others = (
        (at.S, at.row, at.sib),
        (at.N1, 1 - at.row, at.col),
        (at.N1S, 1 - at.row, at.sib),
        (at.O, at.row, at.far),
        (at.OS, at.row, at.sibfar),
        (at.N2, 1 - at.row, at.far),
        (at.N2S, 1 - at.row, at.sibfar),
    )
    for device, row, col in others:
        spread.append(
            net.send(
                mid_pair.at[at.row, :, cols_at(col)], mid_cols.at[rows_at(at.block), :], device
            )
        )
    gather_attn.start()
    net.take(to_pair, mid_pair.at[1 - at.row])
    for j in (0, 1):
        d_attn[pl.ds(j * BLOCK, BLOCK), :] = dot(mid_pair[j], ow[...], 1, 1).astype(BF)
    d_kv[...] = jnp.zeros_like(d_kv)
    for item in first:
        item.middle()

    for j in (0, 1):
        keys = SEQ // 2 * (j + 1)
        rows = pl.ds(j * BLOCK, BLOCK)

        def back(h, carry):
            lanes = pl.ds(aligned(h, HEAD), HEAD)
            queries, d_out = q_ref[rows, lanes], d_attn[rows, lanes]
            scores = dot(queries, k_ref[:keys, :], 1, 1) * SCALE
            scores = causal(scores, pair[j] * BLOCK)
            probs = jnp.exp(scores - lse_ref[j * HEADS + h])
            d_probs = dot(d_out, v_ref[:keys, :], 1, 1)
            inner = jnp.sum(probs * d_probs, axis=1, keepdims=True)
            d_scores = (probs * (d_probs - inner) * SCALE).astype(BF)
            d_q[rows, lanes] = dot(d_scores, k_ref[:keys, :])
            d_kv[:keys, :HEAD] += dot(d_scores, queries, 0, 0)
            d_kv[:keys, HEAD:] += dot(probs.astype(BF), d_out, 0, 0)
            return carry

        lax.fori_loop(0, HEADS, back, 0)
    gather_attn.middle()

    kv_out[...] = d_kv[...].astype(BF)
    kv_keys = [
        [
            net.send(kv_out.at[rows_at(col + j * (7 - 2 * col)), :], kv_in.at[i, j], device)
            for j in (0, 1)
        ]
        for i, (device, col) in enumerate(peers)
    ]
    cosines = [cos_ref[rows_at(pair[j]), :] for j in (0, 1)]
    sines = [sin_ref[rows_at(pair[j]), :] for j in (0, 1)]
    for j in (0, 1):
        for h in range(HEADS):
            one = d_q[pl.ds(j * BLOCK, BLOCK), pl.ds(h * HEAD, HEAD)]
            d_qkv_all[rows_at(pair[j]), pl.ds(h * HEAD, HEAD)] = (
                one * cosines[j] - turn(one) * sines[j]
            ).astype(BF)
    for item in first:
        item.end()
    begin(last)
    gather_attn.end()
    for key, (_, row, col) in zip(spread, others, strict=True):
        net.take(key, mid_cols.at[rows_at(block_of(row, col)), :])
    grad_out[...] = dot(attn_all[...], mid_cols[...], 0, 0).astype(BF)
    for j in (0, 1):
        total = d_kv[rows_at(pair[j]), :]
        for i in range(3):
            net.take(kv_keys[i][j], kv_in.at[i, j])
            total = total + kv_in[i, j].astype(F32)
        key = total[:, :HEAD]
        d_qkv_all[rows_at(pair[j]), pl.ds(QCOLS, HEAD)] = (
            key * cosines[j] - turn(key) * sines[j]
        ).astype(BF)
        d_qkv_all[rows_at(pair[j]), pl.ds(QCOLS + HEAD, HEAD)] = total[:, HEAD:].astype(BF)
    gather_qkv = GatherCol(d_qkv_all)
    gather_qkv.start()

    part_out[...] = dot(d_qkv_all[rows_at(block_of(1 - at.row, at.col)), :], qw[...], 1, 1).astype(BF)
    part = net.send(part_out, part_in, at.N1)
    d_normed = dot(d_qkv_all[rows_at(at.block), :], qw[...], 1, 1)
    net.take(part, part_in)
    d_normed = d_normed + part_in[...].astype(F32)
    values = xs_ref[...].astype(F32)
    scale = rms(values)
    unit = values * scale
    sums_ref[0:1, :] = jnp.sum(d_normed * unit, axis=0, keepdims=True)
    bent = d_normed * gain1
    total = d_mid[...] + scale * (bent - unit * jnp.mean(bent * unit, axis=1, keepdims=True))
    gi_out[...] = total.astype(BF)
    sums_in[at.row * 4 + at.col] = sums_ref[:, cols_at(at.col)]
    sums_keys = [
        net.send(sums_ref.at[:, cols_at(col)], sums_in.at[at.row * 4 + at.col], device)
        for device, row, col in others
    ]
    half_rows = pl.ds(pl.multiple_of((at.block - 4 * at.row) * BLOCK, BLOCK), BLOCK)
    gi_keys = [
        net.send(gi_out.at[:, cols_at(col)], gi_in.at[half_rows, :], device)
        for device, col in peers
    ]
    gi_in[half_rows, :] = gi_out[:, cols_at(at.col)]
    for item in last:
        item.middle()
    gather_qkv.middle()
    gather_qkv.end()
    grad_qkv[...] = dot(n1c[...], d_qkv_all[...], 0, 0).astype(BF)
    ones = jnp.ones((8, SEQ), BF)
    small_ref[:, FEAT:] = dot(ones, d_qkv_all[...])
    for key, (_, row, col) in zip(sums_keys, others, strict=True):
        net.take(key, sums_in.at[row * 4 + col])
    total = sums_in[0]
    for i in range(1, 8):
        total = total + sums_in[i]
    small_ref[:, :FEAT] = total
    for key, (_, col) in zip(gi_keys, peers, strict=True):
        offset = block_of(at.row, col) - 4 * at.row
        net.take(key, gi_in.at[pl.ds(pl.multiple_of(offset * BLOCK, BLOCK), BLOCK), :])
    for item in last:
        item.end()
    grad_in[...] = gi_in[...].astype(F32)
    net.finish()


def run_backward(*args):
    def out(shape, dtype):
        return jax.ShapeDtypeStruct(shape, dtype)

    outs = (
        out((SEQ // 2, FEAT), F32),
        out((QCOLS, FEAT), BF),
        out((FEAT, QKV), BF),
        out((8, FEAT + QKV), F32),
        out((4, 48, PART), BF),
        out((80, MODEL), BF),
    )
    return pl.pallas_call(
        backward_kernel,
        out_shape=outs,
        in_specs=[vmem()] * len(args),
        out_specs=[vmem()] * len(outs),
        scratch_shapes=[
            pltpu.VMEM((8, MODEL), F32),
            pltpu.VMEM((8, 8, FEAT), F32),
            pltpu.VMEM((SEQ, QCOLS), BF),
            pltpu.VMEM((SEQ, FEAT), BF),
            pltpu.VMEM((2, BLOCK, MODEL), BF),
            pltpu.VMEM((BLOCK, MODEL), F32),
            pltpu.VMEM((2 * BLOCK, QCOLS), BF),
            pltpu.VMEM((2 * BLOCK, QCOLS), F32),
            pltpu.VMEM((SEQ, 2 * HEAD), F32),
            pltpu.VMEM((SEQ, 2 * HEAD), BF),
            pltpu.VMEM((3, 2, BLOCK, 2 * HEAD), BF),
            pltpu.VMEM((SEQ, QKV), BF),
            pltpu.VMEM((BLOCK, MODEL), BF),
            pltpu.VMEM((BLOCK, MODEL), BF),
            pltpu.VMEM((BLOCK, MODEL), BF),
            pltpu.VMEM((SEQ // 2, FEAT), BF),
        ]
        + ring_scratch(FFN_FIRST, FFN_LAST)
        + [pltpu.SemaphoreType.DMA((80,)), pltpu.SemaphoreType.DMA((80,))],
        compiler_params=pltpu.CompilerParams(
            collective_id=2, has_side_effects=True, vmem_limit_bytes=VMEM_LIMIT
        ),
        cost_estimate=pl.CostEstimate(
            flops=10 * 10**9, bytes_accessed=40 * 10**6, transcendentals=2 * 10**6
        ),
        name="attention_backward",
    )(*args)


def sums_kernel(
    gu_own,
    down_own,
    qkv,
    out,
    small_ref,
    all_gu,
    all_down,
    all_qkv,
    all_out,
    small_out,
    small_y,
    small_z,
    *rest,
):
    bufs, (send_sems, recv_sems) = rest[:-2], rest[-2:]
    at = Place()
    net = Net(send_sems, recv_sems, at)
    at.meet((at.S, at.O, at.OS, at.YP, at.YM, at.ZP, at.ZM, at.Y2, at.Z2))
    z, y = at.z, at.y

    def gu_piece(k, lanes):
        rows = pl.ds(pl.multiple_of((k % 8) * 48, 16), 48)
        return all_gu.at[k // 8, rows, lanes]

    def part_lanes(col):
        return pl.ds(aligned(col, PART), PART)

    def down_piece(k):
        return all_down.at[:, pl.ds(pl.multiple_of(k * 80, 16), 80), :]

    def down_slot(col):
        return all_down.at[col, pl.ds(pl.multiple_of(at.dp * 80, 16), 80), :]

    def feat_lanes(col):
        return pl.ds(aligned(col, FEAT), FEAT)

    def qkv_piece(k):
        rows = pl.ds(pl.multiple_of((k % 8) * 48, 16), 48)
        return all_qkv.at[rows, pl.ds(pl.multiple_of((k // 8) * 512, 512), 512)]

    def out_piece(k):
        return all_out.at[pl.ds(pl.multiple_of(k * 48, 16), 48), :]

    peers = ((at.O, at.far), (at.OS, at.sibfar), (at.S, at.sib))
    keys = []
    for device, col in peers:
        keys.append(
            (
                net.send(gu_own.at[col], gu_piece(at.dp, part_lanes(at.col)), device),
                net.send(down_own.at[:, feat_lanes(col)], down_slot(at.col), device),
            )
        )
    small_y[y] = small_ref[...]
    small_keys = [net.send(small_ref, small_y.at[y], d) for d in (at.YP, at.YM, at.Y2)]
    first, last = small_items(net, at, qkv, out, qkv_piece(at.dp), out_piece(at.dp), bufs)
    begin(first)
    gu_piece(at.dp, part_lanes(at.col))[...] = gu_own[at.col]
    down_slot(at.col)[...] = down_own[:, feat_lanes(at.col)]
    for (one, two), (_, col) in zip(keys, peers, strict=True):
        net.take(one, gu_piece(at.dp, part_lanes(col)))
        net.take(two, down_slot(col))

    def half0(zz, yy):
        return [gu_piece(zz * 4 + yy, pl.ds(0, 3456))]

    def half1(zz, yy):
        return [gu_piece(zz * 4 + yy, pl.ds(3456, 1152)), down_piece(zz * 4 + yy)]

    ring = ring_dp(net, at, (half0, half1))
    next(ring)
    for item in first:
        item.middle()
    for key, k in zip(small_keys, (y - 1, y + 1, y + 2), strict=True):
        net.take(key, small_y.at[lax.rem(k + 4, 4)])
    small_z[z] = (small_y[0] + small_y[1]) + (small_y[2] + small_y[3])
    small_keys = [net.send(small_z.at[z], small_z.at[z], d) for d in (at.ZP, at.ZM, at.Z2)]
    next(ring)
    for item in first:
        item.end()
    begin(last)
    next(ring)
    for item in last:
        item.middle()
    for key, k in zip(small_keys, (z - 1, z + 1, z + 2), strict=True):
        net.take(key, small_z.at[lax.rem(k + 4, 4)])
    small_out[...] = (small_z[0] + small_z[1]) + (small_z[2] + small_z[3])
    next(ring)
    for item in last:
        item.end()
    after = ring_dp(
        net,
        at,
        (lambda zz, yy: [qkv_piece(zz * 4 + yy)], lambda zz, yy: [out_piece(zz * 4 + yy)]),
    )
    next(after)
    for _ in ring:
        next(after, None)
    drain(after)
    net.finish()


def run_sums(gu, down, qkv, out, small):
    def shape(dims, dtype):
        return jax.ShapeDtypeStruct(dims, dtype)

    outs = (
        shape((2, FEAT, 4 * PART), BF),
        shape((4, 1280, FEAT), BF),
        shape((FEAT, QKV), BF),
        shape((QCOLS, FEAT), BF),
        shape(small.shape, F32),
    )
    return pl.pallas_call(
        sums_kernel,
        out_shape=outs,
        in_specs=[vmem()] * 5,
        out_specs=[vmem()] * len(outs),
        scratch_shapes=[pltpu.VMEM((4,) + small.shape, F32)] * 2
        + ring_scratch(SMALL_FIRST, SMALL_LAST)
        + [pltpu.SemaphoreType.DMA((128,)), pltpu.SemaphoreType.DMA((128,))],
        compiler_params=pltpu.CompilerParams(
            collective_id=3, has_side_effects=True, vmem_limit_bytes=VMEM_LIMIT
        ),
        cost_estimate=pl.CostEstimate(
            flops=10**8, bytes_accessed=60 * 10**6, transcendentals=0
        ),
        name="sums_over_sequences",
    )(gu, down, qkv, out, small)


def widen_kernel(gu, down, gate_out, up_out, down_out, gate_buf, up_buf, down_buf, sems):
    skip = 3 * PART
    slots = [None, None]

    def chunk(n):
        rows = pl.ds(n * 48, 48)
        place = n % 2
        if slots[place] is not None:
            for copy in slots[place]:
                copy.wait()
        copies = []
        for i, (buf, out) in enumerate(((gate_buf, gate_out), (up_buf, up_out))):
            buf[place, :, :skip] = gu[i, rows, :skip].astype(F32)
            buf[place, :, skip:] = gu[i, rows, skip + HEAD :].astype(F32)
            copies.append(pltpu.make_async_copy(buf.at[place], out.at[rows, :], sems.at[place, i]))
        quarter, part = n // 2, n % 2
        for m in range(4):
            slot = 160 * (4 * part + m)
            down_buf[place, pl.ds(144 * m, 80), :] = down[quarter, pl.ds(slot, 80), :].astype(F32)
            down_buf[place, pl.ds(144 * m + 80, 64), :] = down[
                quarter, pl.ds(slot + 96, 64), :
            ].astype(F32)
        drop = HEAD if quarter == 3 and part == 0 else 0
        start = PART * quarter + 576 * part - (HEAD if quarter == 3 and part == 1 else 0)
        copies.append(
            pltpu.make_async_copy(
                down_buf.at[place, pl.ds(drop, 576 - drop), :],
                down_out.at[pl.ds(start, 576 - drop), :],
                sems.at[place, 2],
            )
        )
        for copy in copies:
            copy.start()
        slots[place] = copies

    for n in range(8):
        chunk(n)
    for copies in slots:
        for copy in copies:
            copy.wait()


def run_widen(gu, down):
    outs = [jax.ShapeDtypeStruct((FEAT, UNITS), F32)] * 2
    outs.append(jax.ShapeDtypeStruct((UNITS, FEAT), F32))
    return pl.pallas_call(
        widen_kernel,
        out_shape=outs,
        in_specs=[vmem()] * 2,
        out_specs=[anywhere()] * 3,
        scratch_shapes=[
            pltpu.VMEM((2, 48, UNITS), F32),
            pltpu.VMEM((2, 48, UNITS), F32),
            pltpu.VMEM((2, 576, FEAT), F32),
            pltpu.SemaphoreType.DMA((2, 3)),
        ],
        compiler_params=pltpu.CompilerParams(vmem_limit_bytes=VMEM_LIMIT),
        cost_estimate=pl.CostEstimate(
            flops=10**7, bytes_accessed=36 * 10**6, transcendentals=0
        ),
        name="widen",
    )(gu, down)


def rope_tables(count):
    places = jnp.arange(count, dtype=jnp.int32).astype(F32)
    inverse = 1.0 / THETA ** (jnp.arange(0, HEAD, 2).astype(F32) / HEAD)
    angles = places[:, None] * inverse[None, :]
    cosine, sine = jnp.cos(angles), jnp.sin(angles)
    return jnp.concatenate([cosine, cosine], axis=-1), jnp.concatenate([-sine, sine], axis=-1)


def body(
    layer_input,
    gain_attn,
    w_query,
    w_key,
    w_value,
    b_query,
    b_key,
    b_value,
    w_out,
    gain_ffn,
    w_gate,
    w_up,
    w_down,
    out_grad,
):
    cosine, sine = rope_tables(SEQ)
    w_qkv = jnp.concatenate([w_query, w_key, w_value], axis=1)
    bias = jnp.concatenate([b_query, b_key, b_value]).astype(F32)[None]
    gains = jnp.zeros((8, FEAT), F32).at[0].set(gain_attn.astype(F32)).at[1].set(gain_ffn.astype(F32))
    (
        xs,
        normed1_cols,
        grads_all,
        normed2_all,
        qkv_w,
        out_w,
        gate_w,
        up_w,
        down_w,
        queries,
        key,
        value,
        lse,
        attn,
        mid,
        gains_all,
    ) = run_forward(
        layer_input, out_grad, w_qkv, w_out, w_gate, w_up, w_down, gains, bias, cosine, sine
    )
    dn2, layer_output, grad_gu, grad_down = run_ffn(
        normed2_all, grads_all, gate_w, up_w, down_w, mid
    )
    grad_input, grad_out, grad_qkv, small, grad_gu, grad_down = run_backward(
        dn2,
        mid,
        grads_all,
        gains_all,
        xs,
        normed1_cols,
        attn,
        queries,
        key,
        value,
        lse,
        out_w,
        qkv_w,
        cosine,
        sine,
        grad_gu.reshape(2, 4, 2, 4, 48, PART),
        grad_down.reshape(2, 2, 288, MODEL),
    )
    grad_gu, grad_down, grad_qkv, grad_out, small = run_sums(
        grad_gu,
        grad_down,
        grad_qkv.reshape(2, 4, 48, QKV),
        grad_out.reshape(2, 2, 4, 48, FEAT),
        small,
    )
    grad_gate, grad_up, grad_down = run_widen(grad_gu, grad_down)
    grad_qkv = grad_qkv.astype(F32)
    key_end, bias_start = QCOLS + HEAD, FEAT + QCOLS
    return (
        layer_output,
        grad_input,
        small[0, :FEAT],
        grad_qkv[:, :QCOLS],
        grad_qkv[:, QCOLS:key_end],
        grad_qkv[:, key_end:],
        small[0, FEAT:bias_start],
        small[0, bias_start : bias_start + HEAD],
        small[0, bias_start + HEAD :],
        grad_out.astype(F32),
        small[1, :FEAT],
        grad_gate,
        grad_up,
        grad_down,
    )


def solution(mesh):
    in_specs = (
        P(("dp", "row"), "col"),
        P("col"),
        P("col", "row"),
        P("col", "row"),
        P("col", "row"),
        P("row"),
        P("row"),
        P("row"),
        P("row", "col"),
        P("col"),
        P("col", "row"),
        P("col", "row"),
        P("row", "col"),
        P(("dp", "row"), "col"),
    )
    out_specs = (
        P(("dp", "row"), "col"),
        P(("dp", "row"), "col"),
        P("col"),
        P("col", "row"),
        P("col", "row"),
        P("col", "row"),
        P("row"),
        P("row"),
        P("row"),
        P("row", "col"),
        P("col"),
        P("col", "row"),
        P("col", "row"),
        P("row", "col"),
    )
    return jax.shard_map(body, mesh=mesh, in_specs=in_specs, out_specs=out_specs, check_vma=False)
```

```python
import functools

import jax
import jax.numpy as jnp
from jax import lax
from jax.experimental import pallas as pl
from jax.experimental.pallas import tpu as pltpu
from jax.sharding import PartitionSpec as P

EPS = 1e-06
THETA = 1000000.0
NEG = -1e30
BF = jnp.bfloat16
F32 = jnp.float32
MESH = pl.DeviceIdType.MESH
HEAD = 128
HEADS = 6
SEQ = 1024
MODEL = 1536
FEAT = 384
BLOCK = 128
UNITS = 4480
PART = 1152
QCOLS = 768
QKV = 1024
VMEM_LIMIT = 62 * 2**20
SCALE = HEAD ** (-0.5)


def dot(left, right, left_dim=1, right_dim=0):
    return lax.dot_general(
        left, right, (((left_dim,), (right_dim,)), ((), ())), preferred_element_type=F32
    )


def aligned(index, step):
    return pl.multiple_of(index * step, step)


def block_of(row, col):
    return col + row * (7 - 2 * col)


def quarter_start(col):
    return pl.multiple_of(col * PART - (col // 3) * HEAD, HEAD)


class Place:
    def __init__(self):
        self.dp, self.row, self.col = (lax.axis_index(a) for a in ("dp", "row", "col"))
        self.hi, self.core = self.col // 2, self.col % 2
        self.z, self.y = self.dp // 4, self.dp % 4
        self.sib = 2 * self.hi + 1 - self.core
        self.far = 2 * (1 - self.hi) + self.core
        self.sibfar = 2 * (1 - self.hi) + 1 - self.core
        self.block = block_of(self.row, self.col)
        self.S = {"col": self.sib}
        self.O = {"col": self.far}
        self.OS = {"col": self.sibfar}
        self.N1 = {"row": 1 - self.row}
        self.N2 = {"row": 1 - self.row, "col": self.far}
        self.N1S = {"row": 1 - self.row, "col": self.sib}
        self.N2S = {"row": 1 - self.row, "col": self.sibfar}

        def dp_at(z, y):
            return {"dp": lax.rem(z + 4, 4) * 4 + lax.rem(y + 4, 4)}

        self.YP, self.YM = dp_at(self.z, self.y + 1), dp_at(self.z, self.y - 1)
        self.Y2, self.Z2 = dp_at(self.z, self.y + 2), dp_at(self.z + 2, self.y)
        self.ZP, self.ZM = dp_at(self.z + 1, self.y), dp_at(self.z - 1, self.y)

    def meet(self, partners):
        barrier = pltpu.get_barrier_semaphore()
        for device in partners:
            pl.semaphore_signal(barrier, inc=1, device_id=device, device_id_type=MESH)
        pl.semaphore_wait(barrier, len(partners))


class Net:
    def __init__(self, send_sems, recv_sems, at):
        self.ss, self.rs, self.at, self.count, self.sent = send_sems, recv_sems, at, 0, []

    def key(self):
        self.count += 1
        return self.count - 1

    def copy(self, key, src, dst, device):
        return pltpu.make_async_remote_copy(
            src_ref=src,
            dst_ref=dst,
            send_sem=self.ss.at[key],
            recv_sem=self.rs.at[key],
            device_id=device,
            device_id_type=MESH,
        )

    def send(self, src, dst, device):
        key = self.key()
        copy = self.copy(key, src, dst, device)
        copy.start()
        self.sent.append(copy)
        return key

    def take(self, key, dst):
        self.copy(key, dst, dst, self.at.S).wait_recv()

    def finish(self, copies=None):
        copies = list(self.sent) if copies is None else copies
        for copy in copies:
            copy.wait_send()
            self.sent.remove(copy)


class Gather8:
    def __init__(self, net, at, place):
        self.net, self.at, self.place = net, at, place

    def start(self, src):
        net, at = self.net, self.at
        mine = self.place(at.row, at.col, None)
        self.k1 = net.send(src, mine, at.N1)
        self.k2 = net.send(src, mine, at.N2)
        self.k0 = net.send(src, mine, at.S)

    def middle(self):
        net, at, place = self.net, self.at, self.place
        near, away = place(1 - at.row, at.col, None), place(1 - at.row, at.far, None)
        first, last = place(1 - at.row, at.col, 0), place(1 - at.row, at.far, 1)
        net.take(self.k1, near)
        self.ka = net.send(first, first, at.N2)
        self.f1 = net.send(near, near, at.S)
        net.take(self.k2, away)
        self.kb = net.send(last, last, at.N1)
        self.f2 = net.send(away, away, at.S)

    def late(self):
        net, at, place = self.net, self.at, self.place
        first, last = place(at.row, at.far, 0), place(at.row, at.far, 1)
        net.take(self.ka, first)
        self.f3 = net.send(first, first, at.S)
        net.take(self.kb, last)
        self.f4 = net.send(last, last, at.S)

    def end(self, chip=None):
        net, at, place = self.net, self.at, self.place
        if chip in (None, 3):
            net.take(self.k0, place(at.row, at.sib, None))
        if chip in (None, 1):
            net.take(self.f1, place(1 - at.row, at.sib, None))
        if chip in (None, 2):
            net.take(self.f2, place(1 - at.row, at.sibfar, None))
        if chip in (None, 0):
            net.take(self.f3, place(at.row, at.sibfar, 0))
            net.take(self.f4, place(at.row, at.sibfar, 1))


def ring_dp(net, at, halves):
    def wrap(index):
        return lax.rem(index + 4, 4)

    sides = (((at.YP, at.YM), (at.ZP, at.ZM)), ((at.ZP, at.ZM), (at.YP, at.YM)))
    firsts, seconds = (at.y, at.z), (at.z, at.y)

    def refs(i, a, b):
        return halves[i](b, a) if i == 0 else halves[i](a, b)

    def send(i, a, b, device):
        return [net.send(ref, ref, device) for ref in refs(i, a, b)]

    def take(i, a, b, keys):
        for key, ref in zip(keys, refs(i, a, b), strict=True):
            net.take(key, ref)

    one, two, onward = {}, {}, {}
    for i in (0, 1):
        one[i] = [send(i, firsts[i], seconds[i], side) for side in sides[i][0]]
    for i in (0, 1):
        two[i, 0] = [send(i, firsts[i], seconds[i], side) for side in sides[i][1]]
    yield
    for i in (0, 1):
        minus = wrap(firsts[i] - 1)
        take(i, minus, seconds[i], one[i][0])
        one[i].append(send(i, minus, seconds[i], sides[i][0][0]))
        two[i, 1] = [send(i, minus, seconds[i], side) for side in sides[i][1]]
    yield
    for i in (0, 1):
        plus = wrap(firsts[i] + 1)
        take(i, plus, seconds[i], one[i][1])
        two[i, 2] = [send(i, plus, seconds[i], side) for side in sides[i][1]]
    offsets = (0, -1, 1, 2)
    for q in (0, 1, 2, 3):
        yield
        for i in (0, 1):
            if q == 1:
                across = wrap(firsts[i] + 2)
                take(i, across, seconds[i], one[i][2])
                two[i, 3] = [send(i, across, seconds[i], side) for side in sides[i][1]]
            slot = wrap(firsts[i] + offsets[q])
            minus, plus = wrap(seconds[i] - 1), wrap(seconds[i] + 1)
            take(i, slot, minus, two[i, q][0])
            if q < 2:
                onward[i, q] = send(i, slot, minus, sides[i][1][0])
            take(i, slot, plus, two[i, q][1])
            if q >= 2:
                onward[i, q] = send(i, slot, plus, sides[i][1][1])
    for q in (0, 1, 2, 3):
        yield
        for i in (0, 1):
            slot = wrap(firsts[i] + offsets[q])
            take(i, slot, wrap(seconds[i] + 2), onward[i, q])


def drain(steps):
    for _ in steps:
        pass


def rms(values):
    return lax.rsqrt(jnp.mean(values * values, axis=1, keepdims=True) + EPS)


def turn(values):
    return pltpu.roll(values, HEAD // 2, 1)


def causal(scores, start):
    places = start + lax.broadcasted_iota(jnp.int32, scores.shape, 0)
    keys = lax.broadcasted_iota(jnp.int32, scores.shape, 1)
    return jnp.where(keys <= places, scores, NEG)


def vmem():
    return pl.BlockSpec(memory_space=pltpu.VMEM)


def anywhere():
    return pl.BlockSpec(memory_space=pl.ANY)


class Reduce8:
    def __init__(self, net, at, own, other, sib_in, first_in, last_in, near_in, away_in):
        self.net, self.at, self.own, self.other, self.sib_in = net, at, own, other, sib_in
        self.first_in, self.last_in, self.near_in, self.away_in = first_in, last_in, near_in, away_in
        self.half = own.shape[1] // 2
        self.keys = {}

    def put(self, j, mine, theirs):
        self.own[j] = mine
        self.other[j] = theirs
        self.keys[j] = self.net.send(self.other.at[j], self.sib_in.at[j], self.at.S)

    def step(self, j):
        net, at, half = self.net, self.at, self.half
        net.take(self.keys[j], self.sib_in.at[j])
        total = self.own[j].astype(F32) + self.sib_in[j].astype(F32)
        if j == 0:
            self.own[j] = total.astype(BF)
            self.first = net.send(self.own.at[j, pl.ds(0, half)], self.first_in, at.N1)
            self.last = net.send(self.own.at[j, pl.ds(half, half)], self.last_in, at.N2)
        elif j == 1:
            net.take(self.last, self.last_in)
            self.own[j, :half] = total[:half].astype(BF)
            self.own[j, half:] = (total[half:] + self.last_in[...].astype(F32)).astype(BF)
            self.near = net.send(self.own.at[j], self.near_in, at.N1)
        elif j == 2:
            net.take(self.first, self.first_in)
            self.own[j, :half] = (total[:half] + self.first_in[...].astype(F32)).astype(BF)
            self.own[j, half:] = total[half:].astype(BF)
            self.away = net.send(self.own.at[j], self.away_in, at.N2)
        else:
            net.take(self.near, self.near_in)
            net.take(self.away, self.away_in)
            return total + self.near_in[...].astype(F32) + self.away_in[...].astype(F32)
        return None


def reduce8_scratch(rows, columns):
    return [
        pltpu.VMEM((4, rows, columns), BF),
        pltpu.VMEM((4, rows, columns), BF),
        pltpu.VMEM((4, rows, columns), BF),
        pltpu.VMEM((rows // 2, columns), BF),
        pltpu.VMEM((rows // 2, columns), BF),
        pltpu.VMEM((rows, columns), BF),
        pltpu.VMEM((rows, columns), BF),
    ]


def tiles_of(width, step):
    return [(first, min(step, width - first)) for first in range(0, width, step)]


def forward_kernel(
    x_ref,
    og_ref,
    wq_ref,
    wk_ref,
    wv_ref,
    wout_ref,
    wg_ref,
    wu_ref,
    wd_ref,
    gains_ref,
    bias_ref,
    cos_ref,
    sin_ref,
    xs_ref,
    n1c_ref,
    og_out,
    qw_out,
    ow_out,
    q_ref,
    k_ref,
    v_ref,
    lse_ref,
    attn_ref,
    mid_ref,
    gains_all,
    dn2_ref,
    out_ref,
    grad_gu,
    grad_down,
    wqkv_ref,
    x_all,
    n1,
    og_all,
    n2_all,
    qw,
    ow,
    gw,
    uw,
    dw,
    part_out,
    part_in,
    d_up,
    ffn,
    tile_buf,
    *rest,
):
    red_a, red_b, sems = rest[:7], rest[7:14], rest[14:]
    send_sems, recv_sems, local_sems, tile_sems = sems
    at = Place()
    net = Net(send_sems, recv_sems, at)
    local, local_count = [], iter(range(32))

    def move(src, dst):
        copy = pltpu.make_async_copy(src, dst, local_sems.at[next(local_count)])
        copy.start()
        local.append(copy)
        return copy

    joined = [
        move(wq_ref, wqkv_ref.at[:, pl.ds(0, QCOLS)]),
        move(wk_ref, wqkv_ref.at[:, pl.ds(QCOLS, HEAD)]),
        move(wv_ref, wqkv_ref.at[:, pl.ds(QCOLS + HEAD, HEAD)]),
    ]
    at.meet((at.S, at.N1, at.N2, at.O, at.OS, at.YP, at.YM, at.ZP, at.ZM))
    for copy in joined:
        copy.wait()
    local.clear()

    def tokens_of(array):
        def place(row, col, part):
            if part is None:
                rows = pl.ds(aligned(row, SEQ // 2), SEQ // 2)
            else:
                rows = pl.ds(aligned(row * 2 + part, SEQ // 4), SEQ // 4)
            return array.at[rows, pl.ds(aligned(col, FEAT), FEAT)]

        return place

    mine, mine_far = aligned(at.col, FEAT), aligned(1 - at.hi, 2 * FEAT)
    move(x_ref, tokens_of(x_all)(at.row, at.col, None))
    move(wqkv_ref, qw.at[pl.ds(mine, FEAT), :])
    move(wout_ref, ow.at[:, pl.ds(mine, FEAT)])
    move(gains_ref, gains_all.at[:, pl.ds(mine, FEAT)])
    start = quarter_start(at.col)
    move(wg_ref.at[:, pl.ds(start, PART)], gw.at[pl.ds(mine, FEAT), :])
    move(wu_ref.at[:, pl.ds(start, PART)], uw.at[pl.ds(mine, FEAT), :])
    move(wd_ref.at[pl.ds(start, PART), :], dw.at[:, pl.ds(mine, FEAT)])
    move(og_ref, tokens_of(og_all)(at.row, at.col, None))

    eighth = at.dp % 8
    across = [net.key() for _ in range(5)]

    def slice_copies(core, first, last):
        device = {"col": 2 * (1 - at.hi) + core}
        rows = pl.ds(aligned(eighth, 48), 48)
        target = pl.ds(pl.multiple_of(mine + eighth * 48, 16), 48)
        columns = pl.ds(core * 512, 512)
        out_rows = pl.ds(pl.multiple_of(core * FEAT + eighth * 48, 16), 48)
        theirs = quarter_start(2 * (1 - at.hi) + core)
        down_rows = pl.ds(pl.multiple_of(theirs + eighth * 144, 16), 144)
        down_target = pl.ds(aligned(eighth, 144), 144)
        pairs = (
            (wqkv_ref.at[rows, columns], qw.at[target, columns]),
            (wout_ref.at[out_rows, :], ow.at[out_rows, pl.ds(mine, FEAT)]),
            (wg_ref.at[rows, pl.ds(theirs, PART)], gw.at[target, :]),
            (wu_ref.at[rows, pl.ds(theirs, PART)], uw.at[target, :]),
            (wd_ref.at[down_rows, :], dw.at[down_target, pl.ds(mine, FEAT)]),
        )
        return [
            pltpu.make_async_remote_copy(
                src_ref=pairs[i][0],
                dst_ref=pairs[i][1],
                send_sem=net.ss.at[spare[core][i]],
                recv_sem=net.rs.at[across[i]],
                device_id=device,
                device_id_type=MESH,
            )
            for i in range(first, last)
        ]

    spare = ([net.key() for _ in range(5)], [net.key() for _ in range(5)])
    chosen = at.core == at.dp // 8

    @pl.when(chosen)
    def _():
        for core in (0, 1):
            for copy in slice_copies(core, 0, 2):
                copy.start()

    gather_x = Gather8(net, at, tokens_of(x_all))
    gather_x.start(x_ref)
    gain_far = net.send(gains_ref, gains_all.at[:, pl.ds(mine, FEAT)], at.N2)
    gain_sib = net.send(gains_ref, gains_all.at[:, pl.ds(mine, FEAT)], at.S)
    near_qw = net.send(wqkv_ref, qw.at[pl.ds(mine, FEAT), :], at.S)
    near_ow = net.send(wout_ref, ow.at[:, pl.ds(mine, FEAT)], at.S)

    @pl.when(chosen)
    def _():
        for core in (0, 1):
            for copy in slice_copies(core, 2, 5):
                copy.start()

    far_half = pl.ds(mine_far, 2 * FEAT)

    def qkv_slices(z, y):
        rows = pl.ds(pl.multiple_of(mine_far + (z * 4 + y) * 48, 16), 48)
        return [qw.at[rows, pl.ds(aligned(at.core, 512), 512)]]

    def out_slices(z, y):
        index = z * 4 + y
        rows = pl.ds(pl.multiple_of(at.core * FEAT + (index % 8) * 48, 16), 48)
        return [ow.at[rows, pl.ds(pl.multiple_of(mine_far + (index // 8) * FEAT, HEAD), FEAT)]]

    def ffn_slices(weights, first, count):
        def slices(z, y):
            index = z * 4 + y
            rows = pl.ds(pl.multiple_of(mine_far + index * 48, 16), 48)
            down_rows = pl.ds(pl.multiple_of((index % 8) * 144 + first, 16), count)
            lanes = pl.ds(pl.multiple_of(mine_far + (index // 8) * FEAT, HEAD), FEAT)
            return [weights.at[rows, :], dw.at[down_rows, lanes]]

        return slices

    net.take(across[0], qkv_slices(at.z, at.y)[0])
    ring = ring_dp(
        net,
        at,
        (
            lambda z, y: [qkv_slices(z, y)[0].at[:, pl.ds(0, 256)]],
            lambda z, y: [qkv_slices(z, y)[0].at[:, pl.ds(256, 256)]],
        ),
    )
    next(ring)
    near = [
        net.send(wg_ref.at[:, pl.ds(quarter_start(at.sib), PART)], gw.at[pl.ds(mine, FEAT), :], at.S),
        net.send(wu_ref.at[:, pl.ds(quarter_start(at.sib), PART)], uw.at[pl.ds(mine, FEAT), :], at.S),
        net.send(wd_ref.at[pl.ds(quarter_start(at.sib), PART), :], dw.at[:, pl.ds(mine, FEAT)], at.S),
    ]
    next(ring)
    next(ring)
    gather_x.middle()
    gains_far = gains_all.at[:, pl.ds(aligned(at.far, FEAT), FEAT)]
    net.take(gain_far, gains_far)
    gain_sibfar = net.send(gains_far, gains_far, at.S)
    next(ring)
    net.take(across[1], out_slices(at.z, at.y)[0])
    net.take(across[2], ffn_slices(gw, 0, 80)(at.z, at.y)[0])
    net.take(across[3], ffn_slices(uw, 80, 64)(at.z, at.y)[0])
    net.take(across[4], ffn_slices(uw, 0, 144)(at.z, at.y)[1])
    drain(ring)
    ring = ring_dp(
        net,
        at,
        (
            ffn_slices(gw, 0, 80),
            lambda z, y: ffn_slices(uw, 80, 64)(z, y) + out_slices(z, y),
        ),
    )
    next(ring)
    cols_half, rows_half = pl.ds(aligned(at.core, 512), 512), pl.ds(aligned(at.core, FEAT), FEAT)
    far_qw = net.send(qw.at[far_half, cols_half], qw.at[far_half, cols_half], at.S)
    gather_og = Gather8(net, at, tokens_of(og_all))
    gather_x.late()
    gather_og.start(og_ref)
    gather_x.end()
    early = list(net.sent)
    net.take(gain_sib, gains_all.at[:, pl.ds(aligned(at.sib, FEAT), FEAT)])
    net.take(gain_sibfar, gains_all.at[:, pl.ds(aligned(at.sibfar, FEAT), FEAT)])
    for copy in local:
        copy.wait()
    local.clear()

    gain1, gain2 = gains_all[0:1, :], gains_all[1:2, :]

    def norm_block(i, carry):
        rows = pl.ds(aligned(i, BLOCK), BLOCK)
        values = x_all[rows, :].astype(F32)
        n1[rows, :] = (values * rms(values) * gain1).astype(BF)
        return carry

    lax.fori_loop(0, SEQ // BLOCK // 2, norm_block, 0)
    next(ring)
    lax.fori_loop(SEQ // BLOCK // 2, SEQ // BLOCK, norm_block, 0)
    next(ring)
    gather_og.middle()
    my_rows = pl.ds(aligned(at.block, BLOCK), BLOCK)
    xs_ref[...] = x_all[my_rows, :]
    n1c_ref[...] = n1[:, pl.ds(mine, FEAT)]
    net.take(near_qw, qw.at[pl.ds(aligned(at.sib, FEAT), FEAT), :])
    other_cols = pl.ds(aligned(1 - at.core, 512), 512)
    net.take(far_qw, qw.at[far_half, other_cols])
    move(qw, qw_out)

    def kv_block(i, carry):
        rows = pl.ds(aligned(i, 256), 256)
        both = dot(n1[rows, :], qw[:, QCOLS:]) + bias_ref[:, QCOLS:]
        key = both[:, :HEAD]
        k_ref[rows, :] = (key * cos_ref[rows, :] + turn(key) * sin_ref[rows, :]).astype(BF)
        v_ref[rows, :] = both[:, HEAD:].astype(BF)
        return carry

    lax.fori_loop(0, SEQ // 256, kv_block, 0)
    next(ring)
    pair = (at.col, 7 - at.col)
    for j in (0, 1):
        rows = pl.ds(aligned(pair[j], BLOCK), BLOCK)
        queries = dot(n1[rows, :], qw[:, :QCOLS]) + bias_ref[:, :QCOLS]
        cosine, sine = cos_ref[rows, :], sin_ref[rows, :]
        for h in range(HEADS):
            one = queries[:, h * HEAD : (h + 1) * HEAD]
            q_ref[pl.ds(j * BLOCK, BLOCK), pl.ds(h * HEAD, HEAD)] = (
                one * cosine + turn(one) * sine
            ).astype(BF)
    next(ring)
    gather_og.late()

    for j in (0, 1):
        keys = SEQ // 2 * (j + 1)
        rows = pl.ds(j * BLOCK, BLOCK)

        def attend(h, carry):
            lanes = pl.ds(aligned(h, HEAD), HEAD)
            scores = dot(q_ref[rows, lanes], k_ref[:keys, :], 1, 1) * SCALE
            scores = causal(scores, pair[j] * BLOCK)
            top = jnp.max(scores, axis=1, keepdims=True)
            weights = jnp.exp(scores - top)
            total = jnp.sum(weights, axis=1, keepdims=True)
            lse_ref[j * HEADS + h] = top + jnp.log(total)
            probs = (weights * (1.0 / total)).astype(BF)
            attn_ref[rows, lanes] = dot(probs, v_ref[:keys, :]).astype(BF)
            return carry

        lax.fori_loop(0, HEADS // 2, attend, 0)
        next(ring)
        lax.fori_loop(HEADS // 2, HEADS, attend, 0)
        next(ring)

    drain(ring)
    far_ow = net.send(ow.at[rows_half, far_half], ow.at[rows_half, far_half], at.S)
    gather_og.end()
    move(og_all.at[my_rows, :], og_out)

    net.take(near_ow, ow.at[:, pl.ds(aligned(at.sib, FEAT), FEAT)])
    other_rows = pl.ds(aligned(1 - at.core, FEAT), FEAT)
    net.take(far_ow, ow.at[other_rows, far_half])
    move(ow, ow_out)
    part_out[...] = dot(attn_ref[pl.ds(aligned(1 - at.row, BLOCK), BLOCK), :], ow[...]).astype(BF)
    part = net.send(part_out, part_in, at.N1)
    own = dot(attn_ref[pl.ds(aligned(at.row, BLOCK), BLOCK), :], ow[...])
    net.take(part, part_in)
    mid = xs_ref[...].astype(F32) + own + part_in[...].astype(F32)
    mid_ref[...] = mid

    def place_n2(row, col, part):
        first = block_of(row, col) * BLOCK
        if part is None:
            return n2_all.at[pl.ds(pl.multiple_of(first, BLOCK), BLOCK), :]
        return n2_all.at[pl.ds(pl.multiple_of(first + part * 64, 64), 64), :]

    n2_all[my_rows, :] = (mid * rms(mid) * gain2).astype(BF)
    gather_n2 = Gather8(net, at, place_n2)
    gather_n2.start(place_n2(at.row, at.col, None))
    net.take(near[2], dw.at[:, pl.ds(aligned(at.sib, FEAT), FEAT)])

    def hidden_back(i, carry):
        rows = pl.ds(aligned(i, 256), 256)
        for first, width in tiles_of(PART, 512):
            lanes = pl.ds(first, width)
            d_up[rows, lanes] = dot(og_all[rows, :], dw[lanes, :], 1, 1).astype(BF)
        return carry

    lax.fori_loop(0, 3, hidden_back, 0)
    gather_n2.middle()
    lax.fori_loop(3, 4, hidden_back, 0)
    net.take(near[0], gw.at[pl.ds(aligned(at.sib, FEAT), FEAT), :])
    net.take(near[1], uw.at[pl.ds(aligned(at.sib, FEAT), FEAT), :])

    net.finish(early)
    hidden, d_gate = x_all.at[:, pl.ds(0, PART)], n1.at[:, pl.ds(0, PART)]
    norms = Reduce8(net, at, *red_a)
    outs = Reduce8(net, at, *red_b)
    chips = ((at.row, 1 - at.hi), (1 - at.row, at.hi), (1 - at.row, 1 - at.hi), (at.row, at.hi))
    last_part = at.col == 3

    def tokens(j):
        row, hi = chips[j]
        first = 2 * hi + row * (6 - 4 * hi)
        return pl.ds(aligned(first, BLOCK), 256), at.core + row * (1 - 2 * at.core)

    for j in (3, 1, 2, 0):
        if j == 0:
            gather_n2.late()
        gather_n2.end(j)
        rows, _ = tokens(j)
        for first, width in tiles_of(PART, 512):
            lanes = pl.ds(first, width)
            gate = dot(n2_all[rows, :], gw[:, lanes])
            up = dot(n2_all[rows, :], uw[:, lanes])
            d_hidden = d_up[rows, lanes].astype(F32)
            sig = jax.nn.sigmoid(gate)
            act = gate * sig
            d_act = d_hidden * up * sig * (1.0 + gate * (1.0 - sig))
            values = [act * up, d_act, d_hidden * act]
            if first == 0:
                lane = lax.broadcasted_iota(jnp.int32, (1, width), 1)
                fresh = jnp.logical_or(lane >= HEAD, jnp.logical_not(last_part))
                values = [jnp.where(fresh, value, 0.0) for value in values]
            for ref, value in zip((hidden, d_gate, d_up), values, strict=True):
                ref[rows, lanes] = value.astype(BF)
    for j in range(4):
        rows, place = tokens(j)
        own_rows = pl.ds(pl.multiple_of(rows.start + place * BLOCK, BLOCK), BLOCK)
        other_rows = pl.ds(pl.multiple_of(rows.start + (1 - place) * BLOCK, BLOCK), BLOCK)
        parts = [
            (dot(d_gate[r, :], gw[...], 1, 1) + dot(d_up[r, :], uw[...], 1, 1)).astype(BF)
            for r in (other_rows, own_rows)
        ]
        norms.put(j, parts[1], parts[0])
        if j:
            norms.step(j - 1)

    writes = []

    def outer_sum(left, right, out):
        height = left.shape[1] // 2
        for first, width in tiles_of(right.shape[1], 256):
            place = len(writes) % 2
            if len(writes) > 1:
                writes[-2].wait()
            for i in (0, 1):
                rows = pl.ds(i * height, height)
                tile_buf[place, rows, :width] = dot(
                    left[:, rows], right[:, pl.ds(first, width)], 0, 0
                ).astype(BF)
            writes.append(
                pltpu.make_async_copy(
                    tile_buf.at[place, pl.ds(0, 2 * height), pl.ds(0, width)],
                    out.at[:, pl.ds(first, width)],
                    tile_sems.at[place],
                )
            )
            writes[-1].start()

    outer_sum(hidden, og_all, grad_down)
    for j in range(4):
        row, hi = chips[j]
        rows = pl.ds(aligned(row, SEQ // 2), SEQ // 2)
        lanes = pl.ds(aligned(hi, QCOLS), QCOLS)
        ffn[...] = dot(hidden[rows, :], dw[:, lanes])
        if j in (0, 3):
            mine_mid = pl.ds(pl.multiple_of((at.block - 4 * at.row) * BLOCK, BLOCK), BLOCK)
            ffn[mine_mid, :] += mid_ref[:, lanes]
        own = ffn[:, pl.ds(aligned(at.core, FEAT), FEAT)].astype(BF)
        outs.put(j, own, ffn[:, pl.ds(aligned(1 - at.core, FEAT), FEAT)].astype(BF))
        if j:
            outs.step(j - 1)
        if j == 1:
            dn2_ref[...] = norms.step(3)
    outer_sum(n2_all, d_gate, grad_gu.at[0])
    outer_sum(n2_all, d_up, grad_gu.at[1])
    out_ref[...] = outs.step(3)
    for copy in writes[-2:]:
        copy.wait()
    for copy in local:
        copy.wait()
    net.finish()

    @pl.when(chosen)
    def _():
        for core in (0, 1):
            for copy in slice_copies(core, 0, 5):
                copy.wait_send()


def run_forward(x, og, wq, wk, wv, wout, wg, wu, wd, gains, bias, cosine, sine):
    outs = (
        ((BLOCK, MODEL), BF, vmem),
        ((SEQ, FEAT), BF, vmem),
        ((BLOCK, MODEL), BF, anywhere),
        ((MODEL, QKV), BF, anywhere),
        ((QCOLS, MODEL), BF, anywhere),
        ((2 * BLOCK, QCOLS), BF, vmem),
        ((SEQ, HEAD), BF, vmem),
        ((SEQ, HEAD), BF, vmem),
        ((2 * HEADS, BLOCK, 1), F32, vmem),
        ((2 * BLOCK, QCOLS), BF, vmem),
        ((BLOCK, MODEL), F32, vmem),
        ((8, MODEL), F32, vmem),
        ((BLOCK, MODEL), F32, vmem),
        ((SEQ // 2, FEAT), F32, vmem),
        ((2, MODEL, PART), BF, anywhere),
        ((PART, MODEL), BF, anywhere),
    )
    return pl.pallas_call(
        forward_kernel,
        out_shape=[jax.ShapeDtypeStruct(dims, dtype) for dims, dtype, _ in outs],
        in_specs=[anywhere()] * 9 + [vmem()] * 4,
        out_specs=[place() for _, _, place in outs],
        scratch_shapes=[
            pltpu.VMEM((FEAT, QKV), BF),
            pltpu.VMEM((SEQ, MODEL), BF),
            pltpu.VMEM((SEQ, MODEL), BF),
            pltpu.VMEM((SEQ, MODEL), BF),
            pltpu.VMEM((SEQ, MODEL), BF),
            pltpu.VMEM((MODEL, QKV), BF),
            pltpu.VMEM((QCOLS, MODEL), BF),
            pltpu.VMEM((MODEL, PART), BF),
            pltpu.VMEM((MODEL, PART), BF),
            pltpu.VMEM((PART, MODEL), BF),
            pltpu.VMEM((BLOCK, MODEL), BF),
            pltpu.VMEM((BLOCK, MODEL), BF),
            pltpu.VMEM((SEQ, PART), BF),
            pltpu.VMEM((SEQ // 2, QCOLS), F32),
            pltpu.VMEM((2, MODEL, 256), BF),
        ]
        + reduce8_scratch(BLOCK, MODEL)
        + reduce8_scratch(SEQ // 2, FEAT)
        + [
            pltpu.SemaphoreType.DMA((200,)),
            pltpu.SemaphoreType.DMA((200,)),
            pltpu.SemaphoreType.DMA((32,)),
            pltpu.SemaphoreType.DMA((2,)),
        ],
        compiler_params=pltpu.CompilerParams(
            collective_id=0, has_side_effects=True, vmem_limit_bytes=VMEM_LIMIT
        ),
        cost_estimate=pl.CostEstimate(
            flops=37 * 10**9, bytes_accessed=80 * 10**6, transcendentals=4 * 10**6
        ),
        name="forward_and_feed_forward",
    )(x, og, wq, wk, wv, wout, wg, wu, wd, gains, bias, cosine, sine)


def add_up(out, terms):
    lead = out.shape[:-2]
    if not lead:
        total = terms[0][...].astype(F32)
        for term in terms[1:]:
            total = total + term[...].astype(F32)
        out[...] = total.astype(out.dtype)
        return
    count = 1
    for size in lead:
        count *= size

    def step(i, carry):
        index = []
        for size in reversed(lead):
            index.insert(0, i % size)
            i = i // size
        index = tuple(index)
        total = terms[0].at[index][...].astype(F32)
        for term in terms[1:]:
            total = total + term.at[index][...].astype(F32)
        out.at[index][...] = total.astype(out.dtype)
        return carry

    lax.fori_loop(0, count, step, 0)


class RingItem:
    def __init__(self, net, sides, place, part, way, bufs, own):
        self.net, self.part, self.own = net, part, own
        self.relay, self.staged, self.from_last, self.from_next = bufs
        self.onward, self.back = (sides[0], sides[1]) if way == 0 else (sides[1], sides[0])
        step = 1 - 2 * way
        self.here, self.next, self.across, self.last = (
            lax.rem(place + 4 + step * i, 4) for i in (0, 1, 2, 3)
        )

    def start(self):
        self.k_relay = self.net.send(self.part(self.across), self.relay, self.onward)

    def direct(self):
        self.k_next = self.net.send(self.part(self.last), self.from_next, self.back)

    def middle(self):
        self.net.take(self.k_relay, self.relay)
        add_up(self.staged, [self.part(self.next), self.relay])
        self.k_last = self.net.send(self.staged, self.from_last, self.onward)

    def end(self):
        self.net.take(self.k_next, self.from_next)
        self.net.take(self.k_last, self.from_last)
        add_up(self.own, [self.part(self.here), self.from_next, self.from_last])


def begin(items):
    for item in items:
        item.start()
    for item in items:
        item.direct()


LEFT, RIGHT = pl.ds(0, QCOLS), pl.ds(QCOLS, QCOLS)
FFN_FIRST = (((2, 2, 48, PART), (2, 80, QCOLS)), ((2, 2, 48, PART), (144, QCOLS)))
FFN_LAST = (((2, 48, PART), (80, QCOLS)), ((2, 48, PART), (80, QCOLS)))
SMALL_FIRST = (((2, 48, 512),), ((2, 48, FEAT),))
SMALL_LAST = (((48, 512),), ((48, FEAT),))


def down_rows(k):
    return pl.ds(pl.multiple_of(72 * k - 8 * (k % 2), 16), 80)


def ring_scratch(first, last):
    scratch = []
    for i in (0, 1):
        for dims in first[i]:
            scratch += [pltpu.VMEM(dims, BF)] * 8
            scratch.append(pltpu.VMEM((2,) + dims, BF))
        for dims in last[i]:
            scratch += [pltpu.VMEM(dims, BF)] * 4
    return scratch


def ring_items(net, at, first, last, parts, seconds, finals, bufs):
    sides = (((at.YP, at.YM), (at.ZP, at.ZM)), ((at.ZP, at.ZM), (at.YP, at.YM)))
    places = ((at.y, at.z), (at.z, at.y))
    bufs = list(bufs)
    one, two = ([], []), ([], [])
    for i in (0, 1):
        owns = []
        for n in range(len(first[i])):
            own = bufs[8]
            for way in (0, 1):
                part = functools.partial(lambda k, f, w: f(k, w), f=parts[i][n], w=way)
                four = bufs[4 * way : 4 * way + 4]
                one[i].append(
                    RingItem(net, sides[i][0], places[i][0], part, way, four, own.at[way])
                )
            owns.append(own)
            bufs = bufs[9:]
        for n in range(len(last[i])):
            part = functools.partial(lambda k, f, o: f(o, k), f=seconds[i][n], o=owns[n])
            two[i].append(
                RingItem(net, sides[i][1], places[i][1], part, n % 2, bufs[:4], finals[i][n])
            )
            bufs = bufs[4:]

    def mix(pair):
        return [item for items in zip(*pair, strict=True) for item in items]

    return mix(one), mix(two)


def ffn_items(net, at, gu, down, gu_own, down_own, bufs):
    parts = (
        (
            lambda k, way: gu.at[way, pl.ds(0, 2), :, k],
            lambda k, way: down.at[way, :, down_rows(k), LEFT],
        ),
        (
            lambda k, way: gu.at[k // 2, pl.ds(2, 2), k % 2, pl.ds(2 * way, 2)],
            lambda k, way: down.at[k // 2, k % 2, pl.ds(144 * way, 144), RIGHT],
        ),
    )
    seconds = (
        (lambda own, k: own.at[k // 2, :, k % 2], lambda own, k: own.at[k // 2, k % 2]),
        (
            lambda own, k: own.at[k // 2, :, k % 2],
            lambda own, k: own.at[k // 2, pl.ds(pl.multiple_of((k % 2) * 64, 64), 80)],
        ),
    )
    finals = (
        (gu_own.at[pl.ds(0, 2)], down_own.at[:, LEFT]),
        (gu_own.at[pl.ds(2, 2)], down_own.at[:, RIGHT]),
    )
    return ring_items(net, at, FFN_FIRST, FFN_LAST, parts, seconds, finals, bufs)


def small_items(net, at, qkv, out, qkv_own, out_own, bufs):
    parts = (
        (lambda k, way: qkv.at[:, k, :, pl.ds(512 * way, 512)],),
        (lambda k, way: out.at[k // 2, k % 2, pl.ds(2 * way, 2)],),
    )
    seconds = ((lambda own, k: own.at[k // 2, k % 2],), (lambda own, k: own.at[k // 2, k % 2],))
    finals = ((qkv_own,), (out_own,))
    return ring_items(net, at, SMALL_FIRST, SMALL_LAST, parts, seconds, finals, bufs)


def backward_kernel(
    dn2_ref,
    mid_ref,
    og_ref,
    gains_all,
    xs_ref,
    n1c,
    attn_ref,
    q_ref,
    k_ref,
    v_ref,
    lse_ref,
    ow,
    qw,
    cos_ref,
    sin_ref,
    gu,
    down,
    grad_in,
    grad_out,
    grad_qkv,
    small_ref,
    gu_own,
    down_own,
    sums_ref,
    sums_in,
    attn_all,
    mid_cols,
    mid_pair,
    d_mid,
    d_attn,
    d_q,
    d_kv,
    kv_out,
    kv_in,
    d_qkv_all,
    part_out,
    part_in,
    gi_out,
    gi_in,
    *rest,
):
    bufs, (send_sems, recv_sems) = rest[:-2], rest[-2:]
    at = Place()
    net = Net(send_sems, recv_sems, at)
    at.meet(
        (at.S, at.O, at.OS, at.N1, at.N2, at.N1S, at.N2S, at.YP, at.YM, at.ZP, at.ZM)
    )
    first, last = ffn_items(net, at, gu, down, gu_own, down_own, bufs)
    begin(first)
    peers = ((at.S, at.sib), (at.O, at.far), (at.OS, at.sibfar))
    pair = (at.col, 7 - at.col)

    def rows_at(block):
        return pl.ds(aligned(block, BLOCK), BLOCK)

    def cols_at(col):
        return pl.ds(aligned(col, FEAT), FEAT)

    class GatherCol:
        def __init__(self, array):
            self.array = array

        def rows(self, col, j):
            return self.array.at[rows_at(col + j * (7 - 2 * col)), :]

        def start(self):
            self.far = [net.send(self.rows(at.col, j), self.rows(at.col, j), at.O) for j in (0, 1)]
            self.sib = [net.send(self.rows(at.col, j), self.rows(at.col, j), at.S) for j in (0, 1)]

        def middle(self):
            self.onward = []
            for j in (0, 1):
                net.take(self.far[j], self.rows(at.far, j))
                self.onward.append(net.send(self.rows(at.far, j), self.rows(at.far, j), at.S))

        def end(self):
            for j in (0, 1):
                net.take(self.sib[j], self.rows(at.sib, j))
                net.take(self.onward[j], self.rows(at.sibfar, j))

    gather_attn = GatherCol(attn_all)
    for j in (0, 1):
        attn_all[rows_at(pair[j]), :] = attn_ref[pl.ds(j * BLOCK, BLOCK), :]

    gain1, gain2 = gains_all[0:1, :], gains_all[1:2, :]
    mid = mid_ref[...]
    scale = rms(mid)
    unit = mid * scale
    d_normed = dn2_ref[...]
    sums_ref[...] = jnp.zeros_like(sums_ref)
    sums_ref[1:2, :] = jnp.sum(d_normed * unit, axis=0, keepdims=True)
    bent = d_normed * gain2
    d_mid[...] = og_ref[...].astype(F32) + scale * (
        bent - unit * jnp.mean(bent * unit, axis=1, keepdims=True)
    )
    mid_pair[at.row] = d_mid[...].astype(BF)
    to_pair = net.send(mid_pair.at[at.row], mid_pair.at[at.row], at.N1)
    mid_cols[rows_at(at.block), :] = d_mid[:, cols_at(at.col)].astype(BF)
    spread = []
    others = (
        (at.S, at.row, at.sib),
        (at.N1, 1 - at.row, at.col),
        (at.N1S, 1 - at.row, at.sib),
        (at.O, at.row, at.far),
        (at.OS, at.row, at.sibfar),
        (at.N2, 1 - at.row, at.far),
        (at.N2S, 1 - at.row, at.sibfar),
    )
    for device, row, col in others:
        spread.append(
            net.send(
                mid_pair.at[at.row, :, cols_at(col)], mid_cols.at[rows_at(at.block), :], device
            )
        )
    gather_attn.start()
    net.take(to_pair, mid_pair.at[1 - at.row])
    for j in (0, 1):
        d_attn[pl.ds(j * BLOCK, BLOCK), :] = dot(mid_pair[j], ow[...], 1, 1).astype(BF)
    d_kv[...] = jnp.zeros_like(d_kv)
    for item in first:
        item.middle()

    for j in (0, 1):
        keys = SEQ // 2 * (j + 1)
        rows = pl.ds(j * BLOCK, BLOCK)

        def back(h, carry):
            lanes = pl.ds(aligned(h, HEAD), HEAD)
            queries, d_out = q_ref[rows, lanes], d_attn[rows, lanes]
            scores = dot(queries, k_ref[:keys, :], 1, 1) * SCALE
            scores = causal(scores, pair[j] * BLOCK)
            probs = jnp.exp(scores - lse_ref[j * HEADS + h])
            d_probs = dot(d_out, v_ref[:keys, :], 1, 1)
            inner = jnp.sum(probs * d_probs, axis=1, keepdims=True)
            d_scores = (probs * (d_probs - inner) * SCALE).astype(BF)
            d_q[rows, lanes] = dot(d_scores, k_ref[:keys, :])
            d_kv[:keys, :HEAD] += dot(d_scores, queries, 0, 0)
            d_kv[:keys, HEAD:] += dot(probs.astype(BF), d_out, 0, 0)
            return carry

        lax.fori_loop(0, HEADS, back, 0)
    gather_attn.middle()

    kv_out[...] = d_kv[...].astype(BF)
    kv_keys = [
        [
            net.send(kv_out.at[rows_at(col + j * (7 - 2 * col)), :], kv_in.at[i, j], device)
            for j in (0, 1)
        ]
        for i, (device, col) in enumerate(peers)
    ]
    cosines = [cos_ref[rows_at(pair[j]), :] for j in (0, 1)]
    sines = [sin_ref[rows_at(pair[j]), :] for j in (0, 1)]
    for j in (0, 1):
        for h in range(HEADS):
            one = d_q[pl.ds(j * BLOCK, BLOCK), pl.ds(h * HEAD, HEAD)]
            d_qkv_all[rows_at(pair[j]), pl.ds(h * HEAD, HEAD)] = (
                one * cosines[j] - turn(one) * sines[j]
            ).astype(BF)
    for item in first:
        item.end()
    begin(last)
    gather_attn.end()
    for key, (_, row, col) in zip(spread, others, strict=True):
        net.take(key, mid_cols.at[rows_at(block_of(row, col)), :])
    grad_out[...] = dot(attn_all[...], mid_cols[...], 0, 0).astype(BF)
    for j in (0, 1):
        total = d_kv[rows_at(pair[j]), :]
        for i in range(3):
            net.take(kv_keys[i][j], kv_in.at[i, j])
            total = total + kv_in[i, j].astype(F32)
        key = total[:, :HEAD]
        d_qkv_all[rows_at(pair[j]), pl.ds(QCOLS, HEAD)] = (
            key * cosines[j] - turn(key) * sines[j]
        ).astype(BF)
        d_qkv_all[rows_at(pair[j]), pl.ds(QCOLS + HEAD, HEAD)] = total[:, HEAD:].astype(BF)
    gather_qkv = GatherCol(d_qkv_all)
    gather_qkv.start()

    part_out[...] = dot(d_qkv_all[rows_at(block_of(1 - at.row, at.col)), :], qw[...], 1, 1).astype(BF)
    part = net.send(part_out, part_in, at.N1)
    d_normed = dot(d_qkv_all[rows_at(at.block), :], qw[...], 1, 1)
    net.take(part, part_in)
    d_normed = d_normed + part_in[...].astype(F32)
    values = xs_ref[...].astype(F32)
    scale = rms(values)
    unit = values * scale
    sums_ref[0:1, :] = jnp.sum(d_normed * unit, axis=0, keepdims=True)
    bent = d_normed * gain1
    total = d_mid[...] + scale * (bent - unit * jnp.mean(bent * unit, axis=1, keepdims=True))
    gi_out[...] = total.astype(BF)
    sums_in[at.row * 4 + at.col] = sums_ref[:, cols_at(at.col)]
    sums_keys = [
        net.send(sums_ref.at[:, cols_at(col)], sums_in.at[at.row * 4 + at.col], device)
        for device, row, col in others
    ]
    half_rows = pl.ds(pl.multiple_of((at.block - 4 * at.row) * BLOCK, BLOCK), BLOCK)
    gi_keys = [
        net.send(gi_out.at[:, cols_at(col)], gi_in.at[half_rows, :], device)
        for device, col in peers
    ]
    gi_in[half_rows, :] = gi_out[:, cols_at(at.col)]
    for item in last:
        item.middle()
    gather_qkv.middle()
    gather_qkv.end()
    grad_qkv[...] = dot(n1c[...], d_qkv_all[...], 0, 0).astype(BF)
    ones = jnp.ones((8, SEQ), BF)
    small_ref[:, FEAT:] = dot(ones, d_qkv_all[...])
    for key, (_, row, col) in zip(sums_keys, others, strict=True):
        net.take(key, sums_in.at[row * 4 + col])
    total = sums_in[0]
    for i in range(1, 8):
        total = total + sums_in[i]
    small_ref[:, :FEAT] = total
    for key, (_, col) in zip(gi_keys, peers, strict=True):
        offset = block_of(at.row, col) - 4 * at.row
        net.take(key, gi_in.at[pl.ds(pl.multiple_of(offset * BLOCK, BLOCK), BLOCK), :])
    for item in last:
        item.end()
    grad_in[...] = gi_in[...].astype(F32)
    net.finish()


def run_backward(*args):
    def out(shape, dtype):
        return jax.ShapeDtypeStruct(shape, dtype)

    outs = (
        out((SEQ // 2, FEAT), F32),
        out((QCOLS, FEAT), BF),
        out((FEAT, QKV), BF),
        out((8, FEAT + QKV), F32),
        out((4, 48, PART), BF),
        out((80, MODEL), BF),
    )
    return pl.pallas_call(
        backward_kernel,
        out_shape=outs,
        in_specs=[vmem()] * len(args),
        out_specs=[vmem()] * len(outs),
        scratch_shapes=[
            pltpu.VMEM((8, MODEL), F32),
            pltpu.VMEM((8, 8, FEAT), F32),
            pltpu.VMEM((SEQ, QCOLS), BF),
            pltpu.VMEM((SEQ, FEAT), BF),
            pltpu.VMEM((2, BLOCK, MODEL), BF),
            pltpu.VMEM((BLOCK, MODEL), F32),
            pltpu.VMEM((2 * BLOCK, QCOLS), BF),
            pltpu.VMEM((2 * BLOCK, QCOLS), F32),
            pltpu.VMEM((SEQ, 2 * HEAD), F32),
            pltpu.VMEM((SEQ, 2 * HEAD), BF),
            pltpu.VMEM((3, 2, BLOCK, 2 * HEAD), BF),
            pltpu.VMEM((SEQ, QKV), BF),
            pltpu.VMEM((BLOCK, MODEL), BF),
            pltpu.VMEM((BLOCK, MODEL), BF),
            pltpu.VMEM((BLOCK, MODEL), BF),
            pltpu.VMEM((SEQ // 2, FEAT), BF),
        ]
        + ring_scratch(FFN_FIRST, FFN_LAST)
        + [pltpu.SemaphoreType.DMA((80,)), pltpu.SemaphoreType.DMA((80,))],
        compiler_params=pltpu.CompilerParams(
            collective_id=2, has_side_effects=True, vmem_limit_bytes=VMEM_LIMIT
        ),
        cost_estimate=pl.CostEstimate(
            flops=10 * 10**9, bytes_accessed=40 * 10**6, transcendentals=2 * 10**6
        ),
        name="attention_backward",
    )(*args)


def sums_kernel(
    gu_own,
    down_own,
    qkv,
    out,
    small_ref,
    all_gu,
    all_down,
    all_qkv,
    all_out,
    small_out,
    small_y,
    small_z,
    *rest,
):
    bufs, (send_sems, recv_sems) = rest[:-2], rest[-2:]
    at = Place()
    net = Net(send_sems, recv_sems, at)
    at.meet((at.S, at.O, at.OS, at.YP, at.YM, at.ZP, at.ZM, at.Y2, at.Z2))
    z, y = at.z, at.y

    def gu_piece(k, lanes):
        rows = pl.ds(pl.multiple_of((k % 8) * 48, 16), 48)
        return all_gu.at[k // 8, rows, lanes]

    def part_lanes(col):
        return pl.ds(aligned(col, PART), PART)

    def down_piece(k):
        return all_down.at[:, pl.ds(pl.multiple_of(k * 80, 16), 80), :]

    def down_slot(col):
        return all_down.at[col, pl.ds(pl.multiple_of(at.dp * 80, 16), 80), :]

    def feat_lanes(col):
        return pl.ds(aligned(col, FEAT), FEAT)

    def qkv_piece(k):
        rows = pl.ds(pl.multiple_of((k % 8) * 48, 16), 48)
        return all_qkv.at[rows, pl.ds(pl.multiple_of((k // 8) * 512, 512), 512)]

    def out_piece(k):
        return all_out.at[pl.ds(pl.multiple_of(k * 48, 16), 48), :]

    peers = ((at.O, at.far), (at.OS, at.sibfar), (at.S, at.sib))
    keys = []
    for device, col in peers:
        keys.append(
            (
                net.send(gu_own.at[col], gu_piece(at.dp, part_lanes(at.col)), device),
                net.send(down_own.at[:, feat_lanes(col)], down_slot(at.col), device),
            )
        )
    small_y[y] = small_ref[...]
    small_keys = [net.send(small_ref, small_y.at[y], d) for d in (at.YP, at.YM, at.Y2)]
    first, last = small_items(net, at, qkv, out, qkv_piece(at.dp), out_piece(at.dp), bufs)
    begin(first)
    gu_piece(at.dp, part_lanes(at.col))[...] = gu_own[at.col]
    down_slot(at.col)[...] = down_own[:, feat_lanes(at.col)]
    for (one, two), (_, col) in zip(keys, peers, strict=True):
        net.take(one, gu_piece(at.dp, part_lanes(col)))
        net.take(two, down_slot(col))

    def half0(zz, yy):
        return [gu_piece(zz * 4 + yy, pl.ds(0, 3456))]

    def half1(zz, yy):
        return [gu_piece(zz * 4 + yy, pl.ds(3456, 1152)), down_piece(zz * 4 + yy)]

    ring = ring_dp(net, at, (half0, half1))
    next(ring)
    for item in first:
        item.middle()
    for key, k in zip(small_keys, (y - 1, y + 1, y + 2), strict=True):
        net.take(key, small_y.at[lax.rem(k + 4, 4)])
    small_z[z] = (small_y[0] + small_y[1]) + (small_y[2] + small_y[3])
    small_keys = [net.send(small_z.at[z], small_z.at[z], d) for d in (at.ZP, at.ZM, at.Z2)]
    next(ring)
    for item in first:
        item.end()
    begin(last)
    next(ring)
    for item in last:
        item.middle()
    for key, k in zip(small_keys, (z - 1, z + 1, z + 2), strict=True):
        net.take(key, small_z.at[lax.rem(k + 4, 4)])
    small_out[...] = (small_z[0] + small_z[1]) + (small_z[2] + small_z[3])
    next(ring)
    for item in last:
        item.end()
    after = ring_dp(
        net,
        at,
        (lambda zz, yy: [qkv_piece(zz * 4 + yy)], lambda zz, yy: [out_piece(zz * 4 + yy)]),
    )
    next(after)
    for _ in ring:
        next(after, None)
    drain(after)
    net.finish()


def run_sums(gu, down, qkv, out, small):
    def shape(dims, dtype):
        return jax.ShapeDtypeStruct(dims, dtype)

    outs = (
        shape((2, FEAT, 4 * PART), BF),
        shape((4, 1280, FEAT), BF),
        shape((FEAT, QKV), BF),
        shape((QCOLS, FEAT), BF),
        shape(small.shape, F32),
    )
    return pl.pallas_call(
        sums_kernel,
        out_shape=outs,
        in_specs=[vmem()] * 5,
        out_specs=[vmem()] * len(outs),
        scratch_shapes=[pltpu.VMEM((4,) + small.shape, F32)] * 2
        + ring_scratch(SMALL_FIRST, SMALL_LAST)
        + [pltpu.SemaphoreType.DMA((128,)), pltpu.SemaphoreType.DMA((128,))],
        compiler_params=pltpu.CompilerParams(
            collective_id=3, has_side_effects=True, vmem_limit_bytes=VMEM_LIMIT
        ),
        cost_estimate=pl.CostEstimate(
            flops=10**8, bytes_accessed=60 * 10**6, transcendentals=0
        ),
        name="sums_over_sequences",
    )(gu, down, qkv, out, small)


def widen_kernel(gu, down, gate_out, up_out, down_out, gate_buf, up_buf, down_buf, sems):
    skip = 3 * PART
    slots = [None, None]

    def chunk(n):
        rows = pl.ds(n * 48, 48)
        place = n % 2
        if slots[place] is not None:
            for copy in slots[place]:
                copy.wait()
        copies = []
        for i, (buf, out) in enumerate(((gate_buf, gate_out), (up_buf, up_out))):
            buf[place, :, :skip] = gu[i, rows, :skip].astype(F32)
            buf[place, :, skip:] = gu[i, rows, skip + HEAD :].astype(F32)
            copies.append(pltpu.make_async_copy(buf.at[place], out.at[rows, :], sems.at[place, i]))
        quarter, part = n // 2, n % 2
        for m in range(4):
            slot = 160 * (4 * part + m)
            down_buf[place, pl.ds(144 * m, 80), :] = down[quarter, pl.ds(slot, 80), :].astype(F32)
            down_buf[place, pl.ds(144 * m + 80, 64), :] = down[
                quarter, pl.ds(slot + 96, 64), :
            ].astype(F32)
        drop = HEAD if quarter == 3 and part == 0 else 0
        start = PART * quarter + 576 * part - (HEAD if quarter == 3 and part == 1 else 0)
        copies.append(
            pltpu.make_async_copy(
                down_buf.at[place, pl.ds(drop, 576 - drop), :],
                down_out.at[pl.ds(start, 576 - drop), :],
                sems.at[place, 2],
            )
        )
        for copy in copies:
            copy.start()
        slots[place] = copies

    for n in range(8):
        chunk(n)
    for copies in slots:
        for copy in copies:
            copy.wait()


def run_widen(gu, down):
    outs = [jax.ShapeDtypeStruct((FEAT, UNITS), F32)] * 2
    outs.append(jax.ShapeDtypeStruct((UNITS, FEAT), F32))
    return pl.pallas_call(
        widen_kernel,
        out_shape=outs,
        in_specs=[vmem()] * 2,
        out_specs=[anywhere()] * 3,
        scratch_shapes=[
            pltpu.VMEM((2, 48, UNITS), F32),
            pltpu.VMEM((2, 48, UNITS), F32),
            pltpu.VMEM((2, 576, FEAT), F32),
            pltpu.SemaphoreType.DMA((2, 3)),
        ],
        compiler_params=pltpu.CompilerParams(vmem_limit_bytes=VMEM_LIMIT),
        cost_estimate=pl.CostEstimate(
            flops=10**7, bytes_accessed=36 * 10**6, transcendentals=0
        ),
        name="widen",
    )(gu, down)


def rope_tables(count):
    places = jnp.arange(count, dtype=jnp.int32).astype(F32)
    inverse = 1.0 / THETA ** (jnp.arange(0, HEAD, 2).astype(F32) / HEAD)
    angles = places[:, None] * inverse[None, :]
    cosine, sine = jnp.cos(angles), jnp.sin(angles)
    return jnp.concatenate([cosine, cosine], axis=-1), jnp.concatenate([-sine, sine], axis=-1)


def body(
    layer_input,
    gain_attn,
    w_query,
    w_key,
    w_value,
    b_query,
    b_key,
    b_value,
    w_out,
    gain_ffn,
    w_gate,
    w_up,
    w_down,
    out_grad,
):
    cosine, sine = rope_tables(SEQ)
    bias = jnp.concatenate([b_query, b_key, b_value]).astype(F32)[None]
    gains = jnp.zeros((8, FEAT), F32).at[0].set(gain_attn.astype(F32)).at[1].set(gain_ffn.astype(F32))
    (
        xs,
        normed1_cols,
        grads_block,
        qkv_w,
        out_w,
        queries,
        key,
        value,
        lse,
        attn,
        mid,
        gains_all,
        dn2,
        layer_output,
        grad_gu,
        grad_down,
    ) = run_forward(
        layer_input,
        out_grad,
        w_query,
        w_key,
        w_value,
        w_out,
        w_gate,
        w_up,
        w_down,
        gains,
        bias,
        cosine,
        sine,
    )
    grad_input, grad_out, grad_qkv, small, grad_gu, grad_down = run_backward(
        dn2,
        mid,
        grads_block,
        gains_all,
        xs,
        normed1_cols,
        attn,
        queries,
        key,
        value,
        lse,
        out_w,
        qkv_w,
        cosine,
        sine,
        grad_gu.reshape(2, 4, 2, 4, 48, PART),
        grad_down.reshape(2, 2, 288, MODEL),
    )
    grad_gu, grad_down, grad_qkv, grad_out, small = run_sums(
        grad_gu,
        grad_down,
        grad_qkv.reshape(2, 4, 48, QKV),
        grad_out.reshape(2, 2, 4, 48, FEAT),
        small,
    )
    grad_gate, grad_up, grad_down = run_widen(grad_gu, grad_down)
    grad_qkv = grad_qkv.astype(F32)
    key_end, bias_start = QCOLS + HEAD, FEAT + QCOLS
    return (
        layer_output,
        grad_input,
        small[0, :FEAT],
        grad_qkv[:, :QCOLS],
        grad_qkv[:, QCOLS:key_end],
        grad_qkv[:, key_end:],
        small[0, FEAT:bias_start],
        small[0, bias_start : bias_start + HEAD],
        small[0, bias_start + HEAD :],
        grad_out.astype(F32),
        small[1, :FEAT],
        grad_gate,
        grad_up,
        grad_down,
    )


def solution(mesh):
    in_specs = (
        P(("dp", "row"), "col"),
        P("col"),
        P("col", "row"),
        P("col", "row"),
        P("col", "row"),
        P("row"),
        P("row"),
        P("row"),
        P("row", "col"),
        P("col"),
        P("col", "row"),
        P("col", "row"),
        P("row", "col"),
        P(("dp", "row"), "col"),
    )
    out_specs = (
        P(("dp", "row"), "col"),
        P(("dp", "row"), "col"),
        P("col"),
        P("col", "row"),
        P("col", "row"),
        P("col", "row"),
        P("row"),
        P("row"),
        P("row"),
        P("row", "col"),
        P("col"),
        P("col", "row"),
        P("col", "row"),
        P("row", "col"),
    )
    return jax.shard_map(body, mesh=mesh, in_specs=in_specs, out_specs=out_specs, check_vma=False)
```

```python
import functools

import jax
import jax.numpy as jnp
import numpy as np
from jax import lax
from jax.experimental import pallas as pl
from jax.experimental.pallas import tpu as pltpu
from jax.sharding import PartitionSpec as P

EPS = 1e-06
THETA = 1000000.0
NEG = -1e30
BF = jnp.bfloat16
F32 = jnp.float32
MESH = pl.DeviceIdType.MESH
HEAD = 128
HEADS = 6
SEQ = 1024
MODEL = 1536
FEAT = 384
BLOCK = 128
UNITS = 4480
PART = 1152
QCOLS = 768
QKV = 1024
VMEM_LIMIT = 62 * 2**20
SCALE = HEAD ** (-0.5)


def dot(left, right, left_dim=1, right_dim=0):
    return lax.dot_general(
        left, right, (((left_dim,), (right_dim,)), ((), ())), preferred_element_type=F32
    )


def aligned(index, step):
    return pl.multiple_of(index * step, step)


def block_of(row, col):
    return col + row * (7 - 2 * col)


def quarter_start(col):
    return pl.multiple_of(col * PART - (col // 3) * HEAD, HEAD)


class Place:
    def __init__(self):
        self.dp, self.row, self.col = (lax.axis_index(a) for a in ("dp", "row", "col"))
        self.hi, self.core = self.col // 2, self.col % 2
        self.z, self.y = self.dp // 4, self.dp % 4
        self.sib = 2 * self.hi + 1 - self.core
        self.far = 2 * (1 - self.hi) + self.core
        self.sibfar = 2 * (1 - self.hi) + 1 - self.core
        self.block = block_of(self.row, self.col)
        self.S = {"col": self.sib}
        self.O = {"col": self.far}
        self.OS = {"col": self.sibfar}
        self.N1 = {"row": 1 - self.row}
        self.N2 = {"row": 1 - self.row, "col": self.far}
        self.N1S = {"row": 1 - self.row, "col": self.sib}
        self.N2S = {"row": 1 - self.row, "col": self.sibfar}

        def dp_at(z, y):
            return {"dp": lax.rem(z + 4, 4) * 4 + lax.rem(y + 4, 4)}

        self.YP, self.YM = dp_at(self.z, self.y + 1), dp_at(self.z, self.y - 1)
        self.Y2, self.Z2 = dp_at(self.z, self.y + 2), dp_at(self.z + 2, self.y)
        self.ZP, self.ZM = dp_at(self.z + 1, self.y), dp_at(self.z - 1, self.y)

    def meet(self, partners):
        barrier = pltpu.get_barrier_semaphore()
        for device in partners:
            pl.semaphore_signal(barrier, inc=1, device_id=device, device_id_type=MESH)
        pl.semaphore_wait(barrier, len(partners))


class Net:
    def __init__(self, send_sems, recv_sems, at):
        self.ss, self.rs, self.at, self.count, self.sent = send_sems, recv_sems, at, 0, []

    def key(self):
        self.count += 1
        return self.count - 1

    def copy(self, key, src, dst, device):
        return pltpu.make_async_remote_copy(
            src_ref=src,
            dst_ref=dst,
            send_sem=self.ss.at[key],
            recv_sem=self.rs.at[key],
            device_id=device,
            device_id_type=MESH,
        )

    def send(self, src, dst, device):
        key = self.key()
        copy = self.copy(key, src, dst, device)
        copy.start()
        self.sent.append(copy)
        return key

    def take(self, key, dst):
        self.copy(key, dst, dst, self.at.S).wait_recv()

    def finish(self, copies=None):
        copies = list(self.sent) if copies is None else copies
        for copy in copies:
            copy.wait_send()
            self.sent.remove(copy)


class Gather8:
    def __init__(self, net, at, place):
        self.net, self.at, self.place = net, at, place

    def start(self, src):
        net, at = self.net, self.at
        mine = self.place(at.row, at.col, None)
        self.k1 = net.send(src, mine, at.N1)
        self.k2 = net.send(src, mine, at.N2)
        self.k0 = net.send(src, mine, at.S)

    def middle(self):
        net, at, place = self.net, self.at, self.place
        near, away = place(1 - at.row, at.col, None), place(1 - at.row, at.far, None)
        first, last = place(1 - at.row, at.col, 0), place(1 - at.row, at.far, 1)
        net.take(self.k1, near)
        self.ka = net.send(first, first, at.N2)
        self.f1 = net.send(near, near, at.S)
        net.take(self.k2, away)
        self.kb = net.send(last, last, at.N1)
        self.f2 = net.send(away, away, at.S)

    def late(self):
        net, at, place = self.net, self.at, self.place
        first, last = place(at.row, at.far, 0), place(at.row, at.far, 1)
        net.take(self.ka, first)
        self.f3 = net.send(first, first, at.S)
        net.take(self.kb, last)
        self.f4 = net.send(last, last, at.S)

    def end(self, chip=None):
        net, at, place = self.net, self.at, self.place
        if chip in (None, 3):
            net.take(self.k0, place(at.row, at.sib, None))
        if chip in (None, 1):
            net.take(self.f1, place(1 - at.row, at.sib, None))
        if chip in (None, 2):
            net.take(self.f2, place(1 - at.row, at.sibfar, None))
        if chip in (None, 0):
            net.take(self.f3, place(at.row, at.sibfar, 0))
            net.take(self.f4, place(at.row, at.sibfar, 1))


def ring_dp(net, at, halves, ready=(None, None)):
    def wrap(index):
        return lax.rem(index + 4, 4)

    sides = (((at.YP, at.YM), (at.ZP, at.ZM)), ((at.ZP, at.ZM), (at.YP, at.YM)))
    firsts, seconds = (at.y, at.z), (at.z, at.y)

    def refs(i, a, b):
        return halves[i](b, a) if i == 0 else halves[i](a, b)

    def send(i, a, b, device):
        return [net.send(ref, ref, device) for ref in refs(i, a, b)]

    def take(i, a, b, keys):
        for key, ref in zip(keys, refs(i, a, b), strict=True):
            net.take(key, ref)

    one, two, onward = {}, {}, {}
    for i in (0, 1):
        if ready[i]:
            ready[i]()
        one[i] = [send(i, firsts[i], seconds[i], side) for side in sides[i][0]]
        if ready[i]:
            two[i, 0] = [send(i, firsts[i], seconds[i], side) for side in sides[i][1]]
    for i in (0, 1):
        if not ready[i]:
            two[i, 0] = [send(i, firsts[i], seconds[i], side) for side in sides[i][1]]
    yield
    for i in (0, 1):
        minus = wrap(firsts[i] - 1)
        take(i, minus, seconds[i], one[i][0])
        one[i].append(send(i, minus, seconds[i], sides[i][0][0]))
        two[i, 1] = [send(i, minus, seconds[i], side) for side in sides[i][1]]
    yield
    for i in (0, 1):
        plus = wrap(firsts[i] + 1)
        take(i, plus, seconds[i], one[i][1])
        two[i, 2] = [send(i, plus, seconds[i], side) for side in sides[i][1]]
    offsets = (0, -1, 1, 2)
    for q in (0, 1, 2, 3):
        yield
        for i in (0, 1):
            if q == 1:
                across = wrap(firsts[i] + 2)
                take(i, across, seconds[i], one[i][2])
                two[i, 3] = [send(i, across, seconds[i], side) for side in sides[i][1]]
            slot = wrap(firsts[i] + offsets[q])
            minus, plus = wrap(seconds[i] - 1), wrap(seconds[i] + 1)
            take(i, slot, minus, two[i, q][0])
            if q < 2:
                onward[i, q] = send(i, slot, minus, sides[i][1][0])
            take(i, slot, plus, two[i, q][1])
            if q >= 2:
                onward[i, q] = send(i, slot, plus, sides[i][1][1])
    for q in (0, 1, 2, 3):
        yield
        for i in (0, 1):
            slot = wrap(firsts[i] + offsets[q])
            take(i, slot, wrap(seconds[i] + 2), onward[i, q])


def drain(steps):
    for _ in steps:
        pass


def rms(values):
    return lax.rsqrt(jnp.mean(values * values, axis=1, keepdims=True) + EPS)


def turn(values):
    return pltpu.roll(values, HEAD // 2, 1)


def causal(scores, start):
    places = start + lax.broadcasted_iota(jnp.int32, scores.shape, 0)
    keys = lax.broadcasted_iota(jnp.int32, scores.shape, 1)
    return jnp.where(keys <= places, scores, NEG)


def vmem():
    return pl.BlockSpec(memory_space=pltpu.VMEM)


def anywhere():
    return pl.BlockSpec(memory_space=pl.ANY)


class Reduce8:
    def __init__(self, net, at, own, other, sib_in, first_in, last_in, near_in, away_in):
        self.net, self.at, self.own, self.other, self.sib_in = net, at, own, other, sib_in
        self.first_in, self.last_in, self.near_in, self.away_in = first_in, last_in, near_in, away_in
        self.half = own.shape[1] // 2
        self.keys = {}

    def put(self, j, mine, theirs):
        self.own[j] = mine
        self.other[j] = theirs
        self.keys[j] = self.net.send(self.other.at[j], self.sib_in.at[j], self.at.S)

    def step(self, j):
        net, at, half = self.net, self.at, self.half
        net.take(self.keys[j], self.sib_in.at[j])
        total = self.own[j].astype(F32) + self.sib_in[j].astype(F32)
        if j == 0:
            self.own[j] = total.astype(BF)
            self.first = net.send(self.own.at[j, pl.ds(0, half)], self.first_in, at.N1)
            self.last = net.send(self.own.at[j, pl.ds(half, half)], self.last_in, at.N2)
        elif j == 1:
            net.take(self.last, self.last_in)
            self.own[j, :half] = total[:half].astype(BF)
            self.own[j, half:] = (total[half:] + self.last_in[...].astype(F32)).astype(BF)
            self.near = net.send(self.own.at[j], self.near_in, at.N1)
        elif j == 2:
            net.take(self.first, self.first_in)
            self.own[j, :half] = (total[:half] + self.first_in[...].astype(F32)).astype(BF)
            self.own[j, half:] = total[half:].astype(BF)
            self.away = net.send(self.own.at[j], self.away_in, at.N2)
        else:
            net.take(self.near, self.near_in)
            net.take(self.away, self.away_in)
            return total + self.near_in[...].astype(F32) + self.away_in[...].astype(F32)
        return None


def reduce8_scratch(rows, columns):
    return [
        pltpu.VMEM((4, rows, columns), BF),
        pltpu.VMEM((4, rows, columns), BF),
        pltpu.VMEM((4, rows, columns), BF),
        pltpu.VMEM((rows // 2, columns), BF),
        pltpu.VMEM((rows // 2, columns), BF),
        pltpu.VMEM((rows, columns), BF),
        pltpu.VMEM((rows, columns), BF),
    ]


def tiles_of(width, step):
    return [(first, min(step, width - first)) for first in range(0, width, step)]


def forward_kernel(
    x_ref,
    og_ref,
    wq_ref,
    wk_ref,
    wv_ref,
    wout_ref,
    wg_ref,
    wu_ref,
    wd_ref,
    gains_ref,
    bias_ref,
    cos_ref,
    sin_ref,
    xs_ref,
    n1c_ref,
    og_out,
    qw_out,
    ow_out,
    q_ref,
    k_ref,
    v_ref,
    lse_ref,
    attn_ref,
    mid_ref,
    gains_all,
    dn2_ref,
    out_ref,
    grad_gu,
    grad_down,
    wqkv_ref,
    x_all,
    n1,
    og_all,
    n2_all,
    qw,
    ow,
    gw,
    uw,
    dw,
    part_out,
    part_in,
    d_up,
    ffn,
    tile_buf,
    *rest,
):
    red_a, red_b, sems = rest[:7], rest[7:14], rest[14:]
    send_sems, recv_sems, local_sems, tile_sems = sems
    at = Place()
    net = Net(send_sems, recv_sems, at)
    local, local_count = [], iter(range(32))

    def move(src, dst):
        copy = pltpu.make_async_copy(src, dst, local_sems.at[next(local_count)])
        copy.start()
        local.append(copy)
        return copy

    joined = [
        move(wq_ref, wqkv_ref.at[:, pl.ds(0, QCOLS)]),
        move(wk_ref, wqkv_ref.at[:, pl.ds(QCOLS, HEAD)]),
        move(wv_ref, wqkv_ref.at[:, pl.ds(QCOLS + HEAD, HEAD)]),
    ]
    at.meet((at.S, at.N1, at.N2, at.O, at.OS, at.YP, at.YM, at.ZP, at.ZM))
    for copy in joined:
        copy.wait()
    local.clear()

    def tokens_of(array):
        def place(row, col, part):
            if part is None:
                rows = pl.ds(aligned(row, SEQ // 2), SEQ // 2)
            else:
                rows = pl.ds(aligned(row * 2 + part, SEQ // 4), SEQ // 4)
            return array.at[rows, pl.ds(aligned(col, FEAT), FEAT)]

        return place

    mine, mine_far = aligned(at.col, FEAT), aligned(1 - at.hi, 2 * FEAT)
    move(x_ref, tokens_of(x_all)(at.row, at.col, None))
    move(wqkv_ref, qw.at[pl.ds(mine, FEAT), :])
    move(wout_ref, ow.at[:, pl.ds(mine, FEAT)])
    move(gains_ref, gains_all.at[:, pl.ds(mine, FEAT)])
    start = quarter_start(at.col)
    move(wg_ref.at[:, pl.ds(start, PART)], gw.at[pl.ds(mine, FEAT), :])
    move(wu_ref.at[:, pl.ds(start, PART)], uw.at[pl.ds(mine, FEAT), :])
    move(wd_ref.at[pl.ds(start, PART), :], dw.at[:, pl.ds(mine, FEAT)])
    move(og_ref, tokens_of(og_all)(at.row, at.col, None))

    eighth = at.dp % 8
    across = [net.key() for _ in range(5)]

    def slice_copies(core, first, last):
        device = {"col": 2 * (1 - at.hi) + core}
        rows = pl.ds(aligned(eighth, 48), 48)
        target = pl.ds(pl.multiple_of(mine + eighth * 48, 16), 48)
        columns = pl.ds(core * 512, 512)
        out_rows = pl.ds(pl.multiple_of(core * FEAT + eighth * 48, 16), 48)
        theirs = quarter_start(2 * (1 - at.hi) + core)
        down_rows = pl.ds(pl.multiple_of(theirs + eighth * 144, 16), 144)
        down_target = pl.ds(aligned(eighth, 144), 144)
        pairs = (
            (wqkv_ref.at[rows, columns], qw.at[target, columns]),
            (wout_ref.at[out_rows, :], ow.at[out_rows, pl.ds(mine, FEAT)]),
            (wg_ref.at[rows, pl.ds(theirs, PART)], gw.at[target, :]),
            (wu_ref.at[rows, pl.ds(theirs, PART)], uw.at[target, :]),
            (wd_ref.at[down_rows, :], dw.at[down_target, pl.ds(mine, FEAT)]),
        )
        return [
            pltpu.make_async_remote_copy(
                src_ref=pairs[i][0],
                dst_ref=pairs[i][1],
                send_sem=net.ss.at[spare[core][i]],
                recv_sem=net.rs.at[across[i]],
                device_id=device,
                device_id_type=MESH,
            )
            for i in range(first, last)
        ]

    spare = ([net.key() for _ in range(5)], [net.key() for _ in range(5)])
    chosen = at.core == at.dp // 8

    @pl.when(chosen)
    def _():
        for core in (0, 1):
            for copy in slice_copies(core, 0, 2):
                copy.start()

    gather_x = Gather8(net, at, tokens_of(x_all))
    gather_x.start(x_ref)
    gain_far = net.send(gains_ref, gains_all.at[:, pl.ds(mine, FEAT)], at.N2)
    gain_sib = net.send(gains_ref, gains_all.at[:, pl.ds(mine, FEAT)], at.S)
    near_qw = net.send(wqkv_ref, qw.at[pl.ds(mine, FEAT), :], at.S)
    near_ow = net.send(wout_ref, ow.at[:, pl.ds(mine, FEAT)], at.S)

    @pl.when(chosen)
    def _():
        for core in (0, 1):
            for copy in slice_copies(core, 2, 5):
                copy.start()

    far_half = pl.ds(mine_far, 2 * FEAT)

    def qkv_slices(z, y):
        rows = pl.ds(pl.multiple_of(mine_far + (z * 4 + y) * 48, 16), 48)
        return [qw.at[rows, pl.ds(aligned(at.core, 512), 512)]]

    def out_slices(z, y):
        index = z * 4 + y
        rows = pl.ds(pl.multiple_of(at.core * FEAT + (index % 8) * 48, 16), 48)
        return [ow.at[rows, pl.ds(pl.multiple_of(mine_far + (index // 8) * FEAT, HEAD), FEAT)]]

    def ffn_slices(weights, first, count):
        def slices(z, y):
            index = z * 4 + y
            rows = pl.ds(pl.multiple_of(mine_far + index * 48, 16), 48)
            down_rows = pl.ds(pl.multiple_of((index % 8) * 144 + first, 16), count)
            lanes = pl.ds(pl.multiple_of(mine_far + (index // 8) * FEAT, HEAD), FEAT)
            return [weights.at[rows, :], dw.at[down_rows, lanes]]

        return slices

    net.take(across[0], qkv_slices(at.z, at.y)[0])
    ring = ring_dp(
        net,
        at,
        (
            lambda z, y: [qkv_slices(z, y)[0].at[:, pl.ds(0, 256)]],
            lambda z, y: [qkv_slices(z, y)[0].at[:, pl.ds(256, 256)]],
        ),
    )
    next(ring)
    near = [
        net.send(wg_ref.at[:, pl.ds(quarter_start(at.sib), PART)], gw.at[pl.ds(mine, FEAT), :], at.S),
        net.send(wu_ref.at[:, pl.ds(quarter_start(at.sib), PART)], uw.at[pl.ds(mine, FEAT), :], at.S),
        net.send(wd_ref.at[pl.ds(quarter_start(at.sib), PART), :], dw.at[:, pl.ds(mine, FEAT)], at.S),
    ]
    next(ring)
    next(ring)
    gather_x.middle()
    gains_far = gains_all.at[:, pl.ds(aligned(at.far, FEAT), FEAT)]
    net.take(gain_far, gains_far)
    gain_sibfar = net.send(gains_far, gains_far, at.S)
    next(ring)
    net.take(across[1], out_slices(at.z, at.y)[0])
    net.take(across[2], ffn_slices(gw, 0, 80)(at.z, at.y)[0])
    net.take(across[3], ffn_slices(uw, 80, 64)(at.z, at.y)[0])
    net.take(across[4], ffn_slices(uw, 0, 144)(at.z, at.y)[1])
    drain(ring)
    ring = ring_dp(
        net,
        at,
        (
            ffn_slices(gw, 0, 80),
            lambda z, y: ffn_slices(uw, 80, 64)(z, y) + out_slices(z, y),
        ),
    )
    next(ring)
    cols_half, rows_half = pl.ds(aligned(at.core, 512), 512), pl.ds(aligned(at.core, FEAT), FEAT)
    far_qw = net.send(qw.at[far_half, cols_half], qw.at[far_half, cols_half], at.S)
    gather_og = Gather8(net, at, tokens_of(og_all))
    gather_x.late()
    gather_og.start(og_ref)
    gather_x.end()
    early = list(net.sent)
    net.take(gain_sib, gains_all.at[:, pl.ds(aligned(at.sib, FEAT), FEAT)])
    net.take(gain_sibfar, gains_all.at[:, pl.ds(aligned(at.sibfar, FEAT), FEAT)])
    for copy in local:
        copy.wait()
    local.clear()

    gain1, gain2 = gains_all[0:1, :], gains_all[1:2, :]

    def norm_block(i, carry):
        rows = pl.ds(aligned(i, BLOCK), BLOCK)
        values = x_all[rows, :].astype(F32)
        n1[rows, :] = (values * rms(values) * gain1).astype(BF)
        return carry

    lax.fori_loop(0, SEQ // BLOCK // 2, norm_block, 0)
    next(ring)
    lax.fori_loop(SEQ // BLOCK // 2, SEQ // BLOCK, norm_block, 0)
    next(ring)
    gather_og.middle()
    my_rows = pl.ds(aligned(at.block, BLOCK), BLOCK)
    xs_ref[...] = x_all[my_rows, :]
    n1c_ref[...] = n1[:, pl.ds(mine, FEAT)]
    net.take(near_qw, qw.at[pl.ds(aligned(at.sib, FEAT), FEAT), :])
    other_cols = pl.ds(aligned(1 - at.core, 512), 512)
    net.take(far_qw, qw.at[far_half, other_cols])
    move(qw, qw_out)

    def kv_block(i, carry):
        rows = pl.ds(aligned(i, 256), 256)
        both = dot(n1[rows, :], qw[:, QCOLS:]) + bias_ref[:, QCOLS:]
        key = both[:, :HEAD]
        k_ref[rows, :] = (key * cos_ref[rows, :] + turn(key) * sin_ref[rows, :]).astype(BF)
        v_ref[rows, :] = both[:, HEAD:].astype(BF)
        return carry

    lax.fori_loop(0, SEQ // 256, kv_block, 0)
    next(ring)
    pair = (at.col, 7 - at.col)
    for j in (0, 1):
        rows = pl.ds(aligned(pair[j], BLOCK), BLOCK)
        queries = dot(n1[rows, :], qw[:, :QCOLS]) + bias_ref[:, :QCOLS]
        cosine, sine = cos_ref[rows, :], sin_ref[rows, :]
        for h in range(HEADS):
            one = queries[:, h * HEAD : (h + 1) * HEAD]
            q_ref[pl.ds(j * BLOCK, BLOCK), pl.ds(h * HEAD, HEAD)] = (
                one * cosine + turn(one) * sine
            ).astype(BF)
    next(ring)
    gather_og.late()

    for j in (0, 1):
        keys = SEQ // 2 * (j + 1)
        rows = pl.ds(j * BLOCK, BLOCK)

        def attend(h, carry):
            lanes = pl.ds(aligned(h, HEAD), HEAD)
            scores = dot(q_ref[rows, lanes], k_ref[:keys, :], 1, 1) * SCALE
            scores = causal(scores, pair[j] * BLOCK)
            top = jnp.max(scores, axis=1, keepdims=True)
            weights = jnp.exp(scores - top)
            total = jnp.sum(weights, axis=1, keepdims=True)
            lse_ref[j * HEADS + h] = top + jnp.log(total)
            probs = (weights * (1.0 / total)).astype(BF)
            attn_ref[rows, lanes] = dot(probs, v_ref[:keys, :]).astype(BF)
            return carry

        lax.fori_loop(0, HEADS // 2, attend, 0)
        next(ring)
        lax.fori_loop(HEADS // 2, HEADS, attend, 0)
        next(ring)

    drain(ring)
    far_ow = net.send(ow.at[rows_half, far_half], ow.at[rows_half, far_half], at.S)
    gather_og.end()
    move(og_all.at[my_rows, :], og_out)

    net.take(near_ow, ow.at[:, pl.ds(aligned(at.sib, FEAT), FEAT)])
    other_rows = pl.ds(aligned(1 - at.core, FEAT), FEAT)
    net.take(far_ow, ow.at[other_rows, far_half])
    move(ow, ow_out)
    part_out[...] = dot(attn_ref[pl.ds(aligned(1 - at.row, BLOCK), BLOCK), :], ow[...]).astype(BF)
    part = net.send(part_out, part_in, at.N1)
    own = dot(attn_ref[pl.ds(aligned(at.row, BLOCK), BLOCK), :], ow[...])
    net.take(part, part_in)
    mid = xs_ref[...].astype(F32) + own + part_in[...].astype(F32)
    mid_ref[...] = mid

    def place_n2(row, col, part):
        first = block_of(row, col) * BLOCK
        if part is None:
            return n2_all.at[pl.ds(pl.multiple_of(first, BLOCK), BLOCK), :]
        return n2_all.at[pl.ds(pl.multiple_of(first + part * 64, 64), 64), :]

    n2_all[my_rows, :] = (mid * rms(mid) * gain2).astype(BF)
    gather_n2 = Gather8(net, at, place_n2)
    gather_n2.start(place_n2(at.row, at.col, None))
    net.take(near[2], dw.at[:, pl.ds(aligned(at.sib, FEAT), FEAT)])

    def hidden_back(i, carry):
        rows = pl.ds(aligned(i, 256), 256)
        for first, width in tiles_of(PART, 512):
            lanes = pl.ds(first, width)
            d_up[rows, lanes] = dot(og_all[rows, :], dw[lanes, :], 1, 1).astype(BF)
        return carry

    lax.fori_loop(0, 3, hidden_back, 0)
    gather_n2.middle()
    lax.fori_loop(3, 4, hidden_back, 0)
    net.take(near[0], gw.at[pl.ds(aligned(at.sib, FEAT), FEAT), :])
    net.take(near[1], uw.at[pl.ds(aligned(at.sib, FEAT), FEAT), :])

    net.finish(early)
    hidden, d_gate = x_all.at[:, pl.ds(0, PART)], n1.at[:, pl.ds(0, PART)]
    norms = Reduce8(net, at, *red_a)
    outs = Reduce8(net, at, *red_b)
    chips = ((at.row, 1 - at.hi), (1 - at.row, at.hi), (1 - at.row, 1 - at.hi), (at.row, at.hi))
    last_part = at.col == 3

    def tokens(j):
        row, hi = chips[j]
        first = 2 * hi + row * (6 - 4 * hi)
        return pl.ds(aligned(first, BLOCK), 256), at.core + row * (1 - 2 * at.core)

    for j in (3, 1, 2, 0):
        if j == 0:
            gather_n2.late()
        gather_n2.end(j)
        rows, _ = tokens(j)
        for first, width in tiles_of(PART, 512):
            lanes = pl.ds(first, width)
            gate = dot(n2_all[rows, :], gw[:, lanes])
            up = dot(n2_all[rows, :], uw[:, lanes])
            d_hidden = d_up[rows, lanes].astype(F32)
            sig = jax.nn.sigmoid(gate)
            act = gate * sig
            d_act = d_hidden * up * sig * (1.0 + gate * (1.0 - sig))
            values = [act * up, d_act, d_hidden * act]
            if first == 0:
                lane = lax.broadcasted_iota(jnp.int32, (1, width), 1)
                fresh = jnp.logical_or(lane >= HEAD, jnp.logical_not(last_part))
                values = [jnp.where(fresh, value, 0.0) for value in values]
            for ref, value in zip((hidden, d_gate, d_up), values, strict=True):
                ref[rows, lanes] = value.astype(BF)
    for j in range(4):
        rows, place = tokens(j)
        own_rows = pl.ds(pl.multiple_of(rows.start + place * BLOCK, BLOCK), BLOCK)
        other_rows = pl.ds(pl.multiple_of(rows.start + (1 - place) * BLOCK, BLOCK), BLOCK)
        parts = [
            (dot(d_gate[r, :], gw[...], 1, 1) + dot(d_up[r, :], uw[...], 1, 1)).astype(BF)
            for r in (other_rows, own_rows)
        ]
        norms.put(j, parts[1], parts[0])
        if j:
            norms.step(j - 1)

    writes = []

    def outer_sum(left, right, out):
        height = left.shape[1] // 2
        for first, width in tiles_of(right.shape[1], 256):
            place = len(writes) % 2
            if len(writes) > 1:
                writes[-2].wait()
            for i in (0, 1):
                rows = pl.ds(i * height, height)
                tile_buf[place, rows, :width] = dot(
                    left[:, rows], right[:, pl.ds(first, width)], 0, 0
                ).astype(BF)
            writes.append(
                pltpu.make_async_copy(
                    tile_buf.at[place, pl.ds(0, 2 * height), pl.ds(0, width)],
                    out.at[:, pl.ds(first, width)],
                    tile_sems.at[place],
                )
            )
            writes[-1].start()

    outer_sum(hidden, og_all, grad_down)
    for j in range(4):
        row, hi = chips[j]
        rows = pl.ds(aligned(row, SEQ // 2), SEQ // 2)
        lanes = pl.ds(aligned(hi, QCOLS), QCOLS)
        ffn[...] = dot(hidden[rows, :], dw[:, lanes])
        if j in (0, 3):
            mine_mid = pl.ds(pl.multiple_of((at.block - 4 * at.row) * BLOCK, BLOCK), BLOCK)
            ffn[mine_mid, :] += mid_ref[:, lanes]
        own = ffn[:, pl.ds(aligned(at.core, FEAT), FEAT)].astype(BF)
        outs.put(j, own, ffn[:, pl.ds(aligned(1 - at.core, FEAT), FEAT)].astype(BF))
        if j:
            outs.step(j - 1)
        if j == 1:
            dn2_ref[...] = norms.step(3)
    outer_sum(n2_all, d_gate, grad_gu.at[0])
    outer_sum(n2_all, d_up, grad_gu.at[1])
    out_ref[...] = outs.step(3)
    for copy in writes[-2:]:
        copy.wait()
    for copy in local:
        copy.wait()
    net.finish()

    @pl.when(chosen)
    def _():
        for core in (0, 1):
            for copy in slice_copies(core, 0, 5):
                copy.wait_send()


def run_forward(x, og, wq, wk, wv, wout, wg, wu, wd, gains, bias, cosine, sine):
    outs = (
        ((BLOCK, MODEL), BF, vmem),
        ((SEQ, FEAT), BF, vmem),
        ((BLOCK, MODEL), BF, anywhere),
        ((MODEL, QKV), BF, anywhere),
        ((QCOLS, MODEL), BF, anywhere),
        ((2 * BLOCK, QCOLS), BF, vmem),
        ((SEQ, HEAD), BF, vmem),
        ((SEQ, HEAD), BF, vmem),
        ((2 * HEADS, BLOCK, 1), F32, vmem),
        ((2 * BLOCK, QCOLS), BF, vmem),
        ((BLOCK, MODEL), F32, vmem),
        ((8, MODEL), F32, vmem),
        ((BLOCK, MODEL), F32, vmem),
        ((SEQ // 2, FEAT), F32, vmem),
        ((2, MODEL, PART), BF, anywhere),
        ((PART, MODEL), BF, anywhere),
    )
    return pl.pallas_call(
        forward_kernel,
        out_shape=[jax.ShapeDtypeStruct(dims, dtype) for dims, dtype, _ in outs],
        in_specs=[anywhere()] * 9 + [vmem()] * 4,
        out_specs=[place() for _, _, place in outs],
        scratch_shapes=[
            pltpu.VMEM((FEAT, QKV), BF),
            pltpu.VMEM((SEQ, MODEL), BF),
            pltpu.VMEM((SEQ, MODEL), BF),
            pltpu.VMEM((SEQ, MODEL), BF),
            pltpu.VMEM((SEQ, MODEL), BF),
            pltpu.VMEM((MODEL, QKV), BF),
            pltpu.VMEM((QCOLS, MODEL), BF),
            pltpu.VMEM((MODEL, PART), BF),
            pltpu.VMEM((MODEL, PART), BF),
            pltpu.VMEM((PART, MODEL), BF),
            pltpu.VMEM((BLOCK, MODEL), BF),
            pltpu.VMEM((BLOCK, MODEL), BF),
            pltpu.VMEM((SEQ, PART), BF),
            pltpu.VMEM((SEQ // 2, QCOLS), F32),
            pltpu.VMEM((2, MODEL, 256), BF),
        ]
        + reduce8_scratch(BLOCK, MODEL)
        + reduce8_scratch(SEQ // 2, FEAT)
        + [
            pltpu.SemaphoreType.DMA((200,)),
            pltpu.SemaphoreType.DMA((200,)),
            pltpu.SemaphoreType.DMA((32,)),
            pltpu.SemaphoreType.DMA((2,)),
        ],
        compiler_params=pltpu.CompilerParams(
            collective_id=0, has_side_effects=True, vmem_limit_bytes=VMEM_LIMIT
        ),
        cost_estimate=pl.CostEstimate(
            flops=37 * 10**9, bytes_accessed=80 * 10**6, transcendentals=4 * 10**6
        ),
        name="forward_and_feed_forward",
    )(x, og, wq, wk, wv, wout, wg, wu, wd, gains, bias, cosine, sine)


def add_up(out, terms):
    lead = out.shape[:-2]
    if not lead:
        total = terms[0][...].astype(F32)
        for term in terms[1:]:
            total = total + term[...].astype(F32)
        out[...] = total.astype(out.dtype)
        return
    count = 1
    for size in lead:
        count *= size

    def step(i, carry):
        index = []
        for size in reversed(lead):
            index.insert(0, i % size)
            i = i // size
        index = tuple(index)
        total = terms[0].at[index][...].astype(F32)
        for term in terms[1:]:
            total = total + term.at[index][...].astype(F32)
        out.at[index][...] = total.astype(out.dtype)
        return carry

    lax.fori_loop(0, count, step, 0)


class RingItem:
    def __init__(self, net, sides, place, part, held, way, bufs, own):
        self.net, self.part, self.held, self.own = net, part, held, own
        self.relay, self.staged, self.from_last, self.from_next = bufs
        self.onward, self.back = (sides[0], sides[1]) if way == 0 else (sides[1], sides[0])
        step = 1 - 2 * way
        self.here, self.next, self.across, self.last = (
            lax.rem(place + 4 + step * i, 4) for i in (0, 1, 2, 3)
        )

    def start(self):
        self.k_relay = self.net.send(self.part(self.across), self.relay, self.onward)

    def direct(self):
        self.k_next = self.net.send(self.part(self.last), self.from_next, self.back)

    def middle(self):
        self.net.take(self.k_relay, self.relay)
        add_up(self.staged, [self.held(self.next), self.relay])
        self.k_last = self.net.send(self.staged, self.from_last, self.onward)

    def end(self):
        self.net.take(self.k_next, self.from_next)
        self.net.take(self.k_last, self.from_last)
        add_up(self.own, [self.held(self.here), self.from_next, self.from_last])


def begin(items):
    for item in items:
        item.start()
    for item in items:
        item.direct()


LEFT, RIGHT = pl.ds(0, QCOLS), pl.ds(QCOLS, QCOLS)
FFN_FIRST = (((2, 2, 48, PART), (2, 80, QCOLS)), ((2, 2, 48, PART), (144, QCOLS)))
FFN_LAST = (((2, 48, PART), (80, QCOLS)), ((2, 48, PART), (80, QCOLS)))
SMALL_FIRST = (((2, 48, 512),), ((2, 48, FEAT),))
SMALL_LAST = (((48, 512),), ((48, FEAT),))


def down_rows(k):
    return pl.ds(pl.multiple_of(72 * k - 8 * (k % 2), 16), 80)


def ring_scratch(first, last):
    scratch = []
    for i in (0, 1):
        for dims in first[i]:
            scratch += [pltpu.VMEM(dims, BF)] * 8
            scratch.append(pltpu.VMEM((2,) + dims, BF))
        for dims in last[i]:
            scratch += [pltpu.VMEM(dims, BF)] * 4
    return scratch


def ring_items(net, at, first, last, parts, helds, seconds, finals, bufs):
    sides = (((at.YP, at.YM), (at.ZP, at.ZM)), ((at.ZP, at.ZM), (at.YP, at.YM)))
    places = ((at.y, at.z), (at.z, at.y))
    bufs = list(bufs)
    one, two = ([], []), ([], [])
    for i in (0, 1):
        owns = []
        for n in range(len(first[i])):
            own = bufs[8]
            for way in (0, 1):
                part = functools.partial(lambda k, f, w: f(k, w), f=parts[i][n], w=way)
                held = functools.partial(lambda k, f, w: f(k, w), f=helds[i][n], w=way)
                four = bufs[4 * way : 4 * way + 4]
                one[i].append(
                    RingItem(net, sides[i][0], places[i][0], part, held, way, four, own.at[way])
                )
            owns.append(own)
            bufs = bufs[9:]
        for n in range(len(last[i])):
            part = functools.partial(lambda k, f, o: f(o, k), f=seconds[i][n], o=owns[n])
            two[i].append(
                RingItem(net, sides[i][1], places[i][1], part, part, n % 2, bufs[:4], finals[i][n])
            )
            bufs = bufs[4:]

    def mix(pair):
        return [item for items in zip(*pair, strict=True) for item in items]

    return mix(one), mix(two)


def ffn_items(net, at, far_refs, near_refs, gu_own, down_own, bufs):
    def parts_of(gu, down):
        return (
            (
                lambda k, way: gu.at[way, pl.ds(0, 2), :, k],
                lambda k, way: down.at[way, :, down_rows(k), LEFT],
            ),
            (
                lambda k, way: gu.at[k // 2, pl.ds(2, 2), k % 2, pl.ds(2 * way, 2)],
                lambda k, way: down.at[k // 2, k % 2, pl.ds(144 * way, 144), RIGHT],
            ),
        )

    parts, helds = parts_of(*far_refs), parts_of(*near_refs)
    seconds = (
        (lambda own, k: own.at[k // 2, :, k % 2], lambda own, k: own.at[k // 2, k % 2]),
        (
            lambda own, k: own.at[k // 2, :, k % 2],
            lambda own, k: own.at[k // 2, pl.ds(pl.multiple_of((k % 2) * 64, 64), 80)],
        ),
    )
    finals = (
        (gu_own.at[pl.ds(0, 2)], down_own.at[:, LEFT]),
        (gu_own.at[pl.ds(2, 2)], down_own.at[:, RIGHT]),
    )
    return ring_items(net, at, FFN_FIRST, FFN_LAST, parts, helds, seconds, finals, bufs)


def small_items(net, at, qkv, out, qkv_own, out_own, bufs):
    parts = (
        (lambda k, way: qkv.at[:, k, :, pl.ds(512 * way, 512)],),
        (lambda k, way: out.at[k // 2, k % 2, pl.ds(2 * way, 2)],),
    )
    seconds = ((lambda own, k: own.at[k // 2, k % 2],), (lambda own, k: own.at[k // 2, k % 2],))
    finals = ((qkv_own,), (out_own,))
    return ring_items(net, at, SMALL_FIRST, SMALL_LAST, parts, parts, seconds, finals, bufs)


def backward_kernel(
    dn2_ref,
    mid_ref,
    og_ref,
    gains_all,
    xs_ref,
    n1c,
    attn_ref,
    q_ref,
    k_ref,
    v_ref,
    lse_ref,
    cos_ref,
    sin_ref,
    ow_far,
    qw_far,
    gu_far,
    down_far,
    grad_in,
    grad_out,
    grad_qkv,
    small_ref,
    gu_own,
    down_own,
    sums_ref,
    sums_in,
    attn_all,
    mid_cols,
    mid_pair,
    d_mid,
    d_attn,
    d_q,
    d_kv,
    kv_out,
    kv_in,
    d_qkv_all,
    part_out,
    part_in,
    gi_out,
    gi_in,
    ow,
    qw,
    gu,
    down,
    *rest,
):
    bufs, (send_sems, recv_sems, local_sems) = rest[:-3], rest[-3:]
    at = Place()
    net = Net(send_sems, recv_sems, at)
    held = [
        pltpu.make_async_copy(src, dst, local_sems.at[i])
        for i, (src, dst) in enumerate(
            ((ow_far, ow), (gu_far, gu), (down_far, down), (qw_far, qw))
        )
    ]
    for copy in held:
        copy.start()
    at.meet(
        (at.S, at.O, at.OS, at.N1, at.N2, at.N1S, at.N2S, at.YP, at.YM, at.ZP, at.ZM)
    )
    first, last = ffn_items(net, at, (gu_far, down_far), (gu, down), gu_own, down_own, bufs)
    begin(first)
    peers = ((at.S, at.sib), (at.O, at.far), (at.OS, at.sibfar))
    pair = (at.col, 7 - at.col)

    def rows_at(block):
        return pl.ds(aligned(block, BLOCK), BLOCK)

    def cols_at(col):
        return pl.ds(aligned(col, FEAT), FEAT)

    class GatherCol:
        def __init__(self, array):
            self.array = array

        def rows(self, col, j):
            return self.array.at[rows_at(col + j * (7 - 2 * col)), :]

        def start(self):
            self.far = [net.send(self.rows(at.col, j), self.rows(at.col, j), at.O) for j in (0, 1)]
            self.sib = [net.send(self.rows(at.col, j), self.rows(at.col, j), at.S) for j in (0, 1)]

        def middle(self):
            self.onward = []
            for j in (0, 1):
                net.take(self.far[j], self.rows(at.far, j))
                self.onward.append(net.send(self.rows(at.far, j), self.rows(at.far, j), at.S))

        def end(self):
            for j in (0, 1):
                net.take(self.sib[j], self.rows(at.sib, j))
                net.take(self.onward[j], self.rows(at.sibfar, j))

    gather_attn = GatherCol(attn_all)
    for j in (0, 1):
        attn_all[rows_at(pair[j]), :] = attn_ref[pl.ds(j * BLOCK, BLOCK), :]

    gain1, gain2 = gains_all[0:1, :], gains_all[1:2, :]
    mid = mid_ref[...]
    scale = rms(mid)
    unit = mid * scale
    d_normed = dn2_ref[...]
    sums_ref[...] = jnp.zeros_like(sums_ref)
    sums_ref[1:2, :] = jnp.sum(d_normed * unit, axis=0, keepdims=True)
    bent = d_normed * gain2
    d_mid[...] = og_ref[...].astype(F32) + scale * (
        bent - unit * jnp.mean(bent * unit, axis=1, keepdims=True)
    )
    mid_pair[at.row] = d_mid[...].astype(BF)
    to_pair = net.send(mid_pair.at[at.row], mid_pair.at[at.row], at.N1)
    mid_cols[rows_at(at.block), :] = d_mid[:, cols_at(at.col)].astype(BF)
    spread = []
    others = (
        (at.S, at.row, at.sib),
        (at.N1, 1 - at.row, at.col),
        (at.N1S, 1 - at.row, at.sib),
        (at.O, at.row, at.far),
        (at.OS, at.row, at.sibfar),
        (at.N2, 1 - at.row, at.far),
        (at.N2S, 1 - at.row, at.sibfar),
    )
    for device, row, col in others:
        spread.append(
            net.send(
                mid_pair.at[at.row, :, cols_at(col)], mid_cols.at[rows_at(at.block), :], device
            )
        )
    gather_attn.start()
    net.take(to_pair, mid_pair.at[1 - at.row])
    held[0].wait()
    for j in (0, 1):
        d_attn[pl.ds(j * BLOCK, BLOCK), :] = dot(mid_pair[j], ow[...], 1, 1).astype(BF)
    d_kv[...] = jnp.zeros_like(d_kv)
    held[1].wait()
    held[2].wait()
    for item in first:
        item.middle()

    for j in (0, 1):
        keys = SEQ // 2 * (j + 1)
        rows = pl.ds(j * BLOCK, BLOCK)

        def back(h, carry):
            lanes = pl.ds(aligned(h, HEAD), HEAD)
            queries, d_out = q_ref[rows, lanes], d_attn[rows, lanes]
            scores = dot(queries, k_ref[:keys, :], 1, 1) * SCALE
            scores = causal(scores, pair[j] * BLOCK)
            probs = jnp.exp(scores - lse_ref[j * HEADS + h])
            d_probs = dot(d_out, v_ref[:keys, :], 1, 1)
            inner = jnp.sum(probs * d_probs, axis=1, keepdims=True)
            d_scores = (probs * (d_probs - inner) * SCALE).astype(BF)
            d_q[rows, lanes] = dot(d_scores, k_ref[:keys, :])
            d_kv[:keys, :HEAD] += dot(d_scores, queries, 0, 0)
            d_kv[:keys, HEAD:] += dot(probs.astype(BF), d_out, 0, 0)
            return carry

        lax.fori_loop(0, HEADS, back, 0)
    gather_attn.middle()

    kv_out[...] = d_kv[...].astype(BF)
    kv_keys = [
        [
            net.send(kv_out.at[rows_at(col + j * (7 - 2 * col)), :], kv_in.at[i, j], device)
            for j in (0, 1)
        ]
        for i, (device, col) in enumerate(peers)
    ]
    cosines = [cos_ref[rows_at(pair[j]), :] for j in (0, 1)]
    sines = [sin_ref[rows_at(pair[j]), :] for j in (0, 1)]
    for j in (0, 1):
        for h in range(HEADS):
            one = d_q[pl.ds(j * BLOCK, BLOCK), pl.ds(h * HEAD, HEAD)]
            d_qkv_all[rows_at(pair[j]), pl.ds(h * HEAD, HEAD)] = (
                one * cosines[j] - turn(one) * sines[j]
            ).astype(BF)
    for item in first:
        item.end()
    begin(last)
    gather_attn.end()
    for key, (_, row, col) in zip(spread, others, strict=True):
        net.take(key, mid_cols.at[rows_at(block_of(row, col)), :])
    grad_out[...] = dot(attn_all[...], mid_cols[...], 0, 0).astype(BF)
    for j in (0, 1):
        total = d_kv[rows_at(pair[j]), :]
        for i in range(3):
            net.take(kv_keys[i][j], kv_in.at[i, j])
            total = total + kv_in[i, j].astype(F32)
        key = total[:, :HEAD]
        d_qkv_all[rows_at(pair[j]), pl.ds(QCOLS, HEAD)] = (
            key * cosines[j] - turn(key) * sines[j]
        ).astype(BF)
        d_qkv_all[rows_at(pair[j]), pl.ds(QCOLS + HEAD, HEAD)] = total[:, HEAD:].astype(BF)
    gather_qkv = GatherCol(d_qkv_all)
    gather_qkv.start()

    held[3].wait()
    part_out[...] = dot(d_qkv_all[rows_at(block_of(1 - at.row, at.col)), :], qw[...], 1, 1).astype(BF)
    part = net.send(part_out, part_in, at.N1)
    d_normed = dot(d_qkv_all[rows_at(at.block), :], qw[...], 1, 1)
    net.take(part, part_in)
    d_normed = d_normed + part_in[...].astype(F32)
    values = xs_ref[...].astype(F32)
    scale = rms(values)
    unit = values * scale
    sums_ref[0:1, :] = jnp.sum(d_normed * unit, axis=0, keepdims=True)
    bent = d_normed * gain1
    total = d_mid[...] + scale * (bent - unit * jnp.mean(bent * unit, axis=1, keepdims=True))
    gi_out[...] = total.astype(BF)
    sums_in[at.row * 4 + at.col] = sums_ref[:, cols_at(at.col)]
    sums_keys = [
        net.send(sums_ref.at[:, cols_at(col)], sums_in.at[at.row * 4 + at.col], device)
        for device, row, col in others
    ]
    half_rows = pl.ds(pl.multiple_of((at.block - 4 * at.row) * BLOCK, BLOCK), BLOCK)
    gi_keys = [
        net.send(gi_out.at[:, cols_at(col)], gi_in.at[half_rows, :], device)
        for device, col in peers
    ]
    gi_in[half_rows, :] = gi_out[:, cols_at(at.col)]
    for item in last:
        item.middle()
    gather_qkv.middle()
    gather_qkv.end()
    grad_qkv[...] = dot(n1c[...], d_qkv_all[...], 0, 0).astype(BF)
    ones = jnp.ones((8, SEQ), BF)
    small_ref[:, FEAT:] = dot(ones, d_qkv_all[...])
    for key, (_, row, col) in zip(sums_keys, others, strict=True):
        net.take(key, sums_in.at[row * 4 + col])
    total = sums_in[0]
    for i in range(1, 8):
        total = total + sums_in[i]
    small_ref[:, :FEAT] = total
    for key, (_, col) in zip(gi_keys, peers, strict=True):
        offset = block_of(at.row, col) - 4 * at.row
        net.take(key, gi_in.at[pl.ds(pl.multiple_of(offset * BLOCK, BLOCK), BLOCK), :])
    for item in last:
        item.end()
    grad_in[...] = gi_in[...].astype(F32)
    net.finish()


def run_backward(*args):
    def out(shape, dtype):
        return jax.ShapeDtypeStruct(shape, dtype)

    outs = (
        out((SEQ // 2, FEAT), F32),
        out((QCOLS, FEAT), BF),
        out((FEAT, QKV), BF),
        out((8, FEAT + QKV), F32),
        out((4, 48, PART), BF),
        out((80, MODEL), BF),
    )
    return pl.pallas_call(
        backward_kernel,
        out_shape=outs,
        in_specs=[vmem()] * (len(args) - 4) + [anywhere()] * 4,
        out_specs=[vmem()] * len(outs),
        scratch_shapes=[
            pltpu.VMEM((8, MODEL), F32),
            pltpu.VMEM((8, 8, FEAT), F32),
            pltpu.VMEM((SEQ, QCOLS), BF),
            pltpu.VMEM((SEQ, FEAT), BF),
            pltpu.VMEM((2, BLOCK, MODEL), BF),
            pltpu.VMEM((BLOCK, MODEL), F32),
            pltpu.VMEM((2 * BLOCK, QCOLS), BF),
            pltpu.VMEM((2 * BLOCK, QCOLS), F32),
            pltpu.VMEM((SEQ, 2 * HEAD), F32),
            pltpu.VMEM((SEQ, 2 * HEAD), BF),
            pltpu.VMEM((3, 2, BLOCK, 2 * HEAD), BF),
            pltpu.VMEM((SEQ, QKV), BF),
            pltpu.VMEM((BLOCK, MODEL), BF),
            pltpu.VMEM((BLOCK, MODEL), BF),
            pltpu.VMEM((BLOCK, MODEL), BF),
            pltpu.VMEM((SEQ // 2, FEAT), BF),
            pltpu.VMEM((QCOLS, MODEL), BF),
            pltpu.VMEM((MODEL, QKV), BF),
            pltpu.VMEM((2, 4, 2, 4, 48, PART), BF),
            pltpu.VMEM((2, 2, 288, MODEL), BF),
        ]
        + ring_scratch(FFN_FIRST, FFN_LAST)
        + [pltpu.SemaphoreType.DMA((80,)), pltpu.SemaphoreType.DMA((80,))]
        + [pltpu.SemaphoreType.DMA((4,))],
        compiler_params=pltpu.CompilerParams(
            collective_id=2, has_side_effects=True, vmem_limit_bytes=VMEM_LIMIT
        ),
        cost_estimate=pl.CostEstimate(
            flops=10 * 10**9, bytes_accessed=40 * 10**6, transcendentals=2 * 10**6
        ),
        name="attention_backward",
    )(*args)


def sums_kernel(
    gu_own,
    down_own,
    qkv,
    out,
    small_ref,
    all_gu,
    all_down,
    all_qkv,
    all_out,
    small_out,
    small_y,
    small_z,
    *rest,
):
    bufs, (send_sems, recv_sems, local_sems) = rest[:-3], rest[-3:]
    at = Place()
    net = Net(send_sems, recv_sems, at)
    at.meet((at.S, at.O, at.OS, at.YP, at.YM, at.ZP, at.ZM, at.Y2, at.Z2))
    z, y = at.z, at.y

    def gu_piece(k, lanes):
        rows = pl.ds(pl.multiple_of((k % 8) * 48, 16), 48)
        return all_gu.at[k // 8, rows, lanes]

    def part_lanes(col):
        return pl.ds(aligned(col, PART), PART)

    def down_slot(col):
        return all_down.at[col, pl.ds(pl.multiple_of(at.dp * 80, 16), 80), :]

    def feat_lanes(col):
        return pl.ds(aligned(col, FEAT), FEAT)

    def qkv_piece(k):
        rows = pl.ds(pl.multiple_of((k % 8) * 48, 16), 48)
        return all_qkv.at[rows, pl.ds(pl.multiple_of((k // 8) * 512, 512), 512)]

    def out_piece(k):
        return all_out.at[pl.ds(pl.multiple_of(k * 48, 16), 48), :]

    peers = ((at.O, at.far), (at.OS, at.sibfar), (at.S, at.sib))
    keys = []
    for device, col in peers:
        keys.append(
            (
                net.send(gu_own.at[col], gu_piece(at.dp, part_lanes(at.col)), device),
                net.send(down_own.at[:, feat_lanes(col)], down_slot(at.col), device),
            )
        )
    small_y[y] = small_ref[...]
    small_keys = [net.send(small_ref, small_y.at[y], d) for d in (at.YP, at.YM, at.Y2)]
    first, last = small_items(net, at, qkv, out, qkv_piece(at.dp), out_piece(at.dp), bufs)
    begin(first)
    own_copies = [
        pltpu.make_async_copy(
            gu_own.at[at.col], gu_piece(at.dp, part_lanes(at.col)), local_sems.at[0]
        ),
        pltpu.make_async_copy(
            down_own.at[:, feat_lanes(at.col)], down_slot(at.col), local_sems.at[1]
        ),
    ]
    for copy in own_copies:
        copy.start()

    def take_from(i):
        net.take(keys[i][0], gu_piece(at.dp, part_lanes(peers[i][1])))
        net.take(keys[i][1], down_slot(peers[i][1]))

    def chip_ready():
        for copy in own_copies:
            copy.wait()
        take_from(2)

    def far_ready():
        take_from(0)
        take_from(1)

    def half_of(hi):
        def half(zz, yy):
            k = zz * 4 + yy
            rows = pl.ds(pl.multiple_of(k * 80, 16), 80)
            return [
                gu_piece(k, pl.ds(aligned(hi, 2 * PART), 2 * PART)),
                all_down.at[pl.ds(2 * hi, 2), rows, :],
            ]

        return half

    ring = ring_dp(
        net, at, (half_of(at.hi), half_of(1 - at.hi)), (chip_ready, far_ready)
    )
    next(ring)
    for item in first:
        item.middle()
    for key, k in zip(small_keys, (y - 1, y + 1, y + 2), strict=True):
        net.take(key, small_y.at[lax.rem(k + 4, 4)])
    small_z[z] = (small_y[0] + small_y[1]) + (small_y[2] + small_y[3])
    small_keys = [net.send(small_z.at[z], small_z.at[z], d) for d in (at.ZP, at.ZM, at.Z2)]
    next(ring)
    for item in first:
        item.end()
    begin(last)
    next(ring)
    for item in last:
        item.middle()
    for key, k in zip(small_keys, (z - 1, z + 1, z + 2), strict=True):
        net.take(key, small_z.at[lax.rem(k + 4, 4)])
    small_out[...] = (small_z[0] + small_z[1]) + (small_z[2] + small_z[3])
    next(ring)
    for item in last:
        item.end()
    after = ring_dp(
        net,
        at,
        (lambda zz, yy: [qkv_piece(zz * 4 + yy)], lambda zz, yy: [out_piece(zz * 4 + yy)]),
    )
    next(after)
    for _ in ring:
        next(after, None)
    drain(after)
    net.finish()


def run_sums(gu, down, qkv, out, small):
    def shape(dims, dtype):
        return jax.ShapeDtypeStruct(dims, dtype)

    outs = (
        shape((2, FEAT, 4 * PART), BF),
        shape((4, 1280, FEAT), BF),
        shape((FEAT, QKV), BF),
        shape((QCOLS, FEAT), BF),
        shape(small.shape, F32),
    )
    return pl.pallas_call(
        sums_kernel,
        out_shape=outs,
        in_specs=[vmem()] * 5,
        out_specs=[anywhere()] * 2 + [vmem()] * 3,
        scratch_shapes=[pltpu.VMEM((4,) + small.shape, F32)] * 2
        + ring_scratch(SMALL_FIRST, SMALL_LAST)
        + [pltpu.SemaphoreType.DMA((128,)), pltpu.SemaphoreType.DMA((128,))]
        + [pltpu.SemaphoreType.DMA((2,))],
        compiler_params=pltpu.CompilerParams(
            collective_id=3, has_side_effects=True, vmem_limit_bytes=VMEM_LIMIT
        ),
        cost_estimate=pl.CostEstimate(
            flops=10**8, bytes_accessed=60 * 10**6, transcendentals=0
        ),
        name="sums_over_sequences",
    )(gu, down, qkv, out, small)


def widen_kernel(
    gu,
    down,
    qkv,
    out,
    small,
    gate_out,
    up_out,
    down_out,
    query_out,
    key_out,
    value_out,
    proj_out,
    gain1_out,
    gain2_out,
    bq_out,
    bk_out,
    bv_out,
    gu_in,
    down_in,
    gate_buf,
    up_buf,
    down_buf,
    in_sems,
    out_sems,
):
    skip = 3 * PART

    def loads(n):
        place = n % 2
        rows = pl.ds(640 * (n % 2), 640)
        return [
            pltpu.make_async_copy(gu.at[:, pl.ds(n * 48, 48), :], gu_in.at[place], in_sems.at[place, 0]),
            pltpu.make_async_copy(down.at[n // 2, rows, :], down_in.at[place], in_sems.at[place, 1]),
        ]

    def stores(n):
        place, quarter, part = n % 2, n // 2, n % 2
        rows = pl.ds(n * 48, 48)
        drop = HEAD if quarter == 3 and part == 0 else 0
        start = PART * quarter + 576 * part - (HEAD if quarter == 3 and part == 1 else 0)
        return [
            pltpu.make_async_copy(gate_buf.at[place], gate_out.at[rows, :], out_sems.at[place, 0]),
            pltpu.make_async_copy(up_buf.at[place], up_out.at[rows, :], out_sems.at[place, 1]),
            pltpu.make_async_copy(
                down_buf.at[place, pl.ds(drop, 576 - drop), :],
                down_out.at[pl.ds(start, 576 - drop), :],
                out_sems.at[place, 2],
            ),
        ]

    def run(copies):
        for copy in copies:
            copy.start()
        return copies

    def wait(copies):
        for copy in copies:
            copy.wait()

    arriving = {0: run(loads(0)), 1: run(loads(1))}
    query_out[...] = qkv[:, :QCOLS].astype(F32)
    key_out[...] = qkv[:, QCOLS : QCOLS + HEAD].astype(F32)
    value_out[...] = qkv[:, QCOLS + HEAD :].astype(F32)
    proj_out[...] = out[...].astype(F32)
    first = 0
    for ref, row, width in (
        (gain1_out, 0, FEAT),
        (bq_out, 0, QCOLS),
        (bk_out, 0, HEAD),
        (bv_out, 0, HEAD),
    ):
        ref[...] = small[row : row + 1, first : first + width]
        first += width
    gain2_out[...] = small[1:2, :FEAT]
    leaving = {}
    for n in range(8):
        place = n % 2
        wait(arriving[n])
        if n > 1:
            wait(leaving[n - 2])
        for i, buf in enumerate((gate_buf, up_buf)):
            buf[place, :, :skip] = gu_in[place, i, :, :skip].astype(F32)
            buf[place, :, skip:] = gu_in[place, i, :, skip + HEAD :].astype(F32)
        for m in range(4):
            down_buf[place, pl.ds(144 * m, 80), :] = down_in[
                place, pl.ds(160 * m, 80), :
            ].astype(F32)
            down_buf[place, pl.ds(144 * m + 80, 64), :] = down_in[
                place, pl.ds(160 * m + 96, 64), :
            ].astype(F32)
        leaving[n] = run(stores(n))
        if n + 2 < 8:
            arriving[n + 2] = run(loads(n + 2))
    wait(leaving[6])
    wait(leaving[7])


def run_widen(gu, down, qkv, out, small):
    shapes = [(FEAT, UNITS)] * 2 + [(UNITS, FEAT)]
    shapes += [(FEAT, QCOLS), (FEAT, HEAD), (FEAT, HEAD), (QCOLS, FEAT)]
    shapes += [(1, FEAT), (1, FEAT), (1, QCOLS), (1, HEAD), (1, HEAD)]
    return pl.pallas_call(
        widen_kernel,
        out_shape=[jax.ShapeDtypeStruct(dims, F32) for dims in shapes],
        in_specs=[anywhere()] * 2 + [vmem()] * 3,
        out_specs=[anywhere()] * 3 + [vmem()] * 9,
        scratch_shapes=[
            pltpu.VMEM((2, 2, 48, 4 * PART), BF),
            pltpu.VMEM((2, 640, FEAT), BF),
            pltpu.VMEM((2, 48, UNITS), F32),
            pltpu.VMEM((2, 48, UNITS), F32),
            pltpu.VMEM((2, 576, FEAT), F32),
            pltpu.SemaphoreType.DMA((2, 2)),
            pltpu.SemaphoreType.DMA((2, 3)),
        ],
        compiler_params=pltpu.CompilerParams(vmem_limit_bytes=VMEM_LIMIT),
        cost_estimate=pl.CostEstimate(
            flops=10**7, bytes_accessed=36 * 10**6, transcendentals=0
        ),
        name="widen",
    )(gu, down, qkv, out, small)


def rope_tables(count):
    places = np.arange(count, dtype=np.float32)
    inverse = (1.0 / THETA ** (np.arange(0, HEAD, 2) / HEAD)).astype(np.float32)
    angles = places[:, None] * inverse[None, :]
    cosine, sine = np.cos(angles), np.sin(angles)
    tables = np.concatenate([cosine, cosine], axis=-1), np.concatenate([-sine, sine], axis=-1)
    return tuple(jnp.asarray(table, F32) for table in tables)


def body(
    layer_input,
    gain_attn,
    w_query,
    w_key,
    w_value,
    b_query,
    b_key,
    b_value,
    w_out,
    gain_ffn,
    w_gate,
    w_up,
    w_down,
    out_grad,
):
    cosine, sine = rope_tables(SEQ)
    bias = jnp.concatenate([b_query, b_key, b_value]).astype(F32)[None]
    gains = jnp.zeros((8, FEAT), F32).at[0].set(gain_attn.astype(F32)).at[1].set(gain_ffn.astype(F32))
    (
        xs,
        normed1_cols,
        grads_block,
        qkv_w,
        out_w,
        queries,
        key,
        value,
        lse,
        attn,
        mid,
        gains_all,
        dn2,
        layer_output,
        grad_gu,
        grad_down,
    ) = run_forward(
        layer_input,
        out_grad,
        w_query,
        w_key,
        w_value,
        w_out,
        w_gate,
        w_up,
        w_down,
        gains,
        bias,
        cosine,
        sine,
    )
    grad_input, grad_out, grad_qkv, small, grad_gu, grad_down = run_backward(
        dn2,
        mid,
        grads_block,
        gains_all,
        xs,
        normed1_cols,
        attn,
        queries,
        key,
        value,
        lse,
        cosine,
        sine,
        out_w,
        qkv_w,
        grad_gu.reshape(2, 4, 2, 4, 48, PART),
        grad_down.reshape(2, 2, 288, MODEL),
    )
    grad_gu, grad_down, grad_qkv, grad_out, small = run_sums(
        grad_gu,
        grad_down,
        grad_qkv.reshape(2, 4, 48, QKV),
        grad_out.reshape(2, 2, 4, 48, FEAT),
        small,
    )
    (
        grad_gate,
        grad_up,
        grad_down,
        grad_query,
        grad_key,
        grad_value,
        grad_out,
        *vectors,
    ) = run_widen(grad_gu, grad_down, grad_qkv, grad_out, small)
    gain1, gain2, bias_query, bias_key, bias_value = (vector[0] for vector in vectors)
    return (
        layer_output,
        grad_input,
        gain1,
        grad_query,
        grad_key,
        grad_value,
        bias_query,
        bias_key,
        bias_value,
        grad_out,
        gain2,
        grad_gate,
        grad_up,
        grad_down,
    )


def solution(mesh):
    in_specs = (
        P(("dp", "row"), "col"),
        P("col"),
        P("col", "row"),
        P("col", "row"),
        P("col", "row"),
        P("row"),
        P("row"),
        P("row"),
        P("row", "col"),
        P("col"),
        P("col", "row"),
        P("col", "row"),
        P("row", "col"),
        P(("dp", "row"), "col"),
    )
    out_specs = (
        P(("dp", "row"), "col"),
        P(("dp", "row"), "col"),
        P("col"),
        P("col", "row"),
        P("col", "row"),
        P("col", "row"),
        P("row"),
        P("row"),
        P("row"),
        P("row", "col"),
        P("col"),
        P("col", "row"),
        P("col", "row"),
        P("row", "col"),
    )
    return jax.shard_map(body, mesh=mesh, in_specs=in_specs, out_specs=out_specs, check_vma=False)
```

```python
import functools

import jax
import jax.numpy as jnp
import numpy as np
from jax import lax
from jax.experimental import pallas as pl
from jax.experimental.pallas import tpu as pltpu
from jax.sharding import PartitionSpec as P

EPS = 1e-06
THETA = 1000000.0
NEG = -1e30
BF = jnp.bfloat16
F32 = jnp.float32
MESH = pl.DeviceIdType.MESH
HEAD = 128
HEADS = 6
SEQ = 1024
MODEL = 1536
FEAT = 384
BLOCK = 128
UNITS = 4480
PART = 1152
QCOLS = 768
QKV = 1024
VMEM_LIMIT = 62 * 2**20
SCALE = HEAD ** (-0.5)


def dot(left, right, left_dim=1, right_dim=0):
    return lax.dot_general(
        left, right, (((left_dim,), (right_dim,)), ((), ())), preferred_element_type=F32
    )


def aligned(index, step):
    return pl.multiple_of(index * step, step)


def block_of(row, col):
    return col + row * (7 - 2 * col)


def quarter_start(col):
    return pl.multiple_of(col * PART - (col // 3) * HEAD, HEAD)


class Place:
    def __init__(self):
        self.dp, self.row, self.col = (lax.axis_index(a) for a in ("dp", "row", "col"))
        self.hi, self.core = self.col // 2, self.col % 2
        self.z, self.y = self.dp // 4, self.dp % 4
        self.sib = 2 * self.hi + 1 - self.core
        self.far = 2 * (1 - self.hi) + self.core
        self.sibfar = 2 * (1 - self.hi) + 1 - self.core
        self.block = block_of(self.row, self.col)
        self.chips = (
            (self.row, 1 - self.hi),
            (1 - self.row, self.hi),
            (1 - self.row, 1 - self.hi),
            (self.row, self.hi),
        )
        self.S = {"col": self.sib}
        self.O = {"col": self.far}
        self.OS = {"col": self.sibfar}
        self.N1 = {"row": 1 - self.row}
        self.N2 = {"row": 1 - self.row, "col": self.far}
        self.N1S = {"row": 1 - self.row, "col": self.sib}
        self.N2S = {"row": 1 - self.row, "col": self.sibfar}

        def dp_at(z, y):
            return {"dp": lax.rem(z + 4, 4) * 4 + lax.rem(y + 4, 4)}

        self.YP, self.YM = dp_at(self.z, self.y + 1), dp_at(self.z, self.y - 1)
        self.Y2, self.Z2 = dp_at(self.z, self.y + 2), dp_at(self.z + 2, self.y)
        self.ZP, self.ZM = dp_at(self.z + 1, self.y), dp_at(self.z - 1, self.y)

    def meet(self, partners):
        barrier = pltpu.get_barrier_semaphore()
        for device in partners:
            pl.semaphore_signal(barrier, inc=1, device_id=device, device_id_type=MESH)
        pl.semaphore_wait(barrier, len(partners))


class Net:
    def __init__(self, send_sems, recv_sems, at):
        self.ss, self.rs, self.at, self.count, self.sent = send_sems, recv_sems, at, 0, []

    def key(self):
        self.count += 1
        return self.count - 1

    def copy(self, key, src, dst, device):
        return pltpu.make_async_remote_copy(
            src_ref=src,
            dst_ref=dst,
            send_sem=self.ss.at[key],
            recv_sem=self.rs.at[key],
            device_id=device,
            device_id_type=MESH,
        )

    def send(self, src, dst, device):
        key = self.key()
        copy = self.copy(key, src, dst, device)
        copy.start()
        self.sent.append(copy)
        return key

    def take(self, key, dst):
        self.copy(key, dst, dst, self.at.S).wait_recv()

    def finish(self, copies=None):
        copies = list(self.sent) if copies is None else copies
        for copy in copies:
            copy.wait_send()
            self.sent.remove(copy)


class Gather8:
    def __init__(self, net, at, place):
        self.net, self.at, self.place = net, at, place

    def start(self, src):
        net, at = self.net, self.at
        mine = self.place(at.row, at.col, None)
        self.k1 = net.send(src, mine, at.N1)
        self.k2 = net.send(src, mine, at.N2)
        self.k0 = net.send(src, mine, at.S)

    def middle(self):
        net, at, place = self.net, self.at, self.place
        near, away = place(1 - at.row, at.col, None), place(1 - at.row, at.far, None)
        first, last = place(1 - at.row, at.col, 0), place(1 - at.row, at.far, 1)
        net.take(self.k1, near)
        self.ka = net.send(first, first, at.N2)
        self.f1 = net.send(near, near, at.S)
        net.take(self.k2, away)
        self.kb = net.send(last, last, at.N1)
        self.f2 = net.send(away, away, at.S)

    def late(self):
        net, at, place = self.net, self.at, self.place
        first, last = place(at.row, at.far, 0), place(at.row, at.far, 1)
        net.take(self.ka, first)
        self.f3 = net.send(first, first, at.S)
        net.take(self.kb, last)
        self.f4 = net.send(last, last, at.S)

    def end(self, chip=None):
        net, at, place = self.net, self.at, self.place
        if chip in (None, 3):
            net.take(self.k0, place(at.row, at.sib, None))
        if chip in (None, 1):
            net.take(self.f1, place(1 - at.row, at.sib, None))
        if chip in (None, 2):
            net.take(self.f2, place(1 - at.row, at.sibfar, None))
        if chip in (None, 0):
            net.take(self.f3, place(at.row, at.sibfar, 0))
            net.take(self.f4, place(at.row, at.sibfar, 1))


def ring_dp(net, at, halves, ready=(None, None)):
    def wrap(index):
        return lax.rem(index + 4, 4)

    sides = (((at.YP, at.YM), (at.ZP, at.ZM)), ((at.ZP, at.ZM), (at.YP, at.YM)))
    firsts, seconds = (at.y, at.z), (at.z, at.y)

    def refs(i, a, b):
        return halves[i](b, a) if i == 0 else halves[i](a, b)

    def send(i, a, b, device):
        return [net.send(ref, ref, device) for ref in refs(i, a, b)]

    def take(i, a, b, keys):
        for key, ref in zip(keys, refs(i, a, b), strict=True):
            net.take(key, ref)

    one, two, onward = {}, {}, {}
    for i in (0, 1):
        if ready[i]:
            ready[i]()
        one[i] = [send(i, firsts[i], seconds[i], side) for side in sides[i][0]]
        if ready[i]:
            two[i, 0] = [send(i, firsts[i], seconds[i], side) for side in sides[i][1]]
    for i in (0, 1):
        if not ready[i]:
            two[i, 0] = [send(i, firsts[i], seconds[i], side) for side in sides[i][1]]
    yield
    for i in (0, 1):
        minus = wrap(firsts[i] - 1)
        take(i, minus, seconds[i], one[i][0])
        one[i].append(send(i, minus, seconds[i], sides[i][0][0]))
        two[i, 1] = [send(i, minus, seconds[i], side) for side in sides[i][1]]
    yield
    for i in (0, 1):
        plus = wrap(firsts[i] + 1)
        take(i, plus, seconds[i], one[i][1])
        two[i, 2] = [send(i, plus, seconds[i], side) for side in sides[i][1]]
    offsets = (0, -1, 1, 2)
    for q in (0, 1, 2, 3):
        yield
        for i in (0, 1):
            if q == 1:
                across = wrap(firsts[i] + 2)
                take(i, across, seconds[i], one[i][2])
                two[i, 3] = [send(i, across, seconds[i], side) for side in sides[i][1]]
            slot = wrap(firsts[i] + offsets[q])
            minus, plus = wrap(seconds[i] - 1), wrap(seconds[i] + 1)
            take(i, slot, minus, two[i, q][0])
            if q < 2:
                onward[i, q] = send(i, slot, minus, sides[i][1][0])
            take(i, slot, plus, two[i, q][1])
            if q >= 2:
                onward[i, q] = send(i, slot, plus, sides[i][1][1])
    for q in (0, 1, 2, 3):
        yield
        for i in (0, 1):
            slot = wrap(firsts[i] + offsets[q])
            take(i, slot, wrap(seconds[i] + 2), onward[i, q])


def drain(steps):
    for _ in steps:
        pass


def rms(values):
    return lax.rsqrt(jnp.mean(values * values, axis=1, keepdims=True) + EPS)


def turn(values):
    return pltpu.roll(values, HEAD // 2, 1)


def causal(scores, start):
    places = start + lax.broadcasted_iota(jnp.int32, scores.shape, 0)
    keys = lax.broadcasted_iota(jnp.int32, scores.shape, 1)
    return jnp.where(keys <= places, scores, NEG)


def vmem():
    return pl.BlockSpec(memory_space=pltpu.VMEM)


def anywhere():
    return pl.BlockSpec(memory_space=pl.ANY)


class Reduce8:
    def __init__(self, net, at, own, other, sib_in, first_in, last_in, near_in, away_in):
        self.net, self.at, self.own, self.other, self.sib_in = net, at, own, other, sib_in
        self.first_in, self.last_in, self.near_in, self.away_in = first_in, last_in, near_in, away_in
        self.half = own.shape[1] // 2
        self.keys = {}

    def put(self, j, mine, theirs):
        self.own[j] = mine
        self.other[j] = theirs
        self.keys[j] = self.net.send(self.other.at[j], self.sib_in.at[j], self.at.S)

    def step(self, j):
        net, at, half = self.net, self.at, self.half
        net.take(self.keys[j], self.sib_in.at[j])
        total = self.own[j].astype(F32) + self.sib_in[j].astype(F32)
        if j == 0:
            self.own[j] = total.astype(BF)
            self.first = net.send(self.own.at[j, pl.ds(0, half)], self.first_in, at.N1)
            self.last = net.send(self.own.at[j, pl.ds(half, half)], self.last_in, at.N2)
        elif j == 1:
            net.take(self.last, self.last_in)
            self.own[j, :half] = total[:half].astype(BF)
            self.own[j, half:] = (total[half:] + self.last_in[...].astype(F32)).astype(BF)
            self.near = net.send(self.own.at[j], self.near_in, at.N1)
        elif j == 2:
            net.take(self.first, self.first_in)
            self.own[j, :half] = (total[:half] + self.first_in[...].astype(F32)).astype(BF)
            self.own[j, half:] = total[half:].astype(BF)
            self.away = net.send(self.own.at[j], self.away_in, at.N2)
        else:
            net.take(self.near, self.near_in)
            net.take(self.away, self.away_in)
            return total + self.near_in[...].astype(F32) + self.away_in[...].astype(F32)
        return None


def reduce8_scratch(rows, columns):
    return [
        pltpu.VMEM((4, rows, columns), BF),
        pltpu.VMEM((4, rows, columns), BF),
        pltpu.VMEM((4, rows, columns), BF),
        pltpu.VMEM((rows // 2, columns), BF),
        pltpu.VMEM((rows // 2, columns), BF),
        pltpu.VMEM((rows, columns), BF),
        pltpu.VMEM((rows, columns), BF),
    ]


def tiles_of(width, step):
    return [(first, min(step, width - first)) for first in range(0, width, step)]


def forward_kernel(
    x_ref,
    og_ref,
    wq_ref,
    wk_ref,
    wv_ref,
    wout_ref,
    wg_ref,
    wu_ref,
    wd_ref,
    gains_ref,
    bias_ref,
    cos_ref,
    sin_ref,
    xs_ref,
    n1c_ref,
    og_out,
    qw_out,
    ow_out,
    q_ref,
    k_ref,
    v_ref,
    lse_ref,
    attn_ref,
    mid_ref,
    gains_all,
    dn2_ref,
    hidden_out,
    dw_out,
    grad_gu,
    grad_down,
    wqkv_ref,
    x_all,
    n1,
    og_all,
    n2_all,
    qw,
    ow,
    gw,
    uw,
    dw,
    part_out,
    part_in,
    d_up,
    tile_buf,
    *rest,
):
    red_a, sems = rest[:7], rest[7:]
    send_sems, recv_sems, local_sems, tile_sems = sems
    at = Place()
    net = Net(send_sems, recv_sems, at)
    local, local_count = [], iter(range(32))

    def move(src, dst):
        copy = pltpu.make_async_copy(src, dst, local_sems.at[next(local_count)])
        copy.start()
        local.append(copy)
        return copy

    joined = [
        move(wq_ref, wqkv_ref.at[:, pl.ds(0, QCOLS)]),
        move(wk_ref, wqkv_ref.at[:, pl.ds(QCOLS, HEAD)]),
        move(wv_ref, wqkv_ref.at[:, pl.ds(QCOLS + HEAD, HEAD)]),
    ]
    at.meet((at.S, at.N1, at.N2, at.O, at.OS, at.YP, at.YM, at.ZP, at.ZM))
    for copy in joined:
        copy.wait()
    local.clear()

    def tokens_of(array):
        def place(row, col, part):
            if part is None:
                rows = pl.ds(aligned(row, SEQ // 2), SEQ // 2)
            else:
                rows = pl.ds(aligned(row * 2 + part, SEQ // 4), SEQ // 4)
            return array.at[rows, pl.ds(aligned(col, FEAT), FEAT)]

        return place

    mine, mine_far = aligned(at.col, FEAT), aligned(1 - at.hi, 2 * FEAT)
    move(x_ref, tokens_of(x_all)(at.row, at.col, None))
    move(wqkv_ref, qw.at[pl.ds(mine, FEAT), :])
    move(wout_ref, ow.at[:, pl.ds(mine, FEAT)])
    move(gains_ref, gains_all.at[:, pl.ds(mine, FEAT)])
    start = quarter_start(at.col)
    move(wg_ref.at[:, pl.ds(start, PART)], gw.at[pl.ds(mine, FEAT), :])
    move(wu_ref.at[:, pl.ds(start, PART)], uw.at[pl.ds(mine, FEAT), :])
    move(wd_ref.at[pl.ds(start, PART), :], dw.at[:, pl.ds(mine, FEAT)])
    move(og_ref, tokens_of(og_all)(at.row, at.col, None))

    eighth = at.dp % 8
    across = [net.key() for _ in range(5)]

    def slice_copies(core, first, last):
        device = {"col": 2 * (1 - at.hi) + core}
        rows = pl.ds(aligned(eighth, 48), 48)
        target = pl.ds(pl.multiple_of(mine + eighth * 48, 16), 48)
        columns = pl.ds(core * 512, 512)
        out_rows = pl.ds(pl.multiple_of(core * FEAT + eighth * 48, 16), 48)
        theirs = quarter_start(2 * (1 - at.hi) + core)
        down_rows = pl.ds(pl.multiple_of(theirs + eighth * 144, 16), 144)
        down_target = pl.ds(aligned(eighth, 144), 144)
        pairs = (
            (wqkv_ref.at[rows, columns], qw.at[target, columns]),
            (wout_ref.at[out_rows, :], ow.at[out_rows, pl.ds(mine, FEAT)]),
            (wg_ref.at[rows, pl.ds(theirs, PART)], gw.at[target, :]),
            (wu_ref.at[rows, pl.ds(theirs, PART)], uw.at[target, :]),
            (wd_ref.at[down_rows, :], dw.at[down_target, pl.ds(mine, FEAT)]),
        )
        return [
            pltpu.make_async_remote_copy(
                src_ref=pairs[i][0],
                dst_ref=pairs[i][1],
                send_sem=net.ss.at[spare[core][i]],
                recv_sem=net.rs.at[across[i]],
                device_id=device,
                device_id_type=MESH,
            )
            for i in range(first, last)
        ]

    spare = ([net.key() for _ in range(5)], [net.key() for _ in range(5)])
    chosen = at.core == at.dp // 8

    @pl.when(chosen)
    def _():
        for core in (0, 1):
            for copy in slice_copies(core, 0, 2):
                copy.start()

    gather_x = Gather8(net, at, tokens_of(x_all))
    gather_x.start(x_ref)
    gain_far = net.send(gains_ref, gains_all.at[:, pl.ds(mine, FEAT)], at.N2)
    gain_sib = net.send(gains_ref, gains_all.at[:, pl.ds(mine, FEAT)], at.S)
    near_qw = net.send(wqkv_ref, qw.at[pl.ds(mine, FEAT), :], at.S)
    near_ow = net.send(wout_ref, ow.at[:, pl.ds(mine, FEAT)], at.S)

    far_half = pl.ds(mine_far, 2 * FEAT)

    def qkv_slices(z, y):
        rows = pl.ds(pl.multiple_of(mine_far + (z * 4 + y) * 48, 16), 48)
        return [qw.at[rows, pl.ds(aligned(at.core, 512), 512)]]

    def out_slices(z, y):
        index = z * 4 + y
        rows = pl.ds(pl.multiple_of(at.core * FEAT + (index % 8) * 48, 16), 48)
        return [ow.at[rows, pl.ds(pl.multiple_of(mine_far + (index // 8) * FEAT, HEAD), FEAT)]]

    def ffn_slices(weights, first, count):
        def slices(z, y):
            index = z * 4 + y
            rows = pl.ds(pl.multiple_of(mine_far + index * 48, 16), 48)
            down_rows = pl.ds(pl.multiple_of((index % 8) * 144 + first, 16), count)
            lanes = pl.ds(pl.multiple_of(mine_far + (index // 8) * FEAT, HEAD), FEAT)
            return [weights.at[rows, :], dw.at[down_rows, lanes]]

        return slices

    net.take(across[0], qkv_slices(at.z, at.y)[0])
    net.take(across[1], out_slices(at.z, at.y)[0])
    ring = ring_dp(net, at, (qkv_slices, out_slices))
    next(ring)
    next(ring)
    next(ring)
    gather_x.middle()
    gains_far = gains_all.at[:, pl.ds(aligned(at.far, FEAT), FEAT)]
    net.take(gain_far, gains_far)
    gain_sibfar = net.send(gains_far, gains_far, at.S)
    next(ring)
    cols_half, rows_half = pl.ds(aligned(at.core, 512), 512), pl.ds(aligned(at.core, FEAT), FEAT)
    gather_og = Gather8(net, at, tokens_of(og_all))
    gather_x.late()

    @pl.when(chosen)
    def _():
        for core in (0, 1):
            for copy in slice_copies(core, 2, 5):
                copy.start()

    drain(ring)
    far_qw = net.send(qw.at[far_half, cols_half], qw.at[far_half, cols_half], at.S)
    far_ow = net.send(ow.at[rows_half, far_half], ow.at[rows_half, far_half], at.S)
    near = [
        net.send(wg_ref.at[:, pl.ds(quarter_start(at.sib), PART)], gw.at[pl.ds(mine, FEAT), :], at.S),
        net.send(wu_ref.at[:, pl.ds(quarter_start(at.sib), PART)], uw.at[pl.ds(mine, FEAT), :], at.S),
        net.send(wd_ref.at[pl.ds(quarter_start(at.sib), PART), :], dw.at[:, pl.ds(mine, FEAT)], at.S),
    ]
    gather_og.start(og_ref)
    gather_x.end()
    early = list(net.sent)
    net.take(gain_sib, gains_all.at[:, pl.ds(aligned(at.sib, FEAT), FEAT)])
    net.take(gain_sibfar, gains_all.at[:, pl.ds(aligned(at.sibfar, FEAT), FEAT)])
    for copy in local:
        copy.wait()
    local.clear()

    gain1, gain2 = gains_all[0:1, :], gains_all[1:2, :]

    def norm_block(i, carry):
        rows = pl.ds(aligned(i, BLOCK), BLOCK)
        values = x_all[rows, :].astype(F32)
        n1[rows, :] = (values * rms(values) * gain1).astype(BF)
        return carry

    lax.fori_loop(0, SEQ // BLOCK // 2, norm_block, 0)
    net.take(across[2], ffn_slices(gw, 0, 80)(at.z, at.y)[0])
    net.take(across[3], ffn_slices(uw, 80, 64)(at.z, at.y)[0])
    net.take(across[4], ffn_slices(uw, 0, 144)(at.z, at.y)[1])
    ring = ring_dp(net, at, (ffn_slices(gw, 0, 80), ffn_slices(uw, 80, 64)))
    next(ring)
    lax.fori_loop(SEQ // BLOCK // 2, SEQ // BLOCK, norm_block, 0)
    next(ring)
    gather_og.middle()
    my_rows = pl.ds(aligned(at.block, BLOCK), BLOCK)
    xs_ref[...] = x_all[my_rows, :]
    n1c_ref[...] = n1[:, pl.ds(mine, FEAT)]
    net.take(near_qw, qw.at[pl.ds(aligned(at.sib, FEAT), FEAT), :])
    other_cols = pl.ds(aligned(1 - at.core, 512), 512)
    net.take(far_qw, qw.at[far_half, other_cols])
    move(qw, qw_out)

    def kv_block(i, carry):
        rows = pl.ds(aligned(i, 256), 256)
        both = dot(n1[rows, :], qw[:, QCOLS:]) + bias_ref[:, QCOLS:]
        key = both[:, :HEAD]
        k_ref[rows, :] = (key * cos_ref[rows, :] + turn(key) * sin_ref[rows, :]).astype(BF)
        v_ref[rows, :] = both[:, HEAD:].astype(BF)
        return carry

    lax.fori_loop(0, SEQ // 256, kv_block, 0)
    next(ring)
    pair = (at.col, 7 - at.col)
    for j in (0, 1):
        rows = pl.ds(aligned(pair[j], BLOCK), BLOCK)
        queries = dot(n1[rows, :], qw[:, :QCOLS]) + bias_ref[:, :QCOLS]
        cosine, sine = cos_ref[rows, :], sin_ref[rows, :]
        for h in range(HEADS):
            one = queries[:, h * HEAD : (h + 1) * HEAD]
            q_ref[pl.ds(j * BLOCK, BLOCK), pl.ds(h * HEAD, HEAD)] = (
                one * cosine + turn(one) * sine
            ).astype(BF)
    next(ring)
    gather_og.late()

    for j in (0, 1):
        keys = SEQ // 2 * (j + 1)
        rows = pl.ds(j * BLOCK, BLOCK)

        def attend(h, carry):
            lanes = pl.ds(aligned(h, HEAD), HEAD)
            scores = dot(q_ref[rows, lanes], k_ref[:keys, :], 1, 1) * SCALE
            scores = causal(scores, pair[j] * BLOCK)
            top = jnp.max(scores, axis=1, keepdims=True)
            weights = jnp.exp(scores - top)
            total = jnp.sum(weights, axis=1, keepdims=True)
            lse_ref[j * HEADS + h] = top + jnp.log(total)
            probs = (weights * (1.0 / total)).astype(BF)
            attn_ref[rows, lanes] = dot(probs, v_ref[:keys, :]).astype(BF)
            return carry

        lax.fori_loop(0, HEADS, attend, 0)
        next(ring)

    net.take(near_ow, ow.at[:, pl.ds(aligned(at.sib, FEAT), FEAT)])
    other_rows = pl.ds(aligned(1 - at.core, FEAT), FEAT)
    net.take(far_ow, ow.at[other_rows, far_half])
    move(ow, ow_out)
    part_out[...] = dot(attn_ref[pl.ds(aligned(1 - at.row, BLOCK), BLOCK), :], ow[...]).astype(BF)
    part = net.send(part_out, part_in, at.N1)
    own = dot(attn_ref[pl.ds(aligned(at.row, BLOCK), BLOCK), :], ow[...])
    net.take(part, part_in)
    mid = xs_ref[...].astype(F32) + own + part_in[...].astype(F32)
    mid_ref[...] = mid

    def place_n2(row, col, part):
        first = block_of(row, col) * BLOCK
        if part is None:
            return n2_all.at[pl.ds(pl.multiple_of(first, BLOCK), BLOCK), :]
        return n2_all.at[pl.ds(pl.multiple_of(first + part * 64, 64), 64), :]

    n2_all[my_rows, :] = (mid * rms(mid) * gain2).astype(BF)
    gather_n2 = Gather8(net, at, place_n2)
    gather_n2.start(place_n2(at.row, at.col, None))
    gather_og.end()
    move(og_all.at[my_rows, :], og_out)
    next(ring)
    next(ring)
    gather_n2.middle()
    next(ring)
    next(ring)
    gather_n2.late()
    drain(ring)
    net.take(near[2], dw.at[:, pl.ds(aligned(at.sib, FEAT), FEAT)])

    def hidden_back(i, carry):
        rows = pl.ds(aligned(i, 256), 256)
        for first, width in tiles_of(PART, 512):
            lanes = pl.ds(first, width)
            d_up[rows, lanes] = dot(og_all[rows, :], dw[lanes, :], 1, 1).astype(BF)
        return carry

    lax.fori_loop(0, 4, hidden_back, 0)
    move(dw, dw_out)
    net.take(near[0], gw.at[pl.ds(aligned(at.sib, FEAT), FEAT), :])
    net.take(near[1], uw.at[pl.ds(aligned(at.sib, FEAT), FEAT), :])

    net.finish(early)
    hidden, d_gate = x_all.at[:, pl.ds(0, PART)], n1.at[:, pl.ds(0, PART)]
    norms = Reduce8(net, at, *red_a)
    chips = at.chips
    last_part = at.col == 3

    def tokens(j):
        row, hi = chips[j]
        first = 2 * hi + row * (6 - 4 * hi)
        return pl.ds(aligned(first, BLOCK), 256), at.core + row * (1 - 2 * at.core)

    for j in (3, 1, 2, 0):
        gather_n2.end(j)
        rows, _ = tokens(j)
        for first, width in tiles_of(PART, 512):
            lanes = pl.ds(first, width)
            gate = dot(n2_all[rows, :], gw[:, lanes])
            up = dot(n2_all[rows, :], uw[:, lanes])
            d_hidden = d_up[rows, lanes].astype(F32)
            sig = jax.nn.sigmoid(gate)
            act = gate * sig
            d_act = d_hidden * up * sig * (1.0 + gate * (1.0 - sig))
            values = [act * up, d_act, d_hidden * act]
            if first == 0:
                lane = lax.broadcasted_iota(jnp.int32, (1, width), 1)
                fresh = jnp.logical_or(lane >= HEAD, jnp.logical_not(last_part))
                values = [jnp.where(fresh, value, 0.0) for value in values]
            for ref, value in zip((hidden, d_gate, d_up), values, strict=True):
                ref[rows, lanes] = value.astype(BF)
    move(hidden, hidden_out)
    for j in range(4):
        rows, place = tokens(j)
        own_rows = pl.ds(pl.multiple_of(rows.start + place * BLOCK, BLOCK), BLOCK)
        other_rows = pl.ds(pl.multiple_of(rows.start + (1 - place) * BLOCK, BLOCK), BLOCK)
        parts = [
            (dot(d_gate[r, :], gw[...], 1, 1) + dot(d_up[r, :], uw[...], 1, 1)).astype(BF)
            for r in (other_rows, own_rows)
        ]
        norms.put(j, parts[1], parts[0])
        if j:
            norms.step(j - 1)

    writes = []

    def outer_sum(left, right, out):
        height = left.shape[1] // 2
        for first, width in tiles_of(right.shape[1], 256):
            place = len(writes) % 2
            if len(writes) > 1:
                writes[-2].wait()
            for i in (0, 1):
                rows = pl.ds(i * height, height)
                tile_buf[place, rows, :width] = dot(
                    left[:, rows], right[:, pl.ds(first, width)], 0, 0
                ).astype(BF)
            writes.append(
                pltpu.make_async_copy(
                    tile_buf.at[place, pl.ds(0, 2 * height), pl.ds(0, width)],
                    out.at[:, pl.ds(first, width)],
                    tile_sems.at[place],
                )
            )
            writes[-1].start()

    outer_sum(hidden, og_all, grad_down)
    outer_sum(n2_all, d_gate, grad_gu.at[0])
    dn2_ref[...] = norms.step(3)
    outer_sum(n2_all, d_up, grad_gu.at[1])
    for copy in writes[-2:]:
        copy.wait()
    for copy in local:
        copy.wait()
    net.finish()

    @pl.when(chosen)
    def _():
        for core in (0, 1):
            for copy in slice_copies(core, 0, 5):
                copy.wait_send()


def run_forward(x, og, wq, wk, wv, wout, wg, wu, wd, gains, bias, cosine, sine):
    outs = (
        ((BLOCK, MODEL), BF, vmem),
        ((SEQ, FEAT), BF, vmem),
        ((BLOCK, MODEL), BF, anywhere),
        ((MODEL, QKV), BF, anywhere),
        ((QCOLS, MODEL), BF, anywhere),
        ((2 * BLOCK, QCOLS), BF, vmem),
        ((SEQ, HEAD), BF, vmem),
        ((SEQ, HEAD), BF, vmem),
        ((2 * HEADS, BLOCK, 1), F32, vmem),
        ((2 * BLOCK, QCOLS), BF, vmem),
        ((BLOCK, MODEL), F32, vmem),
        ((8, MODEL), F32, vmem),
        ((BLOCK, MODEL), F32, vmem),
        ((SEQ, PART), BF, anywhere),
        ((PART, MODEL), BF, anywhere),
        ((2, MODEL, PART), BF, anywhere),
        ((PART, MODEL), BF, anywhere),
    )
    return pl.pallas_call(
        forward_kernel,
        out_shape=[jax.ShapeDtypeStruct(dims, dtype) for dims, dtype, _ in outs],
        in_specs=[anywhere()] * 9 + [vmem()] * 4,
        out_specs=[place() for _, _, place in outs],
        scratch_shapes=[
            pltpu.VMEM((FEAT, QKV), BF),
            pltpu.VMEM((SEQ, MODEL), BF),
            pltpu.VMEM((SEQ, MODEL), BF),
            pltpu.VMEM((SEQ, MODEL), BF),
            pltpu.VMEM((SEQ, MODEL), BF),
            pltpu.VMEM((MODEL, QKV), BF),
            pltpu.VMEM((QCOLS, MODEL), BF),
            pltpu.VMEM((MODEL, PART), BF),
            pltpu.VMEM((MODEL, PART), BF),
            pltpu.VMEM((PART, MODEL), BF),
            pltpu.VMEM((BLOCK, MODEL), BF),
            pltpu.VMEM((BLOCK, MODEL), BF),
            pltpu.VMEM((SEQ, PART), BF),
            pltpu.VMEM((2, MODEL, 256), BF),
        ]
        + reduce8_scratch(BLOCK, MODEL)
        + [
            pltpu.SemaphoreType.DMA((200,)),
            pltpu.SemaphoreType.DMA((200,)),
            pltpu.SemaphoreType.DMA((32,)),
            pltpu.SemaphoreType.DMA((2,)),
        ],
        compiler_params=pltpu.CompilerParams(
            collective_id=0, has_side_effects=True, vmem_limit_bytes=VMEM_LIMIT
        ),
        cost_estimate=pl.CostEstimate(
            flops=37 * 10**9, bytes_accessed=80 * 10**6, transcendentals=4 * 10**6
        ),
        name="forward_and_feed_forward",
    )(x, og, wq, wk, wv, wout, wg, wu, wd, gains, bias, cosine, sine)


def add_up(out, terms):
    lead = out.shape[:-2]
    if not lead:
        total = terms[0][...].astype(F32)
        for term in terms[1:]:
            total = total + term[...].astype(F32)
        out[...] = total.astype(out.dtype)
        return
    count = 1
    for size in lead:
        count *= size

    def step(i, carry):
        index = []
        for size in reversed(lead):
            index.insert(0, i % size)
            i = i // size
        index = tuple(index)
        total = terms[0].at[index][...].astype(F32)
        for term in terms[1:]:
            total = total + term.at[index][...].astype(F32)
        out.at[index][...] = total.astype(out.dtype)
        return carry

    lax.fori_loop(0, count, step, 0)


class RingItem:
    def __init__(self, net, sides, place, part, held, way, bufs, own):
        self.net, self.part, self.held, self.own = net, part, held, own
        self.relay, self.staged, self.from_last, self.from_next = bufs
        self.onward, self.back = (sides[0], sides[1]) if way == 0 else (sides[1], sides[0])
        step = 1 - 2 * way
        self.here, self.next, self.across, self.last = (
            lax.rem(place + 4 + step * i, 4) for i in (0, 1, 2, 3)
        )

    def start(self):
        self.k_relay = self.net.send(self.part(self.across), self.relay, self.onward)

    def direct(self):
        self.k_next = self.net.send(self.part(self.last), self.from_next, self.back)

    def middle(self):
        self.net.take(self.k_relay, self.relay)
        add_up(self.staged, [self.held(self.next), self.relay])
        self.k_last = self.net.send(self.staged, self.from_last, self.onward)

    def end(self):
        self.net.take(self.k_next, self.from_next)
        self.net.take(self.k_last, self.from_last)
        add_up(self.own, [self.held(self.here), self.from_next, self.from_last])


def begin(items):
    for item in items:
        item.start()
    for item in items:
        item.direct()


LEFT, RIGHT = pl.ds(0, QCOLS), pl.ds(QCOLS, QCOLS)
FFN_FIRST = (((2, 2, 48, PART), (2, 80, QCOLS)), ((2, 2, 48, PART), (144, QCOLS)))
FFN_LAST = (((2, 48, PART), (80, QCOLS)), ((2, 48, PART), (80, QCOLS)))
SMALL_FIRST = (((2, 48, 512),), ((2, 48, FEAT),))
SMALL_LAST = (((48, 512),), ((48, FEAT),))


def down_rows(k):
    return pl.ds(pl.multiple_of(72 * k - 8 * (k % 2), 16), 80)


def ring_scratch(first, last):
    scratch = []
    for i in (0, 1):
        for dims in first[i]:
            scratch += [pltpu.VMEM(dims, BF)] * 8
            scratch.append(pltpu.VMEM((2,) + dims, BF))
        for dims in last[i]:
            scratch += [pltpu.VMEM(dims, BF)] * 4
    return scratch


def ring_items(net, at, first, last, parts, helds, seconds, finals, bufs):
    sides = (((at.YP, at.YM), (at.ZP, at.ZM)), ((at.ZP, at.ZM), (at.YP, at.YM)))
    places = ((at.y, at.z), (at.z, at.y))
    bufs = list(bufs)
    one, two = ([], []), ([], [])
    for i in (0, 1):
        owns = []
        for n in range(len(first[i])):
            own = bufs[8]
            for way in (0, 1):
                part = functools.partial(lambda k, f, w: f(k, w), f=parts[i][n], w=way)
                held = functools.partial(lambda k, f, w: f(k, w), f=helds[i][n], w=way)
                four = bufs[4 * way : 4 * way + 4]
                one[i].append(
                    RingItem(net, sides[i][0], places[i][0], part, held, way, four, own.at[way])
                )
            owns.append(own)
            bufs = bufs[9:]
        for n in range(len(last[i])):
            part = functools.partial(lambda k, f, o: f(o, k), f=seconds[i][n], o=owns[n])
            two[i].append(
                RingItem(net, sides[i][1], places[i][1], part, part, n % 2, bufs[:4], finals[i][n])
            )
            bufs = bufs[4:]

    def mix(pair):
        return [item for items in zip(*pair, strict=True) for item in items]

    return mix(one), mix(two)


def ffn_items(net, at, far_refs, near_refs, gu_own, down_own, bufs):
    def parts_of(gu, down):
        return (
            (
                lambda k, way: gu.at[way, pl.ds(0, 2), :, k],
                lambda k, way: down.at[way, :, down_rows(k), LEFT],
            ),
            (
                lambda k, way: gu.at[k // 2, pl.ds(2, 2), k % 2, pl.ds(2 * way, 2)],
                lambda k, way: down.at[k // 2, k % 2, pl.ds(144 * way, 144), RIGHT],
            ),
        )

    parts, helds = parts_of(*far_refs), parts_of(*near_refs)
    seconds = (
        (lambda own, k: own.at[k // 2, :, k % 2], lambda own, k: own.at[k // 2, k % 2]),
        (
            lambda own, k: own.at[k // 2, :, k % 2],
            lambda own, k: own.at[k // 2, pl.ds(pl.multiple_of((k % 2) * 64, 64), 80)],
        ),
    )
    finals = (
        (gu_own.at[pl.ds(0, 2)], down_own.at[:, LEFT]),
        (gu_own.at[pl.ds(2, 2)], down_own.at[:, RIGHT]),
    )
    return ring_items(net, at, FFN_FIRST, FFN_LAST, parts, helds, seconds, finals, bufs)


def small_items(net, at, qkv, out, qkv_own, out_own, bufs):
    parts = (
        (lambda k, way: qkv.at[:, k, :, pl.ds(512 * way, 512)],),
        (lambda k, way: out.at[k // 2, k % 2, pl.ds(2 * way, 2)],),
    )
    seconds = ((lambda own, k: own.at[k // 2, k % 2],), (lambda own, k: own.at[k // 2, k % 2],))
    finals = ((qkv_own,), (out_own,))
    return ring_items(net, at, SMALL_FIRST, SMALL_LAST, parts, parts, seconds, finals, bufs)


def backward_kernel(
    dn2_ref,
    mid_ref,
    og_ref,
    gains_all,
    xs_ref,
    n1c,
    attn_ref,
    q_ref,
    k_ref,
    v_ref,
    lse_ref,
    cos_ref,
    sin_ref,
    ow_far,
    qw_far,
    gu_far,
    down_far,
    grad_in,
    grad_out,
    grad_qkv,
    small_ref,
    gu_own,
    down_own,
    sums_ref,
    sums_in,
    attn_all,
    mid_cols,
    mid_pair,
    d_mid,
    d_attn,
    d_q,
    d_kv,
    kv_out,
    kv_in,
    d_qkv_all,
    part_out,
    part_in,
    gi_out,
    gi_in,
    ow,
    qw,
    gu,
    down,
    *rest,
):
    bufs, (send_sems, recv_sems, local_sems) = rest[:-3], rest[-3:]
    at = Place()
    net = Net(send_sems, recv_sems, at)
    held = [
        pltpu.make_async_copy(src, dst, local_sems.at[i])
        for i, (src, dst) in enumerate(
            ((ow_far, ow), (gu_far, gu), (down_far, down), (qw_far, qw))
        )
    ]
    for copy in held:
        copy.start()
    at.meet(
        (at.S, at.O, at.OS, at.N1, at.N2, at.N1S, at.N2S, at.YP, at.YM, at.ZP, at.ZM)
    )
    first, last = ffn_items(net, at, (gu_far, down_far), (gu, down), gu_own, down_own, bufs)
    begin(first)
    peers = ((at.S, at.sib), (at.O, at.far), (at.OS, at.sibfar))
    pair = (at.col, 7 - at.col)

    def rows_at(block):
        return pl.ds(aligned(block, BLOCK), BLOCK)

    def cols_at(col):
        return pl.ds(aligned(col, FEAT), FEAT)

    class GatherCol:
        def __init__(self, array):
            self.array = array

        def rows(self, col, j):
            return self.array.at[rows_at(col + j * (7 - 2 * col)), :]

        def start(self):
            self.far = [net.send(self.rows(at.col, j), self.rows(at.col, j), at.O) for j in (0, 1)]
            self.sib = [net.send(self.rows(at.col, j), self.rows(at.col, j), at.S) for j in (0, 1)]

        def middle(self):
            self.onward = []
            for j in (0, 1):
                net.take(self.far[j], self.rows(at.far, j))
                self.onward.append(net.send(self.rows(at.far, j), self.rows(at.far, j), at.S))

        def end(self):
            for j in (0, 1):
                net.take(self.sib[j], self.rows(at.sib, j))
                net.take(self.onward[j], self.rows(at.sibfar, j))

    gather_attn = GatherCol(attn_all)
    for j in (0, 1):
        attn_all[rows_at(pair[j]), :] = attn_ref[pl.ds(j * BLOCK, BLOCK), :]

    gain1, gain2 = gains_all[0:1, :], gains_all[1:2, :]
    mid = mid_ref[...]
    scale = rms(mid)
    unit = mid * scale
    d_normed = dn2_ref[...]
    sums_ref[...] = jnp.zeros_like(sums_ref)
    sums_ref[1:2, :] = jnp.sum(d_normed * unit, axis=0, keepdims=True)
    bent = d_normed * gain2
    d_mid[...] = og_ref[...].astype(F32) + scale * (
        bent - unit * jnp.mean(bent * unit, axis=1, keepdims=True)
    )
    mid_pair[at.row] = d_mid[...].astype(BF)
    to_pair = net.send(mid_pair.at[at.row], mid_pair.at[at.row], at.N1)
    mid_cols[rows_at(at.block), :] = d_mid[:, cols_at(at.col)].astype(BF)
    spread = []
    others = (
        (at.S, at.row, at.sib),
        (at.N1, 1 - at.row, at.col),
        (at.N1S, 1 - at.row, at.sib),
        (at.O, at.row, at.far),
        (at.OS, at.row, at.sibfar),
        (at.N2, 1 - at.row, at.far),
        (at.N2S, 1 - at.row, at.sibfar),
    )
    for device, row, col in others:
        spread.append(
            net.send(
                mid_pair.at[at.row, :, cols_at(col)], mid_cols.at[rows_at(at.block), :], device
            )
        )
    gather_attn.start()
    net.take(to_pair, mid_pair.at[1 - at.row])
    held[0].wait()
    for j in (0, 1):
        d_attn[pl.ds(j * BLOCK, BLOCK), :] = dot(mid_pair[j], ow[...], 1, 1).astype(BF)
    d_kv[...] = jnp.zeros_like(d_kv)
    held[1].wait()
    held[2].wait()
    for item in first:
        item.middle()

    for j in (0, 1):
        keys = SEQ // 2 * (j + 1)
        rows = pl.ds(j * BLOCK, BLOCK)

        def back(h, carry):
            lanes = pl.ds(aligned(h, HEAD), HEAD)
            queries, d_out = q_ref[rows, lanes], d_attn[rows, lanes]
            scores = dot(queries, k_ref[:keys, :], 1, 1) * SCALE
            scores = causal(scores, pair[j] * BLOCK)
            probs = jnp.exp(scores - lse_ref[j * HEADS + h])
            d_probs = dot(d_out, v_ref[:keys, :], 1, 1)
            inner = jnp.sum(probs * d_probs, axis=1, keepdims=True)
            d_scores = (probs * (d_probs - inner) * SCALE).astype(BF)
            d_q[rows, lanes] = dot(d_scores, k_ref[:keys, :])
            d_kv[:keys, :HEAD] += dot(d_scores, queries, 0, 0)
            d_kv[:keys, HEAD:] += dot(probs.astype(BF), d_out, 0, 0)
            return carry

        lax.fori_loop(0, HEADS, back, 0)
    gather_attn.middle()

    kv_out[...] = d_kv[...].astype(BF)
    kv_keys = [
        [
            net.send(kv_out.at[rows_at(col + j * (7 - 2 * col)), :], kv_in.at[i, j], device)
            for j in (0, 1)
        ]
        for i, (device, col) in enumerate(peers)
    ]
    cosines = [cos_ref[rows_at(pair[j]), :] for j in (0, 1)]
    sines = [sin_ref[rows_at(pair[j]), :] for j in (0, 1)]
    for j in (0, 1):
        for h in range(HEADS):
            one = d_q[pl.ds(j * BLOCK, BLOCK), pl.ds(h * HEAD, HEAD)]
            d_qkv_all[rows_at(pair[j]), pl.ds(h * HEAD, HEAD)] = (
                one * cosines[j] - turn(one) * sines[j]
            ).astype(BF)
    for item in first:
        item.end()
    begin(last)
    gather_attn.end()
    for key, (_, row, col) in zip(spread, others, strict=True):
        net.take(key, mid_cols.at[rows_at(block_of(row, col)), :])
    grad_out[...] = dot(attn_all[...], mid_cols[...], 0, 0).astype(BF)
    for j in (0, 1):
        total = d_kv[rows_at(pair[j]), :]
        for i in range(3):
            net.take(kv_keys[i][j], kv_in.at[i, j])
            total = total + kv_in[i, j].astype(F32)
        key = total[:, :HEAD]
        d_qkv_all[rows_at(pair[j]), pl.ds(QCOLS, HEAD)] = (
            key * cosines[j] - turn(key) * sines[j]
        ).astype(BF)
        d_qkv_all[rows_at(pair[j]), pl.ds(QCOLS + HEAD, HEAD)] = total[:, HEAD:].astype(BF)
    gather_qkv = GatherCol(d_qkv_all)
    gather_qkv.start()

    held[3].wait()
    part_out[...] = dot(d_qkv_all[rows_at(block_of(1 - at.row, at.col)), :], qw[...], 1, 1).astype(BF)
    part = net.send(part_out, part_in, at.N1)
    d_normed = dot(d_qkv_all[rows_at(at.block), :], qw[...], 1, 1)
    net.take(part, part_in)
    d_normed = d_normed + part_in[...].astype(F32)
    values = xs_ref[...].astype(F32)
    scale = rms(values)
    unit = values * scale
    sums_ref[0:1, :] = jnp.sum(d_normed * unit, axis=0, keepdims=True)
    bent = d_normed * gain1
    total = d_mid[...] + scale * (bent - unit * jnp.mean(bent * unit, axis=1, keepdims=True))
    gi_out[...] = total.astype(BF)
    sums_in[at.row * 4 + at.col] = sums_ref[:, cols_at(at.col)]
    sums_keys = [
        net.send(sums_ref.at[:, cols_at(col)], sums_in.at[at.row * 4 + at.col], device)
        for device, row, col in others
    ]
    half_rows = pl.ds(pl.multiple_of((at.block - 4 * at.row) * BLOCK, BLOCK), BLOCK)
    gi_keys = [
        net.send(gi_out.at[:, cols_at(col)], gi_in.at[half_rows, :], device)
        for device, col in peers
    ]
    gi_in[half_rows, :] = gi_out[:, cols_at(at.col)]
    for item in last:
        item.middle()
    gather_qkv.middle()
    gather_qkv.end()
    grad_qkv[...] = dot(n1c[...], d_qkv_all[...], 0, 0).astype(BF)
    ones = jnp.ones((8, SEQ), BF)
    small_ref[:, FEAT:] = dot(ones, d_qkv_all[...])
    for key, (_, row, col) in zip(sums_keys, others, strict=True):
        net.take(key, sums_in.at[row * 4 + col])
    total = sums_in[0]
    for i in range(1, 8):
        total = total + sums_in[i]
    small_ref[:, :FEAT] = total
    for key, (_, col) in zip(gi_keys, peers, strict=True):
        offset = block_of(at.row, col) - 4 * at.row
        net.take(key, gi_in.at[pl.ds(pl.multiple_of(offset * BLOCK, BLOCK), BLOCK), :])
    for item in last:
        item.end()
    grad_in[...] = gi_in[...].astype(F32)
    net.finish()


def run_backward(*args):
    def out(shape, dtype):
        return jax.ShapeDtypeStruct(shape, dtype)

    outs = (
        out((SEQ // 2, FEAT), F32),
        out((QCOLS, FEAT), BF),
        out((FEAT, QKV), BF),
        out((8, FEAT + QKV), F32),
        out((4, 48, PART), BF),
        out((80, MODEL), BF),
    )
    return pl.pallas_call(
        backward_kernel,
        out_shape=outs,
        in_specs=[vmem()] * (len(args) - 4) + [anywhere()] * 4,
        out_specs=[vmem()] * len(outs),
        scratch_shapes=[
            pltpu.VMEM((8, MODEL), F32),
            pltpu.VMEM((8, 8, FEAT), F32),
            pltpu.VMEM((SEQ, QCOLS), BF),
            pltpu.VMEM((SEQ, FEAT), BF),
            pltpu.VMEM((2, BLOCK, MODEL), BF),
            pltpu.VMEM((BLOCK, MODEL), F32),
            pltpu.VMEM((2 * BLOCK, QCOLS), BF),
            pltpu.VMEM((2 * BLOCK, QCOLS), F32),
            pltpu.VMEM((SEQ, 2 * HEAD), F32),
            pltpu.VMEM((SEQ, 2 * HEAD), BF),
            pltpu.VMEM((3, 2, BLOCK, 2 * HEAD), BF),
            pltpu.VMEM((SEQ, QKV), BF),
            pltpu.VMEM((BLOCK, MODEL), BF),
            pltpu.VMEM((BLOCK, MODEL), BF),
            pltpu.VMEM((BLOCK, MODEL), BF),
            pltpu.VMEM((SEQ // 2, FEAT), BF),
            pltpu.VMEM((QCOLS, MODEL), BF),
            pltpu.VMEM((MODEL, QKV), BF),
            pltpu.VMEM((2, 4, 2, 4, 48, PART), BF),
            pltpu.VMEM((2, 2, 288, MODEL), BF),
        ]
        + ring_scratch(FFN_FIRST, FFN_LAST)
        + [pltpu.SemaphoreType.DMA((80,)), pltpu.SemaphoreType.DMA((80,))]
        + [pltpu.SemaphoreType.DMA((4,))],
        compiler_params=pltpu.CompilerParams(
            collective_id=2, has_side_effects=True, vmem_limit_bytes=VMEM_LIMIT
        ),
        cost_estimate=pl.CostEstimate(
            flops=10 * 10**9, bytes_accessed=40 * 10**6, transcendentals=2 * 10**6
        ),
        name="attention_backward",
    )(*args)


def sums_kernel(
    gu_own,
    down_own,
    qkv,
    out,
    small_ref,
    mid_ref,
    hidden_far,
    dw_far,
    all_gu,
    all_down,
    all_qkv,
    all_out,
    small_out,
    out_ref,
    small_y,
    small_z,
    hidden,
    dw,
    ffn,
    *rest,
):
    red, bufs, (send_sems, recv_sems, local_sems) = rest[:7], rest[7:-3], rest[-3:]
    at = Place()
    net = Net(send_sems, recv_sems, at)
    held = [
        pltpu.make_async_copy(hidden_far, hidden, local_sems.at[2]),
        pltpu.make_async_copy(dw_far, dw, local_sems.at[3]),
    ]
    for copy in held:
        copy.start()
    at.meet(
        (at.S, at.O, at.OS, at.N1, at.N2, at.YP, at.YM, at.ZP, at.ZM, at.Y2, at.Z2)
    )
    outs = Reduce8(net, at, *red)

    def project(j):
        row, hi = at.chips[j]
        rows = pl.ds(aligned(row, SEQ // 2), SEQ // 2)
        lanes = pl.ds(aligned(hi, QCOLS), QCOLS)
        ffn[...] = dot(hidden[rows, :], dw[:, lanes])
        if j in (0, 3):
            mine = pl.ds(pl.multiple_of((at.block - 4 * at.row) * BLOCK, BLOCK), BLOCK)
            ffn[mine, :] += mid_ref[:, lanes]
        own = ffn[:, pl.ds(aligned(at.core, FEAT), FEAT)].astype(BF)
        outs.put(j, own, ffn[:, pl.ds(aligned(1 - at.core, FEAT), FEAT)].astype(BF))
        if j:
            outs.step(j - 1)

    z, y = at.z, at.y

    def gu_piece(k, lanes):
        rows = pl.ds(pl.multiple_of((k % 8) * 48, 16), 48)
        return all_gu.at[k // 8, rows, lanes]

    def part_lanes(col):
        return pl.ds(aligned(col, PART), PART)

    def down_slot(col):
        return all_down.at[col, pl.ds(pl.multiple_of(at.dp * 80, 16), 80), :]

    def feat_lanes(col):
        return pl.ds(aligned(col, FEAT), FEAT)

    def qkv_piece(k):
        rows = pl.ds(pl.multiple_of((k % 8) * 48, 16), 48)
        return all_qkv.at[rows, pl.ds(pl.multiple_of((k // 8) * 512, 512), 512)]

    def out_piece(k):
        return all_out.at[pl.ds(pl.multiple_of(k * 48, 16), 48), :]

    peers = ((at.O, at.far), (at.OS, at.sibfar), (at.S, at.sib))
    keys = []
    for device, col in peers:
        keys.append(
            (
                net.send(gu_own.at[col], gu_piece(at.dp, part_lanes(at.col)), device),
                net.send(down_own.at[:, feat_lanes(col)], down_slot(at.col), device),
            )
        )
    small_y[y] = small_ref[...]
    small_keys = [net.send(small_ref, small_y.at[y], d) for d in (at.YP, at.YM, at.Y2)]
    first, last = small_items(net, at, qkv, out, qkv_piece(at.dp), out_piece(at.dp), bufs)
    begin(first)
    own_copies = [
        pltpu.make_async_copy(
            gu_own.at[at.col], gu_piece(at.dp, part_lanes(at.col)), local_sems.at[0]
        ),
        pltpu.make_async_copy(
            down_own.at[:, feat_lanes(at.col)], down_slot(at.col), local_sems.at[1]
        ),
    ]
    for copy in own_copies:
        copy.start()

    def take_from(i):
        net.take(keys[i][0], gu_piece(at.dp, part_lanes(peers[i][1])))
        net.take(keys[i][1], down_slot(peers[i][1]))

    def chip_ready():
        for copy in own_copies:
            copy.wait()
        take_from(2)

    def far_ready():
        take_from(0)
        take_from(1)

    def half_of(hi):
        def half(zz, yy):
            k = zz * 4 + yy
            rows = pl.ds(pl.multiple_of(k * 80, 16), 80)
            return [
                gu_piece(k, pl.ds(aligned(hi, 2 * PART), 2 * PART)),
                all_down.at[pl.ds(2 * hi, 2), rows, :],
            ]

        return half

    ring = ring_dp(
        net, at, (half_of(at.hi), half_of(1 - at.hi)), (chip_ready, far_ready)
    )
    next(ring)
    for copy in held:
        copy.wait()
    project(0)
    for item in first:
        item.middle()
    for key, k in zip(small_keys, (y - 1, y + 1, y + 2), strict=True):
        net.take(key, small_y.at[lax.rem(k + 4, 4)])
    small_z[z] = (small_y[0] + small_y[1]) + (small_y[2] + small_y[3])
    small_keys = [net.send(small_z.at[z], small_z.at[z], d) for d in (at.ZP, at.ZM, at.Z2)]
    next(ring)
    project(1)
    for item in first:
        item.end()
    begin(last)
    next(ring)
    project(2)
    for item in last:
        item.middle()
    for key, k in zip(small_keys, (z - 1, z + 1, z + 2), strict=True):
        net.take(key, small_z.at[lax.rem(k + 4, 4)])
    small_out[...] = (small_z[0] + small_z[1]) + (small_z[2] + small_z[3])
    next(ring)
    project(3)
    for item in last:
        item.end()
    after = ring_dp(
        net,
        at,
        (lambda zz, yy: [qkv_piece(zz * 4 + yy)], lambda zz, yy: [out_piece(zz * 4 + yy)]),
    )
    next(after)
    for _ in ring:
        next(after, None)
    drain(after)
    out_ref[...] = outs.step(3)
    net.finish()


def run_sums(gu, down, qkv, out, small, mid, hidden, dw):
    def shape(dims, dtype):
        return jax.ShapeDtypeStruct(dims, dtype)

    outs = (
        shape((2, FEAT, 4 * PART), BF),
        shape((4, 1280, FEAT), BF),
        shape((FEAT, QKV), BF),
        shape((QCOLS, FEAT), BF),
        shape(small.shape, F32),
        shape((SEQ // 2, FEAT), F32),
    )
    return pl.pallas_call(
        sums_kernel,
        out_shape=outs,
        in_specs=[vmem()] * 6 + [anywhere()] * 2,
        out_specs=[anywhere()] * 2 + [vmem()] * 4,
        scratch_shapes=[pltpu.VMEM((4,) + small.shape, F32)] * 2
        + [
            pltpu.VMEM((SEQ, PART), BF),
            pltpu.VMEM((PART, MODEL), BF),
            pltpu.VMEM((SEQ // 2, QCOLS), F32),
        ]
        + reduce8_scratch(SEQ // 2, FEAT)
        + ring_scratch(SMALL_FIRST, SMALL_LAST)
        + [pltpu.SemaphoreType.DMA((128,)), pltpu.SemaphoreType.DMA((128,))]
        + [pltpu.SemaphoreType.DMA((4,))],
        compiler_params=pltpu.CompilerParams(
            collective_id=3, has_side_effects=True, vmem_limit_bytes=VMEM_LIMIT
        ),
        cost_estimate=pl.CostEstimate(
            flops=4 * 10**9, bytes_accessed=60 * 10**6, transcendentals=0
        ),
        name="sums_over_sequences",
    )(gu, down, qkv, out, small, mid, hidden, dw)


def widen_kernel(
    gu,
    down,
    qkv,
    out,
    small,
    gate_out,
    up_out,
    down_out,
    query_out,
    key_out,
    value_out,
    proj_out,
    gain1_out,
    gain2_out,
    bq_out,
    bk_out,
    bv_out,
    gu_in,
    down_in,
    gate_buf,
    up_buf,
    down_buf,
    in_sems,
    out_sems,
):
    skip = 3 * PART

    def loads(n):
        place = n % 2
        rows = pl.ds(640 * (n % 2), 640)
        return [
            pltpu.make_async_copy(gu.at[:, pl.ds(n * 48, 48), :], gu_in.at[place], in_sems.at[place, 0]),
            pltpu.make_async_copy(down.at[n // 2, rows, :], down_in.at[place], in_sems.at[place, 1]),
        ]

    def stores(n):
        place, quarter, part = n % 2, n // 2, n % 2
        rows = pl.ds(n * 48, 48)
        drop = HEAD if quarter == 3 and part == 0 else 0
        start = PART * quarter + 576 * part - (HEAD if quarter == 3 and part == 1 else 0)
        return [
            pltpu.make_async_copy(gate_buf.at[place], gate_out.at[rows, :], out_sems.at[place, 0]),
            pltpu.make_async_copy(up_buf.at[place], up_out.at[rows, :], out_sems.at[place, 1]),
            pltpu.make_async_copy(
                down_buf.at[place, pl.ds(drop, 576 - drop), :],
                down_out.at[pl.ds(start, 576 - drop), :],
                out_sems.at[place, 2],
            ),
        ]

    def run(copies):
        for copy in copies:
            copy.start()
        return copies

    def wait(copies):
        for copy in copies:
            copy.wait()

    arriving = {0: run(loads(0)), 1: run(loads(1))}
    query_out[...] = qkv[:, :QCOLS].astype(F32)
    key_out[...] = qkv[:, QCOLS : QCOLS + HEAD].astype(F32)
    value_out[...] = qkv[:, QCOLS + HEAD :].astype(F32)
    proj_out[...] = out[...].astype(F32)
    first = 0
    for ref, row, width in (
        (gain1_out, 0, FEAT),
        (bq_out, 0, QCOLS),
        (bk_out, 0, HEAD),
        (bv_out, 0, HEAD),
    ):
        ref[...] = small[row : row + 1, first : first + width]
        first += width
    gain2_out[...] = small[1:2, :FEAT]
    leaving = {}
    for n in range(8):
        place = n % 2
        wait(arriving[n])
        if n > 1:
            wait(leaving[n - 2])
        for i, buf in enumerate((gate_buf, up_buf)):
            buf[place, :, :skip] = gu_in[place, i, :, :skip].astype(F32)
            buf[place, :, skip:] = gu_in[place, i, :, skip + HEAD :].astype(F32)
        for m in range(4):
            down_buf[place, pl.ds(144 * m, 80), :] = down_in[
                place, pl.ds(160 * m, 80), :
            ].astype(F32)
            down_buf[place, pl.ds(144 * m + 80, 64), :] = down_in[
                place, pl.ds(160 * m + 96, 64), :
            ].astype(F32)
        leaving[n] = run(stores(n))
        if n + 2 < 8:
            arriving[n + 2] = run(loads(n + 2))
    wait(leaving[6])
    wait(leaving[7])


def run_widen(gu, down, qkv, out, small):
    shapes = [(FEAT, UNITS)] * 2 + [(UNITS, FEAT)]
    shapes += [(FEAT, QCOLS), (FEAT, HEAD), (FEAT, HEAD), (QCOLS, FEAT)]
    shapes += [(1, FEAT), (1, FEAT), (1, QCOLS), (1, HEAD), (1, HEAD)]
    return pl.pallas_call(
        widen_kernel,
        out_shape=[jax.ShapeDtypeStruct(dims, F32) for dims in shapes],
        in_specs=[anywhere()] * 2 + [vmem()] * 3,
        out_specs=[anywhere()] * 3 + [vmem()] * 9,
        scratch_shapes=[
            pltpu.VMEM((2, 2, 48, 4 * PART), BF),
            pltpu.VMEM((2, 640, FEAT), BF),
            pltpu.VMEM((2, 48, UNITS), F32),
            pltpu.VMEM((2, 48, UNITS), F32),
            pltpu.VMEM((2, 576, FEAT), F32),
            pltpu.SemaphoreType.DMA((2, 2)),
            pltpu.SemaphoreType.DMA((2, 3)),
        ],
        compiler_params=pltpu.CompilerParams(vmem_limit_bytes=VMEM_LIMIT),
        cost_estimate=pl.CostEstimate(
            flops=10**7, bytes_accessed=36 * 10**6, transcendentals=0
        ),
        name="widen",
    )(gu, down, qkv, out, small)


def rope_tables(count):
    places = np.arange(count, dtype=np.float32)
    inverse = (1.0 / THETA ** (np.arange(0, HEAD, 2) / HEAD)).astype(np.float32)
    angles = places[:, None] * inverse[None, :]
    cosine, sine = np.cos(angles), np.sin(angles)
    tables = np.concatenate([cosine, cosine], axis=-1), np.concatenate([-sine, sine], axis=-1)
    return tuple(jnp.asarray(table, F32) for table in tables)


def body(
    layer_input,
    gain_attn,
    w_query,
    w_key,
    w_value,
    b_query,
    b_key,
    b_value,
    w_out,
    gain_ffn,
    w_gate,
    w_up,
    w_down,
    out_grad,
):
    cosine, sine = rope_tables(SEQ)
    bias = jnp.concatenate([b_query, b_key, b_value]).astype(F32)[None]
    gains = jnp.zeros((8, FEAT), F32).at[0].set(gain_attn.astype(F32)).at[1].set(gain_ffn.astype(F32))
    (
        xs,
        normed1_cols,
        grads_block,
        qkv_w,
        out_w,
        queries,
        key,
        value,
        lse,
        attn,
        mid,
        gains_all,
        dn2,
        hidden,
        down_w,
        grad_gu,
        grad_down,
    ) = run_forward(
        layer_input,
        out_grad,
        w_query,
        w_key,
        w_value,
        w_out,
        w_gate,
        w_up,
        w_down,
        gains,
        bias,
        cosine,
        sine,
    )
    grad_input, grad_out, grad_qkv, small, grad_gu, grad_down = run_backward(
        dn2,
        mid,
        grads_block,
        gains_all,
        xs,
        normed1_cols,
        attn,
        queries,
        key,
        value,
        lse,
        cosine,
        sine,
        out_w,
        qkv_w,
        grad_gu.reshape(2, 4, 2, 4, 48, PART),
        grad_down.reshape(2, 2, 288, MODEL),
    )
    grad_gu, grad_down, grad_qkv, grad_out, small, layer_output = run_sums(
        grad_gu,
        grad_down,
        grad_qkv.reshape(2, 4, 48, QKV),
        grad_out.reshape(2, 2, 4, 48, FEAT),
        small,
        mid,
        hidden,
        down_w,
    )
    (
        grad_gate,
        grad_up,
        grad_down,
        grad_query,
        grad_key,
        grad_value,
        grad_out,
        *vectors,
    ) = run_widen(grad_gu, grad_down, grad_qkv, grad_out, small)
    gain1, gain2, bias_query, bias_key, bias_value = (vector[0] for vector in vectors)
    return (
        layer_output,
        grad_input,
        gain1,
        grad_query,
        grad_key,
        grad_value,
        bias_query,
        bias_key,
        bias_value,
        grad_out,
        gain2,
        grad_gate,
        grad_up,
        grad_down,
    )


def solution(mesh):
    in_specs = (
        P(("dp", "row"), "col"),
        P("col"),
        P("col", "row"),
        P("col", "row"),
        P("col", "row"),
        P("row"),
        P("row"),
        P("row"),
        P("row", "col"),
        P("col"),
        P("col", "row"),
        P("col", "row"),
        P("row", "col"),
        P(("dp", "row"), "col"),
    )
    out_specs = (
        P(("dp", "row"), "col"),
        P(("dp", "row"), "col"),
        P("col"),
        P("col", "row"),
        P("col", "row"),
        P("col", "row"),
        P("row"),
        P("row"),
        P("row"),
        P("row", "col"),
        P("col"),
        P("col", "row"),
        P("col", "row"),
        P("row", "col"),
    )
    return jax.shard_map(body, mesh=mesh, in_specs=in_specs, out_specs=out_specs, check_vma=False)
```

```python
import functools

import jax
import jax.numpy as jnp
import numpy as np
from jax import lax
from jax.experimental import pallas as pl
from jax.experimental.pallas import tpu as pltpu
from jax.sharding import PartitionSpec as P

EPS = 1e-06
THETA = 1000000.0
NEG = -1e30
BF = jnp.bfloat16
F32 = jnp.float32
MESH = pl.DeviceIdType.MESH
HEAD = 128
HEADS = 6
SEQ = 1024
MODEL = 1536
FEAT = 384
BLOCK = 128
UNITS = 4480
PART = 1152
QCOLS = 768
QKV = 1024
VMEM_LIMIT = 62 * 2**20
SCALE = HEAD ** (-0.5)


def dot(left, right, left_dim=1, right_dim=0):
    return lax.dot_general(
        left, right, (((left_dim,), (right_dim,)), ((), ())), preferred_element_type=F32
    )


def aligned(index, step):
    return pl.multiple_of(index * step, step)


def block_of(row, col):
    return col + row * (7 - 2 * col)


def quarter_start(col):
    return pl.multiple_of(col * PART - (col // 3) * HEAD, HEAD)


class Place:
    def __init__(self):
        self.dp, self.row, self.col = (lax.axis_index(a) for a in ("dp", "row", "col"))
        self.hi, self.core = self.col // 2, self.col % 2
        self.z, self.y = self.dp // 4, self.dp % 4
        self.sib = 2 * self.hi + 1 - self.core
        self.far = 2 * (1 - self.hi) + self.core
        self.sibfar = 2 * (1 - self.hi) + 1 - self.core
        self.block = block_of(self.row, self.col)
        self.chips = (
            (self.row, 1 - self.hi),
            (1 - self.row, self.hi),
            (1 - self.row, 1 - self.hi),
            (self.row, self.hi),
        )
        self.S = {"col": self.sib}
        self.O = {"col": self.far}
        self.OS = {"col": self.sibfar}
        self.N1 = {"row": 1 - self.row}
        self.N2 = {"row": 1 - self.row, "col": self.far}
        self.N1S = {"row": 1 - self.row, "col": self.sib}
        self.N2S = {"row": 1 - self.row, "col": self.sibfar}

        def dp_at(z, y):
            return {"dp": lax.rem(z + 4, 4) * 4 + lax.rem(y + 4, 4)}

        self.YP, self.YM = dp_at(self.z, self.y + 1), dp_at(self.z, self.y - 1)
        self.Y2, self.Z2 = dp_at(self.z, self.y + 2), dp_at(self.z + 2, self.y)
        self.ZP, self.ZM = dp_at(self.z + 1, self.y), dp_at(self.z - 1, self.y)

    def meet(self, partners):
        barrier = pltpu.get_barrier_semaphore()
        for device in partners:
            pl.semaphore_signal(barrier, inc=1, device_id=device, device_id_type=MESH)
        pl.semaphore_wait(barrier, len(partners))


class Net:
    def __init__(self, send_sems, recv_sems, at):
        self.ss, self.rs, self.at, self.count, self.sent = send_sems, recv_sems, at, 0, []

    def key(self):
        self.count += 1
        return self.count - 1

    def copy(self, key, src, dst, device):
        return pltpu.make_async_remote_copy(
            src_ref=src,
            dst_ref=dst,
            send_sem=self.ss.at[key],
            recv_sem=self.rs.at[key],
            device_id=device,
            device_id_type=MESH,
        )

    def send(self, src, dst, device):
        key = self.key()
        copy = self.copy(key, src, dst, device)
        copy.start()
        self.sent.append(copy)
        return key

    def take(self, key, dst):
        self.copy(key, dst, dst, self.at.S).wait_recv()

    def finish(self, copies=None):
        copies = list(self.sent) if copies is None else copies
        for copy in copies:
            copy.wait_send()
            self.sent.remove(copy)


class Gather8:
    def __init__(self, net, at, place):
        self.net, self.at, self.place = net, at, place

    def start(self, src):
        net, at = self.net, self.at
        mine = self.place(at.row, at.col, None)
        self.k1 = net.send(src, mine, at.N1)
        self.k2 = net.send(src, mine, at.N2)
        self.k0 = net.send(src, mine, at.S)

    def middle(self):
        net, at, place = self.net, self.at, self.place
        near, away = place(1 - at.row, at.col, None), place(1 - at.row, at.far, None)
        first, last = place(1 - at.row, at.col, 0), place(1 - at.row, at.far, 1)
        net.take(self.k1, near)
        self.ka = net.send(first, first, at.N2)
        self.f1 = net.send(near, near, at.S)
        net.take(self.k2, away)
        self.kb = net.send(last, last, at.N1)
        self.f2 = net.send(away, away, at.S)

    def late(self):
        net, at, place = self.net, self.at, self.place
        first, last = place(at.row, at.far, 0), place(at.row, at.far, 1)
        net.take(self.ka, first)
        self.f3 = net.send(first, first, at.S)
        net.take(self.kb, last)
        self.f4 = net.send(last, last, at.S)

    def end(self, chip=None):
        net, at, place = self.net, self.at, self.place
        if chip in (None, 3):
            net.take(self.k0, place(at.row, at.sib, None))
        if chip in (None, 1):
            net.take(self.f1, place(1 - at.row, at.sib, None))
        if chip in (None, 2):
            net.take(self.f2, place(1 - at.row, at.sibfar, None))
        if chip in (None, 0):
            net.take(self.f3, place(at.row, at.sibfar, 0))
            net.take(self.f4, place(at.row, at.sibfar, 1))


def ring_dp(net, at, halves, ready=(None, None)):
    def wrap(index):
        return lax.rem(index + 4, 4)

    sides = (((at.YP, at.YM), (at.ZP, at.ZM)), ((at.ZP, at.ZM), (at.YP, at.YM)))
    firsts, seconds = (at.y, at.z), (at.z, at.y)

    def refs(i, a, b):
        return halves[i](b, a) if i == 0 else halves[i](a, b)

    def send(i, a, b, device):
        return [net.send(ref, ref, device) for ref in refs(i, a, b)]

    def take(i, a, b, keys):
        for key, ref in zip(keys, refs(i, a, b), strict=True):
            net.take(key, ref)

    one, two, onward = {}, {}, {}
    for i in (0, 1):
        if ready[i]:
            ready[i]()
        one[i] = [send(i, firsts[i], seconds[i], side) for side in sides[i][0]]
        if ready[i]:
            two[i, 0] = [send(i, firsts[i], seconds[i], side) for side in sides[i][1]]
    for i in (0, 1):
        if not ready[i]:
            two[i, 0] = [send(i, firsts[i], seconds[i], side) for side in sides[i][1]]
    yield
    for i in (0, 1):
        minus = wrap(firsts[i] - 1)
        take(i, minus, seconds[i], one[i][0])
        one[i].append(send(i, minus, seconds[i], sides[i][0][0]))
        two[i, 1] = [send(i, minus, seconds[i], side) for side in sides[i][1]]
    yield
    for i in (0, 1):
        plus = wrap(firsts[i] + 1)
        take(i, plus, seconds[i], one[i][1])
        two[i, 2] = [send(i, plus, seconds[i], side) for side in sides[i][1]]
    offsets = (0, -1, 1, 2)
    for q in (0, 1, 2, 3):
        yield
        for i in (0, 1):
            if q == 1:
                across = wrap(firsts[i] + 2)
                take(i, across, seconds[i], one[i][2])
                two[i, 3] = [send(i, across, seconds[i], side) for side in sides[i][1]]
            slot = wrap(firsts[i] + offsets[q])
            minus, plus = wrap(seconds[i] - 1), wrap(seconds[i] + 1)
            take(i, slot, minus, two[i, q][0])
            if q < 2:
                onward[i, q] = send(i, slot, minus, sides[i][1][0])
            take(i, slot, plus, two[i, q][1])
            if q >= 2:
                onward[i, q] = send(i, slot, plus, sides[i][1][1])
    for q in (0, 1, 2, 3):
        yield
        for i in (0, 1):
            slot = wrap(firsts[i] + offsets[q])
            take(i, slot, wrap(seconds[i] + 2), onward[i, q])


def drain(steps):
    for _ in steps:
        pass


def rms(values):
    return lax.rsqrt(jnp.mean(values * values, axis=1, keepdims=True) + EPS)


def turn(values):
    return pltpu.roll(values, HEAD // 2, 1)


def causal(scores, start):
    places = start + lax.broadcasted_iota(jnp.int32, scores.shape, 0)
    keys = lax.broadcasted_iota(jnp.int32, scores.shape, 1)
    return jnp.where(keys <= places, scores, NEG)


def vmem():
    return pl.BlockSpec(memory_space=pltpu.VMEM)


def anywhere():
    return pl.BlockSpec(memory_space=pl.ANY)


class Reduce8:
    def __init__(self, net, at, own, other, sib_in, first_in, last_in, near_in, away_in):
        self.net, self.at, self.own, self.other, self.sib_in = net, at, own, other, sib_in
        self.first_in, self.last_in, self.near_in, self.away_in = first_in, last_in, near_in, away_in
        self.half = own.shape[1] // 2
        self.keys = {}

    def put(self, j, mine, theirs):
        self.own[j] = mine
        self.other[j] = theirs
        self.keys[j] = self.net.send(self.other.at[j], self.sib_in.at[j], self.at.S)

    def step(self, j):
        net, at, half = self.net, self.at, self.half
        net.take(self.keys[j], self.sib_in.at[j])
        total = self.own[j].astype(F32) + self.sib_in[j].astype(F32)
        if j == 0:
            self.own[j] = total.astype(BF)
            self.first = net.send(self.own.at[j, pl.ds(0, half)], self.first_in, at.N1)
            self.last = net.send(self.own.at[j, pl.ds(half, half)], self.last_in, at.N2)
        elif j == 1:
            net.take(self.last, self.last_in)
            self.own[j, :half] = total[:half].astype(BF)
            self.own[j, half:] = (total[half:] + self.last_in[...].astype(F32)).astype(BF)
            self.near = net.send(self.own.at[j], self.near_in, at.N1)
        elif j == 2:
            net.take(self.first, self.first_in)
            self.own[j, :half] = (total[:half] + self.first_in[...].astype(F32)).astype(BF)
            self.own[j, half:] = total[half:].astype(BF)
            self.away = net.send(self.own.at[j], self.away_in, at.N2)
        else:
            net.take(self.near, self.near_in)
            net.take(self.away, self.away_in)
            return total + self.near_in[...].astype(F32) + self.away_in[...].astype(F32)
        return None


def reduce8_scratch(rows, columns):
    return [
        pltpu.VMEM((4, rows, columns), BF),
        pltpu.VMEM((4, rows, columns), BF),
        pltpu.VMEM((4, rows, columns), BF),
        pltpu.VMEM((rows // 2, columns), BF),
        pltpu.VMEM((rows // 2, columns), BF),
        pltpu.VMEM((rows, columns), BF),
        pltpu.VMEM((rows, columns), BF),
    ]


def tiles_of(width, step):
    return [(first, min(step, width - first)) for first in range(0, width, step)]


def add_up(out, terms):
    lead = out.shape[:-2]
    if not lead:
        total = terms[0][...].astype(F32)
        for term in terms[1:]:
            total = total + term[...].astype(F32)
        out[...] = total.astype(out.dtype)
        return
    count = 1
    for size in lead:
        count *= size

    def step(i, carry):
        index = []
        for size in reversed(lead):
            index.insert(0, i % size)
            i = i // size
        index = tuple(index)
        total = terms[0].at[index][...].astype(F32)
        for term in terms[1:]:
            total = total + term.at[index][...].astype(F32)
        out.at[index][...] = total.astype(out.dtype)
        return carry

    lax.fori_loop(0, count, step, 0)


class RingItem:
    def __init__(self, net, sides, place, part, held, way, bufs, own):
        self.net, self.part, self.held, self.own = net, part, held, own
        self.relay, self.staged, self.from_last, self.from_next = bufs
        self.onward, self.back = (sides[0], sides[1]) if way == 0 else (sides[1], sides[0])
        step = 1 - 2 * way
        self.here, self.next, self.across, self.last = (
            lax.rem(place + 4 + step * i, 4) for i in (0, 1, 2, 3)
        )

    def start(self):
        self.k_relay = self.net.send(self.part(self.across), self.relay, self.onward)

    def direct(self):
        self.k_next = self.net.send(self.part(self.last), self.from_next, self.back)

    def middle(self):
        self.net.take(self.k_relay, self.relay)
        add_up(self.staged, [self.held(self.next), self.relay])
        self.k_last = self.net.send(self.staged, self.from_last, self.onward)

    def end(self):
        self.net.take(self.k_next, self.from_next)
        self.net.take(self.k_last, self.from_last)
        add_up(self.own, [self.held(self.here), self.from_next, self.from_last])


def begin(items):
    for item in items:
        item.start()
    for item in items:
        item.direct()


LEFT, RIGHT = pl.ds(0, QCOLS), pl.ds(QCOLS, QCOLS)
GU_FIRST = (((2, 2, 48, PART),), ((2, 2, 48, PART),))
GU_LAST = (((48, PART),) * 2,) * 2
DOWN_FIRST = (((2, 80, QCOLS),), ((144, QCOLS),))
DOWN_LAST = (((80, QCOLS),),) * 2
SMALL_FIRST = (((2, 48, 512),), ((2, 48, FEAT),))
SMALL_LAST = (((48, 512),), ((48, FEAT),))


def down_rows(k):
    return pl.ds(pl.multiple_of(72 * k - 8 * (k % 2), 16), 80)


def ring_scratch(first, last):
    scratch = []
    for i in (0, 1):
        for dims in first[i]:
            scratch += [pltpu.VMEM(dims, BF)] * 8
            scratch.append(pltpu.VMEM((2,) + dims, BF))
        for dims in last[i]:
            scratch += [pltpu.VMEM(dims, BF)] * 4
    return scratch


def ring_items(net, at, first, last, parts, helds, seconds, finals, bufs):
    sides = (((at.YP, at.YM), (at.ZP, at.ZM)), ((at.ZP, at.ZM), (at.YP, at.YM)))
    places = ((at.y, at.z), (at.z, at.y))
    bufs = list(bufs)
    one, two = ([], []), ([], [])
    for i in (0, 1):
        owns = []
        for n in range(len(first[i])):
            own = bufs[8]
            for way in (0, 1):
                part = functools.partial(lambda k, f, w: f(k, w), f=parts[i][n], w=way)
                held = functools.partial(lambda k, f, w: f(k, w), f=helds[i][n], w=way)
                four = bufs[4 * way : 4 * way + 4]
                one[i].append(
                    RingItem(net, sides[i][0], places[i][0], part, held, way, four, own.at[way])
                )
            owns.append(own)
            bufs = bufs[9:]
        for n in range(len(last[i])):
            part = functools.partial(lambda k, f, o: f(o, k), f=seconds[i][n], o=owns[min(n, len(owns) - 1)])
            two[i].append(
                RingItem(net, sides[i][1], places[i][1], part, part, n % 2, bufs[:4], finals[i][n])
            )
            bufs = bufs[4:]

    def mix(pair):
        return [item for items in zip(*pair, strict=True) for item in items]

    return mix(one), mix(two)


def gu_items(net, at, far_ref, near_ref, gu_own, bufs):
    def parts_of(gu):
        return (
            (lambda k, way: gu.at[way, pl.ds(0, 2), :, k],),
            (lambda k, way: gu.at[k // 2, pl.ds(2, 2), k % 2, pl.ds(2 * way, 2)],),
        )

    seconds = (
        (lambda own, k: own.at[k // 2, 0, k % 2], lambda own, k: own.at[k // 2, 1, k % 2]),
    ) * 2
    finals = ((gu_own.at[0], gu_own.at[1]), (gu_own.at[2], gu_own.at[3]))
    helds = parts_of(near_ref)
    return ring_items(net, at, GU_FIRST, GU_LAST, parts_of(far_ref), helds, seconds, finals, bufs)


def down_items(net, at, down, down_own, bufs):
    parts = (
        (lambda k, way: down.at[way, :, down_rows(k), LEFT],),
        (lambda k, way: down.at[k // 2, k % 2, pl.ds(144 * way, 144), RIGHT],),
    )
    seconds = (
        (lambda own, k: own.at[k // 2, k % 2],),
        (lambda own, k: own.at[k // 2, pl.ds(pl.multiple_of((k % 2) * 64, 64), 80)],),
    )
    finals = ((down_own.at[:, LEFT],), (down_own.at[:, RIGHT],))
    return ring_items(net, at, DOWN_FIRST, DOWN_LAST, parts, parts, seconds, finals, bufs)


def small_items(net, at, qkv, out, qkv_own, out_own, bufs):
    parts = (
        (lambda k, way: qkv.at[:, k, :, pl.ds(512 * way, 512)],),
        (lambda k, way: out.at[k // 2, k % 2, pl.ds(2 * way, 2)],),
    )
    seconds = ((lambda own, k: own.at[k // 2, k % 2],), (lambda own, k: own.at[k // 2, k % 2],))
    finals = ((qkv_own,), (out_own,))
    return ring_items(net, at, SMALL_FIRST, SMALL_LAST, parts, parts, seconds, finals, bufs)


def forward_kernel(
    x_ref,
    og_ref,
    wq_ref,
    wk_ref,
    wv_ref,
    wout_ref,
    wg_ref,
    wu_ref,
    wd_ref,
    gains_ref,
    bias_ref,
    cos_ref,
    sin_ref,
    xs_ref,
    n1c_ref,
    og_out,
    qw_out,
    ow_out,
    q_ref,
    k_ref,
    v_ref,
    lse_ref,
    attn_ref,
    mid_ref,
    gains_all,
    dn2_ref,
    hidden_out,
    dw_out,
    grad_gu,
    down_own,
    wqkv_ref,
    x_all,
    n1,
    og_all,
    n2_all,
    qw,
    ow,
    gw,
    uw,
    dw,
    part_out,
    part_in,
    d_up,
    tile_buf,
    down,
    *rest,
):
    red_a, bufs, sems = rest[:7], rest[7:-4], rest[-4:]
    send_sems, recv_sems, local_sems, tile_sems = sems
    at = Place()
    net = Net(send_sems, recv_sems, at)
    local, local_count = [], iter(range(32))

    def move(src, dst):
        copy = pltpu.make_async_copy(src, dst, local_sems.at[next(local_count)])
        copy.start()
        local.append(copy)
        return copy

    joined = [
        move(wq_ref, wqkv_ref.at[:, pl.ds(0, QCOLS)]),
        move(wk_ref, wqkv_ref.at[:, pl.ds(QCOLS, HEAD)]),
        move(wv_ref, wqkv_ref.at[:, pl.ds(QCOLS + HEAD, HEAD)]),
    ]
    at.meet((at.S, at.N1, at.N2, at.O, at.OS, at.YP, at.YM, at.ZP, at.ZM))
    for copy in joined:
        copy.wait()
    local.clear()

    def tokens_of(array):
        def place(row, col, part):
            if part is None:
                rows = pl.ds(aligned(row, SEQ // 2), SEQ // 2)
            else:
                rows = pl.ds(aligned(row * 2 + part, SEQ // 4), SEQ // 4)
            return array.at[rows, pl.ds(aligned(col, FEAT), FEAT)]

        return place

    mine, mine_far = aligned(at.col, FEAT), aligned(1 - at.hi, 2 * FEAT)
    move(x_ref, tokens_of(x_all)(at.row, at.col, None))
    move(wqkv_ref, qw.at[pl.ds(mine, FEAT), :])
    move(wout_ref, ow.at[:, pl.ds(mine, FEAT)])
    move(gains_ref, gains_all.at[:, pl.ds(mine, FEAT)])
    start = quarter_start(at.col)
    move(wg_ref.at[:, pl.ds(start, PART)], gw.at[pl.ds(mine, FEAT), :])
    move(wu_ref.at[:, pl.ds(start, PART)], uw.at[pl.ds(mine, FEAT), :])
    move(wd_ref.at[pl.ds(start, PART), :], dw.at[:, pl.ds(mine, FEAT)])
    move(og_ref, tokens_of(og_all)(at.row, at.col, None))

    eighth = at.dp % 8
    across = [net.key() for _ in range(5)]

    def slice_copies(core, first, last):
        device = {"col": 2 * (1 - at.hi) + core}
        rows = pl.ds(aligned(eighth, 48), 48)
        target = pl.ds(pl.multiple_of(mine + eighth * 48, 16), 48)
        columns = pl.ds(core * 512, 512)
        out_rows = pl.ds(pl.multiple_of(core * FEAT + eighth * 48, 16), 48)
        theirs = quarter_start(2 * (1 - at.hi) + core)
        down_rows = pl.ds(pl.multiple_of(theirs + eighth * 144, 16), 144)
        down_target = pl.ds(aligned(eighth, 144), 144)
        pairs = (
            (wqkv_ref.at[rows, columns], qw.at[target, columns]),
            (wout_ref.at[out_rows, :], ow.at[out_rows, pl.ds(mine, FEAT)]),
            (wg_ref.at[rows, pl.ds(theirs, PART)], gw.at[target, :]),
            (wu_ref.at[rows, pl.ds(theirs, PART)], uw.at[target, :]),
            (wd_ref.at[down_rows, :], dw.at[down_target, pl.ds(mine, FEAT)]),
        )
        return [
            pltpu.make_async_remote_copy(
                src_ref=pairs[i][0],
                dst_ref=pairs[i][1],
                send_sem=net.ss.at[spare[core][i]],
                recv_sem=net.rs.at[across[i]],
                device_id=device,
                device_id_type=MESH,
            )
            for i in range(first, last)
        ]

    spare = ([net.key() for _ in range(5)], [net.key() for _ in range(5)])
    chosen = at.core == at.dp // 8

    @pl.when(chosen)
    def _():
        for core in (0, 1):
            for copy in slice_copies(core, 0, 2):
                copy.start()

    gather_x = Gather8(net, at, tokens_of(x_all))
    gather_x.start(x_ref)
    gain_far = net.send(gains_ref, gains_all.at[:, pl.ds(mine, FEAT)], at.N2)
    gain_sib = net.send(gains_ref, gains_all.at[:, pl.ds(mine, FEAT)], at.S)
    near_qw = net.send(wqkv_ref, qw.at[pl.ds(mine, FEAT), :], at.S)
    near_ow = net.send(wout_ref, ow.at[:, pl.ds(mine, FEAT)], at.S)

    @pl.when(chosen)
    def _():
        for core in (0, 1):
            for copy in slice_copies(core, 2, 5):
                copy.start()

    far_half = pl.ds(mine_far, 2 * FEAT)

    def qkv_slices(z, y):
        rows = pl.ds(pl.multiple_of(mine_far + (z * 4 + y) * 48, 16), 48)
        return [qw.at[rows, pl.ds(aligned(at.core, 512), 512)]]

    def out_slices(z, y):
        index = z * 4 + y
        rows = pl.ds(pl.multiple_of(at.core * FEAT + (index % 8) * 48, 16), 48)
        return [ow.at[rows, pl.ds(pl.multiple_of(mine_far + (index // 8) * FEAT, HEAD), FEAT)]]

    def ffn_slices(weights, first, count):
        def slices(z, y):
            index = z * 4 + y
            rows = pl.ds(pl.multiple_of(mine_far + index * 48, 16), 48)
            down_rows = pl.ds(pl.multiple_of((index % 8) * 144 + first, 16), count)
            lanes = pl.ds(pl.multiple_of(mine_far + (index // 8) * FEAT, HEAD), FEAT)
            return [weights.at[rows, :], dw.at[down_rows, lanes]]

        return slices

    net.take(across[0], qkv_slices(at.z, at.y)[0])
    net.take(across[1], out_slices(at.z, at.y)[0])
    ring = ring_dp(net, at, (qkv_slices, out_slices))
    next(ring)
    next(ring)
    next(ring)
    gather_x.middle()
    gains_far = gains_all.at[:, pl.ds(aligned(at.far, FEAT), FEAT)]
    net.take(gain_far, gains_far)
    gain_sibfar = net.send(gains_far, gains_far, at.S)
    next(ring)
    cols_half, rows_half = pl.ds(aligned(at.core, 512), 512), pl.ds(aligned(at.core, FEAT), FEAT)
    gather_og = Gather8(net, at, tokens_of(og_all))
    gather_x.late()

    drain(ring)
    far_qw = net.send(qw.at[far_half, cols_half], qw.at[far_half, cols_half], at.S)
    far_ow = net.send(ow.at[rows_half, far_half], ow.at[rows_half, far_half], at.S)
    net.take(across[2], ffn_slices(gw, 0, 80)(at.z, at.y)[0])
    net.take(across[3], ffn_slices(uw, 80, 64)(at.z, at.y)[0])
    net.take(across[4], ffn_slices(uw, 0, 144)(at.z, at.y)[1])
    ring = ring_dp(net, at, (ffn_slices(gw, 0, 80), ffn_slices(uw, 80, 64)))
    next(ring)
    near = [
        net.send(wg_ref.at[:, pl.ds(quarter_start(at.sib), PART)], gw.at[pl.ds(mine, FEAT), :], at.S),
        net.send(wu_ref.at[:, pl.ds(quarter_start(at.sib), PART)], uw.at[pl.ds(mine, FEAT), :], at.S),
        net.send(wd_ref.at[pl.ds(quarter_start(at.sib), PART), :], dw.at[:, pl.ds(mine, FEAT)], at.S),
    ]
    gather_og.start(og_ref)
    gather_x.end()
    early = list(net.sent)
    net.take(gain_sib, gains_all.at[:, pl.ds(aligned(at.sib, FEAT), FEAT)])
    net.take(gain_sibfar, gains_all.at[:, pl.ds(aligned(at.sibfar, FEAT), FEAT)])
    for copy in local:
        copy.wait()
    local.clear()

    gain1, gain2 = gains_all[0:1, :], gains_all[1:2, :]

    def norm_block(i, carry):
        rows = pl.ds(aligned(i, BLOCK), BLOCK)
        values = x_all[rows, :].astype(F32)
        n1[rows, :] = (values * rms(values) * gain1).astype(BF)
        return carry

    lax.fori_loop(0, SEQ // BLOCK // 2, norm_block, 0)
    next(ring)
    lax.fori_loop(SEQ // BLOCK // 2, SEQ // BLOCK, norm_block, 0)
    next(ring)
    gather_og.middle()
    my_rows = pl.ds(aligned(at.block, BLOCK), BLOCK)
    xs_ref[...] = x_all[my_rows, :]
    n1c_ref[...] = n1[:, pl.ds(mine, FEAT)]
    net.take(near_qw, qw.at[pl.ds(aligned(at.sib, FEAT), FEAT), :])
    other_cols = pl.ds(aligned(1 - at.core, 512), 512)
    net.take(far_qw, qw.at[far_half, other_cols])
    move(qw, qw_out)

    def kv_block(i, carry):
        rows = pl.ds(aligned(i, 256), 256)
        both = dot(n1[rows, :], qw[:, QCOLS:]) + bias_ref[:, QCOLS:]
        key = both[:, :HEAD]
        k_ref[rows, :] = (key * cos_ref[rows, :] + turn(key) * sin_ref[rows, :]).astype(BF)
        v_ref[rows, :] = both[:, HEAD:].astype(BF)
        return carry

    lax.fori_loop(0, SEQ // 256, kv_block, 0)
    next(ring)
    pair = (at.col, 7 - at.col)
    for j in (0, 1):
        rows = pl.ds(aligned(pair[j], BLOCK), BLOCK)
        queries = dot(n1[rows, :], qw[:, :QCOLS]) + bias_ref[:, :QCOLS]
        cosine, sine = cos_ref[rows, :], sin_ref[rows, :]
        for h in range(HEADS):
            one = queries[:, h * HEAD : (h + 1) * HEAD]
            q_ref[pl.ds(j * BLOCK, BLOCK), pl.ds(h * HEAD, HEAD)] = (
                one * cosine + turn(one) * sine
            ).astype(BF)
    next(ring)
    gather_og.late()

    for j in (0, 1):
        keys = SEQ // 2 * (j + 1)
        rows = pl.ds(j * BLOCK, BLOCK)

        def attend(h, carry):
            lanes = pl.ds(aligned(h, HEAD), HEAD)
            scores = dot(q_ref[rows, lanes], k_ref[:keys, :], 1, 1) * SCALE
            scores = causal(scores, pair[j] * BLOCK)
            top = jnp.max(scores, axis=1, keepdims=True)
            weights = jnp.exp(scores - top)
            total = jnp.sum(weights, axis=1, keepdims=True)
            lse_ref[j * HEADS + h] = top + jnp.log(total)
            probs = (weights * (1.0 / total)).astype(BF)
            attn_ref[rows, lanes] = dot(probs, v_ref[:keys, :]).astype(BF)
            return carry

        lax.fori_loop(0, HEADS, attend, 0)
        next(ring)

    net.take(near_ow, ow.at[:, pl.ds(aligned(at.sib, FEAT), FEAT)])
    other_rows = pl.ds(aligned(1 - at.core, FEAT), FEAT)
    net.take(far_ow, ow.at[other_rows, far_half])
    move(ow, ow_out)
    part_out[...] = dot(attn_ref[pl.ds(aligned(1 - at.row, BLOCK), BLOCK), :], ow[...]).astype(BF)
    part = net.send(part_out, part_in, at.N1)
    own = dot(attn_ref[pl.ds(aligned(at.row, BLOCK), BLOCK), :], ow[...])
    net.take(part, part_in)
    mid = xs_ref[...].astype(F32) + own + part_in[...].astype(F32)
    mid_ref[...] = mid

    def place_n2(row, col, part):
        first = block_of(row, col) * BLOCK
        if part is None:
            return n2_all.at[pl.ds(pl.multiple_of(first, BLOCK), BLOCK), :]
        return n2_all.at[pl.ds(pl.multiple_of(first + part * 64, 64), 64), :]

    n2_all[my_rows, :] = (mid * rms(mid) * gain2).astype(BF)
    gather_n2 = Gather8(net, at, place_n2)
    gather_n2.start(place_n2(at.row, at.col, None))
    gather_og.end()
    move(og_all.at[my_rows, :], og_out)
    next(ring)
    gather_n2.middle()
    next(ring)
    next(ring)
    gather_n2.late()
    drain(ring)
    net.take(near[2], dw.at[:, pl.ds(aligned(at.sib, FEAT), FEAT)])

    def hidden_back(i, carry):
        rows = pl.ds(aligned(i, 256), 256)
        for first, width in tiles_of(PART, 512):
            lanes = pl.ds(first, width)
            d_up[rows, lanes] = dot(og_all[rows, :], dw[lanes, :], 1, 1).astype(BF)
        return carry

    lax.fori_loop(0, 4, hidden_back, 0)
    move(dw, dw_out)
    net.take(near[0], gw.at[pl.ds(aligned(at.sib, FEAT), FEAT), :])
    net.take(near[1], uw.at[pl.ds(aligned(at.sib, FEAT), FEAT), :])

    net.finish(early)
    hidden, d_gate = x_all.at[:, pl.ds(0, PART)], n1.at[:, pl.ds(0, PART)]
    norms = Reduce8(net, at, *red_a)
    chips = at.chips
    last_part = at.col == 3

    def tokens(j):
        row, hi = chips[j]
        first = 2 * hi + row * (6 - 4 * hi)
        return pl.ds(aligned(first, BLOCK), 256), at.core + row * (1 - 2 * at.core)

    for j in (3, 1, 2, 0):
        gather_n2.end(j)
        rows, _ = tokens(j)
        for first, width in tiles_of(PART, 512):
            lanes = pl.ds(first, width)
            gate = dot(n2_all[rows, :], gw[:, lanes])
            up = dot(n2_all[rows, :], uw[:, lanes])
            d_hidden = d_up[rows, lanes].astype(F32)
            sig = jax.nn.sigmoid(gate)
            act = gate * sig
            d_act = d_hidden * up * sig * (1.0 + gate * (1.0 - sig))
            values = [act * up, d_act, d_hidden * act]
            if first == 0:
                lane = lax.broadcasted_iota(jnp.int32, (1, width), 1)
                fresh = jnp.logical_or(lane >= HEAD, jnp.logical_not(last_part))
                values = [jnp.where(fresh, value, 0.0) for value in values]
            for ref, value in zip((hidden, d_gate, d_up), values, strict=True):
                ref[rows, lanes] = value.astype(BF)
    move(hidden, hidden_out)
    for first, width in tiles_of(MODEL, 256):
        lanes = pl.ds(first, width)
        tile = dot(hidden[...], og_all[:, lanes], 0, 0).astype(BF)
        for q in range(4):
            down[q // 2, q % 2, :, lanes] = tile[288 * q : 288 * (q + 1)]
    sums, last_sums = down_items(net, at, down, down_own, bufs)
    begin(sums)
    for j in range(4):
        rows, place = tokens(j)
        own_rows = pl.ds(pl.multiple_of(rows.start + place * BLOCK, BLOCK), BLOCK)
        other_rows = pl.ds(pl.multiple_of(rows.start + (1 - place) * BLOCK, BLOCK), BLOCK)
        parts = [
            (dot(d_gate[r, :], gw[...], 1, 1) + dot(d_up[r, :], uw[...], 1, 1)).astype(BF)
            for r in (other_rows, own_rows)
        ]
        norms.put(j, parts[1], parts[0])
        if j:
            norms.step(j - 1)

    writes = []

    def outer_sum(left, right, out):
        height = left.shape[1] // 2
        for first, width in tiles_of(right.shape[1], 256):
            place = len(writes) % 2
            if len(writes) > 1:
                writes[-2].wait()
            for i in (0, 1):
                rows = pl.ds(i * height, height)
                tile_buf[place, rows, :width] = dot(
                    left[:, rows], right[:, pl.ds(first, width)], 0, 0
                ).astype(BF)
            writes.append(
                pltpu.make_async_copy(
                    tile_buf.at[place, pl.ds(0, 2 * height), pl.ds(0, width)],
                    out.at[:, pl.ds(first, width)],
                    tile_sems.at[place],
                )
            )
            writes[-1].start()

    for item in sums:
        item.middle()
    outer_sum(n2_all, d_gate, grad_gu.at[0])
    dn2_ref[...] = norms.step(3)
    for item in sums:
        item.end()
    begin(last_sums)
    outer_sum(n2_all, d_up, grad_gu.at[1])
    for item in last_sums:
        item.middle()
    for item in last_sums:
        item.end()
    for copy in writes[-2:]:
        copy.wait()
    for copy in local:
        copy.wait()
    net.finish()

    @pl.when(chosen)
    def _():
        for core in (0, 1):
            for copy in slice_copies(core, 0, 5):
                copy.wait_send()


def run_forward(x, og, wq, wk, wv, wout, wg, wu, wd, gains, bias, cosine, sine):
    outs = (
        ((BLOCK, MODEL), BF, vmem),
        ((SEQ, FEAT), BF, vmem),
        ((BLOCK, MODEL), BF, anywhere),
        ((MODEL, QKV), BF, anywhere),
        ((QCOLS, MODEL), BF, anywhere),
        ((2 * BLOCK, QCOLS), BF, vmem),
        ((SEQ, HEAD), BF, vmem),
        ((SEQ, HEAD), BF, vmem),
        ((2 * HEADS, BLOCK, 1), F32, vmem),
        ((2 * BLOCK, QCOLS), BF, vmem),
        ((BLOCK, MODEL), F32, vmem),
        ((8, MODEL), F32, vmem),
        ((BLOCK, MODEL), F32, vmem),
        ((SEQ, PART), BF, anywhere),
        ((PART, MODEL), BF, anywhere),
        ((2, MODEL, PART), BF, anywhere),
        ((80, MODEL), BF, vmem),
    )
    return pl.pallas_call(
        forward_kernel,
        out_shape=[jax.ShapeDtypeStruct(dims, dtype) for dims, dtype, _ in outs],
        in_specs=[anywhere()] * 9 + [vmem()] * 4,
        out_specs=[place() for _, _, place in outs],
        scratch_shapes=[
            pltpu.VMEM((FEAT, QKV), BF),
            pltpu.VMEM((SEQ, MODEL), BF),
            pltpu.VMEM((SEQ, MODEL), BF),
            pltpu.VMEM((SEQ, MODEL), BF),
            pltpu.VMEM((SEQ, MODEL), BF),
            pltpu.VMEM((MODEL, QKV), BF),
            pltpu.VMEM((QCOLS, MODEL), BF),
            pltpu.VMEM((MODEL, PART), BF),
            pltpu.VMEM((MODEL, PART), BF),
            pltpu.VMEM((PART, MODEL), BF),
            pltpu.VMEM((BLOCK, MODEL), BF),
            pltpu.VMEM((BLOCK, MODEL), BF),
            pltpu.VMEM((SEQ, PART), BF),
            pltpu.VMEM((2, MODEL, 256), BF),
            pltpu.VMEM((2, 2, 288, MODEL), BF),
        ]
        + reduce8_scratch(BLOCK, MODEL)
        + ring_scratch(DOWN_FIRST, DOWN_LAST)
        + [
            pltpu.SemaphoreType.DMA((200,)),
            pltpu.SemaphoreType.DMA((200,)),
            pltpu.SemaphoreType.DMA((32,)),
            pltpu.SemaphoreType.DMA((2,)),
        ],
        compiler_params=pltpu.CompilerParams(
            collective_id=0, has_side_effects=True, vmem_limit_bytes=VMEM_LIMIT
        ),
        cost_estimate=pl.CostEstimate(
            flops=37 * 10**9, bytes_accessed=80 * 10**6, transcendentals=4 * 10**6
        ),
        name="forward_and_feed_forward",
    )(x, og, wq, wk, wv, wout, wg, wu, wd, gains, bias, cosine, sine)


def backward_kernel(
    dn2_ref,
    mid_ref,
    og_ref,
    gains_all,
    xs_ref,
    n1c,
    attn_ref,
    q_ref,
    k_ref,
    v_ref,
    lse_ref,
    cos_ref,
    sin_ref,
    ow_far,
    qw_far,
    gu_far,
    down_own,
    grad_in,
    grad_out,
    grad_qkv,
    small_ref,
    gu_own,
    all_down,
    sums_ref,
    sums_in,
    attn_all,
    mid_cols,
    mid_pair,
    d_mid,
    d_attn,
    d_q,
    d_kv,
    kv_out,
    kv_in,
    d_qkv_all,
    part_out,
    part_in,
    gi_out,
    gi_in,
    ow,
    qw,
    gu,
    *rest,
):
    bufs, (send_sems, recv_sems, local_sems) = rest[:-3], rest[-3:]
    at = Place()
    net = Net(send_sems, recv_sems, at)
    held = [
        pltpu.make_async_copy(src, dst, local_sems.at[i])
        for i, (src, dst) in enumerate(
            ((ow_far, ow), (gu_far, gu), (qw_far, qw))
        )
    ]
    for copy in held:
        copy.start()
    at.meet(
        (at.S, at.O, at.OS, at.N1, at.N2, at.N1S, at.N2S, at.YP, at.YM, at.ZP, at.ZM)
    )
    first, last = gu_items(net, at, gu_far, gu, gu_own, bufs)
    begin(first)

    def down_slot(k, cols):
        return all_down.at[cols, pl.ds(pl.multiple_of(k * 80, 16), 80), :]

    down_keys = [
        net.send(down_own.at[:, pl.ds(aligned(col, FEAT), FEAT)], down_slot(at.dp, at.col), device)
        for device, col in ((at.S, at.sib), (at.O, at.far), (at.OS, at.sibfar))
    ]
    down_mine = pltpu.make_async_copy(
        down_own.at[:, pl.ds(aligned(at.col, FEAT), FEAT)],
        down_slot(at.dp, at.col),
        local_sems.at[3],
    )
    down_mine.start()
    peers = ((at.S, at.sib), (at.O, at.far), (at.OS, at.sibfar))
    pair = (at.col, 7 - at.col)

    def rows_at(block):
        return pl.ds(aligned(block, BLOCK), BLOCK)

    def cols_at(col):
        return pl.ds(aligned(col, FEAT), FEAT)

    class GatherCol:
        def __init__(self, array):
            self.array = array

        def rows(self, col, j):
            return self.array.at[rows_at(col + j * (7 - 2 * col)), :]

        def start(self):
            self.far = [net.send(self.rows(at.col, j), self.rows(at.col, j), at.O) for j in (0, 1)]
            self.sib = [net.send(self.rows(at.col, j), self.rows(at.col, j), at.S) for j in (0, 1)]

        def middle(self):
            self.onward = []
            for j in (0, 1):
                net.take(self.far[j], self.rows(at.far, j))
                self.onward.append(net.send(self.rows(at.far, j), self.rows(at.far, j), at.S))

        def end(self):
            for j in (0, 1):
                net.take(self.sib[j], self.rows(at.sib, j))
                net.take(self.onward[j], self.rows(at.sibfar, j))

    gather_attn = GatherCol(attn_all)
    for j in (0, 1):
        attn_all[rows_at(pair[j]), :] = attn_ref[pl.ds(j * BLOCK, BLOCK), :]

    gain1, gain2 = gains_all[0:1, :], gains_all[1:2, :]
    mid = mid_ref[...]
    scale = rms(mid)
    unit = mid * scale
    d_normed = dn2_ref[...]
    sums_ref[...] = jnp.zeros_like(sums_ref)
    sums_ref[1:2, :] = jnp.sum(d_normed * unit, axis=0, keepdims=True)
    bent = d_normed * gain2
    d_mid[...] = og_ref[...].astype(F32) + scale * (
        bent - unit * jnp.mean(bent * unit, axis=1, keepdims=True)
    )
    mid_pair[at.row] = d_mid[...].astype(BF)
    to_pair = net.send(mid_pair.at[at.row], mid_pair.at[at.row], at.N1)
    mid_cols[rows_at(at.block), :] = d_mid[:, cols_at(at.col)].astype(BF)
    spread = []
    others = (
        (at.S, at.row, at.sib),
        (at.N1, 1 - at.row, at.col),
        (at.N1S, 1 - at.row, at.sib),
        (at.O, at.row, at.far),
        (at.OS, at.row, at.sibfar),
        (at.N2, 1 - at.row, at.far),
        (at.N2S, 1 - at.row, at.sibfar),
    )
    for device, row, col in others:
        spread.append(
            net.send(
                mid_pair.at[at.row, :, cols_at(col)], mid_cols.at[rows_at(at.block), :], device
            )
        )
    gather_attn.start()
    net.take(to_pair, mid_pair.at[1 - at.row])
    held[0].wait()
    for j in (0, 1):
        d_attn[pl.ds(j * BLOCK, BLOCK), :] = dot(mid_pair[j], ow[...], 1, 1).astype(BF)
    d_kv[...] = jnp.zeros_like(d_kv)
    held[1].wait()
    for item in first:
        item.middle()

    for j in (0, 1):
        keys = SEQ // 2 * (j + 1)
        rows = pl.ds(j * BLOCK, BLOCK)

        def back(h, carry):
            lanes = pl.ds(aligned(h, HEAD), HEAD)
            queries, d_out = q_ref[rows, lanes], d_attn[rows, lanes]
            scores = dot(queries, k_ref[:keys, :], 1, 1) * SCALE
            scores = causal(scores, pair[j] * BLOCK)
            probs = jnp.exp(scores - lse_ref[j * HEADS + h])
            d_probs = dot(d_out, v_ref[:keys, :], 1, 1)
            inner = jnp.sum(probs * d_probs, axis=1, keepdims=True)
            d_scores = (probs * (d_probs - inner) * SCALE).astype(BF)
            d_q[rows, lanes] = dot(d_scores, k_ref[:keys, :])
            d_kv[:keys, :HEAD] += dot(d_scores, queries, 0, 0)
            d_kv[:keys, HEAD:] += dot(probs.astype(BF), d_out, 0, 0)
            return carry

        lax.fori_loop(0, HEADS, back, 0)
    gather_attn.middle()

    kv_out[...] = d_kv[...].astype(BF)
    kv_keys = [
        [
            net.send(kv_out.at[rows_at(col + j * (7 - 2 * col)), :], kv_in.at[i, j], device)
            for j in (0, 1)
        ]
        for i, (device, col) in enumerate(peers)
    ]
    cosines = [cos_ref[rows_at(pair[j]), :] for j in (0, 1)]
    sines = [sin_ref[rows_at(pair[j]), :] for j in (0, 1)]
    for j in (0, 1):
        for h in range(HEADS):
            one = d_q[pl.ds(j * BLOCK, BLOCK), pl.ds(h * HEAD, HEAD)]
            d_qkv_all[rows_at(pair[j]), pl.ds(h * HEAD, HEAD)] = (
                one * cosines[j] - turn(one) * sines[j]
            ).astype(BF)
    for item in first:
        item.end()
    begin(last)
    down_mine.wait()
    for key, (_, col) in zip(down_keys, peers, strict=True):
        net.take(key, down_slot(at.dp, col))
    ring = ring_dp(
        net,
        at,
        (
            lambda zz, yy: [down_slot(zz * 4 + yy, pl.ds(2 * at.hi, 2))],
            lambda zz, yy: [down_slot(zz * 4 + yy, pl.ds(2 * (1 - at.hi), 2))],
        ),
    )
    next(ring)
    gather_attn.end()
    for key, (_, row, col) in zip(spread, others, strict=True):
        net.take(key, mid_cols.at[rows_at(block_of(row, col)), :])
    grad_out[...] = dot(attn_all[...], mid_cols[...], 0, 0).astype(BF)
    for j in (0, 1):
        total = d_kv[rows_at(pair[j]), :]
        for i in range(3):
            net.take(kv_keys[i][j], kv_in.at[i, j])
            total = total + kv_in[i, j].astype(F32)
        key = total[:, :HEAD]
        d_qkv_all[rows_at(pair[j]), pl.ds(QCOLS, HEAD)] = (
            key * cosines[j] - turn(key) * sines[j]
        ).astype(BF)
        d_qkv_all[rows_at(pair[j]), pl.ds(QCOLS + HEAD, HEAD)] = total[:, HEAD:].astype(BF)
    gather_qkv = GatherCol(d_qkv_all)
    gather_qkv.start()
    for item in last:
        item.middle()
    next(ring)

    held[2].wait()
    part_out[...] = dot(d_qkv_all[rows_at(block_of(1 - at.row, at.col)), :], qw[...], 1, 1).astype(BF)
    part = net.send(part_out, part_in, at.N1)
    d_normed = dot(d_qkv_all[rows_at(at.block), :], qw[...], 1, 1)
    net.take(part, part_in)
    d_normed = d_normed + part_in[...].astype(F32)
    values = xs_ref[...].astype(F32)
    scale = rms(values)
    unit = values * scale
    sums_ref[0:1, :] = jnp.sum(d_normed * unit, axis=0, keepdims=True)
    bent = d_normed * gain1
    total = d_mid[...] + scale * (bent - unit * jnp.mean(bent * unit, axis=1, keepdims=True))
    gi_out[...] = total.astype(BF)
    sums_in[at.row * 4 + at.col] = sums_ref[:, cols_at(at.col)]
    sums_keys = [
        net.send(sums_ref.at[:, cols_at(col)], sums_in.at[at.row * 4 + at.col], device)
        for device, row, col in others
    ]
    half_rows = pl.ds(pl.multiple_of((at.block - 4 * at.row) * BLOCK, BLOCK), BLOCK)
    gi_keys = [
        net.send(gi_out.at[:, cols_at(col)], gi_in.at[half_rows, :], device)
        for device, col in peers
    ]
    gi_in[half_rows, :] = gi_out[:, cols_at(at.col)]
    next(ring)
    next(ring)
    gather_qkv.middle()
    next(ring)
    gather_qkv.end()
    grad_qkv[...] = dot(n1c[...], d_qkv_all[...], 0, 0).astype(BF)
    ones = jnp.ones((8, SEQ), BF)
    small_ref[:, FEAT:] = dot(ones, d_qkv_all[...])
    for key, (_, row, col) in zip(sums_keys, others, strict=True):
        net.take(key, sums_in.at[row * 4 + col])
    total = sums_in[0]
    for i in range(1, 8):
        total = total + sums_in[i]
    small_ref[:, :FEAT] = total
    for key, (_, col) in zip(gi_keys, peers, strict=True):
        offset = block_of(at.row, col) - 4 * at.row
        net.take(key, gi_in.at[pl.ds(pl.multiple_of(offset * BLOCK, BLOCK), BLOCK), :])
    for item in last:
        item.end()
    drain(ring)
    grad_in[...] = gi_in[...].astype(F32)
    net.finish()


def run_backward(*args):
    def out(shape, dtype):
        return jax.ShapeDtypeStruct(shape, dtype)

    outs = (
        out((SEQ // 2, FEAT), F32),
        out((QCOLS, FEAT), BF),
        out((FEAT, QKV), BF),
        out((8, FEAT + QKV), F32),
        out((4, 48, PART), BF),
        out((4, 1280, FEAT), BF),
    )
    return pl.pallas_call(
        backward_kernel,
        out_shape=outs,
        in_specs=[vmem()] * (len(args) - 4) + [anywhere()] * 3 + [vmem()],
        out_specs=[vmem()] * (len(outs) - 1) + [anywhere()],
        scratch_shapes=[
            pltpu.VMEM((8, MODEL), F32),
            pltpu.VMEM((8, 8, FEAT), F32),
            pltpu.VMEM((SEQ, QCOLS), BF),
            pltpu.VMEM((SEQ, FEAT), BF),
            pltpu.VMEM((2, BLOCK, MODEL), BF),
            pltpu.VMEM((BLOCK, MODEL), F32),
            pltpu.VMEM((2 * BLOCK, QCOLS), BF),
            pltpu.VMEM((2 * BLOCK, QCOLS), F32),
            pltpu.VMEM((SEQ, 2 * HEAD), F32),
            pltpu.VMEM((SEQ, 2 * HEAD), BF),
            pltpu.VMEM((3, 2, BLOCK, 2 * HEAD), BF),
            pltpu.VMEM((SEQ, QKV), BF),
            pltpu.VMEM((BLOCK, MODEL), BF),
            pltpu.VMEM((BLOCK, MODEL), BF),
            pltpu.VMEM((BLOCK, MODEL), BF),
            pltpu.VMEM((SEQ // 2, FEAT), BF),
            pltpu.VMEM((QCOLS, MODEL), BF),
            pltpu.VMEM((MODEL, QKV), BF),
            pltpu.VMEM((2, 4, 2, 4, 48, PART), BF),
        ]
        + ring_scratch(GU_FIRST, GU_LAST)
        + [pltpu.SemaphoreType.DMA((110,)), pltpu.SemaphoreType.DMA((110,))]
        + [pltpu.SemaphoreType.DMA((4,))],
        compiler_params=pltpu.CompilerParams(
            collective_id=2, has_side_effects=True, vmem_limit_bytes=VMEM_LIMIT
        ),
        cost_estimate=pl.CostEstimate(
            flops=10 * 10**9, bytes_accessed=40 * 10**6, transcendentals=2 * 10**6
        ),
        name="attention_backward",
    )(*args)


def sums_kernel(
    gu_own,
    qkv,
    out,
    small_ref,
    mid_ref,
    hidden_far,
    dw_far,
    all_gu,
    all_qkv,
    all_out,
    small_out,
    out_ref,
    small_y,
    small_z,
    hidden,
    dw,
    ffn,
    *rest,
):
    red, bufs, (send_sems, recv_sems, local_sems) = rest[:7], rest[7:-3], rest[-3:]
    at = Place()
    net = Net(send_sems, recv_sems, at)
    held = [
        pltpu.make_async_copy(hidden_far, hidden, local_sems.at[2]),
        pltpu.make_async_copy(dw_far, dw, local_sems.at[3]),
    ]
    for copy in held:
        copy.start()
    at.meet(
        (at.S, at.O, at.OS, at.N1, at.N2, at.YP, at.YM, at.ZP, at.ZM, at.Y2, at.Z2)
    )
    outs = Reduce8(net, at, *red)

    def project(j):
        row, hi = at.chips[j]
        rows = pl.ds(aligned(row, SEQ // 2), SEQ // 2)
        lanes = pl.ds(aligned(hi, QCOLS), QCOLS)
        ffn[...] = dot(hidden[rows, :], dw[:, lanes])
        if j in (0, 3):
            mine = pl.ds(pl.multiple_of((at.block - 4 * at.row) * BLOCK, BLOCK), BLOCK)
            ffn[mine, :] += mid_ref[:, lanes]
        own = ffn[:, pl.ds(aligned(at.core, FEAT), FEAT)].astype(BF)
        outs.put(j, own, ffn[:, pl.ds(aligned(1 - at.core, FEAT), FEAT)].astype(BF))
        if j:
            outs.step(j - 1)

    z, y = at.z, at.y

    def gu_piece(k, lanes):
        rows = pl.ds(pl.multiple_of((k % 8) * 48, 16), 48)
        return all_gu.at[k // 8, rows, lanes]

    def part_lanes(col):
        return pl.ds(aligned(col, PART), PART)

    def qkv_piece(k):
        rows = pl.ds(pl.multiple_of((k % 8) * 48, 16), 48)
        return all_qkv.at[rows, pl.ds(pl.multiple_of((k // 8) * 512, 512), 512)]

    def out_piece(k):
        return all_out.at[pl.ds(pl.multiple_of(k * 48, 16), 48), :]

    peers = ((at.O, at.far), (at.OS, at.sibfar), (at.S, at.sib))
    keys = []
    for device, col in peers:
        keys.append(
            net.send(gu_own.at[col], gu_piece(at.dp, part_lanes(at.col)), device)
        )
    small_y[y] = small_ref[...]
    small_keys = [net.send(small_ref, small_y.at[y], d) for d in (at.YP, at.YM, at.Y2)]
    first, last = small_items(net, at, qkv, out, qkv_piece(at.dp), out_piece(at.dp), bufs)
    begin(first)
    own_copies = [
        pltpu.make_async_copy(
            gu_own.at[at.col], gu_piece(at.dp, part_lanes(at.col)), local_sems.at[0]
        ),
    ]
    for copy in own_copies:
        copy.start()

    def take_from(i):
        net.take(keys[i], gu_piece(at.dp, part_lanes(peers[i][1])))

    def chip_ready():
        for copy in own_copies:
            copy.wait()
        take_from(2)

    def far_ready():
        take_from(0)
        take_from(1)

    def half_of(hi):
        def half(zz, yy):
            k = zz * 4 + yy
            return [gu_piece(k, pl.ds(aligned(hi, 2 * PART), 2 * PART))]

        return half

    ring = ring_dp(
        net, at, (half_of(at.hi), half_of(1 - at.hi)), (chip_ready, far_ready)
    )
    next(ring)
    for copy in held:
        copy.wait()
    project(0)
    for item in first:
        item.middle()
    for key, k in zip(small_keys, (y - 1, y + 1, y + 2), strict=True):
        net.take(key, small_y.at[lax.rem(k + 4, 4)])
    small_z[z] = (small_y[0] + small_y[1]) + (small_y[2] + small_y[3])
    small_keys = [net.send(small_z.at[z], small_z.at[z], d) for d in (at.ZP, at.ZM, at.Z2)]
    next(ring)
    project(1)
    for item in first:
        item.end()
    begin(last)
    next(ring)
    project(2)
    for item in last:
        item.middle()
    for key, k in zip(small_keys, (z - 1, z + 1, z + 2), strict=True):
        net.take(key, small_z.at[lax.rem(k + 4, 4)])
    small_out[...] = (small_z[0] + small_z[1]) + (small_z[2] + small_z[3])
    next(ring)
    project(3)
    for item in last:
        item.end()
    after = ring_dp(
        net,
        at,
        (lambda zz, yy: [qkv_piece(zz * 4 + yy)], lambda zz, yy: [out_piece(zz * 4 + yy)]),
    )
    next(after)
    for _ in ring:
        next(after, None)
    drain(after)
    out_ref[...] = outs.step(3)
    net.finish()


def run_sums(gu, qkv, out, small, mid, hidden, dw):
    def shape(dims, dtype):
        return jax.ShapeDtypeStruct(dims, dtype)

    outs = (
        shape((2, FEAT, 4 * PART), BF),
        shape((FEAT, QKV), BF),
        shape((QCOLS, FEAT), BF),
        shape(small.shape, F32),
        shape((SEQ // 2, FEAT), F32),
    )
    return pl.pallas_call(
        sums_kernel,
        out_shape=outs,
        in_specs=[vmem()] * 5 + [anywhere()] * 2,
        out_specs=[anywhere()] + [vmem()] * 4,
        scratch_shapes=[pltpu.VMEM((4,) + small.shape, F32)] * 2
        + [
            pltpu.VMEM((SEQ, PART), BF),
            pltpu.VMEM((PART, MODEL), BF),
            pltpu.VMEM((SEQ // 2, QCOLS), F32),
        ]
        + reduce8_scratch(SEQ // 2, FEAT)
        + ring_scratch(SMALL_FIRST, SMALL_LAST)
        + [pltpu.SemaphoreType.DMA((128,)), pltpu.SemaphoreType.DMA((128,))]
        + [pltpu.SemaphoreType.DMA((4,))],
        compiler_params=pltpu.CompilerParams(
            collective_id=3, has_side_effects=True, vmem_limit_bytes=VMEM_LIMIT
        ),
        cost_estimate=pl.CostEstimate(
            flops=4 * 10**9, bytes_accessed=60 * 10**6, transcendentals=0
        ),
        name="sums_over_sequences",
    )(gu, qkv, out, small, mid, hidden, dw)


def widen_kernel(
    gu,
    down,
    qkv,
    out,
    small,
    gate_out,
    up_out,
    down_out,
    query_out,
    key_out,
    value_out,
    proj_out,
    gain1_out,
    gain2_out,
    bq_out,
    bk_out,
    bv_out,
    gu_in,
    down_in,
    gate_buf,
    up_buf,
    down_buf,
    in_sems,
    out_sems,
):
    skip = 3 * PART

    def loads(n):
        place = n % 2
        rows = pl.ds(640 * (n % 2), 640)
        return [
            pltpu.make_async_copy(gu.at[:, pl.ds(n * 48, 48), :], gu_in.at[place], in_sems.at[place, 0]),
            pltpu.make_async_copy(down.at[n // 2, rows, :], down_in.at[place], in_sems.at[place, 1]),
        ]

    def stores(n):
        place, quarter, part = n % 2, n // 2, n % 2
        rows = pl.ds(n * 48, 48)
        drop = HEAD if quarter == 3 and part == 0 else 0
        start = PART * quarter + 576 * part - (HEAD if quarter == 3 and part == 1 else 0)
        return [
            pltpu.make_async_copy(gate_buf.at[place], gate_out.at[rows, :], out_sems.at[place, 0]),
            pltpu.make_async_copy(up_buf.at[place], up_out.at[rows, :], out_sems.at[place, 1]),
            pltpu.make_async_copy(
                down_buf.at[place, pl.ds(drop, 576 - drop), :],
                down_out.at[pl.ds(start, 576 - drop), :],
                out_sems.at[place, 2],
            ),
        ]

    def run(copies):
        for copy in copies:
            copy.start()
        return copies

    def wait(copies):
        for copy in copies:
            copy.wait()

    arriving = {0: run(loads(0)), 1: run(loads(1))}
    query_out[...] = qkv[:, :QCOLS].astype(F32)
    key_out[...] = qkv[:, QCOLS : QCOLS + HEAD].astype(F32)
    value_out[...] = qkv[:, QCOLS + HEAD :].astype(F32)
    proj_out[...] = out[...].astype(F32)
    first = 0
    for ref, row, width in (
        (gain1_out, 0, FEAT),
        (bq_out, 0, QCOLS),
        (bk_out, 0, HEAD),
        (bv_out, 0, HEAD),
    ):
        ref[...] = small[row : row + 1, first : first + width]
        first += width
    gain2_out[...] = small[1:2, :FEAT]
    leaving = {}
    for n in range(8):
        place = n % 2
        wait(arriving[n])
        if n > 1:
            wait(leaving[n - 2])
        for i, buf in enumerate((gate_buf, up_buf)):
            buf[place, :, :skip] = gu_in[place, i, :, :skip].astype(F32)
            buf[place, :, skip:] = gu_in[place, i, :, skip + HEAD :].astype(F32)
        for m in range(4):
            down_buf[place, pl.ds(144 * m, 80), :] = down_in[
                place, pl.ds(160 * m, 80), :
            ].astype(F32)
            down_buf[place, pl.ds(144 * m + 80, 64), :] = down_in[
                place, pl.ds(160 * m + 96, 64), :
            ].astype(F32)
        leaving[n] = run(stores(n))
        if n + 2 < 8:
            arriving[n + 2] = run(loads(n + 2))
    wait(leaving[6])
    wait(leaving[7])


def run_widen(gu, down, qkv, out, small):
    shapes = [(FEAT, UNITS)] * 2 + [(UNITS, FEAT)]
    shapes += [(FEAT, QCOLS), (FEAT, HEAD), (FEAT, HEAD), (QCOLS, FEAT)]
    shapes += [(1, FEAT), (1, FEAT), (1, QCOLS), (1, HEAD), (1, HEAD)]
    return pl.pallas_call(
        widen_kernel,
        out_shape=[jax.ShapeDtypeStruct(dims, F32) for dims in shapes],
        in_specs=[anywhere()] * 2 + [vmem()] * 3,
        out_specs=[anywhere()] * 3 + [vmem()] * 9,
        scratch_shapes=[
            pltpu.VMEM((2, 2, 48, 4 * PART), BF),
            pltpu.VMEM((2, 640, FEAT), BF),
            pltpu.VMEM((2, 48, UNITS), F32),
            pltpu.VMEM((2, 48, UNITS), F32),
            pltpu.VMEM((2, 576, FEAT), F32),
            pltpu.SemaphoreType.DMA((2, 2)),
            pltpu.SemaphoreType.DMA((2, 3)),
        ],
        compiler_params=pltpu.CompilerParams(vmem_limit_bytes=VMEM_LIMIT),
        cost_estimate=pl.CostEstimate(
            flops=10**7, bytes_accessed=36 * 10**6, transcendentals=0
        ),
        name="widen",
    )(gu, down, qkv, out, small)


def rope_tables(count):
    places = np.arange(count, dtype=np.float32)
    inverse = (1.0 / THETA ** (np.arange(0, HEAD, 2) / HEAD)).astype(np.float32)
    angles = places[:, None] * inverse[None, :]
    cosine, sine = np.cos(angles), np.sin(angles)
    tables = np.concatenate([cosine, cosine], axis=-1), np.concatenate([-sine, sine], axis=-1)
    return tuple(jnp.asarray(table, F32) for table in tables)


def body(
    layer_input,
    gain_attn,
    w_query,
    w_key,
    w_value,
    b_query,
    b_key,
    b_value,
    w_out,
    gain_ffn,
    w_gate,
    w_up,
    w_down,
    out_grad,
):
    cosine, sine = rope_tables(SEQ)
    bias = jnp.concatenate([b_query, b_key, b_value]).astype(F32)[None]
    gains = jnp.zeros((8, FEAT), F32).at[0].set(gain_attn.astype(F32)).at[1].set(gain_ffn.astype(F32))
    (
        xs,
        normed1_cols,
        grads_block,
        qkv_w,
        out_w,
        queries,
        key,
        value,
        lse,
        attn,
        mid,
        gains_all,
        dn2,
        hidden,
        down_w,
        grad_gu,
        grad_down,
    ) = run_forward(
        layer_input,
        out_grad,
        w_query,
        w_key,
        w_value,
        w_out,
        w_gate,
        w_up,
        w_down,
        gains,
        bias,
        cosine,
        sine,
    )
    grad_input, grad_out, grad_qkv, small, grad_gu, grad_down = run_backward(
        dn2,
        mid,
        grads_block,
        gains_all,
        xs,
        normed1_cols,
        attn,
        queries,
        key,
        value,
        lse,
        cosine,
        sine,
        out_w,
        qkv_w,
        grad_gu.reshape(2, 4, 2, 4, 48, PART),
        grad_down,
    )
    grad_gu, grad_qkv, grad_out, small, layer_output = run_sums(
        grad_gu,
        grad_qkv.reshape(2, 4, 48, QKV),
        grad_out.reshape(2, 2, 4, 48, FEAT),
        small,
        mid,
        hidden,
        down_w,
    )
    (
        grad_gate,
        grad_up,
        grad_down,
        grad_query,
        grad_key,
        grad_value,
        grad_out,
        *vectors,
    ) = run_widen(grad_gu, grad_down, grad_qkv, grad_out, small)
    gain1, gain2, bias_query, bias_key, bias_value = (vector[0] for vector in vectors)
    return (
        layer_output,
        grad_input,
        gain1,
        grad_query,
        grad_key,
        grad_value,
        bias_query,
        bias_key,
        bias_value,
        grad_out,
        gain2,
        grad_gate,
        grad_up,
        grad_down,
    )


def solution(mesh):
    in_specs = (
        P(("dp", "row"), "col"),
        P("col"),
        P("col", "row"),
        P("col", "row"),
        P("col", "row"),
        P("row"),
        P("row"),
        P("row"),
        P("row", "col"),
        P("col"),
        P("col", "row"),
        P("col", "row"),
        P("row", "col"),
        P(("dp", "row"), "col"),
    )
    out_specs = (
        P(("dp", "row"), "col"),
        P(("dp", "row"), "col"),
        P("col"),
        P("col", "row"),
        P("col", "row"),
        P("col", "row"),
        P("row"),
        P("row"),
        P("row"),
        P("row", "col"),
        P("col"),
        P("col", "row"),
        P("col", "row"),
        P("row", "col"),
    )
    return jax.shard_map(body, mesh=mesh, in_specs=in_specs, out_specs=out_specs, check_vma=False)
```

```python
import functools

import jax
import jax.numpy as jnp
import numpy as np
from jax import lax
from jax.experimental import pallas as pl
from jax.experimental.pallas import tpu as pltpu
from jax.sharding import PartitionSpec as P

EPS = 1e-06
THETA = 1000000.0
NEG = -1e30
BF = jnp.bfloat16
F32 = jnp.float32
MESH = pl.DeviceIdType.MESH
HEAD = 128
HEADS = 6
SEQ = 1024
MODEL = 1536
FEAT = 384
BLOCK = 128
UNITS = 4480
PART = 1152
QCOLS = 768
QKV = 1024
VMEM_LIMIT = 62 * 2**20
SCALE = HEAD ** (-0.5)


def dot(left, right, left_dim=1, right_dim=0):
    return lax.dot_general(
        left, right, (((left_dim,), (right_dim,)), ((), ())), preferred_element_type=F32
    )


def aligned(index, step):
    return pl.multiple_of(index * step, step)


def block_of(row, col):
    return col + row * (7 - 2 * col)


def quarter_start(col):
    return pl.multiple_of(col * PART - (col // 3) * HEAD, HEAD)


class Place:
    def __init__(self):
        self.dp, self.row, self.col = (lax.axis_index(a) for a in ("dp", "row", "col"))
        self.hi, self.core = self.col // 2, self.col % 2
        self.z, self.y = self.dp // 4, self.dp % 4
        self.sib = 2 * self.hi + 1 - self.core
        self.far = 2 * (1 - self.hi) + self.core
        self.sibfar = 2 * (1 - self.hi) + 1 - self.core
        self.block = block_of(self.row, self.col)
        self.chips = (
            (self.row, 1 - self.hi),
            (1 - self.row, self.hi),
            (1 - self.row, 1 - self.hi),
            (self.row, self.hi),
        )
        self.S = {"col": self.sib}
        self.O = {"col": self.far}
        self.OS = {"col": self.sibfar}
        self.N1 = {"row": 1 - self.row}
        self.N2 = {"row": 1 - self.row, "col": self.far}
        self.N1S = {"row": 1 - self.row, "col": self.sib}
        self.N2S = {"row": 1 - self.row, "col": self.sibfar}

        def dp_at(z, y):
            return {"dp": lax.rem(z + 4, 4) * 4 + lax.rem(y + 4, 4)}

        self.YP, self.YM = dp_at(self.z, self.y + 1), dp_at(self.z, self.y - 1)
        self.Y2, self.Z2 = dp_at(self.z, self.y + 2), dp_at(self.z + 2, self.y)
        self.ZP, self.ZM = dp_at(self.z + 1, self.y), dp_at(self.z - 1, self.y)

    def meet(self, partners):
        barrier = pltpu.get_barrier_semaphore()
        for device in partners:
            pl.semaphore_signal(barrier, inc=1, device_id=device, device_id_type=MESH)
        pl.semaphore_wait(barrier, len(partners))


class Net:
    def __init__(self, send_sems, recv_sems, at):
        self.ss, self.rs, self.at, self.count, self.sent = send_sems, recv_sems, at, 0, []

    def key(self):
        self.count += 1
        return self.count - 1

    def copy(self, key, src, dst, device):
        return pltpu.make_async_remote_copy(
            src_ref=src,
            dst_ref=dst,
            send_sem=self.ss.at[key],
            recv_sem=self.rs.at[key],
            device_id=device,
            device_id_type=MESH,
        )

    def send(self, src, dst, device):
        key = self.key()
        copy = self.copy(key, src, dst, device)
        copy.start()
        self.sent.append(copy)
        return key

    def take(self, key, dst):
        self.copy(key, dst, dst, self.at.S).wait_recv()

    def finish(self, copies=None):
        copies = list(self.sent) if copies is None else copies
        for copy in copies:
            copy.wait_send()
            self.sent.remove(copy)


class Gather8:
    def __init__(self, net, at, place):
        self.net, self.at, self.place = net, at, place

    def start(self, src):
        net, at = self.net, self.at
        mine = self.place(at.row, at.col, None)
        self.k1 = net.send(src, mine, at.N1)
        self.k2 = net.send(src, mine, at.N2)
        self.k0 = net.send(src, mine, at.S)

    def middle(self):
        net, at, place = self.net, self.at, self.place
        near, away = place(1 - at.row, at.col, None), place(1 - at.row, at.far, None)
        first, last = place(1 - at.row, at.col, 0), place(1 - at.row, at.far, 1)
        net.take(self.k1, near)
        self.ka = net.send(first, first, at.N2)
        self.f1 = net.send(near, near, at.S)
        net.take(self.k2, away)
        self.kb = net.send(last, last, at.N1)
        self.f2 = net.send(away, away, at.S)

    def late(self):
        net, at, place = self.net, self.at, self.place
        first, last = place(at.row, at.far, 0), place(at.row, at.far, 1)
        net.take(self.ka, first)
        self.f3 = net.send(first, first, at.S)
        net.take(self.kb, last)
        self.f4 = net.send(last, last, at.S)

    def end(self, chip=None):
        net, at, place = self.net, self.at, self.place
        if chip in (None, 3):
            net.take(self.k0, place(at.row, at.sib, None))
        if chip in (None, 1):
            net.take(self.f1, place(1 - at.row, at.sib, None))
        if chip in (None, 2):
            net.take(self.f2, place(1 - at.row, at.sibfar, None))
        if chip in (None, 0):
            net.take(self.f3, place(at.row, at.sibfar, 0))
            net.take(self.f4, place(at.row, at.sibfar, 1))


def ring_dp(net, at, halves, ready=(None, None)):
    def wrap(index):
        return lax.rem(index + 4, 4)

    sides = (((at.YP, at.YM), (at.ZP, at.ZM)), ((at.ZP, at.ZM), (at.YP, at.YM)))
    firsts, seconds = (at.y, at.z), (at.z, at.y)

    def refs(i, a, b):
        return halves[i](b, a) if i == 0 else halves[i](a, b)

    def send(i, a, b, device):
        return [net.send(ref, ref, device) for ref in refs(i, a, b)]

    def take(i, a, b, keys):
        for key, ref in zip(keys, refs(i, a, b), strict=True):
            net.take(key, ref)

    one, two, onward = {}, {}, {}
    for i in (0, 1):
        if ready[i]:
            ready[i]()
        one[i] = [send(i, firsts[i], seconds[i], side) for side in sides[i][0]]
        if ready[i]:
            two[i, 0] = [send(i, firsts[i], seconds[i], side) for side in sides[i][1]]
    for i in (0, 1):
        if not ready[i]:
            two[i, 0] = [send(i, firsts[i], seconds[i], side) for side in sides[i][1]]
    yield
    for i in (0, 1):
        minus = wrap(firsts[i] - 1)
        take(i, minus, seconds[i], one[i][0])
        one[i].append(send(i, minus, seconds[i], sides[i][0][0]))
        two[i, 1] = [send(i, minus, seconds[i], side) for side in sides[i][1]]
    yield
    for i in (0, 1):
        plus = wrap(firsts[i] + 1)
        take(i, plus, seconds[i], one[i][1])
        two[i, 2] = [send(i, plus, seconds[i], side) for side in sides[i][1]]
    offsets = (0, -1, 1, 2)
    for q in (0, 1, 2, 3):
        yield
        for i in (0, 1):
            if q == 1:
                across = wrap(firsts[i] + 2)
                take(i, across, seconds[i], one[i][2])
                two[i, 3] = [send(i, across, seconds[i], side) for side in sides[i][1]]
            slot = wrap(firsts[i] + offsets[q])
            minus, plus = wrap(seconds[i] - 1), wrap(seconds[i] + 1)
            take(i, slot, minus, two[i, q][0])
            if q < 2:
                onward[i, q] = send(i, slot, minus, sides[i][1][0])
            take(i, slot, plus, two[i, q][1])
            if q >= 2:
                onward[i, q] = send(i, slot, plus, sides[i][1][1])
    for q in (0, 1, 2, 3):
        yield
        for i in (0, 1):
            slot = wrap(firsts[i] + offsets[q])
            take(i, slot, wrap(seconds[i] + 2), onward[i, q])


def drain(steps):
    for _ in steps:
        pass


def rms(values):
    return lax.rsqrt(jnp.mean(values * values, axis=1, keepdims=True) + EPS)


def turn(values):
    return pltpu.roll(values, HEAD // 2, 1)


def causal(scores, start):
    places = start + lax.broadcasted_iota(jnp.int32, scores.shape, 0)
    keys = lax.broadcasted_iota(jnp.int32, scores.shape, 1)
    return jnp.where(keys <= places, scores, NEG)


def vmem():
    return pl.BlockSpec(memory_space=pltpu.VMEM)


def anywhere():
    return pl.BlockSpec(memory_space=pl.ANY)


class GatherCol:
    def __init__(self, net, at, array):
        self.net, self.at, self.array = net, at, array

    def rows(self, col, j):
        return self.array.at[pl.ds(aligned(col + j * (7 - 2 * col), BLOCK), BLOCK), :]

    def start(self):
        net, at = self.net, self.at
        mine = [self.rows(at.col, j) for j in (0, 1)]
        self.far = [net.send(ref, ref, at.O) for ref in mine]
        self.sib = [net.send(ref, ref, at.S) for ref in mine]

    def middle(self):
        net, at = self.net, self.at
        self.onward = []
        for j in (0, 1):
            ref = self.rows(at.far, j)
            net.take(self.far[j], ref)
            self.onward.append(net.send(ref, ref, at.S))

    def end(self):
        net, at = self.net, self.at
        for j in (0, 1):
            net.take(self.sib[j], self.rows(at.sib, j))
            net.take(self.onward[j], self.rows(at.sibfar, j))


class Reduce8:
    def __init__(self, net, at, own, other, sib_in, first_in, last_in, near_in, away_in):
        self.net, self.at, self.own, self.other, self.sib_in = net, at, own, other, sib_in
        self.first_in, self.last_in, self.near_in, self.away_in = first_in, last_in, near_in, away_in
        self.half = own.shape[1] // 2
        self.keys = {}

    def put(self, j, mine, theirs):
        self.own[j] = mine
        self.other[j] = theirs
        self.keys[j] = self.net.send(self.other.at[j], self.sib_in.at[j], self.at.S)

    def step(self, j):
        net, at, half = self.net, self.at, self.half
        net.take(self.keys[j], self.sib_in.at[j])
        total = self.own[j].astype(F32) + self.sib_in[j].astype(F32)
        if j == 0:
            self.own[j] = total.astype(BF)
            self.first = net.send(self.own.at[j, pl.ds(0, half)], self.first_in, at.N1)
            self.last = net.send(self.own.at[j, pl.ds(half, half)], self.last_in, at.N2)
        elif j == 1:
            net.take(self.last, self.last_in)
            self.own[j, :half] = total[:half].astype(BF)
            self.own[j, half:] = (total[half:] + self.last_in[...].astype(F32)).astype(BF)
            self.near = net.send(self.own.at[j], self.near_in, at.N1)
        elif j == 2:
            net.take(self.first, self.first_in)
            self.own[j, :half] = (total[:half] + self.first_in[...].astype(F32)).astype(BF)
            self.own[j, half:] = total[half:].astype(BF)
            self.away = net.send(self.own.at[j], self.away_in, at.N2)
        else:
            net.take(self.near, self.near_in)
            net.take(self.away, self.away_in)
            return total + self.near_in[...].astype(F32) + self.away_in[...].astype(F32)
        return None


def reduce8_scratch(rows, columns):
    return [
        pltpu.VMEM((4, rows, columns), BF),
        pltpu.VMEM((4, rows, columns), BF),
        pltpu.VMEM((4, rows, columns), BF),
        pltpu.VMEM((rows // 2, columns), BF),
        pltpu.VMEM((rows // 2, columns), BF),
        pltpu.VMEM((rows, columns), BF),
        pltpu.VMEM((rows, columns), BF),
    ]


def tiles_of(width, step):
    return [(first, min(step, width - first)) for first in range(0, width, step)]


def add_up(out, terms):
    lead = out.shape[:-2]
    if not lead:
        total = terms[0][...].astype(F32)
        for term in terms[1:]:
            total = total + term[...].astype(F32)
        out[...] = total.astype(out.dtype)
        return
    count = 1
    for size in lead:
        count *= size

    def step(i, carry):
        index = []
        for size in reversed(lead):
            index.insert(0, i % size)
            i = i // size
        index = tuple(index)
        total = terms[0].at[index][...].astype(F32)
        for term in terms[1:]:
            total = total + term.at[index][...].astype(F32)
        out.at[index][...] = total.astype(out.dtype)
        return carry

    lax.fori_loop(0, count, step, 0)


class RingItem:
    def __init__(self, net, sides, place, part, held, way, bufs, own):
        self.net, self.part, self.held, self.own = net, part, held, own
        self.relay, self.staged, self.from_last, self.from_next = bufs
        self.onward, self.back = (sides[0], sides[1]) if way == 0 else (sides[1], sides[0])
        step = 1 - 2 * way
        self.here, self.next, self.across, self.last = (
            lax.rem(place + 4 + step * i, 4) for i in (0, 1, 2, 3)
        )

    def start(self):
        self.k_relay = self.net.send(self.part(self.across), self.relay, self.onward)

    def direct(self):
        self.k_next = self.net.send(self.part(self.last), self.from_next, self.back)

    def middle(self):
        self.net.take(self.k_relay, self.relay)
        add_up(self.staged, [self.held(self.next), self.relay])
        self.k_last = self.net.send(self.staged, self.from_last, self.onward)

    def end(self):
        self.net.take(self.k_next, self.from_next)
        self.net.take(self.k_last, self.from_last)
        add_up(self.own, [self.held(self.here), self.from_next, self.from_last])


def begin(items):
    for item in items:
        item.start()
    for item in items:
        item.direct()


LEFT, RIGHT = pl.ds(0, QCOLS), pl.ds(QCOLS, QCOLS)
GU_FIRST = (((2, 2, 48, PART),), ((2, 2, 48, PART),))
GU_LAST = (((48, PART),) * 2,) * 2
DOWN_FIRST = (((2, 80, QCOLS),), ((144, QCOLS),))
DOWN_LAST = (((80, QCOLS),),) * 2
SMALL_FIRST = (((2, 48, 512),), ((2, 48, FEAT),))
SMALL_LAST = (((48, 512),), ((48, FEAT),))


def down_rows(k):
    return pl.ds(pl.multiple_of(72 * k - 8 * (k % 2), 16), 80)


def ring_scratch(first, last):
    scratch = []
    for i in (0, 1):
        for dims in first[i]:
            scratch += [pltpu.VMEM(dims, BF)] * 8
            scratch.append(pltpu.VMEM((2,) + dims, BF))
        for dims in last[i]:
            scratch += [pltpu.VMEM(dims, BF)] * 4
    return scratch


def ring_items(net, at, first, last, parts, helds, seconds, finals, bufs):
    sides = (((at.YP, at.YM), (at.ZP, at.ZM)), ((at.ZP, at.ZM), (at.YP, at.YM)))
    places = ((at.y, at.z), (at.z, at.y))
    bufs = list(bufs)
    one, two = ([], []), ([], [])
    for i in (0, 1):
        owns = []
        for n in range(len(first[i])):
            own = bufs[8]
            for way in (0, 1):
                part = functools.partial(lambda k, f, w: f(k, w), f=parts[i][n], w=way)
                held = functools.partial(lambda k, f, w: f(k, w), f=helds[i][n], w=way)
                four = bufs[4 * way : 4 * way + 4]
                one[i].append(
                    RingItem(net, sides[i][0], places[i][0], part, held, way, four, own.at[way])
                )
            owns.append(own)
            bufs = bufs[9:]
        for n in range(len(last[i])):
            part = functools.partial(lambda k, f, o: f(o, k), f=seconds[i][n], o=owns[min(n, len(owns) - 1)])
            two[i].append(
                RingItem(net, sides[i][1], places[i][1], part, part, n % 2, bufs[:4], finals[i][n])
            )
            bufs = bufs[4:]

    def mix(pair):
        return [item for items in zip(*pair, strict=True) for item in items]

    return mix(one), mix(two)


def gu_items(net, at, far_ref, near_ref, gu_own, bufs):
    def parts_of(gu):
        return (
            (lambda k, way: gu.at[way, pl.ds(0, 2), :, k],),
            (lambda k, way: gu.at[k // 2, pl.ds(2, 2), k % 2, pl.ds(2 * way, 2)],),
        )

    seconds = (
        (lambda own, k: own.at[k // 2, 0, k % 2], lambda own, k: own.at[k // 2, 1, k % 2]),
    ) * 2
    finals = ((gu_own.at[0], gu_own.at[1]), (gu_own.at[2], gu_own.at[3]))
    helds = parts_of(near_ref)
    return ring_items(net, at, GU_FIRST, GU_LAST, parts_of(far_ref), helds, seconds, finals, bufs)


def down_items(net, at, down, down_own, bufs):
    parts = (
        (lambda k, way: down.at[way, :, down_rows(k), LEFT],),
        (lambda k, way: down.at[k // 2, k % 2, pl.ds(144 * way, 144), RIGHT],),
    )
    seconds = (
        (lambda own, k: own.at[k // 2, k % 2],),
        (lambda own, k: own.at[k // 2, pl.ds(pl.multiple_of((k % 2) * 64, 64), 80)],),
    )
    finals = ((down_own.at[:, LEFT],), (down_own.at[:, RIGHT],))
    return ring_items(net, at, DOWN_FIRST, DOWN_LAST, parts, parts, seconds, finals, bufs)


def small_items(net, at, qkv, out, qkv_own, out_own, bufs):
    parts = (
        (lambda k, way: qkv.at[:, k, :, pl.ds(512 * way, 512)],),
        (lambda k, way: out.at[k // 2, k % 2, pl.ds(2 * way, 2)],),
    )
    seconds = ((lambda own, k: own.at[k // 2, k % 2],), (lambda own, k: own.at[k // 2, k % 2],))
    finals = ((qkv_own,), (out_own,))
    return ring_items(net, at, SMALL_FIRST, SMALL_LAST, parts, parts, seconds, finals, bufs)


def forward_kernel(
    x_ref,
    og_ref,
    wq_ref,
    wk_ref,
    wv_ref,
    wout_ref,
    wg_ref,
    wu_ref,
    wd_ref,
    gains_ref,
    bias_ref,
    cos_ref,
    sin_ref,
    xs_ref,
    n1c_ref,
    og_out,
    qw_out,
    ow_out,
    q_ref,
    k_ref,
    v_ref,
    lse_ref,
    attn_all,
    mid_ref,
    gains_all,
    dn2_ref,
    hidden_out,
    dw_out,
    grad_gu,
    down_own,
    wqkv_ref,
    x_all,
    n1,
    og_all,
    n2_all,
    qw,
    ow,
    gw,
    uw,
    dw,
    part_out,
    part_in,
    d_up,
    tile_buf,
    down,
    attn_ref,
    *rest,
):
    red_a, bufs, sems = rest[:7], rest[7:-4], rest[-4:]
    send_sems, recv_sems, local_sems, tile_sems = sems
    at = Place()
    net = Net(send_sems, recv_sems, at)
    local, local_count = [], iter(range(32))

    def move(src, dst):
        copy = pltpu.make_async_copy(src, dst, local_sems.at[next(local_count)])
        copy.start()
        local.append(copy)
        return copy

    joined = [
        move(wq_ref, wqkv_ref.at[:, pl.ds(0, QCOLS)]),
        move(wk_ref, wqkv_ref.at[:, pl.ds(QCOLS, HEAD)]),
        move(wv_ref, wqkv_ref.at[:, pl.ds(QCOLS + HEAD, HEAD)]),
    ]
    at.meet((at.S, at.N1, at.N2, at.O, at.OS, at.YP, at.YM, at.ZP, at.ZM))
    for copy in joined:
        copy.wait()
    local.clear()

    def tokens_of(array):
        def place(row, col, part):
            if part is None:
                rows = pl.ds(aligned(row, SEQ // 2), SEQ // 2)
            else:
                rows = pl.ds(aligned(row * 2 + part, SEQ // 4), SEQ // 4)
            return array.at[rows, pl.ds(aligned(col, FEAT), FEAT)]

        return place

    mine, mine_far = aligned(at.col, FEAT), aligned(1 - at.hi, 2 * FEAT)
    move(x_ref, tokens_of(x_all)(at.row, at.col, None))
    move(wqkv_ref, qw.at[pl.ds(mine, FEAT), :])
    move(wout_ref, ow.at[:, pl.ds(mine, FEAT)])
    move(gains_ref, gains_all.at[:, pl.ds(mine, FEAT)])
    start = quarter_start(at.col)
    move(wg_ref.at[:, pl.ds(start, PART)], gw.at[pl.ds(mine, FEAT), :])
    move(wu_ref.at[:, pl.ds(start, PART)], uw.at[pl.ds(mine, FEAT), :])
    move(wd_ref.at[pl.ds(start, PART), :], dw.at[:, pl.ds(mine, FEAT)])
    move(og_ref, tokens_of(og_all)(at.row, at.col, None))

    eighth = at.dp % 8
    across = [net.key() for _ in range(5)]

    def slice_copies(core, first, last):
        device = {"col": 2 * (1 - at.hi) + core}
        rows = pl.ds(aligned(eighth, 48), 48)
        target = pl.ds(pl.multiple_of(mine + eighth * 48, 16), 48)
        columns = pl.ds(core * 512, 512)
        out_rows = pl.ds(pl.multiple_of(core * FEAT + eighth * 48, 16), 48)
        theirs = quarter_start(2 * (1 - at.hi) + core)
        down_rows = pl.ds(pl.multiple_of(theirs + eighth * 144, 16), 144)
        down_target = pl.ds(aligned(eighth, 144), 144)
        pairs = (
            (wqkv_ref.at[rows, columns], qw.at[target, columns]),
            (wout_ref.at[out_rows, :], ow.at[out_rows, pl.ds(mine, FEAT)]),
            (wg_ref.at[rows, pl.ds(theirs, PART)], gw.at[target, :]),
            (wu_ref.at[rows, pl.ds(theirs, PART)], uw.at[target, :]),
            (wd_ref.at[down_rows, :], dw.at[down_target, pl.ds(mine, FEAT)]),
        )
        return [
            pltpu.make_async_remote_copy(
                src_ref=pairs[i][0],
                dst_ref=pairs[i][1],
                send_sem=net.ss.at[spare[core][i]],
                recv_sem=net.rs.at[across[i]],
                device_id=device,
                device_id_type=MESH,
            )
            for i in range(first, last)
        ]

    spare = ([net.key() for _ in range(5)], [net.key() for _ in range(5)])
    chosen = at.core == at.dp // 8

    @pl.when(chosen)
    def _():
        for core in (0, 1):
            for copy in slice_copies(core, 0, 2):
                copy.start()

    gather_x = Gather8(net, at, tokens_of(x_all))
    gather_x.start(x_ref)
    gain_far = net.send(gains_ref, gains_all.at[:, pl.ds(mine, FEAT)], at.N2)
    gain_sib = net.send(gains_ref, gains_all.at[:, pl.ds(mine, FEAT)], at.S)
    near_qw = net.send(wqkv_ref, qw.at[pl.ds(mine, FEAT), :], at.S)
    near_ow = net.send(wout_ref, ow.at[:, pl.ds(mine, FEAT)], at.S)

    @pl.when(chosen)
    def _():
        for core in (0, 1):
            for copy in slice_copies(core, 2, 5):
                copy.start()

    far_half = pl.ds(mine_far, 2 * FEAT)

    def qkv_slices(z, y):
        rows = pl.ds(pl.multiple_of(mine_far + (z * 4 + y) * 48, 16), 48)
        return [qw.at[rows, pl.ds(aligned(at.core, 512), 512)]]

    def out_slices(z, y):
        index = z * 4 + y
        rows = pl.ds(pl.multiple_of(at.core * FEAT + (index % 8) * 48, 16), 48)
        return [ow.at[rows, pl.ds(pl.multiple_of(mine_far + (index // 8) * FEAT, HEAD), FEAT)]]

    def ffn_slices(weights, first, count):
        def slices(z, y):
            index = z * 4 + y
            rows = pl.ds(pl.multiple_of(mine_far + index * 48, 16), 48)
            down_rows = pl.ds(pl.multiple_of((index % 8) * 144 + first, 16), count)
            lanes = pl.ds(pl.multiple_of(mine_far + (index // 8) * FEAT, HEAD), FEAT)
            return [weights.at[rows, :], dw.at[down_rows, lanes]]

        return slices

    net.take(across[0], qkv_slices(at.z, at.y)[0])
    net.take(across[1], out_slices(at.z, at.y)[0])
    ring = ring_dp(net, at, (qkv_slices, out_slices))
    next(ring)
    next(ring)
    next(ring)
    gather_x.middle()
    gains_far = gains_all.at[:, pl.ds(aligned(at.far, FEAT), FEAT)]
    net.take(gain_far, gains_far)
    gain_sibfar = net.send(gains_far, gains_far, at.S)
    next(ring)
    cols_half, rows_half = pl.ds(aligned(at.core, 512), 512), pl.ds(aligned(at.core, FEAT), FEAT)
    gather_og = Gather8(net, at, tokens_of(og_all))
    gather_x.late()

    drain(ring)
    far_qw = net.send(qw.at[far_half, cols_half], qw.at[far_half, cols_half], at.S)
    far_ow = net.send(ow.at[rows_half, far_half], ow.at[rows_half, far_half], at.S)
    net.take(across[2], ffn_slices(gw, 0, 80)(at.z, at.y)[0])
    net.take(across[3], ffn_slices(uw, 80, 64)(at.z, at.y)[0])
    net.take(across[4], ffn_slices(uw, 0, 144)(at.z, at.y)[1])
    ring = ring_dp(net, at, (ffn_slices(gw, 0, 80), ffn_slices(uw, 80, 64)))
    next(ring)
    near = [
        net.send(wg_ref.at[:, pl.ds(quarter_start(at.sib), PART)], gw.at[pl.ds(mine, FEAT), :], at.S),
        net.send(wu_ref.at[:, pl.ds(quarter_start(at.sib), PART)], uw.at[pl.ds(mine, FEAT), :], at.S),
        net.send(wd_ref.at[pl.ds(quarter_start(at.sib), PART), :], dw.at[:, pl.ds(mine, FEAT)], at.S),
    ]
    gather_og.start(og_ref)
    gather_x.end()
    early = list(net.sent)
    net.take(gain_sib, gains_all.at[:, pl.ds(aligned(at.sib, FEAT), FEAT)])
    net.take(gain_sibfar, gains_all.at[:, pl.ds(aligned(at.sibfar, FEAT), FEAT)])
    for copy in local:
        copy.wait()
    local.clear()

    gain1, gain2 = gains_all[0:1, :], gains_all[1:2, :]

    def norm_block(i, carry):
        rows = pl.ds(aligned(i, BLOCK), BLOCK)
        values = x_all[rows, :].astype(F32)
        n1[rows, :] = (values * rms(values) * gain1).astype(BF)
        return carry

    lax.fori_loop(0, SEQ // BLOCK // 2, norm_block, 0)
    next(ring)
    lax.fori_loop(SEQ // BLOCK // 2, SEQ // BLOCK, norm_block, 0)
    next(ring)
    gather_og.middle()
    my_rows = pl.ds(aligned(at.block, BLOCK), BLOCK)
    xs_ref[...] = x_all[my_rows, :]
    n1c_ref[...] = n1[:, pl.ds(mine, FEAT)]
    net.take(near_qw, qw.at[pl.ds(aligned(at.sib, FEAT), FEAT), :])
    other_cols = pl.ds(aligned(1 - at.core, 512), 512)
    net.take(far_qw, qw.at[far_half, other_cols])
    move(qw, qw_out)

    def kv_block(i, carry):
        rows = pl.ds(aligned(i, 256), 256)
        both = dot(n1[rows, :], qw[:, QCOLS:]) + bias_ref[:, QCOLS:]
        key = both[:, :HEAD]
        k_ref[rows, :] = (key * cos_ref[rows, :] + turn(key) * sin_ref[rows, :]).astype(BF)
        v_ref[rows, :] = both[:, HEAD:].astype(BF)
        return carry

    lax.fori_loop(0, SEQ // 256, kv_block, 0)
    next(ring)
    pair = (at.col, 7 - at.col)
    for j in (0, 1):
        rows = pl.ds(aligned(pair[j], BLOCK), BLOCK)
        queries = dot(n1[rows, :], qw[:, :QCOLS]) + bias_ref[:, :QCOLS]
        cosine, sine = cos_ref[rows, :], sin_ref[rows, :]
        for h in range(HEADS):
            one = queries[:, h * HEAD : (h + 1) * HEAD]
            q_ref[pl.ds(j * BLOCK, BLOCK), pl.ds(h * HEAD, HEAD)] = (
                one * cosine + turn(one) * sine
            ).astype(BF)
    next(ring)
    gather_og.late()

    for j in (0, 1):
        keys = SEQ // 2 * (j + 1)
        rows = pl.ds(j * BLOCK, BLOCK)

        def attend(h, carry):
            lanes = pl.ds(aligned(h, HEAD), HEAD)
            scores = dot(q_ref[rows, lanes], k_ref[:keys, :], 1, 1) * SCALE
            scores = causal(scores, pair[j] * BLOCK)
            top = jnp.max(scores, axis=1, keepdims=True)
            weights = jnp.exp(scores - top)
            total = jnp.sum(weights, axis=1, keepdims=True)
            lse_ref[j * HEADS + h] = top + jnp.log(total)
            probs = (weights * (1.0 / total)).astype(BF)
            attn_ref[rows, lanes] = dot(probs, v_ref[:keys, :]).astype(BF)
            return carry

        lax.fori_loop(0, HEADS, attend, 0)
        next(ring)

    net.take(near_ow, ow.at[:, pl.ds(aligned(at.sib, FEAT), FEAT)])
    other_rows = pl.ds(aligned(1 - at.core, FEAT), FEAT)
    net.take(far_ow, ow.at[other_rows, far_half])
    move(ow, ow_out)
    part_out[...] = dot(attn_ref[pl.ds(aligned(1 - at.row, BLOCK), BLOCK), :], ow[...]).astype(BF)
    part = net.send(part_out, part_in, at.N1)
    own = dot(attn_ref[pl.ds(aligned(at.row, BLOCK), BLOCK), :], ow[...])
    net.take(part, part_in)
    mid = xs_ref[...].astype(F32) + own + part_in[...].astype(F32)
    mid_ref[...] = mid

    def place_n2(row, col, part):
        first = block_of(row, col) * BLOCK
        if part is None:
            return n2_all.at[pl.ds(pl.multiple_of(first, BLOCK), BLOCK), :]
        return n2_all.at[pl.ds(pl.multiple_of(first + part * 64, 64), 64), :]

    n2_all[my_rows, :] = (mid * rms(mid) * gain2).astype(BF)
    gather_n2 = Gather8(net, at, place_n2)
    gather_n2.start(place_n2(at.row, at.col, None))
    gather_og.end()
    move(og_all.at[my_rows, :], og_out)
    next(ring)
    gather_n2.middle()
    next(ring)
    next(ring)
    gather_n2.late()
    drain(ring)
    net.take(near[2], dw.at[:, pl.ds(aligned(at.sib, FEAT), FEAT)])

    def hidden_back(i, carry):
        rows = pl.ds(aligned(i, 256), 256)
        for first, width in tiles_of(PART, 512):
            lanes = pl.ds(first, width)
            d_up[rows, lanes] = dot(og_all[rows, :], dw[lanes, :], 1, 1).astype(BF)
        return carry

    gather_attn = GatherCol(net, at, attn_all)
    for j in (0, 1):
        gather_attn.rows(at.col, j)[...] = attn_ref[pl.ds(j * BLOCK, BLOCK), :]
    gather_attn.start()
    lax.fori_loop(0, 4, hidden_back, 0)
    move(dw, dw_out)
    net.take(near[0], gw.at[pl.ds(aligned(at.sib, FEAT), FEAT), :])
    net.take(near[1], uw.at[pl.ds(aligned(at.sib, FEAT), FEAT), :])

    net.finish(early)
    hidden, d_gate = x_all.at[:, pl.ds(0, PART)], n1.at[:, pl.ds(0, PART)]
    norms = Reduce8(net, at, *red_a)
    chips = at.chips
    last_part = at.col == 3

    def tokens(j):
        row, hi = chips[j]
        first = 2 * hi + row * (6 - 4 * hi)
        return pl.ds(aligned(first, BLOCK), 256), at.core + row * (1 - 2 * at.core)

    for j in (3, 1, 2, 0):
        gather_n2.end(j)
        rows, _ = tokens(j)
        for first, width in tiles_of(PART, 512):
            lanes = pl.ds(first, width)
            gate = dot(n2_all[rows, :], gw[:, lanes])
            up = dot(n2_all[rows, :], uw[:, lanes])
            d_hidden = d_up[rows, lanes].astype(F32)
            sig = jax.nn.sigmoid(gate)
            act = gate * sig
            d_act = d_hidden * up * sig * (1.0 + gate * (1.0 - sig))
            values = [act * up, d_act, d_hidden * act]
            if first == 0:
                lane = lax.broadcasted_iota(jnp.int32, (1, width), 1)
                fresh = jnp.logical_or(lane >= HEAD, jnp.logical_not(last_part))
                values = [jnp.where(fresh, value, 0.0) for value in values]
            for ref, value in zip((hidden, d_gate, d_up), values, strict=True):
                ref[rows, lanes] = value.astype(BF)
    move(hidden, hidden_out)
    for first, width in tiles_of(MODEL, 256):
        lanes = pl.ds(first, width)
        tile = dot(hidden[...], og_all[:, lanes], 0, 0).astype(BF)
        for q in range(4):
            down[q // 2, q % 2, :, lanes] = tile[288 * q : 288 * (q + 1)]
    gather_attn.middle()
    sums, last_sums = down_items(net, at, down, down_own, bufs)
    begin(sums)
    for j in range(4):
        rows, place = tokens(j)
        own_rows = pl.ds(pl.multiple_of(rows.start + place * BLOCK, BLOCK), BLOCK)
        other_rows = pl.ds(pl.multiple_of(rows.start + (1 - place) * BLOCK, BLOCK), BLOCK)
        parts = [
            (dot(d_gate[r, :], gw[...], 1, 1) + dot(d_up[r, :], uw[...], 1, 1)).astype(BF)
            for r in (other_rows, own_rows)
        ]
        norms.put(j, parts[1], parts[0])
        if j:
            norms.step(j - 1)

    writes = []

    def outer_sum(left, right, out):
        height = left.shape[1] // 2
        for first, width in tiles_of(right.shape[1], 256):
            place = len(writes) % 2
            if len(writes) > 1:
                writes[-2].wait()
            for i in (0, 1):
                rows = pl.ds(i * height, height)
                tile_buf[place, rows, :width] = dot(
                    left[:, rows], right[:, pl.ds(first, width)], 0, 0
                ).astype(BF)
            writes.append(
                pltpu.make_async_copy(
                    tile_buf.at[place, pl.ds(0, 2 * height), pl.ds(0, width)],
                    out.at[:, pl.ds(first, width)],
                    tile_sems.at[place],
                )
            )
            writes[-1].start()

    gather_attn.end()
    for item in sums:
        item.middle()
    outer_sum(n2_all, d_gate, grad_gu.at[0])
    dn2_ref[...] = norms.step(3)
    for item in sums:
        item.end()
    begin(last_sums)
    outer_sum(n2_all, d_up, grad_gu.at[1])
    for item in last_sums:
        item.middle()
    for item in last_sums:
        item.end()
    for copy in writes[-2:]:
        copy.wait()
    for copy in local:
        copy.wait()
    net.finish()

    @pl.when(chosen)
    def _():
        for core in (0, 1):
            for copy in slice_copies(core, 0, 5):
                copy.wait_send()


def run_forward(x, og, wq, wk, wv, wout, wg, wu, wd, gains, bias, cosine, sine):
    outs = (
        ((BLOCK, MODEL), BF, vmem),
        ((SEQ, FEAT), BF, vmem),
        ((BLOCK, MODEL), BF, anywhere),
        ((MODEL, QKV), BF, anywhere),
        ((QCOLS, MODEL), BF, anywhere),
        ((2 * BLOCK, QCOLS), BF, vmem),
        ((SEQ, HEAD), BF, vmem),
        ((SEQ, HEAD), BF, vmem),
        ((2 * HEADS, BLOCK, 1), F32, vmem),
        ((SEQ, QCOLS), BF, vmem),
        ((BLOCK, MODEL), F32, vmem),
        ((8, MODEL), F32, vmem),
        ((BLOCK, MODEL), F32, vmem),
        ((SEQ, PART), BF, anywhere),
        ((PART, MODEL), BF, anywhere),
        ((2, MODEL, PART), BF, anywhere),
        ((80, MODEL), BF, vmem),
    )
    return pl.pallas_call(
        forward_kernel,
        out_shape=[jax.ShapeDtypeStruct(dims, dtype) for dims, dtype, _ in outs],
        in_specs=[anywhere()] * 9 + [vmem()] * 4,
        out_specs=[place() for _, _, place in outs],
        scratch_shapes=[
            pltpu.VMEM((FEAT, QKV), BF),
            pltpu.VMEM((SEQ, MODEL), BF),
            pltpu.VMEM((SEQ, MODEL), BF),
            pltpu.VMEM((SEQ, MODEL), BF),
            pltpu.VMEM((SEQ, MODEL), BF),
            pltpu.VMEM((MODEL, QKV), BF),
            pltpu.VMEM((QCOLS, MODEL), BF),
            pltpu.VMEM((MODEL, PART), BF),
            pltpu.VMEM((MODEL, PART), BF),
            pltpu.VMEM((PART, MODEL), BF),
            pltpu.VMEM((BLOCK, MODEL), BF),
            pltpu.VMEM((BLOCK, MODEL), BF),
            pltpu.VMEM((SEQ, PART), BF),
            pltpu.VMEM((2, MODEL, 256), BF),
            pltpu.VMEM((2, 2, 288, MODEL), BF),
            pltpu.VMEM((2 * BLOCK, QCOLS), BF),
        ]
        + reduce8_scratch(BLOCK, MODEL)
        + ring_scratch(DOWN_FIRST, DOWN_LAST)
        + [
            pltpu.SemaphoreType.DMA((200,)),
            pltpu.SemaphoreType.DMA((200,)),
            pltpu.SemaphoreType.DMA((32,)),
            pltpu.SemaphoreType.DMA((2,)),
        ],
        compiler_params=pltpu.CompilerParams(
            collective_id=0, has_side_effects=True, vmem_limit_bytes=VMEM_LIMIT
        ),
        cost_estimate=pl.CostEstimate(
            flops=37 * 10**9, bytes_accessed=80 * 10**6, transcendentals=4 * 10**6
        ),
        name="forward_and_feed_forward",
    )(x, og, wq, wk, wv, wout, wg, wu, wd, gains, bias, cosine, sine)


def backward_kernel(
    dn2_ref,
    mid_ref,
    og_ref,
    gains_all,
    n1c,
    attn_all,
    q_ref,
    k_ref,
    v_ref,
    lse_ref,
    cos_ref,
    sin_ref,
    ow_far,
    gu_far,
    down_own,
    grad_out,
    grad_qkv,
    sums_ref,
    d_mid,
    d_qkv_own,
    bias_ref,
    gu_own,
    all_down,
    mid_cols,
    mid_pair,
    d_attn,
    d_q,
    d_kv,
    kv_out,
    kv_in,
    d_qkv_all,
    ow,
    gu,
    *rest,
):
    bufs, (send_sems, recv_sems, local_sems) = rest[:-3], rest[-3:]
    at = Place()
    net = Net(send_sems, recv_sems, at)
    held = [
        pltpu.make_async_copy(src, dst, local_sems.at[i])
        for i, (src, dst) in enumerate(
            ((ow_far, ow), (gu_far, gu))
        )
    ]
    for copy in held:
        copy.start()
    at.meet(
        (at.S, at.O, at.OS, at.N1, at.N2, at.N1S, at.N2S, at.YP, at.YM, at.ZP, at.ZM)
    )
    first, last = gu_items(net, at, gu_far, gu, gu_own, bufs)
    begin(first)

    def down_slot(k, cols):
        return all_down.at[cols, pl.ds(pl.multiple_of(k * 80, 16), 80), :]

    down_keys = [
        net.send(down_own.at[:, pl.ds(aligned(col, FEAT), FEAT)], down_slot(at.dp, at.col), device)
        for device, col in ((at.S, at.sib), (at.O, at.far), (at.OS, at.sibfar))
    ]
    down_mine = pltpu.make_async_copy(
        down_own.at[:, pl.ds(aligned(at.col, FEAT), FEAT)],
        down_slot(at.dp, at.col),
        local_sems.at[3],
    )
    down_mine.start()
    peers = ((at.S, at.sib), (at.O, at.far), (at.OS, at.sibfar))
    pair = (at.col, 7 - at.col)

    def rows_at(block):
        return pl.ds(aligned(block, BLOCK), BLOCK)

    def cols_at(col):
        return pl.ds(aligned(col, FEAT), FEAT)

    gain2 = gains_all[1:2, :]
    mid = mid_ref[...]
    scale = rms(mid)
    unit = mid * scale
    d_normed = dn2_ref[...]
    sums_ref[...] = jnp.zeros_like(sums_ref)
    sums_ref[1:2, :] = jnp.sum(d_normed * unit, axis=0, keepdims=True)
    bent = d_normed * gain2
    d_mid[...] = og_ref[...].astype(F32) + scale * (
        bent - unit * jnp.mean(bent * unit, axis=1, keepdims=True)
    )
    mid_pair[at.row] = d_mid[...].astype(BF)
    to_pair = net.send(mid_pair.at[at.row], mid_pair.at[at.row], at.N1)
    mid_cols[rows_at(at.block), :] = d_mid[:, cols_at(at.col)].astype(BF)
    spread = []
    others = (
        (at.S, at.row, at.sib),
        (at.N1, 1 - at.row, at.col),
        (at.N1S, 1 - at.row, at.sib),
        (at.O, at.row, at.far),
        (at.OS, at.row, at.sibfar),
        (at.N2, 1 - at.row, at.far),
        (at.N2S, 1 - at.row, at.sibfar),
    )
    for device, row, col in others:
        spread.append(
            net.send(
                mid_pair.at[at.row, :, cols_at(col)], mid_cols.at[rows_at(at.block), :], device
            )
        )
    net.take(to_pair, mid_pair.at[1 - at.row])
    held[0].wait()
    for j in (0, 1):
        d_attn[pl.ds(j * BLOCK, BLOCK), :] = dot(mid_pair[j], ow[...], 1, 1).astype(BF)
    d_kv[...] = jnp.zeros_like(d_kv)
    held[1].wait()
    for item in first:
        item.middle()

    for j in (0, 1):
        keys = SEQ // 2 * (j + 1)
        rows = pl.ds(j * BLOCK, BLOCK)

        def back(h, carry):
            lanes = pl.ds(aligned(h, HEAD), HEAD)
            queries, d_out = q_ref[rows, lanes], d_attn[rows, lanes]
            scores = dot(queries, k_ref[:keys, :], 1, 1) * SCALE
            scores = causal(scores, pair[j] * BLOCK)
            probs = jnp.exp(scores - lse_ref[j * HEADS + h])
            d_probs = dot(d_out, v_ref[:keys, :], 1, 1)
            inner = jnp.sum(probs * d_probs, axis=1, keepdims=True)
            d_scores = (probs * (d_probs - inner) * SCALE).astype(BF)
            d_q[rows, lanes] = dot(d_scores, k_ref[:keys, :])
            d_kv[:keys, :HEAD] += dot(d_scores, queries, 0, 0)
            d_kv[:keys, HEAD:] += dot(probs.astype(BF), d_out, 0, 0)
            return carry

        lax.fori_loop(0, HEADS, back, 0)

    kv_out[...] = d_kv[...].astype(BF)
    kv_keys = [
        [
            net.send(kv_out.at[rows_at(col + j * (7 - 2 * col)), :], kv_in.at[i, j], device)
            for j in (0, 1)
        ]
        for i, (device, col) in enumerate(peers)
    ]
    cosines = [cos_ref[rows_at(pair[j]), :] for j in (0, 1)]
    sines = [sin_ref[rows_at(pair[j]), :] for j in (0, 1)]
    for j in (0, 1):
        for h in range(HEADS):
            one = d_q[pl.ds(j * BLOCK, BLOCK), pl.ds(h * HEAD, HEAD)]
            d_qkv_all[rows_at(pair[j]), pl.ds(h * HEAD, HEAD)] = (
                one * cosines[j] - turn(one) * sines[j]
            ).astype(BF)
    for item in first:
        item.end()
    begin(last)
    down_mine.wait()
    for key, (_, col) in zip(down_keys, peers, strict=True):
        net.take(key, down_slot(at.dp, col))
    ring = ring_dp(
        net,
        at,
        (
            lambda zz, yy: [down_slot(zz * 4 + yy, pl.ds(2 * at.hi, 2))],
            lambda zz, yy: [down_slot(zz * 4 + yy, pl.ds(2 * (1 - at.hi), 2))],
        ),
    )
    next(ring)
    for key, (_, row, col) in zip(spread, others, strict=True):
        net.take(key, mid_cols.at[rows_at(block_of(row, col)), :])
    grad_out[...] = dot(attn_all[...], mid_cols[...], 0, 0).astype(BF)
    for j in (0, 1):
        total = d_kv[rows_at(pair[j]), :]
        for i in range(3):
            net.take(kv_keys[i][j], kv_in.at[i, j])
            total = total + kv_in[i, j].astype(F32)
        key = total[:, :HEAD]
        d_qkv_all[rows_at(pair[j]), pl.ds(QCOLS, HEAD)] = (
            key * cosines[j] - turn(key) * sines[j]
        ).astype(BF)
        d_qkv_all[rows_at(pair[j]), pl.ds(QCOLS + HEAD, HEAD)] = total[:, HEAD:].astype(BF)
    gather_qkv = GatherCol(net, at, d_qkv_all)
    gather_qkv.start()
    for item in last:
        item.middle()
    next(ring)

    for j in (0, 1):
        d_qkv_own[j] = d_qkv_all[rows_at(pair[j]), :]
    next(ring)
    next(ring)
    gather_qkv.middle()
    next(ring)
    gather_qkv.end()
    grad_qkv[...] = dot(n1c[...], d_qkv_all[...], 0, 0).astype(BF)
    ones = jnp.ones((8, SEQ), BF)
    bias_ref[...] = dot(ones, d_qkv_all[...])
    for item in last:
        item.end()
    drain(ring)
    net.finish()


def run_backward(*args):
    def out(shape, dtype):
        return jax.ShapeDtypeStruct(shape, dtype)

    outs = (
        out((QCOLS, FEAT), BF),
        out((FEAT, QKV), BF),
        out((8, MODEL), F32),
        out((BLOCK, MODEL), F32),
        out((2, BLOCK, QKV), BF),
        out((8, QKV), F32),
        out((4, 48, PART), BF),
        out((4, 1280, FEAT), BF),
    )
    return pl.pallas_call(
        backward_kernel,
        out_shape=outs,
        in_specs=[vmem()] * (len(args) - 3) + [anywhere()] * 2 + [vmem()],
        out_specs=[vmem()] * (len(outs) - 1) + [anywhere()],
        scratch_shapes=[
            pltpu.VMEM((SEQ, FEAT), BF),
            pltpu.VMEM((2, BLOCK, MODEL), BF),
            pltpu.VMEM((2 * BLOCK, QCOLS), BF),
            pltpu.VMEM((2 * BLOCK, QCOLS), F32),
            pltpu.VMEM((SEQ, 2 * HEAD), F32),
            pltpu.VMEM((SEQ, 2 * HEAD), BF),
            pltpu.VMEM((3, 2, BLOCK, 2 * HEAD), BF),
            pltpu.VMEM((SEQ, QKV), BF),
            pltpu.VMEM((QCOLS, MODEL), BF),
            pltpu.VMEM((2, 4, 2, 4, 48, PART), BF),
        ]
        + ring_scratch(GU_FIRST, GU_LAST)
        + [pltpu.SemaphoreType.DMA((110,)), pltpu.SemaphoreType.DMA((110,))]
        + [pltpu.SemaphoreType.DMA((4,))],
        compiler_params=pltpu.CompilerParams(
            collective_id=2, has_side_effects=True, vmem_limit_bytes=VMEM_LIMIT
        ),
        cost_estimate=pl.CostEstimate(
            flops=10 * 10**9, bytes_accessed=40 * 10**6, transcendentals=2 * 10**6
        ),
        name="attention_backward",
    )(*args)


def sums_kernel(
    gu_own,
    qkv,
    out,
    sums_ref,
    d_mid,
    d_qkv,
    bias_ref,
    xs_ref,
    gains_all,
    mid_ref,
    hidden_far,
    dw_far,
    qw_far,
    all_gu,
    all_qkv,
    all_out,
    small_out,
    out_ref,
    grad_in,
    small_y,
    small_z,
    hidden,
    dw,
    ffn,
    qw,
    part_out,
    part_in,
    gi_out,
    gi_in,
    gain_sums,
    sums_in,
    *rest,
):
    red, bufs, (send_sems, recv_sems, local_sems) = rest[:7], rest[7:-3], rest[-3:]
    at = Place()
    net = Net(send_sems, recv_sems, at)
    held = [
        pltpu.make_async_copy(qw_far, qw, local_sems.at[1]),
        pltpu.make_async_copy(hidden_far, hidden, local_sems.at[2]),
        pltpu.make_async_copy(dw_far, dw, local_sems.at[3]),
    ]
    for copy in held:
        copy.start()
    at.meet(
        (at.S, at.O, at.OS, at.N1, at.N2, at.N1S, at.N2S)
        + (at.YP, at.YM, at.ZP, at.ZM, at.Y2, at.Z2)
    )
    outs = Reduce8(net, at, *red)

    def project(j):
        row, hi = at.chips[j]
        rows = pl.ds(aligned(row, SEQ // 2), SEQ // 2)
        lanes = pl.ds(aligned(hi, QCOLS), QCOLS)
        ffn[...] = dot(hidden[rows, :], dw[:, lanes])
        if j in (0, 3):
            mine = pl.ds(pl.multiple_of((at.block - 4 * at.row) * BLOCK, BLOCK), BLOCK)
            ffn[mine, :] += mid_ref[:, lanes]
        own = ffn[:, pl.ds(aligned(at.core, FEAT), FEAT)].astype(BF)
        outs.put(j, own, ffn[:, pl.ds(aligned(1 - at.core, FEAT), FEAT)].astype(BF))
        if j:
            outs.step(j - 1)

    z, y = at.z, at.y

    def gu_piece(k, lanes):
        rows = pl.ds(pl.multiple_of((k % 8) * 48, 16), 48)
        return all_gu.at[k // 8, rows, lanes]

    def part_lanes(col):
        return pl.ds(aligned(col, PART), PART)

    def feat_lanes(col):
        return pl.ds(aligned(col, FEAT), FEAT)

    def qkv_piece(k):
        rows = pl.ds(pl.multiple_of((k % 8) * 48, 16), 48)
        return all_qkv.at[rows, pl.ds(pl.multiple_of((k // 8) * 512, 512), 512)]

    def out_piece(k):
        return all_out.at[pl.ds(pl.multiple_of(k * 48, 16), 48), :]

    peers = ((at.O, at.far), (at.OS, at.sibfar), (at.S, at.sib))
    keys = []
    for device, col in peers:
        keys.append(
            net.send(gu_own.at[col], gu_piece(at.dp, part_lanes(at.col)), device)
        )
    held[0].wait()
    part_out[...] = dot(d_qkv[1 - at.row], qw[...], 1, 1).astype(BF)
    part = net.send(part_out, part_in, at.N1)
    first, last = small_items(net, at, qkv, out, qkv_piece(at.dp), out_piece(at.dp), bufs)
    begin(first)
    own_copies = [
        pltpu.make_async_copy(
            gu_own.at[at.col], gu_piece(at.dp, part_lanes(at.col)), local_sems.at[0]
        ),
    ]
    for copy in own_copies:
        copy.start()

    def take_from(i):
        net.take(keys[i], gu_piece(at.dp, part_lanes(peers[i][1])))

    def chip_ready():
        for copy in own_copies:
            copy.wait()
        take_from(2)

    def far_ready():
        take_from(0)
        take_from(1)

    def half_of(hi):
        def half(zz, yy):
            k = zz * 4 + yy
            return [gu_piece(k, pl.ds(aligned(hi, 2 * PART), 2 * PART))]

        return half

    ring = ring_dp(
        net, at, (half_of(at.hi), half_of(1 - at.hi)), (chip_ready, far_ready)
    )
    next(ring)
    for item in first:
        item.middle()
    d_normed = dot(d_qkv[at.row], qw[...], 1, 1)
    net.take(part, part_in)
    d_normed = d_normed + part_in[...].astype(F32)
    values = xs_ref[...].astype(F32)
    scale = rms(values)
    unit = values * scale
    gain_sums[...] = sums_ref[...]
    gain_sums[0:1, :] = jnp.sum(d_normed * unit, axis=0, keepdims=True)
    bent = d_normed * gains_all[0:1, :]
    total = d_mid[...] + scale * (bent - unit * jnp.mean(bent * unit, axis=1, keepdims=True))
    gi_out[...] = total.astype(BF)

    def half_block(col):
        offset = block_of(at.row, col) - 4 * at.row
        return gi_in.at[pl.ds(pl.multiple_of(offset * BLOCK, BLOCK), BLOCK), :]

    gi_keys = [
        net.send(gi_out.at[:, feat_lanes(col)], half_block(at.col), device)
        for device, col in peers
    ]
    half_block(at.col)[...] = gi_out[:, feat_lanes(at.col)]
    others = (
        (at.S, at.row, at.sib),
        (at.N1, 1 - at.row, at.col),
        (at.N1S, 1 - at.row, at.sib),
        (at.O, at.row, at.far),
        (at.OS, at.row, at.sibfar),
        (at.N2, 1 - at.row, at.far),
        (at.N2S, 1 - at.row, at.sibfar),
    )
    sums_in[at.row * 4 + at.col] = gain_sums[:, feat_lanes(at.col)]
    sums_keys = [
        net.send(gain_sums.at[:, feat_lanes(col)], sums_in.at[at.row * 4 + at.col], device)
        for device, row, col in others
    ]
    next(ring)
    held[1].wait()
    held[2].wait()
    project(0)
    for item in first:
        item.end()
    begin(last)
    next(ring)
    project(1)
    for key, (_, row, col) in zip(sums_keys, others, strict=True):
        net.take(key, sums_in.at[row * 4 + col])
    total = sums_in[0]
    for i in range(1, 8):
        total = total + sums_in[i]
    small_y[y, :, :FEAT] = total
    small_y[y, :, FEAT:] = bias_ref[...]
    small_keys = [net.send(small_y.at[y], small_y.at[y], d) for d in (at.YP, at.YM, at.Y2)]
    for item in last:
        item.middle()
    next(ring)
    project(2)
    for key, k in zip(small_keys, (y - 1, y + 1, y + 2), strict=True):
        net.take(key, small_y.at[lax.rem(k + 4, 4)])
    small_z[z] = (small_y[0] + small_y[1]) + (small_y[2] + small_y[3])
    small_keys = [net.send(small_z.at[z], small_z.at[z], d) for d in (at.ZP, at.ZM, at.Z2)]
    for item in last:
        item.end()
    after = ring_dp(
        net,
        at,
        (lambda zz, yy: [qkv_piece(zz * 4 + yy)], lambda zz, yy: [out_piece(zz * 4 + yy)]),
    )
    next(after)
    next(ring)
    project(3)
    next(after)
    for key, k in zip(small_keys, (z - 1, z + 1, z + 2), strict=True):
        net.take(key, small_z.at[lax.rem(k + 4, 4)])
    small_out[...] = (small_z[0] + small_z[1]) + (small_z[2] + small_z[3])
    for key, (_, col) in zip(gi_keys, peers, strict=True):
        net.take(key, half_block(col))
    grad_in[...] = gi_in[...].astype(F32)
    for _ in ring:
        next(after, None)
    drain(after)
    out_ref[...] = outs.step(3)
    net.finish()


def run_sums(gu, qkv, out, *args):
    def shape(dims, dtype):
        return jax.ShapeDtypeStruct(dims, dtype)

    outs = (
        shape((2, FEAT, 4 * PART), BF),
        shape((FEAT, QKV), BF),
        shape((QCOLS, FEAT), BF),
        shape((8, FEAT + QKV), F32),
        shape((SEQ // 2, FEAT), F32),
        shape((SEQ // 2, FEAT), F32),
    )
    return pl.pallas_call(
        sums_kernel,
        out_shape=outs,
        in_specs=[vmem()] * len(args) + [anywhere()] * 3,
        out_specs=[anywhere()] + [vmem()] * 5,
        scratch_shapes=[pltpu.VMEM((4, 8, FEAT + QKV), F32)] * 2
        + [
            pltpu.VMEM((SEQ, PART), BF),
            pltpu.VMEM((PART, MODEL), BF),
            pltpu.VMEM((SEQ // 2, QCOLS), F32),
            pltpu.VMEM((MODEL, QKV), BF),
            pltpu.VMEM((BLOCK, MODEL), BF),
            pltpu.VMEM((BLOCK, MODEL), BF),
            pltpu.VMEM((BLOCK, MODEL), BF),
            pltpu.VMEM((SEQ // 2, FEAT), BF),
            pltpu.VMEM((8, MODEL), F32),
            pltpu.VMEM((8, 8, FEAT), F32),
        ]
        + reduce8_scratch(SEQ // 2, FEAT)
        + ring_scratch(SMALL_FIRST, SMALL_LAST)
        + [pltpu.SemaphoreType.DMA((128,)), pltpu.SemaphoreType.DMA((128,))]
        + [pltpu.SemaphoreType.DMA((4,))],
        compiler_params=pltpu.CompilerParams(
            collective_id=3, has_side_effects=True, vmem_limit_bytes=VMEM_LIMIT
        ),
        cost_estimate=pl.CostEstimate(
            flops=4 * 10**9, bytes_accessed=60 * 10**6, transcendentals=0
        ),
        name="sums_over_sequences",
    )(gu, qkv, out, *args)


def widen_kernel(
    gu,
    down,
    qkv,
    out,
    small,
    gate_out,
    up_out,
    down_out,
    query_out,
    key_out,
    value_out,
    proj_out,
    gain1_out,
    gain2_out,
    bq_out,
    bk_out,
    bv_out,
    gu_in,
    down_in,
    gate_buf,
    up_buf,
    down_buf,
    in_sems,
    out_sems,
):
    skip = 3 * PART

    def loads(n):
        place = n % 2
        rows = pl.ds(640 * (n % 2), 640)
        return [
            pltpu.make_async_copy(gu.at[:, pl.ds(n * 48, 48), :], gu_in.at[place], in_sems.at[place, 0]),
            pltpu.make_async_copy(down.at[n // 2, rows, :], down_in.at[place], in_sems.at[place, 1]),
        ]

    def stores(n):
        place, quarter, part = n % 2, n // 2, n % 2
        rows = pl.ds(n * 48, 48)
        drop = HEAD if quarter == 3 and part == 0 else 0
        start = PART * quarter + 576 * part - (HEAD if quarter == 3 and part == 1 else 0)
        return [
            pltpu.make_async_copy(gate_buf.at[place], gate_out.at[rows, :], out_sems.at[place, 0]),
            pltpu.make_async_copy(up_buf.at[place], up_out.at[rows, :], out_sems.at[place, 1]),
            pltpu.make_async_copy(
                down_buf.at[place, pl.ds(drop, 576 - drop), :],
                down_out.at[pl.ds(start, 576 - drop), :],
                out_sems.at[place, 2],
            ),
        ]

    def run(copies):
        for copy in copies:
            copy.start()
        return copies

    def wait(copies):
        for copy in copies:
            copy.wait()

    arriving = {0: run(loads(0)), 1: run(loads(1))}
    query_out[...] = qkv[:, :QCOLS].astype(F32)
    key_out[...] = qkv[:, QCOLS : QCOLS + HEAD].astype(F32)
    value_out[...] = qkv[:, QCOLS + HEAD :].astype(F32)
    proj_out[...] = out[...].astype(F32)
    first = 0
    for ref, row, width in (
        (gain1_out, 0, FEAT),
        (bq_out, 0, QCOLS),
        (bk_out, 0, HEAD),
        (bv_out, 0, HEAD),
    ):
        ref[...] = small[row, first : first + width]
        first += width
    gain2_out[...] = small[1, :FEAT]
    leaving = {}
    for n in range(8):
        place = n % 2
        wait(arriving[n])
        if n > 1:
            wait(leaving[n - 2])
        for i, buf in enumerate((gate_buf, up_buf)):
            buf[place, :, :skip] = gu_in[place, i, :, :skip].astype(F32)
            buf[place, :, skip:] = gu_in[place, i, :, skip + HEAD :].astype(F32)
        for m in range(4):
            down_buf[place, pl.ds(144 * m, 80), :] = down_in[
                place, pl.ds(160 * m, 80), :
            ].astype(F32)
            down_buf[place, pl.ds(144 * m + 80, 64), :] = down_in[
                place, pl.ds(160 * m + 96, 64), :
            ].astype(F32)
        leaving[n] = run(stores(n))
        if n + 2 < 8:
            arriving[n + 2] = run(loads(n + 2))
    wait(leaving[6])
    wait(leaving[7])


def run_widen(gu, down, qkv, out, small):
    shapes = [(FEAT, UNITS)] * 2 + [(UNITS, FEAT)]
    shapes += [(FEAT, QCOLS), (FEAT, HEAD), (FEAT, HEAD), (QCOLS, FEAT)]
    shapes += [(FEAT,), (FEAT,), (QCOLS,), (HEAD,), (HEAD,)]
    return pl.pallas_call(
        widen_kernel,
        out_shape=[jax.ShapeDtypeStruct(dims, F32) for dims in shapes],
        in_specs=[anywhere()] * 2 + [vmem()] * 3,
        out_specs=[anywhere()] * 3 + [vmem()] * 9,
        scratch_shapes=[
            pltpu.VMEM((2, 2, 48, 4 * PART), BF),
            pltpu.VMEM((2, 640, FEAT), BF),
            pltpu.VMEM((2, 48, UNITS), F32),
            pltpu.VMEM((2, 48, UNITS), F32),
            pltpu.VMEM((2, 576, FEAT), F32),
            pltpu.SemaphoreType.DMA((2, 2)),
            pltpu.SemaphoreType.DMA((2, 3)),
        ],
        compiler_params=pltpu.CompilerParams(vmem_limit_bytes=VMEM_LIMIT),
        cost_estimate=pl.CostEstimate(
            flops=10**7, bytes_accessed=36 * 10**6, transcendentals=0
        ),
        name="widen",
    )(gu, down, qkv, out, small)


def rope_tables(count):
    places = np.arange(count, dtype=np.float32)
    inverse = (1.0 / THETA ** (np.arange(0, HEAD, 2) / HEAD)).astype(np.float32)
    angles = places[:, None] * inverse[None, :]
    cosine, sine = np.cos(angles), np.sin(angles)
    tables = np.concatenate([cosine, cosine], axis=-1), np.concatenate([-sine, sine], axis=-1)
    return tuple(jnp.asarray(table, F32) for table in tables)


def body(
    layer_input,
    gain_attn,
    w_query,
    w_key,
    w_value,
    b_query,
    b_key,
    b_value,
    w_out,
    gain_ffn,
    w_gate,
    w_up,
    w_down,
    out_grad,
):
    cosine, sine = rope_tables(SEQ)
    bias = jnp.concatenate([b_query, b_key, b_value]).astype(F32)[None]
    gains = jnp.zeros((8, FEAT), F32).at[0].set(gain_attn.astype(F32)).at[1].set(gain_ffn.astype(F32))
    (
        xs,
        normed1_cols,
        grads_block,
        qkv_w,
        out_w,
        queries,
        key,
        value,
        lse,
        attn,
        mid,
        gains_all,
        dn2,
        hidden,
        down_w,
        grad_gu,
        grad_down,
    ) = run_forward(
        layer_input,
        out_grad,
        w_query,
        w_key,
        w_value,
        w_out,
        w_gate,
        w_up,
        w_down,
        gains,
        bias,
        cosine,
        sine,
    )
    grad_out, grad_qkv, sums, d_mid, d_qkv, bias_sums, grad_gu, grad_down = run_backward(
        dn2,
        mid,
        grads_block,
        gains_all,
        normed1_cols,
        attn,
        queries,
        key,
        value,
        lse,
        cosine,
        sine,
        out_w,
        grad_gu.reshape(2, 4, 2, 4, 48, PART),
        grad_down,
    )
    grad_gu, grad_qkv, grad_out, small, layer_output, grad_input = run_sums(
        grad_gu,
        grad_qkv.reshape(2, 4, 48, QKV),
        grad_out.reshape(2, 2, 4, 48, FEAT),
        sums,
        d_mid,
        d_qkv,
        bias_sums,
        xs,
        gains_all,
        mid,
        hidden,
        down_w,
        qkv_w,
    )
    (
        grad_gate,
        grad_up,
        grad_down,
        grad_query,
        grad_key,
        grad_value,
        grad_out,
        *vectors,
    ) = run_widen(grad_gu, grad_down, grad_qkv, grad_out, small)
    gain1, gain2, bias_query, bias_key, bias_value = vectors
    return (
        layer_output,
        grad_input,
        gain1,
        grad_query,
        grad_key,
        grad_value,
        bias_query,
        bias_key,
        bias_value,
        grad_out,
        gain2,
        grad_gate,
        grad_up,
        grad_down,
    )


def solution(mesh):
    in_specs = (
        P(("dp", "row"), "col"),
        P("col"),
        P("col", "row"),
        P("col", "row"),
        P("col", "row"),
        P("row"),
        P("row"),
        P("row"),
        P("row", "col"),
        P("col"),
        P("col", "row"),
        P("col", "row"),
        P("row", "col"),
        P(("dp", "row"), "col"),
    )
    out_specs = (
        P(("dp", "row"), "col"),
        P(("dp", "row"), "col"),
        P("col"),
        P("col", "row"),
        P("col", "row"),
        P("col", "row"),
        P("row"),
        P("row"),
        P("row"),
        P("row", "col"),
        P("col"),
        P("col", "row"),
        P("col", "row"),
        P("row", "col"),
    )
    return jax.shard_map(body, mesh=mesh, in_specs=in_specs, out_specs=out_specs, check_vma=False)
```

```python
import functools

import jax
import jax.numpy as jnp
import numpy as np
from jax import lax
from jax.experimental import pallas as pl
from jax.experimental.pallas import tpu as pltpu
from jax.sharding import PartitionSpec as P

EPS = 1e-06
THETA = 1000000.0
NEG = -1e30
BF = jnp.bfloat16
F32 = jnp.float32
MESH = pl.DeviceIdType.MESH
HEAD = 128
HEADS = 6
SEQ = 1024
MODEL = 1536
FEAT = 384
BLOCK = 128
UNITS = 4480
PART = 1152
QCOLS = 768
QKV = 1024
VMEM_LIMIT = 62 * 2**20
SCALE = HEAD ** (-0.5)


def dot(left, right, left_dim=1, right_dim=0):
    return lax.dot_general(
        left, right, (((left_dim,), (right_dim,)), ((), ())), preferred_element_type=F32
    )


def aligned(index, step):
    return pl.multiple_of(index * step, step)


def block_of(row, col):
    return col + row * (7 - 2 * col)


def quarter_start(col):
    return pl.multiple_of(col * PART - (col // 3) * HEAD, HEAD)


class Place:
    def __init__(self):
        self.dp, self.row, self.col = (lax.axis_index(a) for a in ("dp", "row", "col"))
        self.hi, self.core = self.col // 2, self.col % 2
        self.z, self.y = self.dp // 4, self.dp % 4
        self.sib = 2 * self.hi + 1 - self.core
        self.far = 2 * (1 - self.hi) + self.core
        self.sibfar = 2 * (1 - self.hi) + 1 - self.core
        self.block = block_of(self.row, self.col)
        self.chips = (
            (self.row, 1 - self.hi),
            (1 - self.row, self.hi),
            (1 - self.row, 1 - self.hi),
            (self.row, self.hi),
        )
        self.S = {"col": self.sib}
        self.O = {"col": self.far}
        self.OS = {"col": self.sibfar}
        self.N1 = {"row": 1 - self.row}
        self.N2 = {"row": 1 - self.row, "col": self.far}
        self.N1S = {"row": 1 - self.row, "col": self.sib}
        self.N2S = {"row": 1 - self.row, "col": self.sibfar}

        def dp_at(z, y):
            return {"dp": lax.rem(z + 4, 4) * 4 + lax.rem(y + 4, 4)}

        self.YP, self.YM = dp_at(self.z, self.y + 1), dp_at(self.z, self.y - 1)
        self.Y2, self.Z2 = dp_at(self.z, self.y + 2), dp_at(self.z + 2, self.y)
        self.ZP, self.ZM = dp_at(self.z + 1, self.y), dp_at(self.z - 1, self.y)

    def meet(self, partners):
        barrier = pltpu.get_barrier_semaphore()
        for device in partners:
            pl.semaphore_signal(barrier, inc=1, device_id=device, device_id_type=MESH)
        pl.semaphore_wait(barrier, len(partners))


class Net:
    def __init__(self, send_sems, recv_sems, at):
        self.ss, self.rs, self.at, self.count, self.sent = send_sems, recv_sems, at, 0, []

    def key(self):
        self.count += 1
        return self.count - 1

    def copy(self, key, src, dst, device):
        return pltpu.make_async_remote_copy(
            src_ref=src,
            dst_ref=dst,
            send_sem=self.ss.at[key],
            recv_sem=self.rs.at[key],
            device_id=device,
            device_id_type=MESH,
        )

    def send(self, src, dst, device):
        key = self.key()
        copy = self.copy(key, src, dst, device)
        copy.start()
        self.sent.append(copy)
        return key

    def take(self, key, dst):
        self.copy(key, dst, dst, self.at.S).wait_recv()

    def finish(self, copies=None):
        copies = list(self.sent) if copies is None else copies
        for copy in copies:
            copy.wait_send()
            self.sent.remove(copy)


class Gather8:
    def __init__(self, net, at, place):
        self.net, self.at, self.place = net, at, place

    def start(self, src):
        net, at = self.net, self.at
        mine = self.place(at.row, at.col, None)
        self.k1 = net.send(src, mine, at.N1)
        self.k2 = net.send(src, mine, at.N2)
        self.k0 = net.send(src, mine, at.S)

    def middle(self):
        net, at, place = self.net, self.at, self.place
        near, away = place(1 - at.row, at.col, None), place(1 - at.row, at.far, None)
        first, last = place(1 - at.row, at.col, 0), place(1 - at.row, at.far, 1)
        net.take(self.k1, near)
        self.ka = net.send(first, first, at.N2)
        self.f1 = net.send(near, near, at.S)
        net.take(self.k2, away)
        self.kb = net.send(last, last, at.N1)
        self.f2 = net.send(away, away, at.S)

    def late(self):
        net, at, place = self.net, self.at, self.place
        first, last = place(at.row, at.far, 0), place(at.row, at.far, 1)
        net.take(self.ka, first)
        self.f3 = net.send(first, first, at.S)
        net.take(self.kb, last)
        self.f4 = net.send(last, last, at.S)

    def end(self, chip=None):
        net, at, place = self.net, self.at, self.place
        if chip in (None, 3):
            net.take(self.k0, place(at.row, at.sib, None))
        if chip in (None, 1):
            net.take(self.f1, place(1 - at.row, at.sib, None))
        if chip in (None, 2):
            net.take(self.f2, place(1 - at.row, at.sibfar, None))
        if chip in (None, 0):
            net.take(self.f3, place(at.row, at.sibfar, 0))
            net.take(self.f4, place(at.row, at.sibfar, 1))


def ring_dp(net, at, halves, ready=(None, None)):
    def wrap(index):
        return lax.rem(index + 4, 4)

    sides = (((at.YP, at.YM), (at.ZP, at.ZM)), ((at.ZP, at.ZM), (at.YP, at.YM)))
    firsts, seconds = (at.y, at.z), (at.z, at.y)

    def refs(i, a, b):
        return halves[i](b, a) if i == 0 else halves[i](a, b)

    def send(i, a, b, device):
        return [net.send(ref, ref, device) for ref in refs(i, a, b)]

    def take(i, a, b, keys):
        for key, ref in zip(keys, refs(i, a, b), strict=True):
            net.take(key, ref)

    one, two, onward = {}, {}, {}
    for i in (0, 1):
        if ready[i]:
            ready[i]()
        one[i] = [send(i, firsts[i], seconds[i], side) for side in sides[i][0]]
        if ready[i]:
            two[i, 0] = [send(i, firsts[i], seconds[i], side) for side in sides[i][1]]
    for i in (0, 1):
        if not ready[i]:
            two[i, 0] = [send(i, firsts[i], seconds[i], side) for side in sides[i][1]]
    yield
    for i in (0, 1):
        minus = wrap(firsts[i] - 1)
        take(i, minus, seconds[i], one[i][0])
        one[i].append(send(i, minus, seconds[i], sides[i][0][0]))
        two[i, 1] = [send(i, minus, seconds[i], side) for side in sides[i][1]]
    yield
    for i in (0, 1):
        plus = wrap(firsts[i] + 1)
        take(i, plus, seconds[i], one[i][1])
        two[i, 2] = [send(i, plus, seconds[i], side) for side in sides[i][1]]
    offsets = (0, -1, 1, 2)
    for q in (0, 1, 2, 3):
        yield
        for i in (0, 1):
            if q == 1:
                across = wrap(firsts[i] + 2)
                take(i, across, seconds[i], one[i][2])
                two[i, 3] = [send(i, across, seconds[i], side) for side in sides[i][1]]
            slot = wrap(firsts[i] + offsets[q])
            minus, plus = wrap(seconds[i] - 1), wrap(seconds[i] + 1)
            take(i, slot, minus, two[i, q][0])
            if q < 2:
                onward[i, q] = send(i, slot, minus, sides[i][1][0])
            take(i, slot, plus, two[i, q][1])
            if q >= 2:
                onward[i, q] = send(i, slot, plus, sides[i][1][1])
    for q in (0, 1, 2, 3):
        yield
        for i in (0, 1):
            slot = wrap(firsts[i] + offsets[q])
            take(i, slot, wrap(seconds[i] + 2), onward[i, q])


def drain(steps):
    for _ in steps:
        pass


def rms(values):
    return lax.rsqrt(jnp.mean(values * values, axis=1, keepdims=True) + EPS)


def turn(values):
    return pltpu.roll(values, HEAD // 2, 1)


def causal(scores, start):
    places = start + lax.broadcasted_iota(jnp.int32, scores.shape, 0)
    keys = lax.broadcasted_iota(jnp.int32, scores.shape, 1)
    return jnp.where(keys <= places, scores, NEG)


def vmem():
    return pl.BlockSpec(memory_space=pltpu.VMEM)


def anywhere():
    return pl.BlockSpec(memory_space=pl.ANY)


class GatherCol:
    def __init__(self, net, at, array):
        self.net, self.at, self.array = net, at, array

    def rows(self, col, j):
        return self.array.at[pl.ds(aligned(col + j * (7 - 2 * col), BLOCK), BLOCK), :]

    def start(self):
        net, at = self.net, self.at
        mine = [self.rows(at.col, j) for j in (0, 1)]
        self.far = [net.send(ref, ref, at.O) for ref in mine]
        self.sib = [net.send(ref, ref, at.S) for ref in mine]

    def middle(self):
        net, at = self.net, self.at
        self.onward = []
        for j in (0, 1):
            ref = self.rows(at.far, j)
            net.take(self.far[j], ref)
            self.onward.append(net.send(ref, ref, at.S))

    def end(self):
        net, at = self.net, self.at
        for j in (0, 1):
            net.take(self.sib[j], self.rows(at.sib, j))
            net.take(self.onward[j], self.rows(at.sibfar, j))


class Reduce8:
    def __init__(self, net, at, own, other, sib_in, first_in, last_in, near_in, away_in):
        self.net, self.at, self.own, self.other, self.sib_in = net, at, own, other, sib_in
        self.first_in, self.last_in, self.near_in, self.away_in = first_in, last_in, near_in, away_in
        self.half = own.shape[1] // 2
        self.keys = {}

    def put(self, j, mine, theirs):
        self.own[j] = mine
        self.other[j] = theirs
        self.keys[j] = self.net.send(self.other.at[j], self.sib_in.at[j], self.at.S)

    def step(self, j):
        net, at, half = self.net, self.at, self.half
        net.take(self.keys[j], self.sib_in.at[j])
        total = self.own[j].astype(F32) + self.sib_in[j].astype(F32)
        if j == 0:
            self.own[j] = total.astype(BF)
            self.first = net.send(self.own.at[j, pl.ds(0, half)], self.first_in, at.N1)
            self.last = net.send(self.own.at[j, pl.ds(half, half)], self.last_in, at.N2)
        elif j == 1:
            net.take(self.last, self.last_in)
            self.own[j, :half] = total[:half].astype(BF)
            self.own[j, half:] = (total[half:] + self.last_in[...].astype(F32)).astype(BF)
            self.near = net.send(self.own.at[j], self.near_in, at.N1)
        elif j == 2:
            net.take(self.first, self.first_in)
            self.own[j, :half] = (total[:half] + self.first_in[...].astype(F32)).astype(BF)
            self.own[j, half:] = total[half:].astype(BF)
            self.away = net.send(self.own.at[j], self.away_in, at.N2)
        else:
            net.take(self.near, self.near_in)
            net.take(self.away, self.away_in)
            return total + self.near_in[...].astype(F32) + self.away_in[...].astype(F32)
        return None


def reduce8_scratch(rows, columns):
    return [
        pltpu.VMEM((4, rows, columns), BF),
        pltpu.VMEM((4, rows, columns), BF),
        pltpu.VMEM((4, rows, columns), BF),
        pltpu.VMEM((rows // 2, columns), BF),
        pltpu.VMEM((rows // 2, columns), BF),
        pltpu.VMEM((rows, columns), BF),
        pltpu.VMEM((rows, columns), BF),
    ]


def tiles_of(width, step):
    return [(first, min(step, width - first)) for first in range(0, width, step)]


def add_up(out, terms):
    lead = out.shape[:-2]
    if not lead:
        total = terms[0][...].astype(F32)
        for term in terms[1:]:
            total = total + term[...].astype(F32)
        out[...] = total.astype(out.dtype)
        return
    count = 1
    for size in lead:
        count *= size

    def step(i, carry):
        index = []
        for size in reversed(lead):
            index.insert(0, i % size)
            i = i // size
        index = tuple(index)
        total = terms[0].at[index][...].astype(F32)
        for term in terms[1:]:
            total = total + term.at[index][...].astype(F32)
        out.at[index][...] = total.astype(out.dtype)
        return carry

    lax.fori_loop(0, count, step, 0)


class RingItem:
    def __init__(self, net, sides, place, part, held, way, bufs, own):
        self.net, self.part, self.held, self.own = net, part, held, own
        self.relay, self.staged, self.from_last, self.from_next = bufs
        self.onward, self.back = (sides[0], sides[1]) if way == 0 else (sides[1], sides[0])
        step = 1 - 2 * way
        self.here, self.next, self.across, self.last = (
            lax.rem(place + 4 + step * i, 4) for i in (0, 1, 2, 3)
        )

    def start(self):
        self.k_relay = self.net.send(self.part(self.across), self.relay, self.onward)

    def direct(self):
        self.k_next = self.net.send(self.part(self.last), self.from_next, self.back)

    def middle(self):
        self.net.take(self.k_relay, self.relay)
        add_up(self.staged, [self.held(self.next), self.relay])
        self.k_last = self.net.send(self.staged, self.from_last, self.onward)

    def end(self):
        self.net.take(self.k_next, self.from_next)
        self.net.take(self.k_last, self.from_last)
        add_up(self.own, [self.held(self.here), self.from_next, self.from_last])


def begin(items):
    for item in items:
        item.start()
    for item in items:
        item.direct()


LEFT, RIGHT = pl.ds(0, QCOLS), pl.ds(QCOLS, QCOLS)
GU_FIRST = (((2, 2, 48, PART),), ((2, 2, 48, PART),))
GU_LAST = (((48, PART),) * 2,) * 2
DOWN_FIRST = (((2, 80, QCOLS),), ((144, QCOLS),))
DOWN_LAST = (((80, QCOLS),),) * 2
SMALL_FIRST = (((2, 48, 512),), ((2, 48, FEAT),))
SMALL_LAST = (((48, 512),), ((48, FEAT),))


def down_rows(k):
    return pl.ds(pl.multiple_of(72 * k - 8 * (k % 2), 16), 80)


def ring_scratch(first, last):
    scratch = []
    for i in (0, 1):
        for dims in first[i]:
            scratch += [pltpu.VMEM(dims, BF)] * 8
            scratch.append(pltpu.VMEM((2,) + dims, BF))
        for dims in last[i]:
            scratch += [pltpu.VMEM(dims, BF)] * 4
    return scratch


def ring_items(net, at, first, last, parts, helds, seconds, finals, bufs):
    sides = (((at.YP, at.YM), (at.ZP, at.ZM)), ((at.ZP, at.ZM), (at.YP, at.YM)))
    places = ((at.y, at.z), (at.z, at.y))
    bufs = list(bufs)
    one, two = ([], []), ([], [])
    for i in (0, 1):
        owns = []
        for n in range(len(first[i])):
            own = bufs[8]
            for way in (0, 1):
                part = functools.partial(lambda k, f, w: f(k, w), f=parts[i][n], w=way)
                held = functools.partial(lambda k, f, w: f(k, w), f=helds[i][n], w=way)
                four = bufs[4 * way : 4 * way + 4]
                one[i].append(
                    RingItem(net, sides[i][0], places[i][0], part, held, way, four, own.at[way])
                )
            owns.append(own)
            bufs = bufs[9:]
        for n in range(len(last[i])):
            part = functools.partial(lambda k, f, o: f(o, k), f=seconds[i][n], o=owns[min(n, len(owns) - 1)])
            two[i].append(
                RingItem(net, sides[i][1], places[i][1], part, part, n % 2, bufs[:4], finals[i][n])
            )
            bufs = bufs[4:]

    def mix(pair):
        return [item for items in zip(*pair, strict=True) for item in items]

    return mix(one), mix(two)


def gu_items(net, at, far_ref, near_ref, gu_own, bufs):
    def parts_of(gu):
        return (
            (lambda k, way: gu.at[way, pl.ds(0, 2), :, k],),
            (lambda k, way: gu.at[k // 2, pl.ds(2, 2), k % 2, pl.ds(2 * way, 2)],),
        )

    seconds = (
        (lambda own, k: own.at[k // 2, 0, k % 2], lambda own, k: own.at[k // 2, 1, k % 2]),
    ) * 2
    finals = ((gu_own.at[0], gu_own.at[1]), (gu_own.at[2], gu_own.at[3]))
    helds = parts_of(near_ref)
    return ring_items(net, at, GU_FIRST, GU_LAST, parts_of(far_ref), helds, seconds, finals, bufs)


def down_items(net, at, down, down_own, bufs):
    parts = (
        (lambda k, way: down.at[way, :, down_rows(k), LEFT],),
        (lambda k, way: down.at[k // 2, k % 2, pl.ds(144 * way, 144), RIGHT],),
    )
    seconds = (
        (lambda own, k: own.at[k // 2, k % 2],),
        (lambda own, k: own.at[k // 2, pl.ds(pl.multiple_of((k % 2) * 64, 64), 80)],),
    )
    finals = ((down_own.at[:, LEFT],), (down_own.at[:, RIGHT],))
    return ring_items(net, at, DOWN_FIRST, DOWN_LAST, parts, parts, seconds, finals, bufs)


def small_items(net, at, qkv, out, qkv_own, out_own, bufs):
    parts = (
        (lambda k, way: qkv.at[:, k, :, pl.ds(512 * way, 512)],),
        (lambda k, way: out.at[k // 2, k % 2, pl.ds(2 * way, 2)],),
    )
    seconds = ((lambda own, k: own.at[k // 2, k % 2],), (lambda own, k: own.at[k // 2, k % 2],))
    finals = ((qkv_own,), (out_own,))
    return ring_items(net, at, SMALL_FIRST, SMALL_LAST, parts, parts, seconds, finals, bufs)


def forward_kernel(
    x_ref,
    og_ref,
    wq_ref,
    wk_ref,
    wv_ref,
    wout_ref,
    wg_ref,
    wu_ref,
    wd_ref,
    bias_ref,
    cos_ref,
    sin_ref,
    xs_ref,
    n1c_ref,
    og_out,
    qw_out,
    ow_out,
    q_ref,
    k_ref,
    v_ref,
    lse_ref,
    attn_all,
    mid_ref,
    gains_all,
    dn2_ref,
    hidden_out,
    dw_out,
    grad_gu,
    down_own,
    wqkv_ref,
    x_all,
    n1,
    og_all,
    n2_all,
    qw,
    ow,
    gw,
    uw,
    dw,
    part_out,
    part_in,
    d_up,
    tile_buf,
    down,
    attn_ref,
    gains_ref,
    *rest,
):
    red_a, bufs, sems = rest[:7], rest[7:-4], rest[-4:]
    send_sems, recv_sems, local_sems, tile_sems = sems
    at = Place()
    net = Net(send_sems, recv_sems, at)
    local, local_count = [], iter(range(32))

    def move(src, dst):
        copy = pltpu.make_async_copy(src, dst, local_sems.at[next(local_count)])
        copy.start()
        local.append(copy)
        return copy

    gains_ref[...] = jnp.zeros_like(gains_ref)
    for i in (0, 1):
        gains_ref[i : i + 1, :] = bias_ref[:, QKV + i * FEAT : QKV + (i + 1) * FEAT]
    joined = [
        move(wq_ref, wqkv_ref.at[:, pl.ds(0, QCOLS)]),
        move(wk_ref, wqkv_ref.at[:, pl.ds(QCOLS, HEAD)]),
        move(wv_ref, wqkv_ref.at[:, pl.ds(QCOLS + HEAD, HEAD)]),
    ]
    at.meet((at.S, at.N1, at.N2, at.O, at.OS, at.YP, at.YM, at.ZP, at.ZM))
    for copy in joined:
        copy.wait()
    local.clear()

    def tokens_of(array):
        def place(row, col, part):
            if part is None:
                rows = pl.ds(aligned(row, SEQ // 2), SEQ // 2)
            else:
                rows = pl.ds(aligned(row * 2 + part, SEQ // 4), SEQ // 4)
            return array.at[rows, pl.ds(aligned(col, FEAT), FEAT)]

        return place

    mine, mine_far = aligned(at.col, FEAT), aligned(1 - at.hi, 2 * FEAT)
    move(x_ref, tokens_of(x_all)(at.row, at.col, None))
    move(wqkv_ref, qw.at[pl.ds(mine, FEAT), :])
    move(wout_ref, ow.at[:, pl.ds(mine, FEAT)])
    move(gains_ref, gains_all.at[:, pl.ds(mine, FEAT)])
    start = quarter_start(at.col)
    move(wg_ref.at[:, pl.ds(start, PART)], gw.at[pl.ds(mine, FEAT), :])
    move(wu_ref.at[:, pl.ds(start, PART)], uw.at[pl.ds(mine, FEAT), :])
    move(wd_ref.at[pl.ds(start, PART), :], dw.at[:, pl.ds(mine, FEAT)])
    move(og_ref, tokens_of(og_all)(at.row, at.col, None))

    eighth = at.dp % 8
    across = [net.key() for _ in range(5)]

    def slice_copies(core, first, last):
        device = {"col": 2 * (1 - at.hi) + core}
        rows = pl.ds(aligned(eighth, 48), 48)
        target = pl.ds(pl.multiple_of(mine + eighth * 48, 16), 48)
        columns = pl.ds(core * 512, 512)
        out_rows = pl.ds(pl.multiple_of(core * FEAT + eighth * 48, 16), 48)
        theirs = quarter_start(2 * (1 - at.hi) + core)
        down_rows = pl.ds(pl.multiple_of(theirs + eighth * 144, 16), 144)
        down_target = pl.ds(aligned(eighth, 144), 144)
        pairs = (
            (wqkv_ref.at[rows, columns], qw.at[target, columns]),
            (wout_ref.at[out_rows, :], ow.at[out_rows, pl.ds(mine, FEAT)]),
            (wg_ref.at[rows, pl.ds(theirs, PART)], gw.at[target, :]),
            (wu_ref.at[rows, pl.ds(theirs, PART)], uw.at[target, :]),
            (wd_ref.at[down_rows, :], dw.at[down_target, pl.ds(mine, FEAT)]),
        )
        return [
            pltpu.make_async_remote_copy(
                src_ref=pairs[i][0],
                dst_ref=pairs[i][1],
                send_sem=net.ss.at[spare[core][i]],
                recv_sem=net.rs.at[across[i]],
                device_id=device,
                device_id_type=MESH,
            )
            for i in range(first, last)
        ]

    spare = ([net.key() for _ in range(5)], [net.key() for _ in range(5)])
    chosen = at.core == at.dp // 8

    @pl.when(chosen)
    def _():
        for core in (0, 1):
            for copy in slice_copies(core, 0, 2):
                copy.start()

    gather_x = Gather8(net, at, tokens_of(x_all))
    gather_x.start(x_ref)
    gain_far = net.send(gains_ref, gains_all.at[:, pl.ds(mine, FEAT)], at.N2)
    gain_sib = net.send(gains_ref, gains_all.at[:, pl.ds(mine, FEAT)], at.S)
    near_qw = net.send(wqkv_ref, qw.at[pl.ds(mine, FEAT), :], at.S)
    near_ow = net.send(wout_ref, ow.at[:, pl.ds(mine, FEAT)], at.S)

    @pl.when(chosen)
    def _():
        for core in (0, 1):
            for copy in slice_copies(core, 2, 5):
                copy.start()

    far_half = pl.ds(mine_far, 2 * FEAT)

    def qkv_slices(z, y):
        rows = pl.ds(pl.multiple_of(mine_far + (z * 4 + y) * 48, 16), 48)
        return [qw.at[rows, pl.ds(aligned(at.core, 512), 512)]]

    def out_slices(z, y):
        index = z * 4 + y
        rows = pl.ds(pl.multiple_of(at.core * FEAT + (index % 8) * 48, 16), 48)
        return [ow.at[rows, pl.ds(pl.multiple_of(mine_far + (index // 8) * FEAT, HEAD), FEAT)]]

    def rows_of(weights):
        def slices(z, y):
            return [weights.at[pl.ds(pl.multiple_of(mine_far + (z * 4 + y) * 48, 16), 48), :]]

        return slices

    def down_of(first, count):
        def slices(z, y):
            index = z * 4 + y
            rows = pl.ds(pl.multiple_of((index % 8) * 144 + first, 16), count)
            lanes = pl.ds(pl.multiple_of(mine_far + (index // 8) * FEAT, HEAD), FEAT)
            return [dw.at[rows, lanes]]

        return slices

    def ffn_rings():
        down = ring_dp(net, at, (down_of(0, 80), down_of(80, 64)))
        both = ring_dp(net, at, (rows_of(gw), rows_of(uw)))
        for _ in range(3):
            next(down)
            yield
        next(both)
        yield
        yield from down
        yield
        yield from both

    net.take(across[0], qkv_slices(at.z, at.y)[0])
    net.take(across[1], out_slices(at.z, at.y)[0])
    ring = ring_dp(net, at, (qkv_slices, out_slices))
    next(ring)
    next(ring)
    next(ring)
    gather_x.middle()
    gains_far = gains_all.at[:, pl.ds(aligned(at.far, FEAT), FEAT)]
    net.take(gain_far, gains_far)
    gain_sibfar = net.send(gains_far, gains_far, at.S)
    next(ring)
    cols_half, rows_half = pl.ds(aligned(at.core, 512), 512), pl.ds(aligned(at.core, FEAT), FEAT)
    gather_og = Gather8(net, at, tokens_of(og_all))
    gather_x.late()

    drain(ring)
    far_qw = net.send(qw.at[far_half, cols_half], qw.at[far_half, cols_half], at.S)
    far_ow = net.send(ow.at[rows_half, far_half], ow.at[rows_half, far_half], at.S)
    net.take(across[2], rows_of(gw)(at.z, at.y)[0])
    net.take(across[3], rows_of(uw)(at.z, at.y)[0])
    net.take(across[4], down_of(0, 144)(at.z, at.y)[0])
    ring = ffn_rings()
    next(ring)
    near = [
        net.send(wg_ref.at[:, pl.ds(quarter_start(at.sib), PART)], gw.at[pl.ds(mine, FEAT), :], at.S),
        net.send(wu_ref.at[:, pl.ds(quarter_start(at.sib), PART)], uw.at[pl.ds(mine, FEAT), :], at.S),
        net.send(wd_ref.at[pl.ds(quarter_start(at.sib), PART), :], dw.at[:, pl.ds(mine, FEAT)], at.S),
    ]
    gather_og.start(og_ref)
    gather_x.end()
    early = list(net.sent)
    net.take(gain_sib, gains_all.at[:, pl.ds(aligned(at.sib, FEAT), FEAT)])
    net.take(gain_sibfar, gains_all.at[:, pl.ds(aligned(at.sibfar, FEAT), FEAT)])
    for copy in local:
        copy.wait()
    local.clear()

    gain1, gain2 = gains_all[0:1, :], gains_all[1:2, :]

    def norm_block(i, carry):
        rows = pl.ds(aligned(i, BLOCK), BLOCK)
        values = x_all[rows, :].astype(F32)
        n1[rows, :] = (values * rms(values) * gain1).astype(BF)
        return carry

    lax.fori_loop(0, SEQ // BLOCK // 2, norm_block, 0)
    next(ring)
    lax.fori_loop(SEQ // BLOCK // 2, SEQ // BLOCK, norm_block, 0)
    next(ring)
    gather_og.middle()
    my_rows = pl.ds(aligned(at.block, BLOCK), BLOCK)
    xs_ref[...] = x_all[my_rows, :]
    n1c_ref[...] = n1[:, pl.ds(mine, FEAT)]
    net.take(near_qw, qw.at[pl.ds(aligned(at.sib, FEAT), FEAT), :])
    other_cols = pl.ds(aligned(1 - at.core, 512), 512)
    net.take(far_qw, qw.at[far_half, other_cols])
    move(qw, qw_out)

    def kv_block(i, carry):
        rows = pl.ds(aligned(i, 256), 256)
        both = dot(n1[rows, :], qw[:, QCOLS:]) + bias_ref[:, QCOLS:QKV]
        key = both[:, :HEAD]
        k_ref[rows, :] = (key * cos_ref[rows, :] + turn(key) * sin_ref[rows, :]).astype(BF)
        v_ref[rows, :] = both[:, HEAD:].astype(BF)
        return carry

    lax.fori_loop(0, SEQ // 256, kv_block, 0)
    next(ring)
    pair = (at.col, 7 - at.col)
    for j in (0, 1):
        rows = pl.ds(aligned(pair[j], BLOCK), BLOCK)
        queries = dot(n1[rows, :], qw[:, :QCOLS]) + bias_ref[:, :QCOLS]
        cosine, sine = cos_ref[rows, :], sin_ref[rows, :]
        for h in range(HEADS):
            one = queries[:, h * HEAD : (h + 1) * HEAD]
            q_ref[pl.ds(j * BLOCK, BLOCK), pl.ds(h * HEAD, HEAD)] = (
                one * cosine + turn(one) * sine
            ).astype(BF)
    next(ring)
    gather_og.late()

    for j in (0, 1):
        keys = SEQ // 2 * (j + 1)
        rows = pl.ds(j * BLOCK, BLOCK)

        def attend(h, carry):
            lanes = pl.ds(aligned(h, HEAD), HEAD)
            scores = dot(q_ref[rows, lanes], k_ref[:keys, :], 1, 1) * SCALE
            scores = causal(scores, pair[j] * BLOCK)
            top = jnp.max(scores, axis=1, keepdims=True)
            weights = jnp.exp(scores - top)
            total = jnp.sum(weights, axis=1, keepdims=True)
            lse_ref[j * HEADS + h] = top + jnp.log(total)
            probs = (weights * (1.0 / total)).astype(BF)
            attn_ref[rows, lanes] = dot(probs, v_ref[:keys, :]).astype(BF)
            return carry

        lax.fori_loop(0, HEADS // 2, attend, 0)
        next(ring)
        lax.fori_loop(HEADS // 2, HEADS, attend, 0)
        next(ring)

    net.take(near_ow, ow.at[:, pl.ds(aligned(at.sib, FEAT), FEAT)])
    other_rows = pl.ds(aligned(1 - at.core, FEAT), FEAT)
    net.take(far_ow, ow.at[other_rows, far_half])
    move(ow, ow_out)
    part_out[...] = dot(attn_ref[pl.ds(aligned(1 - at.row, BLOCK), BLOCK), :], ow[...]).astype(BF)
    part = net.send(part_out, part_in, at.N1)
    next(ring)
    own = dot(attn_ref[pl.ds(aligned(at.row, BLOCK), BLOCK), :], ow[...])
    net.take(part, part_in)
    mid = xs_ref[...].astype(F32) + own + part_in[...].astype(F32)
    mid_ref[...] = mid

    def place_n2(row, col, part):
        first = block_of(row, col) * BLOCK
        if part is None:
            return n2_all.at[pl.ds(pl.multiple_of(first, BLOCK), BLOCK), :]
        return n2_all.at[pl.ds(pl.multiple_of(first + part * 64, 64), 64), :]

    n2_all[my_rows, :] = (mid * rms(mid) * gain2).astype(BF)
    gather_n2 = Gather8(net, at, place_n2)
    gather_n2.start(place_n2(at.row, at.col, None))
    gather_og.end()
    move(og_all.at[my_rows, :], og_out)
    next(ring)
    next(ring)
    net.take(near[2], dw.at[:, pl.ds(aligned(at.sib, FEAT), FEAT)])

    def hidden_back(i, carry):
        rows = pl.ds(aligned(i, 256), 256)
        for first, width in tiles_of(PART, 512):
            lanes = pl.ds(first, width)
            d_up[rows, lanes] = dot(og_all[rows, :], dw[lanes, :], 1, 1).astype(BF)
        return carry

    lax.fori_loop(0, 1, hidden_back, 0)
    next(ring)
    lax.fori_loop(1, 2, hidden_back, 0)
    next(ring)
    gather_n2.middle()
    next(ring)
    lax.fori_loop(2, 3, hidden_back, 0)
    next(ring)
    lax.fori_loop(3, 4, hidden_back, 0)
    move(dw, dw_out)
    drain(ring)
    gather_attn = GatherCol(net, at, attn_all)
    for j in (0, 1):
        gather_attn.rows(at.col, j)[...] = attn_ref[pl.ds(j * BLOCK, BLOCK), :]
    net.take(near[0], gw.at[pl.ds(aligned(at.sib, FEAT), FEAT), :])
    net.take(near[1], uw.at[pl.ds(aligned(at.sib, FEAT), FEAT), :])

    net.finish(early)
    hidden, d_gate = x_all.at[:, pl.ds(0, PART)], n1.at[:, pl.ds(0, PART)]
    norms = Reduce8(net, at, *red_a)
    chips = at.chips
    last_part = at.col == 3

    def tokens(j):
        row, hi = chips[j]
        first = 2 * hi + row * (6 - 4 * hi)
        return pl.ds(aligned(first, BLOCK), 256), at.core + row * (1 - 2 * at.core)

    for j in (3, 1, 2, 0):
        gather_n2.end(j)
        if j == 3:
            gather_n2.late()
            gather_attn.start()
        rows, _ = tokens(j)
        for first, width in tiles_of(PART, 512):
            lanes = pl.ds(first, width)
            gate = dot(n2_all[rows, :], gw[:, lanes])
            up = dot(n2_all[rows, :], uw[:, lanes])
            d_hidden = d_up[rows, lanes].astype(F32)
            sig = jax.nn.sigmoid(gate)
            act = gate * sig
            d_act = d_hidden * up * sig * (1.0 + gate * (1.0 - sig))
            values = [act * up, d_act, d_hidden * act]
            if first == 0:
                lane = lax.broadcasted_iota(jnp.int32, (1, width), 1)
                fresh = jnp.logical_or(lane >= HEAD, jnp.logical_not(last_part))
                values = [jnp.where(fresh, value, 0.0) for value in values]
            for ref, value in zip((hidden, d_gate, d_up), values, strict=True):
                ref[rows, lanes] = value.astype(BF)
    move(hidden, hidden_out)
    for first, width in tiles_of(MODEL, 256):
        lanes = pl.ds(first, width)
        tile = dot(hidden[...], og_all[:, lanes], 0, 0).astype(BF)
        for q in range(4):
            down[q // 2, q % 2, :, lanes] = tile[288 * q : 288 * (q + 1)]
    gather_attn.middle()
    sums, last_sums = down_items(net, at, down, down_own, bufs)
    begin(sums)
    for j in range(4):
        rows, place = tokens(j)
        own_rows = pl.ds(pl.multiple_of(rows.start + place * BLOCK, BLOCK), BLOCK)
        other_rows = pl.ds(pl.multiple_of(rows.start + (1 - place) * BLOCK, BLOCK), BLOCK)
        parts = [
            (dot(d_gate[r, :], gw[...], 1, 1) + dot(d_up[r, :], uw[...], 1, 1)).astype(BF)
            for r in (other_rows, own_rows)
        ]
        norms.put(j, parts[1], parts[0])
        if j:
            norms.step(j - 1)

    writes = []

    def outer_sum(left, right, out):
        height = left.shape[1] // 2
        for first, width in tiles_of(right.shape[1], 256):
            place = len(writes) % 2
            if len(writes) > 1:
                writes[-2].wait()
            for i in (0, 1):
                rows = pl.ds(i * height, height)
                tile_buf[place, rows, :width] = dot(
                    left[:, rows], right[:, pl.ds(first, width)], 0, 0
                ).astype(BF)
            writes.append(
                pltpu.make_async_copy(
                    tile_buf.at[place, pl.ds(0, 2 * height), pl.ds(0, width)],
                    out.at[:, pl.ds(first, width)],
                    tile_sems.at[place],
                )
            )
            writes[-1].start()

    gather_attn.end()
    for item in sums:
        item.middle()
    outer_sum(n2_all, d_gate, grad_gu.at[0])
    dn2_ref[...] = norms.step(3)
    for item in sums:
        item.end()
    begin(last_sums)
    outer_sum(n2_all, d_up, grad_gu.at[1])
    for item in last_sums:
        item.middle()
    for item in last_sums:
        item.end()
    for copy in writes[-2:]:
        copy.wait()
    for copy in local:
        copy.wait()
    net.finish()

    @pl.when(chosen)
    def _():
        for core in (0, 1):
            for copy in slice_copies(core, 0, 5):
                copy.wait_send()


def run_forward(x, og, wq, wk, wv, wout, wg, wu, wd, vectors, cosine, sine):
    outs = (
        ((BLOCK, MODEL), BF, vmem),
        ((SEQ, FEAT), BF, vmem),
        ((BLOCK, MODEL), BF, anywhere),
        ((MODEL, QKV), BF, anywhere),
        ((QCOLS, MODEL), BF, anywhere),
        ((2 * BLOCK, QCOLS), BF, vmem),
        ((SEQ, HEAD), BF, vmem),
        ((SEQ, HEAD), BF, vmem),
        ((2 * HEADS, BLOCK, 1), F32, vmem),
        ((SEQ, QCOLS), BF, vmem),
        ((BLOCK, MODEL), F32, vmem),
        ((8, MODEL), F32, vmem),
        ((BLOCK, MODEL), F32, vmem),
        ((SEQ, PART), BF, anywhere),
        ((PART, MODEL), BF, anywhere),
        ((2, MODEL, PART), BF, anywhere),
        ((80, MODEL), BF, vmem),
    )
    return pl.pallas_call(
        forward_kernel,
        out_shape=[jax.ShapeDtypeStruct(dims, dtype) for dims, dtype, _ in outs],
        in_specs=[anywhere()] * 9 + [vmem()] * 3,
        out_specs=[place() for _, _, place in outs],
        scratch_shapes=[
            pltpu.VMEM((FEAT, QKV), BF),
            pltpu.VMEM((SEQ, MODEL), BF),
            pltpu.VMEM((SEQ, MODEL), BF),
            pltpu.VMEM((SEQ, MODEL), BF),
            pltpu.VMEM((SEQ, MODEL), BF),
            pltpu.VMEM((MODEL, QKV), BF),
            pltpu.VMEM((QCOLS, MODEL), BF),
            pltpu.VMEM((MODEL, PART), BF),
            pltpu.VMEM((MODEL, PART), BF),
            pltpu.VMEM((PART, MODEL), BF),
            pltpu.VMEM((BLOCK, MODEL), BF),
            pltpu.VMEM((BLOCK, MODEL), BF),
            pltpu.VMEM((SEQ, PART), BF),
            pltpu.VMEM((2, MODEL, 256), BF),
            pltpu.VMEM((2, 2, 288, MODEL), BF),
            pltpu.VMEM((2 * BLOCK, QCOLS), BF),
            pltpu.VMEM((8, FEAT), F32),
        ]
        + reduce8_scratch(BLOCK, MODEL)
        + ring_scratch(DOWN_FIRST, DOWN_LAST)
        + [
            pltpu.SemaphoreType.DMA((200,)),
            pltpu.SemaphoreType.DMA((200,)),
            pltpu.SemaphoreType.DMA((32,)),
            pltpu.SemaphoreType.DMA((2,)),
        ],
        compiler_params=pltpu.CompilerParams(
            collective_id=0, has_side_effects=True, vmem_limit_bytes=VMEM_LIMIT
        ),
        cost_estimate=pl.CostEstimate(
            flops=37 * 10**9, bytes_accessed=80 * 10**6, transcendentals=4 * 10**6
        ),
        name="forward_and_feed_forward",
    )(x, og, wq, wk, wv, wout, wg, wu, wd, vectors, cosine, sine)


def backward_kernel(
    dn2_ref,
    mid_ref,
    og_ref,
    gains_all,
    n1c,
    attn_all,
    q_ref,
    k_ref,
    v_ref,
    lse_ref,
    cos_ref,
    sin_ref,
    ow_far,
    gu_far,
    down_own,
    grad_out,
    grad_qkv,
    sums_ref,
    d_mid,
    d_qkv_own,
    bias_ref,
    gu_own,
    all_down,
    mid_cols,
    mid_pair,
    d_attn,
    d_q,
    d_kv,
    kv_out,
    kv_in,
    d_qkv_all,
    ow,
    gu,
    *rest,
):
    bufs, (send_sems, recv_sems, local_sems) = rest[:-3], rest[-3:]
    at = Place()
    net = Net(send_sems, recv_sems, at)
    held = [
        pltpu.make_async_copy(src, dst, local_sems.at[i])
        for i, (src, dst) in enumerate(
            ((ow_far, ow), (gu_far, gu))
        )
    ]
    for copy in held:
        copy.start()
    at.meet(
        (at.S, at.O, at.OS, at.N1, at.N2, at.N1S, at.N2S, at.YP, at.YM, at.ZP, at.ZM)
    )
    first, last = gu_items(net, at, gu_far, gu, gu_own, bufs)
    begin(first)

    def down_slot(k, cols):
        return all_down.at[cols, pl.ds(pl.multiple_of(k * 80, 16), 80), :]

    down_keys = [
        net.send(down_own.at[:, pl.ds(aligned(col, FEAT), FEAT)], down_slot(at.dp, at.col), device)
        for device, col in ((at.S, at.sib), (at.O, at.far), (at.OS, at.sibfar))
    ]
    down_mine = pltpu.make_async_copy(
        down_own.at[:, pl.ds(aligned(at.col, FEAT), FEAT)],
        down_slot(at.dp, at.col),
        local_sems.at[3],
    )
    down_mine.start()
    peers = ((at.S, at.sib), (at.O, at.far), (at.OS, at.sibfar))
    pair = (at.col, 7 - at.col)

    def rows_at(block):
        return pl.ds(aligned(block, BLOCK), BLOCK)

    def cols_at(col):
        return pl.ds(aligned(col, FEAT), FEAT)

    gain2 = gains_all[1:2, :]
    mid = mid_ref[...]
    scale = rms(mid)
    unit = mid * scale
    d_normed = dn2_ref[...]
    sums_ref[...] = jnp.zeros_like(sums_ref)
    sums_ref[1:2, :] = jnp.sum(d_normed * unit, axis=0, keepdims=True)
    bent = d_normed * gain2
    d_mid[...] = og_ref[...].astype(F32) + scale * (
        bent - unit * jnp.mean(bent * unit, axis=1, keepdims=True)
    )
    mid_pair[at.row] = d_mid[...].astype(BF)
    to_pair = net.send(mid_pair.at[at.row], mid_pair.at[at.row], at.N1)
    mid_cols[rows_at(at.block), :] = d_mid[:, cols_at(at.col)].astype(BF)
    spread = []
    others = (
        (at.S, at.row, at.sib),
        (at.N1, 1 - at.row, at.col),
        (at.N1S, 1 - at.row, at.sib),
        (at.O, at.row, at.far),
        (at.OS, at.row, at.sibfar),
        (at.N2, 1 - at.row, at.far),
        (at.N2S, 1 - at.row, at.sibfar),
    )
    for device, row, col in others:
        spread.append(
            net.send(
                mid_pair.at[at.row, :, cols_at(col)], mid_cols.at[rows_at(at.block), :], device
            )
        )
    net.take(to_pair, mid_pair.at[1 - at.row])
    held[0].wait()
    for j in (0, 1):
        d_attn[pl.ds(j * BLOCK, BLOCK), :] = dot(mid_pair[j], ow[...], 1, 1).astype(BF)
    d_kv[...] = jnp.zeros_like(d_kv)
    held[1].wait()
    for item in first:
        item.middle()

    for j in (0, 1):
        keys = SEQ // 2 * (j + 1)
        rows = pl.ds(j * BLOCK, BLOCK)

        def back(h, carry):
            lanes = pl.ds(aligned(h, HEAD), HEAD)
            queries, d_out = q_ref[rows, lanes], d_attn[rows, lanes]
            scores = dot(queries, k_ref[:keys, :], 1, 1) * SCALE
            scores = causal(scores, pair[j] * BLOCK)
            probs = jnp.exp(scores - lse_ref[j * HEADS + h])
            d_probs = dot(d_out, v_ref[:keys, :], 1, 1)
            inner = jnp.sum(probs * d_probs, axis=1, keepdims=True)
            d_scores = (probs * (d_probs - inner) * SCALE).astype(BF)
            d_q[rows, lanes] = dot(d_scores, k_ref[:keys, :])
            d_kv[:keys, :HEAD] += dot(d_scores, queries, 0, 0)
            d_kv[:keys, HEAD:] += dot(probs.astype(BF), d_out, 0, 0)
            return carry

        lax.fori_loop(0, HEADS, back, 0)

    kv_out[...] = d_kv[...].astype(BF)
    kv_keys = [
        [
            net.send(kv_out.at[rows_at(col + j * (7 - 2 * col)), :], kv_in.at[i, j], device)
            for j in (0, 1)
        ]
        for i, (device, col) in enumerate(peers)
    ]
    cosines = [cos_ref[rows_at(pair[j]), :] for j in (0, 1)]
    sines = [sin_ref[rows_at(pair[j]), :] for j in (0, 1)]
    for j in (0, 1):
        for h in range(HEADS):
            one = d_q[pl.ds(j * BLOCK, BLOCK), pl.ds(h * HEAD, HEAD)]
            d_qkv_all[rows_at(pair[j]), pl.ds(h * HEAD, HEAD)] = (
                one * cosines[j] - turn(one) * sines[j]
            ).astype(BF)
    for item in first:
        item.end()
    begin(last)
    down_mine.wait()
    for key, (_, col) in zip(down_keys, peers, strict=True):
        net.take(key, down_slot(at.dp, col))
    ring = ring_dp(
        net,
        at,
        (
            lambda zz, yy: [down_slot(zz * 4 + yy, pl.ds(2 * at.hi, 2))],
            lambda zz, yy: [down_slot(zz * 4 + yy, pl.ds(2 * (1 - at.hi), 2))],
        ),
    )
    next(ring)
    for key, (_, row, col) in zip(spread, others, strict=True):
        net.take(key, mid_cols.at[rows_at(block_of(row, col)), :])
    grad_out[...] = dot(attn_all[...], mid_cols[...], 0, 0).astype(BF)
    for j in (0, 1):
        total = d_kv[rows_at(pair[j]), :]
        for i in range(3):
            net.take(kv_keys[i][j], kv_in.at[i, j])
            total = total + kv_in[i, j].astype(F32)
        key = total[:, :HEAD]
        d_qkv_all[rows_at(pair[j]), pl.ds(QCOLS, HEAD)] = (
            key * cosines[j] - turn(key) * sines[j]
        ).astype(BF)
        d_qkv_all[rows_at(pair[j]), pl.ds(QCOLS + HEAD, HEAD)] = total[:, HEAD:].astype(BF)
    gather_qkv = GatherCol(net, at, d_qkv_all)
    gather_qkv.start()
    for item in last:
        item.middle()
    next(ring)

    for j in (0, 1):
        d_qkv_own[j] = d_qkv_all[rows_at(pair[j]), :]
    next(ring)
    next(ring)
    gather_qkv.middle()
    next(ring)
    gather_qkv.end()
    grad_qkv[...] = dot(n1c[...], d_qkv_all[...], 0, 0).astype(BF)
    ones = jnp.ones((8, SEQ), BF)
    bias_ref[...] = dot(ones, d_qkv_all[...])
    for item in last:
        item.end()
    drain(ring)
    net.finish()


def run_backward(*args):
    def out(shape, dtype):
        return jax.ShapeDtypeStruct(shape, dtype)

    outs = (
        out((QCOLS, FEAT), BF),
        out((FEAT, QKV), BF),
        out((8, MODEL), F32),
        out((BLOCK, MODEL), F32),
        out((2, BLOCK, QKV), BF),
        out((8, QKV), F32),
        out((4, 48, PART), BF),
        out((4, 1280, FEAT), BF),
    )
    return pl.pallas_call(
        backward_kernel,
        out_shape=outs,
        in_specs=[vmem()] * (len(args) - 3) + [anywhere()] * 2 + [vmem()],
        out_specs=[vmem()] * (len(outs) - 1) + [anywhere()],
        scratch_shapes=[
            pltpu.VMEM((SEQ, FEAT), BF),
            pltpu.VMEM((2, BLOCK, MODEL), BF),
            pltpu.VMEM((2 * BLOCK, QCOLS), BF),
            pltpu.VMEM((2 * BLOCK, QCOLS), F32),
            pltpu.VMEM((SEQ, 2 * HEAD), F32),
            pltpu.VMEM((SEQ, 2 * HEAD), BF),
            pltpu.VMEM((3, 2, BLOCK, 2 * HEAD), BF),
            pltpu.VMEM((SEQ, QKV), BF),
            pltpu.VMEM((QCOLS, MODEL), BF),
            pltpu.VMEM((2, 4, 2, 4, 48, PART), BF),
        ]
        + ring_scratch(GU_FIRST, GU_LAST)
        + [pltpu.SemaphoreType.DMA((110,)), pltpu.SemaphoreType.DMA((110,))]
        + [pltpu.SemaphoreType.DMA((4,))],
        compiler_params=pltpu.CompilerParams(
            collective_id=2, has_side_effects=True, vmem_limit_bytes=VMEM_LIMIT
        ),
        cost_estimate=pl.CostEstimate(
            flops=10 * 10**9, bytes_accessed=40 * 10**6, transcendentals=2 * 10**6
        ),
        name="attention_backward",
    )(*args)


def sums_kernel(
    gu_own,
    qkv,
    out,
    sums_ref,
    d_mid,
    d_qkv,
    bias_ref,
    xs_ref,
    gains_all,
    mid_ref,
    hidden_far,
    dw_far,
    qw_far,
    all_gu,
    all_qkv,
    all_out,
    small_out,
    out_ref,
    gi_in,
    small_y,
    small_z,
    hidden,
    dw,
    ffn,
    qw,
    part_out,
    part_in,
    gi_out,
    gain_sums,
    sums_in,
    *rest,
):
    red, bufs, (send_sems, recv_sems, local_sems) = rest[:7], rest[7:-3], rest[-3:]
    at = Place()
    net = Net(send_sems, recv_sems, at)
    held = [
        pltpu.make_async_copy(qw_far, qw, local_sems.at[1]),
        pltpu.make_async_copy(hidden_far, hidden, local_sems.at[2]),
        pltpu.make_async_copy(dw_far, dw, local_sems.at[3]),
    ]
    for copy in held:
        copy.start()
    at.meet(
        (at.S, at.O, at.OS, at.N1, at.N2, at.N1S, at.N2S)
        + (at.YP, at.YM, at.ZP, at.ZM, at.Y2, at.Z2)
    )
    outs = Reduce8(net, at, *red)

    def project(j):
        row, hi = at.chips[j]
        rows = pl.ds(aligned(row, SEQ // 2), SEQ // 2)
        lanes = pl.ds(aligned(hi, QCOLS), QCOLS)
        ffn[...] = dot(hidden[rows, :], dw[:, lanes])
        if j in (0, 3):
            mine = pl.ds(pl.multiple_of((at.block - 4 * at.row) * BLOCK, BLOCK), BLOCK)
            ffn[mine, :] += mid_ref[:, lanes]
        own = ffn[:, pl.ds(aligned(at.core, FEAT), FEAT)].astype(BF)
        outs.put(j, own, ffn[:, pl.ds(aligned(1 - at.core, FEAT), FEAT)].astype(BF))
        if j:
            outs.step(j - 1)

    z, y = at.z, at.y

    def gu_piece(k, lanes):
        rows = pl.ds(pl.multiple_of((k % 8) * 48, 16), 48)
        return all_gu.at[k // 8, rows, lanes]

    def part_lanes(col):
        return pl.ds(aligned(col, PART), PART)

    def feat_lanes(col):
        return pl.ds(aligned(col, FEAT), FEAT)

    def qkv_piece(k):
        rows = pl.ds(pl.multiple_of((k % 8) * 48, 16), 48)
        return all_qkv.at[rows, pl.ds(pl.multiple_of((k // 8) * 512, 512), 512)]

    def out_piece(k):
        return all_out.at[pl.ds(pl.multiple_of(k * 48, 16), 48), :]

    peers = ((at.O, at.far), (at.OS, at.sibfar), (at.S, at.sib))
    keys = []
    for device, col in peers:
        keys.append(
            net.send(gu_own.at[col], gu_piece(at.dp, part_lanes(at.col)), device)
        )
    held[0].wait()
    part_out[...] = dot(d_qkv[1 - at.row], qw[...], 1, 1).astype(BF)
    part = net.send(part_out, part_in, at.N1)
    first, last = small_items(net, at, qkv, out, qkv_piece(at.dp), out_piece(at.dp), bufs)
    begin(first)
    own_copies = [
        pltpu.make_async_copy(
            gu_own.at[at.col], gu_piece(at.dp, part_lanes(at.col)), local_sems.at[0]
        ),
    ]
    for copy in own_copies:
        copy.start()

    def take_from(i):
        net.take(keys[i], gu_piece(at.dp, part_lanes(peers[i][1])))

    def chip_ready():
        for copy in own_copies:
            copy.wait()
        take_from(2)

    def far_ready():
        take_from(0)
        take_from(1)

    def half_of(hi):
        def half(zz, yy):
            k = zz * 4 + yy
            return [gu_piece(k, pl.ds(aligned(hi, 2 * PART), 2 * PART))]

        return half

    ring = ring_dp(
        net, at, (half_of(at.hi), half_of(1 - at.hi)), (chip_ready, far_ready)
    )
    next(ring)
    for item in first:
        item.middle()
    d_normed = dot(d_qkv[at.row], qw[...], 1, 1)
    net.take(part, part_in)
    d_normed = d_normed + part_in[...].astype(F32)
    values = xs_ref[...].astype(F32)
    scale = rms(values)
    unit = values * scale
    gain_sums[...] = sums_ref[...]
    gain_sums[0:1, :] = jnp.sum(d_normed * unit, axis=0, keepdims=True)
    bent = d_normed * gains_all[0:1, :]
    total = d_mid[...] + scale * (bent - unit * jnp.mean(bent * unit, axis=1, keepdims=True))
    gi_out[...] = total.astype(BF)

    def half_block(col):
        offset = block_of(at.row, col) - 4 * at.row
        return gi_in.at[pl.ds(pl.multiple_of(offset * BLOCK, BLOCK), BLOCK), :]

    gi_keys = [
        net.send(gi_out.at[:, feat_lanes(col)], half_block(at.col), device)
        for device, col in peers
    ]
    half_block(at.col)[...] = gi_out[:, feat_lanes(at.col)]
    others = (
        (at.S, at.row, at.sib),
        (at.N1, 1 - at.row, at.col),
        (at.N1S, 1 - at.row, at.sib),
        (at.O, at.row, at.far),
        (at.OS, at.row, at.sibfar),
        (at.N2, 1 - at.row, at.far),
        (at.N2S, 1 - at.row, at.sibfar),
    )
    sums_in[at.row * 4 + at.col] = gain_sums[:, feat_lanes(at.col)]
    sums_keys = [
        net.send(gain_sums.at[:, feat_lanes(col)], sums_in.at[at.row * 4 + at.col], device)
        for device, row, col in others
    ]
    next(ring)
    held[1].wait()
    held[2].wait()
    project(0)
    for item in first:
        item.end()
    begin(last)
    next(ring)
    project(1)
    for key, (_, row, col) in zip(sums_keys, others, strict=True):
        net.take(key, sums_in.at[row * 4 + col])
    total = sums_in[0]
    for i in range(1, 8):
        total = total + sums_in[i]
    small_y[y, :, :FEAT] = total
    small_y[y, :, FEAT:] = bias_ref[...]
    small_keys = [net.send(small_y.at[y], small_y.at[y], d) for d in (at.YP, at.YM, at.Y2)]
    for item in last:
        item.middle()
    next(ring)
    project(2)
    for key, k in zip(small_keys, (y - 1, y + 1, y + 2), strict=True):
        net.take(key, small_y.at[lax.rem(k + 4, 4)])
    small_z[z] = (small_y[0] + small_y[1]) + (small_y[2] + small_y[3])
    small_keys = [net.send(small_z.at[z], small_z.at[z], d) for d in (at.ZP, at.ZM, at.Z2)]
    for item in last:
        item.end()
    after = ring_dp(
        net,
        at,
        (lambda zz, yy: [qkv_piece(zz * 4 + yy)], lambda zz, yy: [out_piece(zz * 4 + yy)]),
    )
    next(after)
    next(ring)
    project(3)
    next(after)
    for key, k in zip(small_keys, (z - 1, z + 1, z + 2), strict=True):
        net.take(key, small_z.at[lax.rem(k + 4, 4)])
    small_out[...] = (small_z[0] + small_z[1]) + (small_z[2] + small_z[3])
    for key, (_, col) in zip(gi_keys, peers, strict=True):
        net.take(key, half_block(col))
    for _ in ring:
        next(after, None)
    drain(after)
    out_ref[...] = outs.step(3)
    net.finish()


def run_sums(gu, qkv, out, *args):
    def shape(dims, dtype):
        return jax.ShapeDtypeStruct(dims, dtype)

    outs = (
        shape((2, FEAT, 4 * PART), BF),
        shape((FEAT, QKV), BF),
        shape((QCOLS, FEAT), BF),
        shape((8, FEAT + QKV), F32),
        shape((SEQ // 2, FEAT), F32),
        shape((SEQ // 2, FEAT), BF),
    )
    return pl.pallas_call(
        sums_kernel,
        out_shape=outs,
        in_specs=[vmem()] * len(args) + [anywhere()] * 3,
        out_specs=[anywhere()] + [vmem()] * 5,
        scratch_shapes=[pltpu.VMEM((4, 8, FEAT + QKV), F32)] * 2
        + [
            pltpu.VMEM((SEQ, PART), BF),
            pltpu.VMEM((PART, MODEL), BF),
            pltpu.VMEM((SEQ // 2, QCOLS), F32),
            pltpu.VMEM((MODEL, QKV), BF),
            pltpu.VMEM((BLOCK, MODEL), BF),
            pltpu.VMEM((BLOCK, MODEL), BF),
            pltpu.VMEM((BLOCK, MODEL), BF),
            pltpu.VMEM((8, MODEL), F32),
            pltpu.VMEM((8, 8, FEAT), F32),
        ]
        + reduce8_scratch(SEQ // 2, FEAT)
        + ring_scratch(SMALL_FIRST, SMALL_LAST)
        + [pltpu.SemaphoreType.DMA((128,)), pltpu.SemaphoreType.DMA((128,))]
        + [pltpu.SemaphoreType.DMA((4,))],
        compiler_params=pltpu.CompilerParams(
            collective_id=3, has_side_effects=True, vmem_limit_bytes=VMEM_LIMIT
        ),
        cost_estimate=pl.CostEstimate(
            flops=4 * 10**9, bytes_accessed=60 * 10**6, transcendentals=0
        ),
        name="sums_over_sequences",
    )(gu, qkv, out, *args)


def widen_kernel(
    gu,
    down,
    qkv,
    out,
    small,
    gi,
    lo,
    gate_out,
    up_out,
    down_out,
    lo_out,
    gi_out,
    query_out,
    key_out,
    value_out,
    proj_out,
    gain1_out,
    gain2_out,
    bq_out,
    bk_out,
    bv_out,
    gu_in,
    down_in,
    gate_buf,
    up_buf,
    down_buf,
    in_sems,
    out_sems,
    lo_sem,
):
    skip = 3 * PART

    def loads(n):
        rows = pl.ds(640 * (n % 2), 640)
        return [
            pltpu.make_async_copy(gu.at[:, pl.ds(n * 48, 48), :], gu_in.at[n], in_sems.at[n, 0]),
            pltpu.make_async_copy(down.at[n // 2, rows, :], down_in.at[n], in_sems.at[n, 1]),
        ]

    def stores(n):
        place, quarter, part = n % 2, n // 2, n % 2
        rows = pl.ds(n * 48, 48)
        drop = HEAD if quarter == 3 and part == 0 else 0
        start = PART * quarter + 576 * part - (HEAD if quarter == 3 and part == 1 else 0)
        return [
            pltpu.make_async_copy(gate_buf.at[place], gate_out.at[rows, :], out_sems.at[place, 0]),
            pltpu.make_async_copy(up_buf.at[place], up_out.at[rows, :], out_sems.at[place, 1]),
            pltpu.make_async_copy(
                down_buf.at[place, pl.ds(drop, 576 - drop), :],
                down_out.at[pl.ds(start, 576 - drop), :],
                out_sems.at[place, 2],
            ),
        ]

    def run(copies):
        for copy in copies:
            copy.start()
        return copies

    def wait(copies):
        for copy in copies:
            copy.wait()

    arriving = [run(loads(n)) for n in range(8)]
    passed = pltpu.make_async_copy(lo, lo_out, lo_sem.at[0])
    passed.start()
    gi_out[...] = gi[...].astype(F32)
    query_out[...] = qkv[:, :QCOLS].astype(F32)
    key_out[...] = qkv[:, QCOLS : QCOLS + HEAD].astype(F32)
    value_out[...] = qkv[:, QCOLS + HEAD :].astype(F32)
    proj_out[...] = out[...].astype(F32)
    first = 0
    for ref, row, width in (
        (gain1_out, 0, FEAT),
        (bq_out, 0, QCOLS),
        (bk_out, 0, HEAD),
        (bv_out, 0, HEAD),
    ):
        ref[...] = small[row, first : first + width]
        first += width
    gain2_out[...] = small[1, :FEAT]
    leaving = {}
    for n in range(8):
        place = n % 2
        wait(arriving[n])
        if n > 1:
            wait(leaving[n - 2])
        for i, buf in enumerate((gate_buf, up_buf)):
            buf[place, :, :skip] = gu_in[n, i, :, :skip].astype(F32)
            buf[place, :, skip:] = gu_in[n, i, :, skip + HEAD :].astype(F32)
        for m in range(4):
            down_buf[place, pl.ds(144 * m, 80), :] = down_in[
                n, pl.ds(160 * m, 80), :
            ].astype(F32)
            down_buf[place, pl.ds(144 * m + 80, 64), :] = down_in[
                n, pl.ds(160 * m + 96, 64), :
            ].astype(F32)
        leaving[n] = run(stores(n))
    wait(leaving[6])
    wait(leaving[7])
    passed.wait()


def run_widen(gu, down, qkv, out, small, grad_input, layer_output):
    shapes = [(FEAT, UNITS)] * 2 + [(UNITS, FEAT)] + [(SEQ // 2, FEAT)] * 2
    shapes += [(FEAT, QCOLS), (FEAT, HEAD), (FEAT, HEAD), (QCOLS, FEAT)]
    shapes += [(FEAT,), (FEAT,), (QCOLS,), (HEAD,), (HEAD,)]
    return pl.pallas_call(
        widen_kernel,
        out_shape=[jax.ShapeDtypeStruct(dims, F32) for dims in shapes],
        in_specs=[anywhere()] * 2 + [vmem()] * 4 + [anywhere()],
        out_specs=[anywhere()] * 4 + [vmem()] * 10,
        scratch_shapes=[
            pltpu.VMEM((8, 2, 48, 4 * PART), BF),
            pltpu.VMEM((8, 640, FEAT), BF),
            pltpu.VMEM((2, 48, UNITS), F32),
            pltpu.VMEM((2, 48, UNITS), F32),
            pltpu.VMEM((2, 576, FEAT), F32),
            pltpu.SemaphoreType.DMA((8, 2)),
            pltpu.SemaphoreType.DMA((2, 3)),
            pltpu.SemaphoreType.DMA((1,)),
        ],
        compiler_params=pltpu.CompilerParams(vmem_limit_bytes=VMEM_LIMIT),
        cost_estimate=pl.CostEstimate(
            flops=10**7, bytes_accessed=36 * 10**6, transcendentals=0
        ),
        name="widen",
    )(gu, down, qkv, out, small, grad_input, layer_output)


def rope_tables(count):
    places = np.arange(count, dtype=np.float32)
    inverse = (1.0 / THETA ** (np.arange(0, HEAD, 2) / HEAD)).astype(np.float32)
    angles = places[:, None] * inverse[None, :]
    cosine, sine = np.cos(angles), np.sin(angles)
    tables = np.concatenate([cosine, cosine], axis=-1), np.concatenate([-sine, sine], axis=-1)
    return tuple(jnp.asarray(table, F32) for table in tables)


def body(
    layer_input,
    gain_attn,
    w_query,
    w_key,
    w_value,
    b_query,
    b_key,
    b_value,
    w_out,
    gain_ffn,
    w_gate,
    w_up,
    w_down,
    out_grad,
):
    cosine, sine = rope_tables(SEQ)
    vectors = jnp.concatenate([b_query, b_key, b_value, gain_attn, gain_ffn]).astype(F32)[None]
    (
        xs,
        normed1_cols,
        grads_block,
        qkv_w,
        out_w,
        queries,
        key,
        value,
        lse,
        attn,
        mid,
        gains_all,
        dn2,
        hidden,
        down_w,
        grad_gu,
        grad_down,
    ) = run_forward(
        layer_input,
        out_grad,
        w_query,
        w_key,
        w_value,
        w_out,
        w_gate,
        w_up,
        w_down,
        vectors,
        cosine,
        sine,
    )
    grad_out, grad_qkv, sums, d_mid, d_qkv, bias_sums, grad_gu, grad_down = run_backward(
        dn2,
        mid,
        grads_block,
        gains_all,
        normed1_cols,
        attn,
        queries,
        key,
        value,
        lse,
        cosine,
        sine,
        out_w,
        grad_gu.reshape(2, 4, 2, 4, 48, PART),
        grad_down,
    )
    grad_gu, grad_qkv, grad_out, small, layer_output, grad_input = run_sums(
        grad_gu,
        grad_qkv.reshape(2, 4, 48, QKV),
        grad_out.reshape(2, 2, 4, 48, FEAT),
        sums,
        d_mid,
        d_qkv,
        bias_sums,
        xs,
        gains_all,
        mid,
        hidden,
        down_w,
        qkv_w,
    )
    (
        grad_gate,
        grad_up,
        grad_down,
        layer_output,
        grad_input,
        grad_query,
        grad_key,
        grad_value,
        grad_out,
        *vectors,
    ) = run_widen(
        grad_gu, grad_down, grad_qkv, grad_out, small, grad_input, layer_output
    )
    gain1, gain2, bias_query, bias_key, bias_value = vectors
    return (
        layer_output,
        grad_input,
        gain1,
        grad_query,
        grad_key,
        grad_value,
        bias_query,
        bias_key,
        bias_value,
        grad_out,
        gain2,
        grad_gate,
        grad_up,
        grad_down,
    )


def solution(mesh):
    in_specs = (
        P(("dp", "row"), "col"),
        P("col"),
        P("col", "row"),
        P("col", "row"),
        P("col", "row"),
        P("row"),
        P("row"),
        P("row"),
        P("row", "col"),
        P("col"),
        P("col", "row"),
        P("col", "row"),
        P("row", "col"),
        P(("dp", "row"), "col"),
    )
    out_specs = (
        P(("dp", "row"), "col"),
        P(("dp", "row"), "col"),
        P("col"),
        P("col", "row"),
        P("col", "row"),
        P("col", "row"),
        P("row"),
        P("row"),
        P("row"),
        P("row", "col"),
        P("col"),
        P("col", "row"),
        P("col", "row"),
        P("row", "col"),
    )
    return jax.shard_map(body, mesh=mesh, in_specs=in_specs, out_specs=out_specs, check_vma=False)
```

```python
import functools

import jax
import jax.numpy as jnp
import numpy as np
from jax import lax
from jax.experimental import pallas as pl
from jax.experimental.pallas import tpu as pltpu
from jax.sharding import PartitionSpec as P

EPS = 1e-06
THETA = 1000000.0
NEG = -1e30
BF = jnp.bfloat16
F32 = jnp.float32
MESH = pl.DeviceIdType.MESH
HEAD = 128
HEADS = 6
SEQ = 1024
MODEL = 1536
FEAT = 384
BLOCK = 128
UNITS = 4480
PART = 1152
QCOLS = 768
QKV = 1024
VMEM_LIMIT = 62 * 2**20
SCALE = HEAD ** (-0.5)


def dot(left, right, left_dim=1, right_dim=0):
    return lax.dot_general(
        left, right, (((left_dim,), (right_dim,)), ((), ())), preferred_element_type=F32
    )


def aligned(index, step):
    return pl.multiple_of(index * step, step)


def block_of(row, col):
    return col + row * (7 - 2 * col)


def quarter_start(col):
    return pl.multiple_of(col * PART - (col // 3) * HEAD, HEAD)


class Place:
    def __init__(self):
        self.dp, self.row, self.col = (lax.axis_index(a) for a in ("dp", "row", "col"))
        self.hi, self.core = self.col // 2, self.col % 2
        self.z, self.y = self.dp // 4, self.dp % 4
        self.sib = 2 * self.hi + 1 - self.core
        self.far = 2 * (1 - self.hi) + self.core
        self.sibfar = 2 * (1 - self.hi) + 1 - self.core
        self.block = block_of(self.row, self.col)
        self.chips = (
            (self.row, 1 - self.hi),
            (1 - self.row, self.hi),
            (1 - self.row, 1 - self.hi),
            (self.row, self.hi),
        )
        self.S = {"col": self.sib}
        self.O = {"col": self.far}
        self.OS = {"col": self.sibfar}
        self.N1 = {"row": 1 - self.row}
        self.N2 = {"row": 1 - self.row, "col": self.far}
        self.N1S = {"row": 1 - self.row, "col": self.sib}
        self.N2S = {"row": 1 - self.row, "col": self.sibfar}

        def dp_at(z, y):
            return {"dp": lax.rem(z + 4, 4) * 4 + lax.rem(y + 4, 4)}

        self.YP, self.YM = dp_at(self.z, self.y + 1), dp_at(self.z, self.y - 1)
        self.Y2, self.Z2 = dp_at(self.z, self.y + 2), dp_at(self.z + 2, self.y)
        self.ZP, self.ZM = dp_at(self.z + 1, self.y), dp_at(self.z - 1, self.y)

    def meet(self, partners):
        barrier = pltpu.get_barrier_semaphore()
        for device in partners:
            pl.semaphore_signal(barrier, inc=1, device_id=device, device_id_type=MESH)
        pl.semaphore_wait(barrier, len(partners))


class Net:
    def __init__(self, send_sems, recv_sems, at):
        self.ss, self.rs, self.at, self.count, self.sent = send_sems, recv_sems, at, 0, []

    def key(self):
        self.count += 1
        return self.count - 1

    def copy(self, key, src, dst, device):
        return pltpu.make_async_remote_copy(
            src_ref=src,
            dst_ref=dst,
            send_sem=self.ss.at[key],
            recv_sem=self.rs.at[key],
            device_id=device,
            device_id_type=MESH,
        )

    def send(self, src, dst, device):
        key = self.key()
        copy = self.copy(key, src, dst, device)
        copy.start()
        self.sent.append(copy)
        return key

    def take(self, key, dst):
        self.copy(key, dst, dst, self.at.S).wait_recv()

    def finish(self, copies=None):
        copies = list(self.sent) if copies is None else copies
        for copy in copies:
            copy.wait_send()
            self.sent.remove(copy)


class Gather8:
    def __init__(self, net, at, place):
        self.net, self.at, self.place = net, at, place

    def start(self, src):
        net, at = self.net, self.at
        mine = self.place(at.row, at.col, None)
        self.k1 = net.send(src, mine, at.N1)
        self.k2 = net.send(src, mine, at.N2)
        self.k0 = net.send(src, mine, at.S)

    def middle(self):
        net, at, place = self.net, self.at, self.place
        near, away = place(1 - at.row, at.col, None), place(1 - at.row, at.far, None)
        first, last = place(1 - at.row, at.col, 0), place(1 - at.row, at.far, 1)
        net.take(self.k1, near)
        self.ka = net.send(first, first, at.N2)
        self.f1 = net.send(near, near, at.S)
        net.take(self.k2, away)
        self.kb = net.send(last, last, at.N1)
        self.f2 = net.send(away, away, at.S)

    def late(self):
        net, at, place = self.net, self.at, self.place
        first, last = place(at.row, at.far, 0), place(at.row, at.far, 1)
        net.take(self.ka, first)
        self.f3 = net.send(first, first, at.S)
        net.take(self.kb, last)
        self.f4 = net.send(last, last, at.S)

    def end(self, chip=None):
        net, at, place = self.net, self.at, self.place
        if chip in (None, 3):
            net.take(self.k0, place(at.row, at.sib, None))
        if chip in (None, 1):
            net.take(self.f1, place(1 - at.row, at.sib, None))
        if chip in (None, 2):
            net.take(self.f2, place(1 - at.row, at.sibfar, None))
        if chip in (None, 0):
            net.take(self.f3, place(at.row, at.sibfar, 0))
            net.take(self.f4, place(at.row, at.sibfar, 1))


def ring_dp(net, at, halves, ready=(None, None)):
    def wrap(index):
        return lax.rem(index + 4, 4)

    sides = (((at.YP, at.YM), (at.ZP, at.ZM)), ((at.ZP, at.ZM), (at.YP, at.YM)))
    firsts, seconds = (at.y, at.z), (at.z, at.y)

    def refs(i, a, b):
        return halves[i](b, a) if i == 0 else halves[i](a, b)

    def send(i, a, b, device):
        return [net.send(ref, ref, device) for ref in refs(i, a, b)]

    def take(i, a, b, keys):
        for key, ref in zip(keys, refs(i, a, b), strict=True):
            net.take(key, ref)

    one, two, onward = {}, {}, {}
    for i in (0, 1):
        if ready[i]:
            ready[i]()
        one[i] = [send(i, firsts[i], seconds[i], side) for side in sides[i][0]]
        if ready[i]:
            two[i, 0] = [send(i, firsts[i], seconds[i], side) for side in sides[i][1]]
    for i in (0, 1):
        if not ready[i]:
            two[i, 0] = [send(i, firsts[i], seconds[i], side) for side in sides[i][1]]
    yield
    for i in (0, 1):
        minus = wrap(firsts[i] - 1)
        take(i, minus, seconds[i], one[i][0])
        one[i].append(send(i, minus, seconds[i], sides[i][0][0]))
        two[i, 1] = [send(i, minus, seconds[i], side) for side in sides[i][1]]
    yield
    for i in (0, 1):
        plus = wrap(firsts[i] + 1)
        take(i, plus, seconds[i], one[i][1])
        two[i, 2] = [send(i, plus, seconds[i], side) for side in sides[i][1]]
    offsets = (0, -1, 1, 2)
    for q in (0, 1, 2, 3):
        yield
        for i in (0, 1):
            if q == 1:
                across = wrap(firsts[i] + 2)
                take(i, across, seconds[i], one[i][2])
                two[i, 3] = [send(i, across, seconds[i], side) for side in sides[i][1]]
            slot = wrap(firsts[i] + offsets[q])
            minus, plus = wrap(seconds[i] - 1), wrap(seconds[i] + 1)
            take(i, slot, minus, two[i, q][0])
            if q < 2:
                onward[i, q] = send(i, slot, minus, sides[i][1][0])
            take(i, slot, plus, two[i, q][1])
            if q >= 2:
                onward[i, q] = send(i, slot, plus, sides[i][1][1])
    for q in (0, 1, 2, 3):
        yield
        for i in (0, 1):
            slot = wrap(firsts[i] + offsets[q])
            take(i, slot, wrap(seconds[i] + 2), onward[i, q])


def drain(steps):
    for _ in steps:
        pass


def rms(values):
    return lax.rsqrt(jnp.mean(values * values, axis=1, keepdims=True) + EPS)


def turn(values):
    return pltpu.roll(values, HEAD // 2, 1)


def causal(scores, start):
    places = start + lax.broadcasted_iota(jnp.int32, scores.shape, 0)
    keys = lax.broadcasted_iota(jnp.int32, scores.shape, 1)
    return jnp.where(keys <= places, scores, NEG)


def vmem():
    return pl.BlockSpec(memory_space=pltpu.VMEM)


def anywhere():
    return pl.BlockSpec(memory_space=pl.ANY)


class GatherCol:
    def __init__(self, net, at, array):
        self.net, self.at, self.array = net, at, array

    def rows(self, col, j):
        return self.array.at[pl.ds(aligned(col + j * (7 - 2 * col), BLOCK), BLOCK), :]

    def start(self):
        net, at = self.net, self.at
        mine = [self.rows(at.col, j) for j in (0, 1)]
        self.far = [net.send(ref, ref, at.O) for ref in mine]
        self.sib = [net.send(ref, ref, at.S) for ref in mine]

    def middle(self):
        net, at = self.net, self.at
        self.onward = []
        for j in (0, 1):
            ref = self.rows(at.far, j)
            net.take(self.far[j], ref)
            self.onward.append(net.send(ref, ref, at.S))

    def end(self):
        net, at = self.net, self.at
        for j in (0, 1):
            net.take(self.sib[j], self.rows(at.sib, j))
            net.take(self.onward[j], self.rows(at.sibfar, j))


class Reduce8:
    def __init__(self, net, at, own, other, sib_in, first_in, last_in, near_in, away_in):
        self.net, self.at, self.own, self.other, self.sib_in = net, at, own, other, sib_in
        self.first_in, self.last_in, self.near_in, self.away_in = first_in, last_in, near_in, away_in
        self.half = own.shape[1] // 2
        self.keys = {}

    def put(self, j, mine, theirs):
        self.own[j] = mine
        self.other[j] = theirs
        self.keys[j] = self.net.send(self.other.at[j], self.sib_in.at[j], self.at.S)

    def step(self, j):
        net, at, half = self.net, self.at, self.half
        net.take(self.keys[j], self.sib_in.at[j])
        total = self.own[j].astype(F32) + self.sib_in[j].astype(F32)
        if j == 0:
            self.own[j] = total.astype(BF)
            self.first = net.send(self.own.at[j, pl.ds(0, half)], self.first_in, at.N1)
            self.last = net.send(self.own.at[j, pl.ds(half, half)], self.last_in, at.N2)
        elif j == 1:
            net.take(self.last, self.last_in)
            self.own[j, :half] = total[:half].astype(BF)
            self.own[j, half:] = (total[half:] + self.last_in[...].astype(F32)).astype(BF)
            self.near = net.send(self.own.at[j], self.near_in, at.N1)
        elif j == 2:
            net.take(self.first, self.first_in)
            self.own[j, :half] = (total[:half] + self.first_in[...].astype(F32)).astype(BF)
            self.own[j, half:] = total[half:].astype(BF)
            self.away = net.send(self.own.at[j], self.away_in, at.N2)
        else:
            net.take(self.near, self.near_in)
            net.take(self.away, self.away_in)
            return total + self.near_in[...].astype(F32) + self.away_in[...].astype(F32)
        return None


def reduce8_scratch(rows, columns):
    return [
        pltpu.VMEM((4, rows, columns), BF),
        pltpu.VMEM((4, rows, columns), BF),
        pltpu.VMEM((4, rows, columns), BF),
        pltpu.VMEM((rows // 2, columns), BF),
        pltpu.VMEM((rows // 2, columns), BF),
        pltpu.VMEM((rows, columns), BF),
        pltpu.VMEM((rows, columns), BF),
    ]


def tiles_of(width, step):
    return [(first, min(step, width - first)) for first in range(0, width, step)]


def add_up(out, terms):
    lead = out.shape[:-2]
    if not lead:
        total = terms[0][...].astype(F32)
        for term in terms[1:]:
            total = total + term[...].astype(F32)
        out[...] = total.astype(out.dtype)
        return
    count = 1
    for size in lead:
        count *= size

    def step(i, carry):
        index = []
        for size in reversed(lead):
            index.insert(0, i % size)
            i = i // size
        index = tuple(index)
        total = terms[0].at[index][...].astype(F32)
        for term in terms[1:]:
            total = total + term.at[index][...].astype(F32)
        out.at[index][...] = total.astype(out.dtype)
        return carry

    lax.fori_loop(0, count, step, 0)


class RingItem:
    def __init__(self, net, sides, place, part, held, way, bufs, own):
        self.net, self.part, self.held, self.own = net, part, held, own
        self.relay, self.staged, self.from_last, self.from_next = bufs
        self.onward, self.back = (sides[0], sides[1]) if way == 0 else (sides[1], sides[0])
        step = 1 - 2 * way
        self.here, self.next, self.across, self.last = (
            lax.rem(place + 4 + step * i, 4) for i in (0, 1, 2, 3)
        )

    def start(self):
        self.k_relay = self.net.send(self.part(self.across), self.relay, self.onward)

    def direct(self):
        self.k_next = self.net.send(self.part(self.last), self.from_next, self.back)

    def middle(self):
        self.net.take(self.k_relay, self.relay)
        add_up(self.staged, [self.held(self.next), self.relay])
        self.k_last = self.net.send(self.staged, self.from_last, self.onward)

    def end(self):
        self.net.take(self.k_next, self.from_next)
        self.net.take(self.k_last, self.from_last)
        add_up(self.own, [self.held(self.here), self.from_next, self.from_last])


def begin(items):
    for item in items:
        item.start()
    for item in items:
        item.direct()


LEFT, RIGHT = pl.ds(0, QCOLS), pl.ds(QCOLS, QCOLS)
GU_FIRST = (((2, 2, 48, PART),), ((2, 2, 48, PART),))
GU_LAST = (((48, PART),) * 2,) * 2
DOWN_FIRST = (((2, 80, QCOLS),), ((144, QCOLS),))
DOWN_LAST = (((80, QCOLS),),) * 2
SMALL_FIRST = (((2, 48, 512),), ((2, 48, FEAT),))
SMALL_LAST = (((48, 512),), ((48, FEAT),))


def down_rows(k):
    return pl.ds(pl.multiple_of(72 * k - 8 * (k % 2), 16), 80)


def ring_scratch(first, last):
    scratch = []
    for i in (0, 1):
        for dims in first[i]:
            scratch += [pltpu.VMEM(dims, BF)] * 8
            scratch.append(pltpu.VMEM((2,) + dims, BF))
        for dims in last[i]:
            scratch += [pltpu.VMEM(dims, BF)] * 4
    return scratch


def ring_items(net, at, first, last, parts, helds, seconds, finals, bufs):
    sides = (((at.YP, at.YM), (at.ZP, at.ZM)), ((at.ZP, at.ZM), (at.YP, at.YM)))
    places = ((at.y, at.z), (at.z, at.y))
    bufs = list(bufs)
    one, two = ([], []), ([], [])
    for i in (0, 1):
        owns = []
        for n in range(len(first[i])):
            own = bufs[8]
            for way in (0, 1):
                part = functools.partial(lambda k, f, w: f(k, w), f=parts[i][n], w=way)
                held = functools.partial(lambda k, f, w: f(k, w), f=helds[i][n], w=way)
                four = bufs[4 * way : 4 * way + 4]
                one[i].append(
                    RingItem(net, sides[i][0], places[i][0], part, held, way, four, own.at[way])
                )
            owns.append(own)
            bufs = bufs[9:]
        for n in range(len(last[i])):
            part = functools.partial(lambda k, f, o: f(o, k), f=seconds[i][n], o=owns[min(n, len(owns) - 1)])
            two[i].append(
                RingItem(net, sides[i][1], places[i][1], part, part, n % 2, bufs[:4], finals[i][n])
            )
            bufs = bufs[4:]

    def mix(pair):
        return [item for items in zip(*pair, strict=True) for item in items]

    return mix(one), mix(two)


def gu_items(net, at, far_ref, near_ref, gu_own, bufs):
    def parts_of(gu):
        return (
            (lambda k, way: gu.at[way, pl.ds(0, 2), :, k],),
            (lambda k, way: gu.at[k // 2, pl.ds(2, 2), k % 2, pl.ds(2 * way, 2)],),
        )

    seconds = (
        (lambda own, k: own.at[k // 2, 0, k % 2], lambda own, k: own.at[k // 2, 1, k % 2]),
    ) * 2
    finals = ((gu_own.at[0], gu_own.at[1]), (gu_own.at[2], gu_own.at[3]))
    helds = parts_of(near_ref)
    return ring_items(net, at, GU_FIRST, GU_LAST, parts_of(far_ref), helds, seconds, finals, bufs)


def down_items(net, at, down, down_own, bufs):
    parts = (
        (lambda k, way: down.at[way, :, down_rows(k), LEFT],),
        (lambda k, way: down.at[k // 2, k % 2, pl.ds(144 * way, 144), RIGHT],),
    )
    seconds = (
        (lambda own, k: own.at[k // 2, k % 2],),
        (lambda own, k: own.at[k // 2, pl.ds(pl.multiple_of((k % 2) * 64, 64), 80)],),
    )
    finals = ((down_own.at[:, LEFT],), (down_own.at[:, RIGHT],))
    return ring_items(net, at, DOWN_FIRST, DOWN_LAST, parts, parts, seconds, finals, bufs)


def small_items(net, at, qkv, out, qkv_own, out_own, bufs):
    parts = (
        (lambda k, way: qkv.at[:, k, :, pl.ds(512 * way, 512)],),
        (lambda k, way: out.at[k // 2, k % 2, pl.ds(2 * way, 2)],),
    )
    seconds = ((lambda own, k: own.at[k // 2, k % 2],), (lambda own, k: own.at[k // 2, k % 2],))
    finals = ((qkv_own,), (out_own,))
    return ring_items(net, at, SMALL_FIRST, SMALL_LAST, parts, parts, seconds, finals, bufs)


def forward_kernel(
    x_ref,
    og_ref,
    wq_ref,
    wk_ref,
    wv_ref,
    wout_ref,
    wg_ref,
    wu_ref,
    wd_ref,
    bias_ref,
    cos_ref,
    sin_ref,
    xs_ref,
    n1c_ref,
    og_out,
    qw_out,
    ow_out,
    q_ref,
    k_ref,
    v_ref,
    lse_ref,
    attn_all,
    mid_ref,
    gains_all,
    dn2_ref,
    hidden_out,
    dw_out,
    grad_gu,
    down_own,
    wqkv_ref,
    x_all,
    n1,
    og_all,
    n2_all,
    qw,
    ow,
    gw,
    uw,
    dw,
    part_out,
    part_in,
    d_up,
    tile_buf,
    down,
    attn_ref,
    gains_ref,
    *rest,
):
    red_a, bufs, sems = rest[:7], rest[7:-4], rest[-4:]
    send_sems, recv_sems, local_sems, tile_sems = sems
    at = Place()
    net = Net(send_sems, recv_sems, at)
    local, local_count = [], iter(range(32))

    def move(src, dst):
        copy = pltpu.make_async_copy(src, dst, local_sems.at[next(local_count)])
        copy.start()
        local.append(copy)
        return copy

    gains_ref[...] = jnp.zeros_like(gains_ref)
    for i in (0, 1):
        gains_ref[i : i + 1, :] = bias_ref[:, QKV + i * FEAT : QKV + (i + 1) * FEAT]
    joined = [
        move(wq_ref, wqkv_ref.at[:, pl.ds(0, QCOLS)]),
        move(wk_ref, wqkv_ref.at[:, pl.ds(QCOLS, HEAD)]),
        move(wv_ref, wqkv_ref.at[:, pl.ds(QCOLS + HEAD, HEAD)]),
    ]
    at.meet((at.S, at.N1, at.N2, at.O, at.OS, at.YP, at.YM, at.ZP, at.ZM))
    for copy in joined:
        copy.wait()
    local.clear()

    def tokens_of(array):
        def place(row, col, part):
            if part is None:
                rows = pl.ds(aligned(row, SEQ // 2), SEQ // 2)
            else:
                rows = pl.ds(aligned(row * 2 + part, SEQ // 4), SEQ // 4)
            return array.at[rows, pl.ds(aligned(col, FEAT), FEAT)]

        return place

    mine, mine_far = aligned(at.col, FEAT), aligned(1 - at.hi, 2 * FEAT)
    move(x_ref, tokens_of(x_all)(at.row, at.col, None))
    move(wqkv_ref, qw.at[pl.ds(mine, FEAT), :])
    move(wout_ref, ow.at[:, pl.ds(mine, FEAT)])
    move(gains_ref, gains_all.at[:, pl.ds(mine, FEAT)])
    start = quarter_start(at.col)
    move(wg_ref.at[:, pl.ds(start, PART)], gw.at[pl.ds(mine, FEAT), :])
    move(wu_ref.at[:, pl.ds(start, PART)], uw.at[pl.ds(mine, FEAT), :])
    move(wd_ref.at[pl.ds(start, PART), :], dw.at[:, pl.ds(mine, FEAT)])
    move(og_ref, tokens_of(og_all)(at.row, at.col, None))

    eighth = at.dp % 8
    across = [net.key() for _ in range(5)]

    def slice_copies(core, first, last):
        device = {"col": 2 * (1 - at.hi) + core}
        rows = pl.ds(aligned(eighth, 48), 48)
        target = pl.ds(pl.multiple_of(mine + eighth * 48, 16), 48)
        columns = pl.ds(core * 512, 512)
        out_rows = pl.ds(pl.multiple_of(core * FEAT + eighth * 48, 16), 48)
        theirs = quarter_start(2 * (1 - at.hi) + core)
        down_rows = pl.ds(pl.multiple_of(theirs + eighth * 144, 16), 144)
        down_target = pl.ds(aligned(eighth, 144), 144)
        pairs = (
            (wqkv_ref.at[rows, columns], qw.at[target, columns]),
            (wout_ref.at[out_rows, :], ow.at[out_rows, pl.ds(mine, FEAT)]),
            (wg_ref.at[rows, pl.ds(theirs, PART)], gw.at[target, :]),
            (wu_ref.at[rows, pl.ds(theirs, PART)], uw.at[target, :]),
            (wd_ref.at[down_rows, :], dw.at[down_target, pl.ds(mine, FEAT)]),
        )
        return [
            pltpu.make_async_remote_copy(
                src_ref=pairs[i][0],
                dst_ref=pairs[i][1],
                send_sem=net.ss.at[spare[core][i]],
                recv_sem=net.rs.at[across[i]],
                device_id=device,
                device_id_type=MESH,
            )
            for i in range(first, last)
        ]

    spare = ([net.key() for _ in range(5)], [net.key() for _ in range(5)])
    chosen = at.core == at.dp // 8

    @pl.when(chosen)
    def _():
        for core in (0, 1):
            for copy in slice_copies(core, 0, 2):
                copy.start()

    gather_x = Gather8(net, at, tokens_of(x_all))
    gather_x.start(x_ref)
    gain_far = net.send(gains_ref, gains_all.at[:, pl.ds(mine, FEAT)], at.N2)
    gain_sib = net.send(gains_ref, gains_all.at[:, pl.ds(mine, FEAT)], at.S)
    near_qw = net.send(wqkv_ref, qw.at[pl.ds(mine, FEAT), :], at.S)
    near_ow = net.send(wout_ref, ow.at[:, pl.ds(mine, FEAT)], at.S)

    @pl.when(chosen)
    def _():
        for core in (0, 1):
            for copy in slice_copies(core, 2, 5):
                copy.start()

    far_half = pl.ds(mine_far, 2 * FEAT)

    def qkv_slices(z, y):
        rows = pl.ds(pl.multiple_of(mine_far + (z * 4 + y) * 48, 16), 48)
        return [qw.at[rows, pl.ds(aligned(at.core, 512), 512)]]

    def out_slices(z, y):
        index = z * 4 + y
        rows = pl.ds(pl.multiple_of(at.core * FEAT + (index % 8) * 48, 16), 48)
        return [ow.at[rows, pl.ds(pl.multiple_of(mine_far + (index // 8) * FEAT, HEAD), FEAT)]]

    def rows_of(weights):
        def slices(z, y):
            return [weights.at[pl.ds(pl.multiple_of(mine_far + (z * 4 + y) * 48, 16), 48), :]]

        return slices

    def down_of(first, count):
        def slices(z, y):
            index = z * 4 + y
            rows = pl.ds(pl.multiple_of((index % 8) * 144 + first, 16), count)
            lanes = pl.ds(pl.multiple_of(mine_far + (index // 8) * FEAT, HEAD), FEAT)
            return [dw.at[rows, lanes]]

        return slices

    def ffn_rings():
        down = ring_dp(net, at, (down_of(0, 80), down_of(80, 64)))
        both = ring_dp(net, at, (rows_of(gw), rows_of(uw)))
        for _ in range(3):
            next(down)
            yield
        next(both)
        yield
        yield from down
        yield
        yield from both

    net.take(across[0], qkv_slices(at.z, at.y)[0])
    net.take(across[1], out_slices(at.z, at.y)[0])
    ring = ring_dp(net, at, (qkv_slices, out_slices))
    next(ring)
    next(ring)
    next(ring)
    gather_x.middle()
    gains_far = gains_all.at[:, pl.ds(aligned(at.far, FEAT), FEAT)]
    net.take(gain_far, gains_far)
    gain_sibfar = net.send(gains_far, gains_far, at.S)
    next(ring)
    cols_half, rows_half = pl.ds(aligned(at.core, 512), 512), pl.ds(aligned(at.core, FEAT), FEAT)
    gather_og = Gather8(net, at, tokens_of(og_all))
    gather_x.late()

    drain(ring)
    far_qw = net.send(qw.at[far_half, cols_half], qw.at[far_half, cols_half], at.S)
    far_ow = net.send(ow.at[rows_half, far_half], ow.at[rows_half, far_half], at.S)
    net.take(across[2], rows_of(gw)(at.z, at.y)[0])
    net.take(across[3], rows_of(uw)(at.z, at.y)[0])
    net.take(across[4], down_of(0, 144)(at.z, at.y)[0])
    ring = ffn_rings()
    next(ring)
    near = [
        net.send(wg_ref.at[:, pl.ds(quarter_start(at.sib), PART)], gw.at[pl.ds(mine, FEAT), :], at.S),
        net.send(wu_ref.at[:, pl.ds(quarter_start(at.sib), PART)], uw.at[pl.ds(mine, FEAT), :], at.S),
        net.send(wd_ref.at[pl.ds(quarter_start(at.sib), PART), :], dw.at[:, pl.ds(mine, FEAT)], at.S),
    ]
    gather_og.start(og_ref)
    gather_x.end()
    early = list(net.sent)
    net.take(gain_sib, gains_all.at[:, pl.ds(aligned(at.sib, FEAT), FEAT)])
    net.take(gain_sibfar, gains_all.at[:, pl.ds(aligned(at.sibfar, FEAT), FEAT)])
    for copy in local:
        copy.wait()
    local.clear()

    gain1, gain2 = gains_all[0:1, :], gains_all[1:2, :]

    def norm_block(i, carry):
        rows = pl.ds(aligned(i, BLOCK), BLOCK)
        values = x_all[rows, :].astype(F32)
        n1[rows, :] = (values * rms(values) * gain1).astype(BF)
        return carry

    lax.fori_loop(0, SEQ // BLOCK // 2, norm_block, 0)
    next(ring)
    lax.fori_loop(SEQ // BLOCK // 2, SEQ // BLOCK, norm_block, 0)
    next(ring)
    gather_og.middle()
    my_rows = pl.ds(aligned(at.block, BLOCK), BLOCK)
    xs_ref[...] = x_all[my_rows, :]
    n1c_ref[...] = n1[:, pl.ds(mine, FEAT)]
    net.take(near_qw, qw.at[pl.ds(aligned(at.sib, FEAT), FEAT), :])
    other_cols = pl.ds(aligned(1 - at.core, 512), 512)
    net.take(far_qw, qw.at[far_half, other_cols])
    move(qw, qw_out)

    def kv_block(i, carry):
        rows = pl.ds(aligned(i, 256), 256)
        both = dot(n1[rows, :], qw[:, QCOLS:]) + bias_ref[:, QCOLS:QKV]
        key = both[:, :HEAD]
        k_ref[rows, :] = (key * cos_ref[rows, :] + turn(key) * sin_ref[rows, :]).astype(BF)
        v_ref[rows, :] = both[:, HEAD:].astype(BF)
        return carry

    lax.fori_loop(0, SEQ // 256, kv_block, 0)
    next(ring)
    pair = (at.col, 7 - at.col)
    for j in (0, 1):
        rows = pl.ds(aligned(pair[j], BLOCK), BLOCK)
        queries = dot(n1[rows, :], qw[:, :QCOLS]) + bias_ref[:, :QCOLS]
        cosine, sine = cos_ref[rows, :], sin_ref[rows, :]
        for h in range(HEADS):
            one = queries[:, h * HEAD : (h + 1) * HEAD]
            q_ref[pl.ds(j * BLOCK, BLOCK), pl.ds(h * HEAD, HEAD)] = (
                one * cosine + turn(one) * sine
            ).astype(BF)
    next(ring)
    gather_og.late()

    for j in (0, 1):
        keys = SEQ // 2 * (j + 1)
        rows = pl.ds(j * BLOCK, BLOCK)

        def attend(h, carry):
            lanes = pl.ds(aligned(h, HEAD), HEAD)
            scores = dot(q_ref[rows, lanes], k_ref[:keys, :], 1, 1) * SCALE
            scores = causal(scores, pair[j] * BLOCK)
            top = jnp.max(scores, axis=1, keepdims=True)
            weights = jnp.exp(scores - top)
            total = jnp.sum(weights, axis=1, keepdims=True)
            lse_ref[j * HEADS + h] = top + jnp.log(total)
            probs = (weights * (1.0 / total)).astype(BF)
            attn_ref[rows, lanes] = dot(probs, v_ref[:keys, :]).astype(BF)
            return carry

        lax.fori_loop(0, HEADS // 2, attend, 0)
        next(ring)
        lax.fori_loop(HEADS // 2, HEADS, attend, 0)
        next(ring)

    net.take(near_ow, ow.at[:, pl.ds(aligned(at.sib, FEAT), FEAT)])
    other_rows = pl.ds(aligned(1 - at.core, FEAT), FEAT)
    net.take(far_ow, ow.at[other_rows, far_half])
    move(ow, ow_out)
    part_out[...] = dot(attn_ref[pl.ds(aligned(1 - at.row, BLOCK), BLOCK), :], ow[...]).astype(BF)
    part = net.send(part_out, part_in, at.N1)
    next(ring)
    own = dot(attn_ref[pl.ds(aligned(at.row, BLOCK), BLOCK), :], ow[...])
    net.take(part, part_in)
    mid = xs_ref[...].astype(F32) + own + part_in[...].astype(F32)
    mid_ref[...] = mid

    def place_n2(row, col, part):
        first = block_of(row, col) * BLOCK
        if part is None:
            return n2_all.at[pl.ds(pl.multiple_of(first, BLOCK), BLOCK), :]
        return n2_all.at[pl.ds(pl.multiple_of(first + part * 64, 64), 64), :]

    n2_all[my_rows, :] = (mid * rms(mid) * gain2).astype(BF)
    gather_n2 = Gather8(net, at, place_n2)
    gather_n2.start(place_n2(at.row, at.col, None))
    gather_og.end()
    move(og_all.at[my_rows, :], og_out)
    next(ring)
    next(ring)
    net.take(near[2], dw.at[:, pl.ds(aligned(at.sib, FEAT), FEAT)])

    def hidden_back(i, carry):
        rows = pl.ds(aligned(i, 256), 256)
        for first, width in tiles_of(PART, 512):
            lanes = pl.ds(first, width)
            d_up[rows, lanes] = dot(og_all[rows, :], dw[lanes, :], 1, 1).astype(BF)
        return carry

    lax.fori_loop(0, 1, hidden_back, 0)
    next(ring)
    lax.fori_loop(1, 2, hidden_back, 0)
    next(ring)
    gather_n2.middle()
    next(ring)
    lax.fori_loop(2, 3, hidden_back, 0)
    next(ring)
    lax.fori_loop(3, 4, hidden_back, 0)
    move(dw, dw_out)
    drain(ring)
    gather_attn = GatherCol(net, at, attn_all)
    for j in (0, 1):
        gather_attn.rows(at.col, j)[...] = attn_ref[pl.ds(j * BLOCK, BLOCK), :]
    net.take(near[0], gw.at[pl.ds(aligned(at.sib, FEAT), FEAT), :])
    net.take(near[1], uw.at[pl.ds(aligned(at.sib, FEAT), FEAT), :])

    net.finish(early)
    hidden, d_gate = x_all.at[:, pl.ds(0, PART)], n1.at[:, pl.ds(0, PART)]
    norms = Reduce8(net, at, *red_a)
    chips = at.chips
    last_part = at.col == 3

    def tokens(j):
        row, hi = chips[j]
        first = 2 * hi + row * (6 - 4 * hi)
        return pl.ds(aligned(first, BLOCK), 256), at.core + row * (1 - 2 * at.core)

    for j in (3, 1, 2, 0):
        gather_n2.end(j)
        if j == 3:
            gather_n2.late()
            gather_attn.start()
        rows, _ = tokens(j)
        for first, width in tiles_of(PART, 512):
            lanes = pl.ds(first, width)
            gate = dot(n2_all[rows, :], gw[:, lanes])
            up = dot(n2_all[rows, :], uw[:, lanes])
            d_hidden = d_up[rows, lanes].astype(F32)
            sig = jax.nn.sigmoid(gate)
            act = gate * sig
            d_act = d_hidden * up * sig * (1.0 + gate * (1.0 - sig))
            values = [act * up, d_act, d_hidden * act]
            if first == 0:
                lane = lax.broadcasted_iota(jnp.int32, (1, width), 1)
                fresh = jnp.logical_or(lane >= HEAD, jnp.logical_not(last_part))
                values = [jnp.where(fresh, value, 0.0) for value in values]
            for ref, value in zip((hidden, d_gate, d_up), values, strict=True):
                ref[rows, lanes] = value.astype(BF)
    move(hidden, hidden_out)
    for first, width in tiles_of(MODEL, 256):
        lanes = pl.ds(first, width)
        tile = dot(hidden[...], og_all[:, lanes], 0, 0).astype(BF)
        for q in range(4):
            down[q // 2, q % 2, :, lanes] = tile[288 * q : 288 * (q + 1)]
    gather_attn.middle()
    sums, last_sums = down_items(net, at, down, down_own, bufs)
    begin(sums)
    for j in range(4):
        rows, place = tokens(j)
        own_rows = pl.ds(pl.multiple_of(rows.start + place * BLOCK, BLOCK), BLOCK)
        other_rows = pl.ds(pl.multiple_of(rows.start + (1 - place) * BLOCK, BLOCK), BLOCK)
        parts = [
            (dot(d_gate[r, :], gw[...], 1, 1) + dot(d_up[r, :], uw[...], 1, 1)).astype(BF)
            for r in (other_rows, own_rows)
        ]
        norms.put(j, parts[1], parts[0])
        if j:
            norms.step(j - 1)

    writes = []

    def outer_sum(left, right, out):
        height = left.shape[1] // 2
        for first, width in tiles_of(right.shape[1], 256):
            place = len(writes) % 2
            if len(writes) > 1:
                writes[-2].wait()
            for i in (0, 1):
                rows = pl.ds(i * height, height)
                tile_buf[place, rows, :width] = dot(
                    left[:, rows], right[:, pl.ds(first, width)], 0, 0
                ).astype(BF)
            writes.append(
                pltpu.make_async_copy(
                    tile_buf.at[place, pl.ds(0, 2 * height), pl.ds(0, width)],
                    out.at[:, pl.ds(first, width)],
                    tile_sems.at[place],
                )
            )
            writes[-1].start()

    gather_attn.end()
    for item in sums:
        item.middle()
    outer_sum(n2_all, d_gate, grad_gu.at[0])
    dn2_ref[...] = norms.step(3)
    for item in sums:
        item.end()
    begin(last_sums)
    outer_sum(n2_all, d_up, grad_gu.at[1])
    for item in last_sums:
        item.middle()
    for item in last_sums:
        item.end()
    for copy in writes[-2:]:
        copy.wait()
    for copy in local:
        copy.wait()
    net.finish()

    @pl.when(chosen)
    def _():
        for core in (0, 1):
            for copy in slice_copies(core, 0, 5):
                copy.wait_send()


def run_forward(x, og, wq, wk, wv, wout, wg, wu, wd, vectors, cosine, sine):
    outs = (
        ((BLOCK, MODEL), BF, vmem),
        ((SEQ, FEAT), BF, vmem),
        ((BLOCK, MODEL), BF, anywhere),
        ((MODEL, QKV), BF, anywhere),
        ((QCOLS, MODEL), BF, anywhere),
        ((2 * BLOCK, QCOLS), BF, vmem),
        ((SEQ, HEAD), BF, vmem),
        ((SEQ, HEAD), BF, vmem),
        ((2 * HEADS, BLOCK, 1), F32, vmem),
        ((SEQ, QCOLS), BF, vmem),
        ((BLOCK, MODEL), F32, vmem),
        ((8, MODEL), F32, vmem),
        ((BLOCK, MODEL), F32, vmem),
        ((SEQ, PART), BF, anywhere),
        ((PART, MODEL), BF, anywhere),
        ((2, MODEL, PART), BF, anywhere),
        ((80, MODEL), BF, vmem),
    )
    return pl.pallas_call(
        forward_kernel,
        out_shape=[jax.ShapeDtypeStruct(dims, dtype) for dims, dtype, _ in outs],
        in_specs=[anywhere()] * 9 + [vmem()] * 3,
        out_specs=[place() for _, _, place in outs],
        scratch_shapes=[
            pltpu.VMEM((FEAT, QKV), BF),
            pltpu.VMEM((SEQ, MODEL), BF),
            pltpu.VMEM((SEQ, MODEL), BF),
            pltpu.VMEM((SEQ, MODEL), BF),
            pltpu.VMEM((SEQ, MODEL), BF),
            pltpu.VMEM((MODEL, QKV), BF),
            pltpu.VMEM((QCOLS, MODEL), BF),
            pltpu.VMEM((MODEL, PART), BF),
            pltpu.VMEM((MODEL, PART), BF),
            pltpu.VMEM((PART, MODEL), BF),
            pltpu.VMEM((BLOCK, MODEL), BF),
            pltpu.VMEM((BLOCK, MODEL), BF),
            pltpu.VMEM((SEQ, PART), BF),
            pltpu.VMEM((2, MODEL, 256), BF),
            pltpu.VMEM((2, 2, 288, MODEL), BF),
            pltpu.VMEM((2 * BLOCK, QCOLS), BF),
            pltpu.VMEM((8, FEAT), F32),
        ]
        + reduce8_scratch(BLOCK, MODEL)
        + ring_scratch(DOWN_FIRST, DOWN_LAST)
        + [
            pltpu.SemaphoreType.DMA((200,)),
            pltpu.SemaphoreType.DMA((200,)),
            pltpu.SemaphoreType.DMA((32,)),
            pltpu.SemaphoreType.DMA((2,)),
        ],
        compiler_params=pltpu.CompilerParams(
            collective_id=0, has_side_effects=True, vmem_limit_bytes=VMEM_LIMIT
        ),
        cost_estimate=pl.CostEstimate(
            flops=37 * 10**9, bytes_accessed=80 * 10**6, transcendentals=4 * 10**6
        ),
        name="forward_and_feed_forward",
    )(x, og, wq, wk, wv, wout, wg, wu, wd, vectors, cosine, sine)


def backward_kernel(
    dn2_ref,
    mid_ref,
    og_ref,
    gains_all,
    n1c,
    attn_all,
    q_ref,
    k_ref,
    v_ref,
    lse_ref,
    cos_ref,
    sin_ref,
    ow_far,
    gu_far,
    down_own,
    grad_out,
    grad_qkv,
    sums_ref,
    d_mid,
    d_qkv_own,
    bias_ref,
    gu_own,
    all_down,
    mid_cols,
    mid_pair,
    d_attn,
    d_q,
    d_kv,
    kv_out,
    kv_in,
    d_qkv_all,
    ow,
    gu,
    *rest,
):
    bufs, (send_sems, recv_sems, local_sems) = rest[:-3], rest[-3:]
    at = Place()
    net = Net(send_sems, recv_sems, at)
    held = [
        pltpu.make_async_copy(src, dst, local_sems.at[i])
        for i, (src, dst) in enumerate(
            ((ow_far, ow), (gu_far, gu))
        )
    ]
    for copy in held:
        copy.start()
    at.meet(
        (at.S, at.O, at.OS, at.N1, at.N2, at.N1S, at.N2S, at.YP, at.YM, at.ZP, at.ZM)
    )
    first, last = gu_items(net, at, gu_far, gu, gu_own, bufs)
    begin(first)

    def down_slot(k, cols):
        return all_down.at[cols, pl.ds(pl.multiple_of(k * 80, 16), 80), :]

    down_keys = [
        net.send(down_own.at[:, pl.ds(aligned(col, FEAT), FEAT)], down_slot(at.dp, at.col), device)
        for device, col in ((at.S, at.sib), (at.O, at.far), (at.OS, at.sibfar))
    ]
    down_mine = pltpu.make_async_copy(
        down_own.at[:, pl.ds(aligned(at.col, FEAT), FEAT)],
        down_slot(at.dp, at.col),
        local_sems.at[3],
    )
    down_mine.start()
    peers = ((at.S, at.sib), (at.O, at.far), (at.OS, at.sibfar))
    pair = (at.col, 7 - at.col)

    def rows_at(block):
        return pl.ds(aligned(block, BLOCK), BLOCK)

    def cols_at(col):
        return pl.ds(aligned(col, FEAT), FEAT)

    gain2 = gains_all[1:2, :]
    mid = mid_ref[...]
    scale = rms(mid)
    unit = mid * scale
    d_normed = dn2_ref[...]
    sums_ref[...] = jnp.zeros_like(sums_ref)
    sums_ref[1:2, :] = jnp.sum(d_normed * unit, axis=0, keepdims=True)
    bent = d_normed * gain2
    d_mid[...] = og_ref[...].astype(F32) + scale * (
        bent - unit * jnp.mean(bent * unit, axis=1, keepdims=True)
    )
    mid_pair[at.row] = d_mid[...].astype(BF)
    to_pair = net.send(mid_pair.at[at.row], mid_pair.at[at.row], at.N1)
    mid_cols[rows_at(at.block), :] = d_mid[:, cols_at(at.col)].astype(BF)
    spread = []
    others = (
        (at.S, at.row, at.sib),
        (at.N1, 1 - at.row, at.col),
        (at.N1S, 1 - at.row, at.sib),
        (at.O, at.row, at.far),
        (at.OS, at.row, at.sibfar),
        (at.N2, 1 - at.row, at.far),
        (at.N2S, 1 - at.row, at.sibfar),
    )
    for device, row, col in others:
        spread.append(
            net.send(
                mid_pair.at[at.row, :, cols_at(col)], mid_cols.at[rows_at(at.block), :], device
            )
        )
    net.take(to_pair, mid_pair.at[1 - at.row])
    held[0].wait()
    for j in (0, 1):
        d_attn[pl.ds(j * BLOCK, BLOCK), :] = dot(mid_pair[j], ow[...], 1, 1).astype(BF)
    d_kv[...] = jnp.zeros_like(d_kv)
    held[1].wait()
    for item in first:
        item.middle()

    for j in (0, 1):
        keys = SEQ // 2 * (j + 1)
        rows = pl.ds(j * BLOCK, BLOCK)

        def back(h, carry):
            lanes = pl.ds(aligned(h, HEAD), HEAD)
            queries, d_out = q_ref[rows, lanes], d_attn[rows, lanes]
            scores = dot(queries, k_ref[:keys, :], 1, 1) * SCALE
            scores = causal(scores, pair[j] * BLOCK)
            probs = jnp.exp(scores - lse_ref[j * HEADS + h])
            d_probs = dot(d_out, v_ref[:keys, :], 1, 1)
            inner = jnp.sum(probs * d_probs, axis=1, keepdims=True)
            d_scores = (probs * (d_probs - inner) * SCALE).astype(BF)
            d_q[rows, lanes] = dot(d_scores, k_ref[:keys, :])
            d_kv[:keys, :HEAD] += dot(d_scores, queries, 0, 0)
            d_kv[:keys, HEAD:] += dot(probs.astype(BF), d_out, 0, 0)
            return carry

        lax.fori_loop(0, HEADS, back, 0)

    kv_out[...] = d_kv[...].astype(BF)
    kv_keys = [
        [
            net.send(kv_out.at[rows_at(col + j * (7 - 2 * col)), :], kv_in.at[i, j], device)
            for j in (0, 1)
        ]
        for i, (device, col) in enumerate(peers)
    ]
    cosines = [cos_ref[rows_at(pair[j]), :] for j in (0, 1)]
    sines = [sin_ref[rows_at(pair[j]), :] for j in (0, 1)]
    for j in (0, 1):
        for h in range(HEADS):
            one = d_q[pl.ds(j * BLOCK, BLOCK), pl.ds(h * HEAD, HEAD)]
            d_qkv_all[rows_at(pair[j]), pl.ds(h * HEAD, HEAD)] = (
                one * cosines[j] - turn(one) * sines[j]
            ).astype(BF)
    for item in first:
        item.end()
    begin(last)
    down_mine.wait()
    for key, (_, col) in zip(down_keys, peers, strict=True):
        net.take(key, down_slot(at.dp, col))
    ring = ring_dp(
        net,
        at,
        (
            lambda zz, yy: [down_slot(zz * 4 + yy, pl.ds(2 * at.hi, 2))],
            lambda zz, yy: [down_slot(zz * 4 + yy, pl.ds(2 * (1 - at.hi), 2))],
        ),
    )
    next(ring)
    for key, (_, row, col) in zip(spread, others, strict=True):
        net.take(key, mid_cols.at[rows_at(block_of(row, col)), :])
    grad_out[...] = dot(attn_all[...], mid_cols[...], 0, 0).astype(BF)
    for j in (0, 1):
        total = d_kv[rows_at(pair[j]), :]
        for i in range(3):
            net.take(kv_keys[i][j], kv_in.at[i, j])
            total = total + kv_in[i, j].astype(F32)
        key = total[:, :HEAD]
        d_qkv_all[rows_at(pair[j]), pl.ds(QCOLS, HEAD)] = (
            key * cosines[j] - turn(key) * sines[j]
        ).astype(BF)
        d_qkv_all[rows_at(pair[j]), pl.ds(QCOLS + HEAD, HEAD)] = total[:, HEAD:].astype(BF)
    gather_qkv = GatherCol(net, at, d_qkv_all)
    gather_qkv.start()
    for item in last:
        item.middle()
    next(ring)

    for j in (0, 1):
        d_qkv_own[j] = d_qkv_all[rows_at(pair[j]), :]
    next(ring)
    next(ring)
    gather_qkv.middle()
    next(ring)
    gather_qkv.end()
    grad_qkv[...] = dot(n1c[...], d_qkv_all[...], 0, 0).astype(BF)
    ones = jnp.ones((8, SEQ), BF)
    bias_ref[...] = dot(ones, d_qkv_all[...])
    for item in last:
        item.end()
    drain(ring)
    net.finish()


def run_backward(*args):
    def out(shape, dtype):
        return jax.ShapeDtypeStruct(shape, dtype)

    outs = (
        out((QCOLS, FEAT), BF),
        out((FEAT, QKV), BF),
        out((8, MODEL), F32),
        out((BLOCK, MODEL), F32),
        out((2, BLOCK, QKV), BF),
        out((8, QKV), F32),
        out((4, 48, PART), BF),
        out((4, 1280, FEAT), BF),
    )
    return pl.pallas_call(
        backward_kernel,
        out_shape=outs,
        in_specs=[vmem()] * (len(args) - 3) + [anywhere()] * 2 + [vmem()],
        out_specs=[vmem()] * (len(outs) - 1) + [anywhere()],
        scratch_shapes=[
            pltpu.VMEM((SEQ, FEAT), BF),
            pltpu.VMEM((2, BLOCK, MODEL), BF),
            pltpu.VMEM((2 * BLOCK, QCOLS), BF),
            pltpu.VMEM((2 * BLOCK, QCOLS), F32),
            pltpu.VMEM((SEQ, 2 * HEAD), F32),
            pltpu.VMEM((SEQ, 2 * HEAD), BF),
            pltpu.VMEM((3, 2, BLOCK, 2 * HEAD), BF),
            pltpu.VMEM((SEQ, QKV), BF),
            pltpu.VMEM((QCOLS, MODEL), BF),
            pltpu.VMEM((2, 4, 2, 4, 48, PART), BF),
        ]
        + ring_scratch(GU_FIRST, GU_LAST)
        + [pltpu.SemaphoreType.DMA((110,)), pltpu.SemaphoreType.DMA((110,))]
        + [pltpu.SemaphoreType.DMA((4,))],
        compiler_params=pltpu.CompilerParams(
            collective_id=2, has_side_effects=True, vmem_limit_bytes=VMEM_LIMIT
        ),
        cost_estimate=pl.CostEstimate(
            flops=10 * 10**9, bytes_accessed=40 * 10**6, transcendentals=2 * 10**6
        ),
        name="attention_backward",
    )(*args)


def sums_kernel(
    gu_own,
    qkv,
    out,
    sums_ref,
    d_mid,
    d_qkv,
    bias_ref,
    xs_ref,
    gains_all,
    mid_ref,
    hidden_far,
    dw_far,
    qw_far,
    all_gu,
    all_qkv,
    all_out,
    small_out,
    out_ref,
    gi_in,
    small_y,
    small_z,
    hidden,
    dw,
    ffn,
    qw,
    part_out,
    part_in,
    gi_out,
    gain_sums,
    sums_in,
    *rest,
):
    red, bufs, (send_sems, recv_sems, local_sems) = rest[:7], rest[7:-3], rest[-3:]
    at = Place()
    net = Net(send_sems, recv_sems, at)
    held = [
        pltpu.make_async_copy(qw_far, qw, local_sems.at[1]),
        pltpu.make_async_copy(hidden_far, hidden, local_sems.at[2]),
        pltpu.make_async_copy(dw_far, dw, local_sems.at[3]),
    ]
    for copy in held:
        copy.start()
    at.meet(
        (at.S, at.O, at.OS, at.N1, at.N2, at.N1S, at.N2S)
        + (at.YP, at.YM, at.ZP, at.ZM, at.Y2, at.Z2)
    )
    outs = Reduce8(net, at, *red)

    def project(j):
        row, hi = at.chips[j]
        rows = pl.ds(aligned(row, SEQ // 2), SEQ // 2)
        lanes = pl.ds(aligned(hi, QCOLS), QCOLS)
        ffn[...] = dot(hidden[rows, :], dw[:, lanes])
        if j in (0, 3):
            mine = pl.ds(pl.multiple_of((at.block - 4 * at.row) * BLOCK, BLOCK), BLOCK)
            ffn[mine, :] += mid_ref[:, lanes]
        own = ffn[:, pl.ds(aligned(at.core, FEAT), FEAT)].astype(BF)
        outs.put(j, own, ffn[:, pl.ds(aligned(1 - at.core, FEAT), FEAT)].astype(BF))
        if j:
            outs.step(j - 1)

    z, y = at.z, at.y

    def gu_piece(k, lanes):
        rows = pl.ds(pl.multiple_of((k % 8) * 48, 16), 48)
        return all_gu.at[k // 8, rows, lanes]

    def part_lanes(col):
        return pl.ds(aligned(col, PART), PART)

    def feat_lanes(col):
        return pl.ds(aligned(col, FEAT), FEAT)

    def qkv_piece(k):
        rows = pl.ds(pl.multiple_of((k % 8) * 48, 16), 48)
        return all_qkv.at[rows, pl.ds(pl.multiple_of((k // 8) * 512, 512), 512)]

    def out_piece(k):
        return all_out.at[pl.ds(pl.multiple_of(k * 48, 16), 48), :]

    peers = ((at.O, at.far), (at.OS, at.sibfar), (at.S, at.sib))
    keys = []
    for device, col in peers:
        keys.append(
            net.send(gu_own.at[col], gu_piece(at.dp, part_lanes(at.col)), device)
        )
    held[0].wait()
    part_out[...] = dot(d_qkv[1 - at.row], qw[...], 1, 1).astype(BF)
    part = net.send(part_out, part_in, at.N1)
    first, last = small_items(net, at, qkv, out, qkv_piece(at.dp), out_piece(at.dp), bufs)
    begin(first)
    own_copies = [
        pltpu.make_async_copy(
            gu_own.at[at.col], gu_piece(at.dp, part_lanes(at.col)), local_sems.at[0]
        ),
    ]
    for copy in own_copies:
        copy.start()

    def take_from(i):
        net.take(keys[i], gu_piece(at.dp, part_lanes(peers[i][1])))

    def chip_ready():
        for copy in own_copies:
            copy.wait()
        take_from(2)

    def far_ready():
        take_from(0)
        take_from(1)

    def half_of(hi):
        def half(zz, yy):
            k = zz * 4 + yy
            return [gu_piece(k, pl.ds(aligned(hi, 2 * PART), 2 * PART))]

        return half

    ring = ring_dp(
        net, at, (half_of(at.hi), half_of(1 - at.hi)), (chip_ready, far_ready)
    )
    next(ring)
    for item in first:
        item.middle()
    d_normed = dot(d_qkv[at.row], qw[...], 1, 1)
    net.take(part, part_in)
    d_normed = d_normed + part_in[...].astype(F32)
    values = xs_ref[...].astype(F32)
    scale = rms(values)
    unit = values * scale
    gain_sums[...] = sums_ref[...]
    gain_sums[0:1, :] = jnp.sum(d_normed * unit, axis=0, keepdims=True)
    bent = d_normed * gains_all[0:1, :]
    total = d_mid[...] + scale * (bent - unit * jnp.mean(bent * unit, axis=1, keepdims=True))
    gi_out[...] = total.astype(BF)

    def half_block(col):
        offset = block_of(at.row, col) - 4 * at.row
        return gi_in.at[pl.ds(pl.multiple_of(offset * BLOCK, BLOCK), BLOCK), :]

    gi_keys = [
        net.send(gi_out.at[:, feat_lanes(col)], half_block(at.col), device)
        for device, col in peers
    ]
    half_block(at.col)[...] = gi_out[:, feat_lanes(at.col)]
    others = (
        (at.S, at.row, at.sib),
        (at.N1, 1 - at.row, at.col),
        (at.N1S, 1 - at.row, at.sib),
        (at.O, at.row, at.far),
        (at.OS, at.row, at.sibfar),
        (at.N2, 1 - at.row, at.far),
        (at.N2S, 1 - at.row, at.sibfar),
    )
    sums_in[at.row * 4 + at.col] = gain_sums[:, feat_lanes(at.col)]
    sums_keys = [
        net.send(gain_sums.at[:, feat_lanes(col)], sums_in.at[at.row * 4 + at.col], device)
        for device, row, col in others
    ]
    next(ring)
    held[1].wait()
    held[2].wait()
    project(0)
    for item in first:
        item.end()
    begin(last)
    next(ring)
    project(1)
    for key, (_, row, col) in zip(sums_keys, others, strict=True):
        net.take(key, sums_in.at[row * 4 + col])
    total = sums_in[0]
    for i in range(1, 8):
        total = total + sums_in[i]
    small_y[y, :, :FEAT] = total
    small_y[y, :, FEAT:] = bias_ref[...]
    small_keys = [net.send(small_y.at[y], small_y.at[y], d) for d in (at.YP, at.YM, at.Y2)]
    for item in last:
        item.middle()
    next(ring)
    project(2)
    for key, k in zip(small_keys, (y - 1, y + 1, y + 2), strict=True):
        net.take(key, small_y.at[lax.rem(k + 4, 4)])
    small_z[z] = (small_y[0] + small_y[1]) + (small_y[2] + small_y[3])
    small_keys = [net.send(small_z.at[z], small_z.at[z], d) for d in (at.ZP, at.ZM, at.Z2)]
    for item in last:
        item.end()
    after = ring_dp(
        net,
        at,
        (lambda zz, yy: [qkv_piece(zz * 4 + yy)], lambda zz, yy: [out_piece(zz * 4 + yy)]),
    )
    next(after)
    next(ring)
    project(3)
    next(after)
    for key, k in zip(small_keys, (z - 1, z + 1, z + 2), strict=True):
        net.take(key, small_z.at[lax.rem(k + 4, 4)])
    small_out[...] = (small_z[0] + small_z[1]) + (small_z[2] + small_z[3])
    for key, (_, col) in zip(gi_keys, peers, strict=True):
        net.take(key, half_block(col))
    for _ in ring:
        next(after, None)
    drain(after)
    out_ref[...] = outs.step(3)
    net.finish()


def run_sums(gu, qkv, out, *args):
    def shape(dims, dtype):
        return jax.ShapeDtypeStruct(dims, dtype)

    outs = (
        shape((2, FEAT, 4 * PART), BF),
        shape((FEAT, QKV), BF),
        shape((QCOLS, FEAT), BF),
        shape((8, FEAT + QKV), F32),
        shape((SEQ // 2, FEAT), F32),
        shape((SEQ // 2, FEAT), BF),
    )
    return pl.pallas_call(
        sums_kernel,
        out_shape=outs,
        in_specs=[vmem()] * len(args) + [anywhere()] * 3,
        out_specs=[anywhere()] + [vmem()] * 5,
        scratch_shapes=[pltpu.VMEM((4, 8, FEAT + QKV), F32)] * 2
        + [
            pltpu.VMEM((SEQ, PART), BF),
            pltpu.VMEM((PART, MODEL), BF),
            pltpu.VMEM((SEQ // 2, QCOLS), F32),
            pltpu.VMEM((MODEL, QKV), BF),
            pltpu.VMEM((BLOCK, MODEL), BF),
            pltpu.VMEM((BLOCK, MODEL), BF),
            pltpu.VMEM((BLOCK, MODEL), BF),
            pltpu.VMEM((8, MODEL), F32),
            pltpu.VMEM((8, 8, FEAT), F32),
        ]
        + reduce8_scratch(SEQ // 2, FEAT)
        + ring_scratch(SMALL_FIRST, SMALL_LAST)
        + [pltpu.SemaphoreType.DMA((128,)), pltpu.SemaphoreType.DMA((128,))]
        + [pltpu.SemaphoreType.DMA((4,))],
        compiler_params=pltpu.CompilerParams(
            collective_id=3, has_side_effects=True, vmem_limit_bytes=VMEM_LIMIT
        ),
        cost_estimate=pl.CostEstimate(
            flops=4 * 10**9, bytes_accessed=60 * 10**6, transcendentals=0
        ),
        name="sums_over_sequences",
    )(gu, qkv, out, *args)


def widen_kernel(
    gu,
    down,
    qkv,
    out,
    small,
    gi,
    lo,
    gate_out,
    up_out,
    down_out,
    lo_out,
    gi_out,
    query_out,
    key_out,
    value_out,
    proj_out,
    gain1_out,
    gain2_out,
    bq_out,
    bk_out,
    bv_out,
    gu_in,
    down_in,
    gate_buf,
    up_buf,
    down_buf,
    in_sems,
    out_sems,
):
    skip = 3 * PART

    def loads(n):
        rows = pl.ds(640 * (n % 2), 640)
        return [
            pltpu.make_async_copy(gu.at[:, pl.ds(n * 48, 48), :], gu_in.at[n], in_sems.at[n, 0]),
            pltpu.make_async_copy(down.at[n // 2, rows, :], down_in.at[n], in_sems.at[n, 1]),
        ]

    def stores(n):
        place, quarter, part = n % 2, n // 2, n % 2
        rows = pl.ds(n * 48, 48)
        drop = HEAD if quarter == 3 and part == 0 else 0
        start = PART * quarter + 576 * part - (HEAD if quarter == 3 and part == 1 else 0)
        return [
            pltpu.make_async_copy(gate_buf.at[place], gate_out.at[rows, :], out_sems.at[place, 0]),
            pltpu.make_async_copy(up_buf.at[place], up_out.at[rows, :], out_sems.at[place, 1]),
            pltpu.make_async_copy(
                down_buf.at[place, pl.ds(drop, 576 - drop), :],
                down_out.at[pl.ds(start, 576 - drop), :],
                out_sems.at[place, 2],
            ),
        ]

    def run(copies):
        for copy in copies:
            copy.start()
        return copies

    def wait(copies):
        for copy in copies:
            copy.wait()

    arriving = [run(loads(n)) for n in range(8)]
    lo_out[...] = lo[...]
    gi_out[...] = gi[...].astype(F32)
    query_out[...] = qkv[:, :QCOLS].astype(F32)
    key_out[...] = qkv[:, QCOLS : QCOLS + HEAD].astype(F32)
    value_out[...] = qkv[:, QCOLS + HEAD :].astype(F32)
    proj_out[...] = out[...].astype(F32)
    first = 0
    for ref, row, width in (
        (gain1_out, 0, FEAT),
        (bq_out, 0, QCOLS),
        (bk_out, 0, HEAD),
        (bv_out, 0, HEAD),
    ):
        ref[...] = small[row, first : first + width]
        first += width
    gain2_out[...] = small[1, :FEAT]
    leaving = {}
    for n in range(8):
        place = n % 2
        wait(arriving[n])
        if n > 1:
            wait(leaving[n - 2])
        for i, buf in enumerate((gate_buf, up_buf)):
            buf[place, :, :skip] = gu_in[n, i, :, :skip].astype(F32)
            buf[place, :, skip:] = gu_in[n, i, :, skip + HEAD :].astype(F32)
        for m in range(4):
            down_buf[place, pl.ds(144 * m, 80), :] = down_in[
                n, pl.ds(160 * m, 80), :
            ].astype(F32)
            down_buf[place, pl.ds(144 * m + 80, 64), :] = down_in[
                n, pl.ds(160 * m + 96, 64), :
            ].astype(F32)
        leaving[n] = run(stores(n))
    wait(leaving[6])
    wait(leaving[7])


def run_widen(gu, down, qkv, out, small, grad_input, layer_output):
    shapes = [(FEAT, UNITS)] * 2 + [(UNITS, FEAT)] + [(SEQ // 2, FEAT)] * 2
    shapes += [(FEAT, QCOLS), (FEAT, HEAD), (FEAT, HEAD), (QCOLS, FEAT)]
    shapes += [(FEAT,), (FEAT,), (QCOLS,), (HEAD,), (HEAD,)]
    return pl.pallas_call(
        widen_kernel,
        out_shape=[jax.ShapeDtypeStruct(dims, F32) for dims in shapes],
        in_specs=[anywhere()] * 2 + [vmem()] * 5,
        out_specs=[anywhere()] * 3 + [vmem()] * 11,
        scratch_shapes=[
            pltpu.VMEM((8, 2, 48, 4 * PART), BF),
            pltpu.VMEM((8, 640, FEAT), BF),
            pltpu.VMEM((2, 48, UNITS), F32),
            pltpu.VMEM((2, 48, UNITS), F32),
            pltpu.VMEM((2, 576, FEAT), F32),
            pltpu.SemaphoreType.DMA((8, 2)),
            pltpu.SemaphoreType.DMA((2, 3)),
        ],
        compiler_params=pltpu.CompilerParams(vmem_limit_bytes=VMEM_LIMIT),
        cost_estimate=pl.CostEstimate(
            flops=10**7, bytes_accessed=36 * 10**6, transcendentals=0
        ),
        name="widen",
    )(gu, down, qkv, out, small, grad_input, layer_output)


def rope_tables(count):
    places = np.arange(count, dtype=np.float32)
    inverse = (1.0 / THETA ** (np.arange(0, HEAD, 2) / HEAD)).astype(np.float32)
    angles = places[:, None] * inverse[None, :]
    cosine, sine = np.cos(angles), np.sin(angles)
    tables = np.concatenate([cosine, cosine], axis=-1), np.concatenate([-sine, sine], axis=-1)
    return tuple(jnp.asarray(table, F32) for table in tables)


def body(
    layer_input,
    gain_attn,
    w_query,
    w_key,
    w_value,
    b_query,
    b_key,
    b_value,
    w_out,
    gain_ffn,
    w_gate,
    w_up,
    w_down,
    out_grad,
):
    cosine, sine = rope_tables(SEQ)
    vectors = jnp.concatenate([b_query, b_key, b_value, gain_attn, gain_ffn]).astype(F32)[None]
    (
        xs,
        normed1_cols,
        grads_block,
        qkv_w,
        out_w,
        queries,
        key,
        value,
        lse,
        attn,
        mid,
        gains_all,
        dn2,
        hidden,
        down_w,
        grad_gu,
        grad_down,
    ) = run_forward(
        layer_input,
        out_grad,
        w_query,
        w_key,
        w_value,
        w_out,
        w_gate,
        w_up,
        w_down,
        vectors,
        cosine,
        sine,
    )
    grad_out, grad_qkv, sums, d_mid, d_qkv, bias_sums, grad_gu, grad_down = run_backward(
        dn2,
        mid,
        grads_block,
        gains_all,
        normed1_cols,
        attn,
        queries,
        key,
        value,
        lse,
        cosine,
        sine,
        out_w,
        grad_gu.reshape(2, 4, 2, 4, 48, PART),
        grad_down,
    )
    grad_gu, grad_qkv, grad_out, small, layer_output, grad_input = run_sums(
        grad_gu,
        grad_qkv.reshape(2, 4, 48, QKV),
        grad_out.reshape(2, 2, 4, 48, FEAT),
        sums,
        d_mid,
        d_qkv,
        bias_sums,
        xs,
        gains_all,
        mid,
        hidden,
        down_w,
        qkv_w,
    )
    (
        grad_gate,
        grad_up,
        grad_down,
        layer_output,
        grad_input,
        grad_query,
        grad_key,
        grad_value,
        grad_out,
        *vectors,
    ) = run_widen(
        grad_gu, grad_down, grad_qkv, grad_out, small, grad_input, layer_output
    )
    gain1, gain2, bias_query, bias_key, bias_value = vectors
    return (
        layer_output,
        grad_input,
        gain1,
        grad_query,
        grad_key,
        grad_value,
        bias_query,
        bias_key,
        bias_value,
        grad_out,
        gain2,
        grad_gate,
        grad_up,
        grad_down,
    )


def solution(mesh):
    in_specs = (
        P(("dp", "row"), "col"),
        P("col"),
        P("col", "row"),
        P("col", "row"),
        P("col", "row"),
        P("row"),
        P("row"),
        P("row"),
        P("row", "col"),
        P("col"),
        P("col", "row"),
        P("col", "row"),
        P("row", "col"),
        P(("dp", "row"), "col"),
    )
    out_specs = (
        P(("dp", "row"), "col"),
        P(("dp", "row"), "col"),
        P("col"),
        P("col", "row"),
        P("col", "row"),
        P("col", "row"),
        P("row"),
        P("row"),
        P("row"),
        P("row", "col"),
        P("col"),
        P("col", "row"),
        P("col", "row"),
        P("row", "col"),
    )
    return jax.shard_map(body, mesh=mesh, in_specs=in_specs, out_specs=out_specs, check_vma=False)
```

```python
import functools

import jax
import jax.numpy as jnp
import numpy as np
from jax import lax
from jax.experimental import pallas as pl
from jax.experimental.pallas import tpu as pltpu
from jax.sharding import PartitionSpec as P

EPS = 1e-06
THETA = 1000000.0
NEG = -1e30
BF = jnp.bfloat16
F32 = jnp.float32
MESH = pl.DeviceIdType.MESH
HEAD = 128
HEADS = 6
SEQ = 1024
MODEL = 1536
FEAT = 384
BLOCK = 128
UNITS = 4480
PART = 1152
QCOLS = 768
QKV = 1024
VMEM_LIMIT = 62 * 2**20
SCALE = HEAD ** (-0.5)


def dot(left, right, left_dim=1, right_dim=0):
    return lax.dot_general(
        left, right, (((left_dim,), (right_dim,)), ((), ())), preferred_element_type=F32
    )


def aligned(index, step):
    return pl.multiple_of(index * step, step)


def block_of(row, col):
    return col + row * (7 - 2 * col)


def quarter_start(col):
    return pl.multiple_of(col * PART - (col // 3) * HEAD, HEAD)


class Place:
    def __init__(self):
        self.dp, self.row, self.col = (lax.axis_index(a) for a in ("dp", "row", "col"))
        self.hi, self.core = self.col // 2, self.col % 2
        self.z, self.y = self.dp // 4, self.dp % 4
        self.sib = 2 * self.hi + 1 - self.core
        self.far = 2 * (1 - self.hi) + self.core
        self.sibfar = 2 * (1 - self.hi) + 1 - self.core
        self.block = block_of(self.row, self.col)
        self.chips = (
            (self.row, 1 - self.hi),
            (1 - self.row, self.hi),
            (1 - self.row, 1 - self.hi),
            (self.row, self.hi),
        )
        self.S = {"col": self.sib}
        self.O = {"col": self.far}
        self.OS = {"col": self.sibfar}
        self.N1 = {"row": 1 - self.row}
        self.N2 = {"row": 1 - self.row, "col": self.far}
        self.N1S = {"row": 1 - self.row, "col": self.sib}
        self.N2S = {"row": 1 - self.row, "col": self.sibfar}

        def dp_at(z, y):
            return {"dp": lax.rem(z + 4, 4) * 4 + lax.rem(y + 4, 4)}

        self.YP, self.YM = dp_at(self.z, self.y + 1), dp_at(self.z, self.y - 1)
        self.Y2, self.Z2 = dp_at(self.z, self.y + 2), dp_at(self.z + 2, self.y)
        self.ZP, self.ZM = dp_at(self.z + 1, self.y), dp_at(self.z - 1, self.y)

    def meet(self, partners):
        barrier = pltpu.get_barrier_semaphore()
        for device in partners:
            pl.semaphore_signal(barrier, inc=1, device_id=device, device_id_type=MESH)
        pl.semaphore_wait(barrier, len(partners))


class Net:
    def __init__(self, send_sems, recv_sems, at):
        self.ss, self.rs, self.at, self.count, self.sent = send_sems, recv_sems, at, 0, []

    def key(self):
        self.count += 1
        return self.count - 1

    def copy(self, key, src, dst, device):
        return pltpu.make_async_remote_copy(
            src_ref=src,
            dst_ref=dst,
            send_sem=self.ss.at[key],
            recv_sem=self.rs.at[key],
            device_id=device,
            device_id_type=MESH,
        )

    def send(self, src, dst, device):
        key = self.key()
        copy = self.copy(key, src, dst, device)
        copy.start()
        self.sent.append(copy)
        return key

    def take(self, key, dst):
        self.copy(key, dst, dst, self.at.S).wait_recv()

    def finish(self, copies=None):
        copies = list(self.sent) if copies is None else copies
        for copy in copies:
            copy.wait_send()
            self.sent.remove(copy)


class Gather8:
    def __init__(self, net, at, place):
        self.net, self.at, self.place = net, at, place

    def start(self, src):
        net, at = self.net, self.at
        mine = self.place(at.row, at.col, None)
        self.k1 = net.send(src, mine, at.N1)
        self.k2 = net.send(src, mine, at.N2)
        self.k0 = net.send(src, mine, at.S)

    def middle(self):
        net, at, place = self.net, self.at, self.place
        near, away = place(1 - at.row, at.col, None), place(1 - at.row, at.far, None)
        first, last = place(1 - at.row, at.col, 0), place(1 - at.row, at.far, 1)
        net.take(self.k1, near)
        self.ka = net.send(first, first, at.N2)
        self.f1 = net.send(near, near, at.S)
        net.take(self.k2, away)
        self.kb = net.send(last, last, at.N1)
        self.f2 = net.send(away, away, at.S)

    def late(self):
        net, at, place = self.net, self.at, self.place
        first, last = place(at.row, at.far, 0), place(at.row, at.far, 1)
        net.take(self.ka, first)
        self.f3 = net.send(first, first, at.S)
        net.take(self.kb, last)
        self.f4 = net.send(last, last, at.S)

    def end(self, chip=None):
        net, at, place = self.net, self.at, self.place
        if chip in (None, 3):
            net.take(self.k0, place(at.row, at.sib, None))
        if chip in (None, 1):
            net.take(self.f1, place(1 - at.row, at.sib, None))
        if chip in (None, 2):
            net.take(self.f2, place(1 - at.row, at.sibfar, None))
        if chip in (None, 0):
            net.take(self.f3, place(at.row, at.sibfar, 0))
            net.take(self.f4, place(at.row, at.sibfar, 1))


def ring_dp(net, at, halves, ready=(None, None)):
    def wrap(index):
        return lax.rem(index + 4, 4)

    sides = (((at.YP, at.YM), (at.ZP, at.ZM)), ((at.ZP, at.ZM), (at.YP, at.YM)))
    firsts, seconds = (at.y, at.z), (at.z, at.y)

    def refs(i, a, b):
        return halves[i](b, a) if i == 0 else halves[i](a, b)

    def send(i, a, b, device):
        return [net.send(ref, ref, device) for ref in refs(i, a, b)]

    def take(i, a, b, keys):
        for key, ref in zip(keys, refs(i, a, b), strict=True):
            net.take(key, ref)

    one, two, onward = {}, {}, {}
    for i in (0, 1):
        if ready[i]:
            ready[i]()
        one[i] = [send(i, firsts[i], seconds[i], side) for side in sides[i][0]]
        if ready[i]:
            two[i, 0] = [send(i, firsts[i], seconds[i], side) for side in sides[i][1]]
    for i in (0, 1):
        if not ready[i]:
            two[i, 0] = [send(i, firsts[i], seconds[i], side) for side in sides[i][1]]
    yield
    for i in (0, 1):
        minus = wrap(firsts[i] - 1)
        take(i, minus, seconds[i], one[i][0])
        one[i].append(send(i, minus, seconds[i], sides[i][0][0]))
        two[i, 1] = [send(i, minus, seconds[i], side) for side in sides[i][1]]
    yield
    for i in (0, 1):
        plus = wrap(firsts[i] + 1)
        take(i, plus, seconds[i], one[i][1])
        two[i, 2] = [send(i, plus, seconds[i], side) for side in sides[i][1]]
    offsets = (0, -1, 1, 2)
    for q in (0, 1, 2, 3):
        yield
        for i in (0, 1):
            if q == 1:
                across = wrap(firsts[i] + 2)
                take(i, across, seconds[i], one[i][2])
                two[i, 3] = [send(i, across, seconds[i], side) for side in sides[i][1]]
            slot = wrap(firsts[i] + offsets[q])
            minus, plus = wrap(seconds[i] - 1), wrap(seconds[i] + 1)
            take(i, slot, minus, two[i, q][0])
            if q < 2:
                onward[i, q] = send(i, slot, minus, sides[i][1][0])
            take(i, slot, plus, two[i, q][1])
            if q >= 2:
                onward[i, q] = send(i, slot, plus, sides[i][1][1])
    for q in (0, 1, 2, 3):
        yield
        for i in (0, 1):
            slot = wrap(firsts[i] + offsets[q])
            take(i, slot, wrap(seconds[i] + 2), onward[i, q])


def drain(steps):
    for _ in steps:
        pass


def rms(values):
    return lax.rsqrt(jnp.mean(values * values, axis=1, keepdims=True) + EPS)


def turn(values):
    return pltpu.roll(values, HEAD // 2, 1)


def causal(scores, start):
    places = start + lax.broadcasted_iota(jnp.int32, scores.shape, 0)
    keys = lax.broadcasted_iota(jnp.int32, scores.shape, 1)
    return jnp.where(keys <= places, scores, NEG)


def vmem():
    return pl.BlockSpec(memory_space=pltpu.VMEM)


def anywhere():
    return pl.BlockSpec(memory_space=pl.ANY)


class GatherCol:
    def __init__(self, net, at, array):
        self.net, self.at, self.array = net, at, array

    def rows(self, col, j):
        return self.array.at[pl.ds(aligned(col + j * (7 - 2 * col), BLOCK), BLOCK), :]

    def start(self):
        net, at = self.net, self.at
        mine = [self.rows(at.col, j) for j in (0, 1)]
        self.far = [net.send(ref, ref, at.O) for ref in mine]
        self.sib = [net.send(ref, ref, at.S) for ref in mine]

    def middle(self):
        net, at = self.net, self.at
        self.onward = []
        for j in (0, 1):
            ref = self.rows(at.far, j)
            net.take(self.far[j], ref)
            self.onward.append(net.send(ref, ref, at.S))

    def end(self):
        net, at = self.net, self.at
        for j in (0, 1):
            net.take(self.sib[j], self.rows(at.sib, j))
            net.take(self.onward[j], self.rows(at.sibfar, j))


class Reduce8:
    def __init__(self, net, at, own, other, sib_in, first_in, last_in, near_in, away_in):
        self.net, self.at, self.own, self.other, self.sib_in = net, at, own, other, sib_in
        self.first_in, self.last_in, self.near_in, self.away_in = first_in, last_in, near_in, away_in
        self.half = own.shape[1] // 2
        self.keys = {}

    def put(self, j, mine, theirs):
        self.own[j] = mine
        self.other[j] = theirs
        self.keys[j] = self.net.send(self.other.at[j], self.sib_in.at[j], self.at.S)

    def step(self, j):
        net, at, half = self.net, self.at, self.half
        net.take(self.keys[j], self.sib_in.at[j])
        total = self.own[j].astype(F32) + self.sib_in[j].astype(F32)
        if j == 0:
            self.own[j] = total.astype(BF)
            self.first = net.send(self.own.at[j, pl.ds(0, half)], self.first_in, at.N1)
            self.last = net.send(self.own.at[j, pl.ds(half, half)], self.last_in, at.N2)
        elif j == 1:
            net.take(self.last, self.last_in)
            self.own[j, :half] = total[:half].astype(BF)
            self.own[j, half:] = (total[half:] + self.last_in[...].astype(F32)).astype(BF)
            self.near = net.send(self.own.at[j], self.near_in, at.N1)
        elif j == 2:
            net.take(self.first, self.first_in)
            self.own[j, :half] = (total[:half] + self.first_in[...].astype(F32)).astype(BF)
            self.own[j, half:] = total[half:].astype(BF)
            self.away = net.send(self.own.at[j], self.away_in, at.N2)
        else:
            net.take(self.near, self.near_in)
            net.take(self.away, self.away_in)
            return total + self.near_in[...].astype(F32) + self.away_in[...].astype(F32)
        return None


def reduce8_scratch(rows, columns):
    return [
        pltpu.VMEM((4, rows, columns), BF),
        pltpu.VMEM((4, rows, columns), BF),
        pltpu.VMEM((4, rows, columns), BF),
        pltpu.VMEM((rows // 2, columns), BF),
        pltpu.VMEM((rows // 2, columns), BF),
        pltpu.VMEM((rows, columns), BF),
        pltpu.VMEM((rows, columns), BF),
    ]


def tiles_of(width, step):
    return [(first, min(step, width - first)) for first in range(0, width, step)]


def add_up(out, terms):
    lead = out.shape[:-2]
    if not lead:
        total = terms[0][...].astype(F32)
        for term in terms[1:]:
            total = total + term[...].astype(F32)
        out[...] = total.astype(out.dtype)
        return
    count = 1
    for size in lead:
        count *= size

    def step(i, carry):
        index = []
        for size in reversed(lead):
            index.insert(0, i % size)
            i = i // size
        index = tuple(index)
        total = terms[0].at[index][...].astype(F32)
        for term in terms[1:]:
            total = total + term.at[index][...].astype(F32)
        out.at[index][...] = total.astype(out.dtype)
        return carry

    lax.fori_loop(0, count, step, 0)


class RingItem:
    def __init__(self, net, sides, place, part, held, way, bufs, own):
        self.net, self.part, self.held, self.own = net, part, held, own
        self.relay, self.staged, self.from_last, self.from_next = bufs
        self.onward, self.back = (sides[0], sides[1]) if way == 0 else (sides[1], sides[0])
        step = 1 - 2 * way
        self.here, self.next, self.across, self.last = (
            lax.rem(place + 4 + step * i, 4) for i in (0, 1, 2, 3)
        )

    def start(self):
        self.k_relay = self.net.send(self.part(self.across), self.relay, self.onward)

    def direct(self):
        self.k_next = self.net.send(self.part(self.last), self.from_next, self.back)

    def middle(self):
        self.net.take(self.k_relay, self.relay)
        add_up(self.staged, [self.held(self.next), self.relay])
        self.k_last = self.net.send(self.staged, self.from_last, self.onward)

    def end(self):
        self.net.take(self.k_next, self.from_next)
        self.net.take(self.k_last, self.from_last)
        add_up(self.own, [self.held(self.here), self.from_next, self.from_last])


def begin(items):
    for item in items:
        item.start()
    for item in items:
        item.direct()


LEFT, RIGHT = pl.ds(0, QCOLS), pl.ds(QCOLS, QCOLS)
GU_FIRST = (((2, 2, 48, PART),), ((2, 2, 48, PART),))
GU_LAST = (((48, PART),) * 2,) * 2
DOWN_FIRST = (((2, 80, QCOLS),), ((144, QCOLS),))
DOWN_LAST = (((80, QCOLS),),) * 2
SMALL_FIRST = (((2, 48, 512),), ((2, 48, FEAT),))
SMALL_LAST = (((48, 512),), ((48, FEAT),))


def down_rows(k):
    return pl.ds(pl.multiple_of(72 * k - 8 * (k % 2), 16), 80)


def ring_scratch(first, last):
    scratch = []
    for i in (0, 1):
        for dims in first[i]:
            scratch += [pltpu.VMEM(dims, BF)] * 8
            scratch.append(pltpu.VMEM((2,) + dims, BF))
        for dims in last[i]:
            scratch += [pltpu.VMEM(dims, BF)] * 4
    return scratch


def ring_items(net, at, first, last, parts, helds, seconds, finals, bufs):
    sides = (((at.YP, at.YM), (at.ZP, at.ZM)), ((at.ZP, at.ZM), (at.YP, at.YM)))
    places = ((at.y, at.z), (at.z, at.y))
    bufs = list(bufs)
    one, two = ([], []), ([], [])
    for i in (0, 1):
        owns = []
        for n in range(len(first[i])):
            own = bufs[8]
            for way in (0, 1):
                part = functools.partial(lambda k, f, w: f(k, w), f=parts[i][n], w=way)
                held = functools.partial(lambda k, f, w: f(k, w), f=helds[i][n], w=way)
                four = bufs[4 * way : 4 * way + 4]
                one[i].append(
                    RingItem(net, sides[i][0], places[i][0], part, held, way, four, own.at[way])
                )
            owns.append(own)
            bufs = bufs[9:]
        for n in range(len(last[i])):
            part = functools.partial(lambda k, f, o: f(o, k), f=seconds[i][n], o=owns[min(n, len(owns) - 1)])
            two[i].append(
                RingItem(net, sides[i][1], places[i][1], part, part, n % 2, bufs[:4], finals[i][n])
            )
            bufs = bufs[4:]

    def mix(pair):
        return [item for items in zip(*pair, strict=True) for item in items]

    return mix(one), mix(two)


def gu_items(net, at, far_ref, near_ref, gu_own, bufs):
    def parts_of(gu):
        return (
            (lambda k, way: gu.at[way, pl.ds(0, 2), :, k],),
            (lambda k, way: gu.at[k // 2, pl.ds(2, 2), k % 2, pl.ds(2 * way, 2)],),
        )

    seconds = (
        (lambda own, k: own.at[k // 2, 0, k % 2], lambda own, k: own.at[k // 2, 1, k % 2]),
    ) * 2
    finals = ((gu_own.at[0], gu_own.at[1]), (gu_own.at[2], gu_own.at[3]))
    helds = parts_of(near_ref)
    return ring_items(net, at, GU_FIRST, GU_LAST, parts_of(far_ref), helds, seconds, finals, bufs)


def down_items(net, at, down, down_own, bufs):
    parts = (
        (lambda k, way: down.at[way, :, down_rows(k), LEFT],),
        (lambda k, way: down.at[k // 2, k % 2, pl.ds(144 * way, 144), RIGHT],),
    )
    seconds = (
        (lambda own, k: own.at[k // 2, k % 2],),
        (lambda own, k: own.at[k // 2, pl.ds(pl.multiple_of((k % 2) * 64, 64), 80)],),
    )
    finals = ((down_own.at[:, LEFT],), (down_own.at[:, RIGHT],))
    return ring_items(net, at, DOWN_FIRST, DOWN_LAST, parts, parts, seconds, finals, bufs)


def small_items(net, at, qkv, out, qkv_own, out_own, bufs):
    parts = (
        (lambda k, way: qkv.at[:, k, :, pl.ds(512 * way, 512)],),
        (lambda k, way: out.at[k // 2, k % 2, pl.ds(2 * way, 2)],),
    )
    seconds = ((lambda own, k: own.at[k // 2, k % 2],), (lambda own, k: own.at[k // 2, k % 2],))
    finals = ((qkv_own,), (out_own,))
    return ring_items(net, at, SMALL_FIRST, SMALL_LAST, parts, parts, seconds, finals, bufs)


def forward_kernel(
    x_ref,
    og_ref,
    wq_ref,
    wk_ref,
    wv_ref,
    wout_ref,
    wg_ref,
    wu_ref,
    wd_ref,
    cos_ref,
    sin_ref,
    bq_ref,
    bk_ref,
    bv_ref,
    g1_ref,
    g2_ref,
    xs_ref,
    n1c_ref,
    og_out,
    qw_out,
    ow_out,
    q_ref,
    k_ref,
    v_ref,
    lse_ref,
    attn_all,
    mid_ref,
    gains_all,
    dn2_ref,
    hidden_out,
    dw_out,
    grad_gu,
    down_own,
    wqkv_ref,
    x_all,
    n1,
    og_all,
    n2_all,
    qw,
    ow,
    gw,
    uw,
    dw,
    part_out,
    part_in,
    d_up,
    tile_buf,
    down,
    attn_ref,
    gains_ref,
    bias_ref,
    *rest,
):
    red_a, bufs, sems = rest[:7], rest[7:-4], rest[-4:]
    send_sems, recv_sems, local_sems, tile_sems = sems
    at = Place()
    net = Net(send_sems, recv_sems, at)
    local, local_count = [], iter(range(32))

    def move(src, dst):
        copy = pltpu.make_async_copy(src, dst, local_sems.at[next(local_count)])
        copy.start()
        local.append(copy)
        return copy

    gains_ref[...] = jnp.zeros_like(gains_ref)
    gains_ref[0:1, :] = g1_ref[...].astype(F32)[None]
    gains_ref[1:2, :] = g2_ref[...].astype(F32)[None]
    bias_ref[:, :QCOLS] = bq_ref[...].astype(F32)[None]
    bias_ref[:, QCOLS : QCOLS + HEAD] = bk_ref[...].astype(F32)[None]
    bias_ref[:, QCOLS + HEAD :] = bv_ref[...].astype(F32)[None]
    joined = [
        move(wq_ref, wqkv_ref.at[:, pl.ds(0, QCOLS)]),
        move(wk_ref, wqkv_ref.at[:, pl.ds(QCOLS, HEAD)]),
        move(wv_ref, wqkv_ref.at[:, pl.ds(QCOLS + HEAD, HEAD)]),
    ]
    at.meet((at.S, at.N1, at.N2, at.O, at.OS, at.YP, at.YM, at.ZP, at.ZM))
    for copy in joined:
        copy.wait()
    local.clear()

    def tokens_of(array):
        def place(row, col, part):
            if part is None:
                rows = pl.ds(aligned(row, SEQ // 2), SEQ // 2)
            else:
                rows = pl.ds(aligned(row * 2 + part, SEQ // 4), SEQ // 4)
            return array.at[rows, pl.ds(aligned(col, FEAT), FEAT)]

        return place

    mine, mine_far = aligned(at.col, FEAT), aligned(1 - at.hi, 2 * FEAT)
    move(x_ref, tokens_of(x_all)(at.row, at.col, None))
    move(wqkv_ref, qw.at[pl.ds(mine, FEAT), :])
    move(wout_ref, ow.at[:, pl.ds(mine, FEAT)])
    move(gains_ref, gains_all.at[:, pl.ds(mine, FEAT)])
    start = quarter_start(at.col)
    move(wg_ref.at[:, pl.ds(start, PART)], gw.at[pl.ds(mine, FEAT), :])
    move(wu_ref.at[:, pl.ds(start, PART)], uw.at[pl.ds(mine, FEAT), :])
    move(wd_ref.at[pl.ds(start, PART), :], dw.at[:, pl.ds(mine, FEAT)])
    move(og_ref, tokens_of(og_all)(at.row, at.col, None))

    eighth = at.dp % 8
    across = [net.key() for _ in range(5)]

    def slice_copies(core, first, last):
        device = {"col": 2 * (1 - at.hi) + core}
        rows = pl.ds(aligned(eighth, 48), 48)
        target = pl.ds(pl.multiple_of(mine + eighth * 48, 16), 48)
        columns = pl.ds(core * 512, 512)
        out_rows = pl.ds(pl.multiple_of(core * FEAT + eighth * 48, 16), 48)
        theirs = quarter_start(2 * (1 - at.hi) + core)
        down_rows = pl.ds(pl.multiple_of(theirs + eighth * 144, 16), 144)
        down_target = pl.ds(aligned(eighth, 144), 144)
        pairs = (
            (wqkv_ref.at[rows, columns], qw.at[target, columns]),
            (wout_ref.at[out_rows, :], ow.at[out_rows, pl.ds(mine, FEAT)]),
            (wg_ref.at[rows, pl.ds(theirs, PART)], gw.at[target, :]),
            (wu_ref.at[rows, pl.ds(theirs, PART)], uw.at[target, :]),
            (wd_ref.at[down_rows, :], dw.at[down_target, pl.ds(mine, FEAT)]),
        )
        return [
            pltpu.make_async_remote_copy(
                src_ref=pairs[i][0],
                dst_ref=pairs[i][1],
                send_sem=net.ss.at[spare[core][i]],
                recv_sem=net.rs.at[across[i]],
                device_id=device,
                device_id_type=MESH,
            )
            for i in range(first, last)
        ]

    spare = ([net.key() for _ in range(5)], [net.key() for _ in range(5)])
    chosen = at.core == at.dp // 8

    @pl.when(chosen)
    def _():
        for core in (0, 1):
            for copy in slice_copies(core, 0, 2):
                copy.start()

    gather_x = Gather8(net, at, tokens_of(x_all))
    gather_x.start(x_ref)
    gain_far = net.send(gains_ref, gains_all.at[:, pl.ds(mine, FEAT)], at.N2)
    gain_sib = net.send(gains_ref, gains_all.at[:, pl.ds(mine, FEAT)], at.S)
    near_qw = net.send(wqkv_ref, qw.at[pl.ds(mine, FEAT), :], at.S)
    near_ow = net.send(wout_ref, ow.at[:, pl.ds(mine, FEAT)], at.S)

    @pl.when(chosen)
    def _():
        for core in (0, 1):
            for copy in slice_copies(core, 2, 5):
                copy.start()

    far_half = pl.ds(mine_far, 2 * FEAT)

    def qkv_slices(z, y):
        rows = pl.ds(pl.multiple_of(mine_far + (z * 4 + y) * 48, 16), 48)
        return [qw.at[rows, pl.ds(aligned(at.core, 512), 512)]]

    def out_slices(z, y):
        index = z * 4 + y
        rows = pl.ds(pl.multiple_of(at.core * FEAT + (index % 8) * 48, 16), 48)
        return [ow.at[rows, pl.ds(pl.multiple_of(mine_far + (index // 8) * FEAT, HEAD), FEAT)]]

    def rows_of(weights):
        def slices(z, y):
            return [weights.at[pl.ds(pl.multiple_of(mine_far + (z * 4 + y) * 48, 16), 48), :]]

        return slices

    def down_of(first, count):
        def slices(z, y):
            index = z * 4 + y
            rows = pl.ds(pl.multiple_of((index % 8) * 144 + first, 16), count)
            lanes = pl.ds(pl.multiple_of(mine_far + (index // 8) * FEAT, HEAD), FEAT)
            return [dw.at[rows, lanes]]

        return slices

    def ffn_rings():
        down = ring_dp(net, at, (down_of(0, 80), down_of(80, 64)))
        both = ring_dp(net, at, (rows_of(gw), rows_of(uw)))
        for _ in range(3):
            next(down)
            yield
        next(both)
        yield
        yield from down
        yield
        yield from both

    net.take(across[0], qkv_slices(at.z, at.y)[0])
    net.take(across[1], out_slices(at.z, at.y)[0])
    ring = ring_dp(net, at, (qkv_slices, out_slices))
    next(ring)
    next(ring)
    next(ring)
    gather_x.middle()
    gains_far = gains_all.at[:, pl.ds(aligned(at.far, FEAT), FEAT)]
    net.take(gain_far, gains_far)
    gain_sibfar = net.send(gains_far, gains_far, at.S)
    next(ring)
    cols_half, rows_half = pl.ds(aligned(at.core, 512), 512), pl.ds(aligned(at.core, FEAT), FEAT)
    gather_og = Gather8(net, at, tokens_of(og_all))
    gather_x.late()

    drain(ring)
    far_qw = net.send(qw.at[far_half, cols_half], qw.at[far_half, cols_half], at.S)
    far_ow = net.send(ow.at[rows_half, far_half], ow.at[rows_half, far_half], at.S)
    net.take(across[2], rows_of(gw)(at.z, at.y)[0])
    net.take(across[3], rows_of(uw)(at.z, at.y)[0])
    net.take(across[4], down_of(0, 144)(at.z, at.y)[0])
    ring = ffn_rings()
    next(ring)
    near = [
        net.send(wg_ref.at[:, pl.ds(quarter_start(at.sib), PART)], gw.at[pl.ds(mine, FEAT), :], at.S),
        net.send(wu_ref.at[:, pl.ds(quarter_start(at.sib), PART)], uw.at[pl.ds(mine, FEAT), :], at.S),
        net.send(wd_ref.at[pl.ds(quarter_start(at.sib), PART), :], dw.at[:, pl.ds(mine, FEAT)], at.S),
    ]
    gather_og.start(og_ref)
    gather_x.end()
    early = list(net.sent)
    net.take(gain_sib, gains_all.at[:, pl.ds(aligned(at.sib, FEAT), FEAT)])
    net.take(gain_sibfar, gains_all.at[:, pl.ds(aligned(at.sibfar, FEAT), FEAT)])
    for copy in local:
        copy.wait()
    local.clear()

    gain1, gain2 = gains_all[0:1, :], gains_all[1:2, :]

    def norm_block(i, carry):
        rows = pl.ds(aligned(i, BLOCK), BLOCK)
        values = x_all[rows, :].astype(F32)
        n1[rows, :] = (values * rms(values) * gain1).astype(BF)
        return carry

    lax.fori_loop(0, SEQ // BLOCK // 2, norm_block, 0)
    next(ring)
    lax.fori_loop(SEQ // BLOCK // 2, SEQ // BLOCK, norm_block, 0)
    next(ring)
    gather_og.middle()
    my_rows = pl.ds(aligned(at.block, BLOCK), BLOCK)
    xs_ref[...] = x_all[my_rows, :]
    n1c_ref[...] = n1[:, pl.ds(mine, FEAT)]
    net.take(near_qw, qw.at[pl.ds(aligned(at.sib, FEAT), FEAT), :])
    other_cols = pl.ds(aligned(1 - at.core, 512), 512)
    net.take(far_qw, qw.at[far_half, other_cols])
    move(qw, qw_out)

    def kv_block(i, carry):
        rows = pl.ds(aligned(i, 256), 256)
        both = dot(n1[rows, :], qw[:, QCOLS:]) + bias_ref[:, QCOLS:QKV]
        key = both[:, :HEAD]
        k_ref[rows, :] = (key * cos_ref[rows, :] + turn(key) * sin_ref[rows, :]).astype(BF)
        v_ref[rows, :] = both[:, HEAD:].astype(BF)
        return carry

    lax.fori_loop(0, SEQ // 256, kv_block, 0)
    next(ring)
    pair = (at.col, 7 - at.col)
    for j in (0, 1):
        rows = pl.ds(aligned(pair[j], BLOCK), BLOCK)
        queries = dot(n1[rows, :], qw[:, :QCOLS]) + bias_ref[:, :QCOLS]
        cosine, sine = cos_ref[rows, :], sin_ref[rows, :]
        for h in range(HEADS):
            one = queries[:, h * HEAD : (h + 1) * HEAD]
            q_ref[pl.ds(j * BLOCK, BLOCK), pl.ds(h * HEAD, HEAD)] = (
                one * cosine + turn(one) * sine
            ).astype(BF)
    next(ring)
    gather_og.late()

    for j in (0, 1):
        keys = SEQ // 2 * (j + 1)
        rows = pl.ds(j * BLOCK, BLOCK)

        def attend(h, carry):
            lanes = pl.ds(aligned(h, HEAD), HEAD)
            scores = dot(q_ref[rows, lanes], k_ref[:keys, :], 1, 1) * SCALE
            scores = causal(scores, pair[j] * BLOCK)
            top = jnp.max(scores, axis=1, keepdims=True)
            weights = jnp.exp(scores - top)
            total = jnp.sum(weights, axis=1, keepdims=True)
            lse_ref[j * HEADS + h] = top + jnp.log(total)
            probs = (weights * (1.0 / total)).astype(BF)
            attn_ref[rows, lanes] = dot(probs, v_ref[:keys, :]).astype(BF)
            return carry

        lax.fori_loop(0, HEADS // 2, attend, 0)
        next(ring)
        lax.fori_loop(HEADS // 2, HEADS, attend, 0)
        next(ring)

    net.take(near_ow, ow.at[:, pl.ds(aligned(at.sib, FEAT), FEAT)])
    other_rows = pl.ds(aligned(1 - at.core, FEAT), FEAT)
    net.take(far_ow, ow.at[other_rows, far_half])
    move(ow, ow_out)
    part_out[...] = dot(attn_ref[pl.ds(aligned(1 - at.row, BLOCK), BLOCK), :], ow[...]).astype(BF)
    part = net.send(part_out, part_in, at.N1)
    next(ring)
    own = dot(attn_ref[pl.ds(aligned(at.row, BLOCK), BLOCK), :], ow[...])
    net.take(part, part_in)
    mid = xs_ref[...].astype(F32) + own + part_in[...].astype(F32)
    mid_ref[...] = mid

    def place_n2(row, col, part):
        first = block_of(row, col) * BLOCK
        if part is None:
            return n2_all.at[pl.ds(pl.multiple_of(first, BLOCK), BLOCK), :]
        return n2_all.at[pl.ds(pl.multiple_of(first + part * 64, 64), 64), :]

    n2_all[my_rows, :] = (mid * rms(mid) * gain2).astype(BF)
    gather_n2 = Gather8(net, at, place_n2)
    gather_n2.start(place_n2(at.row, at.col, None))
    gather_og.end()
    move(og_all.at[my_rows, :], og_out)
    next(ring)
    next(ring)
    net.take(near[2], dw.at[:, pl.ds(aligned(at.sib, FEAT), FEAT)])

    def hidden_back(i, carry):
        rows = pl.ds(aligned(i, 256), 256)
        for first, width in tiles_of(PART, 512):
            lanes = pl.ds(first, width)
            d_up[rows, lanes] = dot(og_all[rows, :], dw[lanes, :], 1, 1).astype(BF)
        return carry

    lax.fori_loop(0, 1, hidden_back, 0)
    next(ring)
    lax.fori_loop(1, 2, hidden_back, 0)
    next(ring)
    gather_n2.middle()
    next(ring)
    lax.fori_loop(2, 3, hidden_back, 0)
    next(ring)
    lax.fori_loop(3, 4, hidden_back, 0)
    move(dw, dw_out)
    drain(ring)
    gather_attn = GatherCol(net, at, attn_all)
    for j in (0, 1):
        gather_attn.rows(at.col, j)[...] = attn_ref[pl.ds(j * BLOCK, BLOCK), :]
    net.take(near[0], gw.at[pl.ds(aligned(at.sib, FEAT), FEAT), :])
    net.take(near[1], uw.at[pl.ds(aligned(at.sib, FEAT), FEAT), :])

    net.finish(early)
    hidden, d_gate = x_all.at[:, pl.ds(0, PART)], n1.at[:, pl.ds(0, PART)]
    norms = Reduce8(net, at, *red_a)
    chips = at.chips
    last_part = at.col == 3

    def tokens(j):
        row, hi = chips[j]
        first = 2 * hi + row * (6 - 4 * hi)
        return pl.ds(aligned(first, BLOCK), 256), at.core + row * (1 - 2 * at.core)

    for j in (3, 1, 2, 0):
        gather_n2.end(j)
        if j == 3:
            gather_n2.late()
            gather_attn.start()
        rows, _ = tokens(j)
        for first, width in tiles_of(PART, 512):
            lanes = pl.ds(first, width)
            gate = dot(n2_all[rows, :], gw[:, lanes])
            up = dot(n2_all[rows, :], uw[:, lanes])
            d_hidden = d_up[rows, lanes].astype(F32)
            sig = jax.nn.sigmoid(gate)
            act = gate * sig
            d_act = d_hidden * up * sig * (1.0 + gate * (1.0 - sig))
            values = [act * up, d_act, d_hidden * act]
            if first == 0:
                lane = lax.broadcasted_iota(jnp.int32, (1, width), 1)
                fresh = jnp.logical_or(lane >= HEAD, jnp.logical_not(last_part))
                values = [jnp.where(fresh, value, 0.0) for value in values]
            for ref, value in zip((hidden, d_gate, d_up), values, strict=True):
                ref[rows, lanes] = value.astype(BF)
    move(hidden, hidden_out)
    for first, width in tiles_of(MODEL, 256):
        lanes = pl.ds(first, width)
        tile = dot(hidden[...], og_all[:, lanes], 0, 0).astype(BF)
        for q in range(4):
            down[q // 2, q % 2, :, lanes] = tile[288 * q : 288 * (q + 1)]
    gather_attn.middle()
    sums, last_sums = down_items(net, at, down, down_own, bufs)
    begin(sums)
    for j in range(4):
        rows, place = tokens(j)
        own_rows = pl.ds(pl.multiple_of(rows.start + place * BLOCK, BLOCK), BLOCK)
        other_rows = pl.ds(pl.multiple_of(rows.start + (1 - place) * BLOCK, BLOCK), BLOCK)
        parts = [
            (dot(d_gate[r, :], gw[...], 1, 1) + dot(d_up[r, :], uw[...], 1, 1)).astype(BF)
            for r in (other_rows, own_rows)
        ]
        norms.put(j, parts[1], parts[0])
        if j:
            norms.step(j - 1)

    writes = []

    def outer_sum(left, right, out):
        height = left.shape[1] // 2
        for first, width in tiles_of(right.shape[1], 256):
            place = len(writes) % 2
            if len(writes) > 1:
                writes[-2].wait()
            for i in (0, 1):
                rows = pl.ds(i * height, height)
                tile_buf[place, rows, :width] = dot(
                    left[:, rows], right[:, pl.ds(first, width)], 0, 0
                ).astype(BF)
            writes.append(
                pltpu.make_async_copy(
                    tile_buf.at[place, pl.ds(0, 2 * height), pl.ds(0, width)],
                    out.at[:, pl.ds(first, width)],
                    tile_sems.at[place],
                )
            )
            writes[-1].start()

    gather_attn.end()
    for item in sums:
        item.middle()
    outer_sum(n2_all, d_gate, grad_gu.at[0])
    dn2_ref[...] = norms.step(3)
    for item in sums:
        item.end()
    begin(last_sums)
    outer_sum(n2_all, d_up, grad_gu.at[1])
    for item in last_sums:
        item.middle()
    for item in last_sums:
        item.end()
    for copy in writes[-2:]:
        copy.wait()
    for copy in local:
        copy.wait()
    net.finish()

    @pl.when(chosen)
    def _():
        for core in (0, 1):
            for copy in slice_copies(core, 0, 5):
                copy.wait_send()


def run_forward(x, og, wq, wk, wv, wout, wg, wu, wd, *small):
    outs = (
        ((BLOCK, MODEL), BF, vmem),
        ((SEQ, FEAT), BF, vmem),
        ((BLOCK, MODEL), BF, anywhere),
        ((MODEL, QKV), BF, anywhere),
        ((QCOLS, MODEL), BF, anywhere),
        ((2 * BLOCK, QCOLS), BF, vmem),
        ((SEQ, HEAD), BF, vmem),
        ((SEQ, HEAD), BF, vmem),
        ((2 * HEADS, BLOCK, 1), F32, vmem),
        ((SEQ, QCOLS), BF, vmem),
        ((BLOCK, MODEL), F32, vmem),
        ((8, MODEL), F32, vmem),
        ((BLOCK, MODEL), F32, vmem),
        ((SEQ, PART), BF, anywhere),
        ((PART, MODEL), BF, anywhere),
        ((2, MODEL, PART), BF, anywhere),
        ((80, MODEL), BF, vmem),
    )
    return pl.pallas_call(
        forward_kernel,
        out_shape=[jax.ShapeDtypeStruct(dims, dtype) for dims, dtype, _ in outs],
        in_specs=[anywhere()] * 9 + [vmem()] * 7,
        out_specs=[place() for _, _, place in outs],
        scratch_shapes=[
            pltpu.VMEM((FEAT, QKV), BF),
            pltpu.VMEM((SEQ, MODEL), BF),
            pltpu.VMEM((SEQ, MODEL), BF),
            pltpu.VMEM((SEQ, MODEL), BF),
            pltpu.VMEM((SEQ, MODEL), BF),
            pltpu.VMEM((MODEL, QKV), BF),
            pltpu.VMEM((QCOLS, MODEL), BF),
            pltpu.VMEM((MODEL, PART), BF),
            pltpu.VMEM((MODEL, PART), BF),
            pltpu.VMEM((PART, MODEL), BF),
            pltpu.VMEM((BLOCK, MODEL), BF),
            pltpu.VMEM((BLOCK, MODEL), BF),
            pltpu.VMEM((SEQ, PART), BF),
            pltpu.VMEM((2, MODEL, 256), BF),
            pltpu.VMEM((2, 2, 288, MODEL), BF),
            pltpu.VMEM((2 * BLOCK, QCOLS), BF),
            pltpu.VMEM((8, FEAT), F32),
            pltpu.VMEM((1, QKV), F32),
        ]
        + reduce8_scratch(BLOCK, MODEL)
        + ring_scratch(DOWN_FIRST, DOWN_LAST)
        + [
            pltpu.SemaphoreType.DMA((200,)),
            pltpu.SemaphoreType.DMA((200,)),
            pltpu.SemaphoreType.DMA((32,)),
            pltpu.SemaphoreType.DMA((2,)),
        ],
        compiler_params=pltpu.CompilerParams(
            collective_id=0, has_side_effects=True, vmem_limit_bytes=VMEM_LIMIT
        ),
        cost_estimate=pl.CostEstimate(
            flops=37 * 10**9, bytes_accessed=80 * 10**6, transcendentals=4 * 10**6
        ),
        name="forward_and_feed_forward",
    )(x, og, wq, wk, wv, wout, wg, wu, wd, *small)


def backward_kernel(
    dn2_ref,
    mid_ref,
    og_ref,
    gains_all,
    n1c,
    attn_all,
    q_ref,
    k_ref,
    v_ref,
    lse_ref,
    cos_ref,
    sin_ref,
    ow_far,
    gu_far,
    down_own,
    grad_out,
    grad_qkv,
    sums_ref,
    d_mid,
    d_qkv_own,
    bias_ref,
    gu_own,
    all_down,
    mid_cols,
    mid_pair,
    d_attn,
    d_q,
    d_kv,
    kv_out,
    kv_in,
    d_qkv_all,
    ow,
    gu,
    *rest,
):
    bufs, (send_sems, recv_sems, local_sems) = rest[:-3], rest[-3:]
    at = Place()
    net = Net(send_sems, recv_sems, at)
    held = [
        pltpu.make_async_copy(src, dst, local_sems.at[i])
        for i, (src, dst) in enumerate(
            ((ow_far, ow), (gu_far, gu))
        )
    ]
    for copy in held:
        copy.start()
    at.meet(
        (at.S, at.O, at.OS, at.N1, at.N2, at.N1S, at.N2S, at.YP, at.YM, at.ZP, at.ZM)
    )
    first, last = gu_items(net, at, gu_far, gu, gu_own, bufs)
    begin(first)

    def down_slot(k, cols):
        return all_down.at[cols, pl.ds(pl.multiple_of(k * 80, 16), 80), :]

    down_keys = [
        net.send(down_own.at[:, pl.ds(aligned(col, FEAT), FEAT)], down_slot(at.dp, at.col), device)
        for device, col in ((at.S, at.sib), (at.O, at.far), (at.OS, at.sibfar))
    ]
    down_mine = pltpu.make_async_copy(
        down_own.at[:, pl.ds(aligned(at.col, FEAT), FEAT)],
        down_slot(at.dp, at.col),
        local_sems.at[3],
    )
    down_mine.start()
    peers = ((at.S, at.sib), (at.O, at.far), (at.OS, at.sibfar))
    pair = (at.col, 7 - at.col)

    def rows_at(block):
        return pl.ds(aligned(block, BLOCK), BLOCK)

    def cols_at(col):
        return pl.ds(aligned(col, FEAT), FEAT)

    gain2 = gains_all[1:2, :]
    mid = mid_ref[...]
    scale = rms(mid)
    unit = mid * scale
    d_normed = dn2_ref[...]
    sums_ref[...] = jnp.zeros_like(sums_ref)
    sums_ref[1:2, :] = jnp.sum(d_normed * unit, axis=0, keepdims=True)
    bent = d_normed * gain2
    d_mid[...] = og_ref[...].astype(F32) + scale * (
        bent - unit * jnp.mean(bent * unit, axis=1, keepdims=True)
    )
    mid_pair[at.row] = d_mid[...].astype(BF)
    to_pair = net.send(mid_pair.at[at.row], mid_pair.at[at.row], at.N1)
    mid_cols[rows_at(at.block), :] = d_mid[:, cols_at(at.col)].astype(BF)
    spread = []
    others = (
        (at.S, at.row, at.sib),
        (at.N1, 1 - at.row, at.col),
        (at.N1S, 1 - at.row, at.sib),
        (at.O, at.row, at.far),
        (at.OS, at.row, at.sibfar),
        (at.N2, 1 - at.row, at.far),
        (at.N2S, 1 - at.row, at.sibfar),
    )
    for device, row, col in others:
        spread.append(
            net.send(
                mid_pair.at[at.row, :, cols_at(col)], mid_cols.at[rows_at(at.block), :], device
            )
        )
    net.take(to_pair, mid_pair.at[1 - at.row])
    held[0].wait()
    for j in (0, 1):
        d_attn[pl.ds(j * BLOCK, BLOCK), :] = dot(mid_pair[j], ow[...], 1, 1).astype(BF)
    d_kv[...] = jnp.zeros_like(d_kv)
    held[1].wait()
    for item in first:
        item.middle()

    for j in (0, 1):
        keys = SEQ // 2 * (j + 1)
        rows = pl.ds(j * BLOCK, BLOCK)

        def back(h, carry):
            lanes = pl.ds(aligned(h, HEAD), HEAD)
            queries, d_out = q_ref[rows, lanes], d_attn[rows, lanes]
            scores = dot(queries, k_ref[:keys, :], 1, 1) * SCALE
            scores = causal(scores, pair[j] * BLOCK)
            probs = jnp.exp(scores - lse_ref[j * HEADS + h])
            d_probs = dot(d_out, v_ref[:keys, :], 1, 1)
            inner = jnp.sum(probs * d_probs, axis=1, keepdims=True)
            d_scores = (probs * (d_probs - inner) * SCALE).astype(BF)
            d_q[rows, lanes] = dot(d_scores, k_ref[:keys, :])
            d_kv[:keys, :HEAD] += dot(d_scores, queries, 0, 0)
            d_kv[:keys, HEAD:] += dot(probs.astype(BF), d_out, 0, 0)
            return carry

        lax.fori_loop(0, HEADS, back, 0)

    kv_out[...] = d_kv[...].astype(BF)
    kv_keys = [
        [
            net.send(kv_out.at[rows_at(col + j * (7 - 2 * col)), :], kv_in.at[i, j], device)
            for j in (0, 1)
        ]
        for i, (device, col) in enumerate(peers)
    ]
    cosines = [cos_ref[rows_at(pair[j]), :] for j in (0, 1)]
    sines = [sin_ref[rows_at(pair[j]), :] for j in (0, 1)]
    for j in (0, 1):
        for h in range(HEADS):
            one = d_q[pl.ds(j * BLOCK, BLOCK), pl.ds(h * HEAD, HEAD)]
            d_qkv_all[rows_at(pair[j]), pl.ds(h * HEAD, HEAD)] = (
                one * cosines[j] - turn(one) * sines[j]
            ).astype(BF)
    for item in first:
        item.end()
    begin(last)
    down_mine.wait()
    for key, (_, col) in zip(down_keys, peers, strict=True):
        net.take(key, down_slot(at.dp, col))
    ring = ring_dp(
        net,
        at,
        (
            lambda zz, yy: [down_slot(zz * 4 + yy, pl.ds(2 * at.hi, 2))],
            lambda zz, yy: [down_slot(zz * 4 + yy, pl.ds(2 * (1 - at.hi), 2))],
        ),
    )
    next(ring)
    for key, (_, row, col) in zip(spread, others, strict=True):
        net.take(key, mid_cols.at[rows_at(block_of(row, col)), :])
    grad_out[...] = dot(attn_all[...], mid_cols[...], 0, 0).astype(BF)
    for j in (0, 1):
        total = d_kv[rows_at(pair[j]), :]
        for i in range(3):
            net.take(kv_keys[i][j], kv_in.at[i, j])
            total = total + kv_in[i, j].astype(F32)
        key = total[:, :HEAD]
        d_qkv_all[rows_at(pair[j]), pl.ds(QCOLS, HEAD)] = (
            key * cosines[j] - turn(key) * sines[j]
        ).astype(BF)
        d_qkv_all[rows_at(pair[j]), pl.ds(QCOLS + HEAD, HEAD)] = total[:, HEAD:].astype(BF)
    gather_qkv = GatherCol(net, at, d_qkv_all)
    gather_qkv.start()
    for item in last:
        item.middle()
    next(ring)

    for j in (0, 1):
        d_qkv_own[j] = d_qkv_all[rows_at(pair[j]), :]
    next(ring)
    next(ring)
    gather_qkv.middle()
    next(ring)
    gather_qkv.end()
    grad_qkv[...] = dot(n1c[...], d_qkv_all[...], 0, 0).astype(BF)
    ones = jnp.ones((8, SEQ), BF)
    bias_ref[...] = dot(ones, d_qkv_all[...])
    for item in last:
        item.end()
    drain(ring)
    net.finish()


def run_backward(*args):
    def out(shape, dtype):
        return jax.ShapeDtypeStruct(shape, dtype)

    outs = (
        out((QCOLS, FEAT), BF),
        out((FEAT, QKV), BF),
        out((8, MODEL), F32),
        out((BLOCK, MODEL), F32),
        out((2, BLOCK, QKV), BF),
        out((8, QKV), F32),
        out((4, 48, PART), BF),
        out((4, 1280, FEAT), BF),
    )
    return pl.pallas_call(
        backward_kernel,
        out_shape=outs,
        in_specs=[vmem()] * (len(args) - 3) + [anywhere()] * 2 + [vmem()],
        out_specs=[vmem()] * (len(outs) - 1) + [anywhere()],
        scratch_shapes=[
            pltpu.VMEM((SEQ, FEAT), BF),
            pltpu.VMEM((2, BLOCK, MODEL), BF),
            pltpu.VMEM((2 * BLOCK, QCOLS), BF),
            pltpu.VMEM((2 * BLOCK, QCOLS), F32),
            pltpu.VMEM((SEQ, 2 * HEAD), F32),
            pltpu.VMEM((SEQ, 2 * HEAD), BF),
            pltpu.VMEM((3, 2, BLOCK, 2 * HEAD), BF),
            pltpu.VMEM((SEQ, QKV), BF),
            pltpu.VMEM((QCOLS, MODEL), BF),
            pltpu.VMEM((2, 4, 2, 4, 48, PART), BF),
        ]
        + ring_scratch(GU_FIRST, GU_LAST)
        + [pltpu.SemaphoreType.DMA((110,)), pltpu.SemaphoreType.DMA((110,))]
        + [pltpu.SemaphoreType.DMA((4,))],
        compiler_params=pltpu.CompilerParams(
            collective_id=2, has_side_effects=True, vmem_limit_bytes=VMEM_LIMIT
        ),
        cost_estimate=pl.CostEstimate(
            flops=10 * 10**9, bytes_accessed=40 * 10**6, transcendentals=2 * 10**6
        ),
        name="attention_backward",
    )(*args)


def sums_kernel(
    gu_own,
    qkv,
    out,
    sums_ref,
    d_mid,
    d_qkv,
    bias_ref,
    xs_ref,
    gains_all,
    mid_ref,
    hidden_far,
    dw_far,
    qw_far,
    all_gu,
    all_qkv,
    all_out,
    small_out,
    out_ref,
    gi_in,
    small_y,
    small_z,
    hidden,
    dw,
    ffn,
    qw,
    part_out,
    part_in,
    gi_out,
    gain_sums,
    sums_in,
    *rest,
):
    red, bufs, (send_sems, recv_sems, local_sems) = rest[:7], rest[7:-3], rest[-3:]
    at = Place()
    net = Net(send_sems, recv_sems, at)
    held = [
        pltpu.make_async_copy(qw_far, qw, local_sems.at[1]),
        pltpu.make_async_copy(hidden_far, hidden, local_sems.at[2]),
        pltpu.make_async_copy(dw_far, dw, local_sems.at[3]),
    ]
    for copy in held:
        copy.start()
    at.meet(
        (at.S, at.O, at.OS, at.N1, at.N2, at.N1S, at.N2S)
        + (at.YP, at.YM, at.ZP, at.ZM, at.Y2, at.Z2)
    )
    outs = Reduce8(net, at, *red)

    def project(j):
        row, hi = at.chips[j]
        rows = pl.ds(aligned(row, SEQ // 2), SEQ // 2)
        lanes = pl.ds(aligned(hi, QCOLS), QCOLS)
        ffn[...] = dot(hidden[rows, :], dw[:, lanes])
        if j in (0, 3):
            mine = pl.ds(pl.multiple_of((at.block - 4 * at.row) * BLOCK, BLOCK), BLOCK)
            ffn[mine, :] += mid_ref[:, lanes]
        own = ffn[:, pl.ds(aligned(at.core, FEAT), FEAT)].astype(BF)
        outs.put(j, own, ffn[:, pl.ds(aligned(1 - at.core, FEAT), FEAT)].astype(BF))
        if j:
            outs.step(j - 1)

    z, y = at.z, at.y

    def gu_piece(k, lanes):
        rows = pl.ds(pl.multiple_of((k % 8) * 48, 16), 48)
        return all_gu.at[k // 8, rows, lanes]

    def part_lanes(col):
        return pl.ds(aligned(col, PART), PART)

    def feat_lanes(col):
        return pl.ds(aligned(col, FEAT), FEAT)

    def qkv_piece(k):
        rows = pl.ds(pl.multiple_of((k % 8) * 48, 16), 48)
        return all_qkv.at[rows, pl.ds(pl.multiple_of((k // 8) * 512, 512), 512)]

    def out_piece(k):
        return all_out.at[pl.ds(pl.multiple_of(k * 48, 16), 48), :]

    peers = ((at.O, at.far), (at.OS, at.sibfar), (at.S, at.sib))
    keys = []
    for device, col in peers:
        keys.append(
            net.send(gu_own.at[col], gu_piece(at.dp, part_lanes(at.col)), device)
        )
    held[0].wait()
    part_out[...] = dot(d_qkv[1 - at.row], qw[...], 1, 1).astype(BF)
    part = net.send(part_out, part_in, at.N1)
    first, last = small_items(net, at, qkv, out, qkv_piece(at.dp), out_piece(at.dp), bufs)
    begin(first)
    own_copies = [
        pltpu.make_async_copy(
            gu_own.at[at.col], gu_piece(at.dp, part_lanes(at.col)), local_sems.at[0]
        ),
    ]
    for copy in own_copies:
        copy.start()

    def take_from(i):
        net.take(keys[i], gu_piece(at.dp, part_lanes(peers[i][1])))

    def chip_ready():
        for copy in own_copies:
            copy.wait()
        take_from(2)

    def far_ready():
        take_from(0)
        take_from(1)

    def half_of(hi):
        def half(zz, yy):
            k = zz * 4 + yy
            return [gu_piece(k, pl.ds(aligned(hi, 2 * PART), 2 * PART))]

        return half

    ring = ring_dp(
        net, at, (half_of(at.hi), half_of(1 - at.hi)), (chip_ready, far_ready)
    )
    next(ring)
    for item in first:
        item.middle()
    d_normed = dot(d_qkv[at.row], qw[...], 1, 1)
    net.take(part, part_in)
    d_normed = d_normed + part_in[...].astype(F32)
    values = xs_ref[...].astype(F32)
    scale = rms(values)
    unit = values * scale
    gain_sums[...] = sums_ref[...]
    gain_sums[0:1, :] = jnp.sum(d_normed * unit, axis=0, keepdims=True)
    bent = d_normed * gains_all[0:1, :]
    total = d_mid[...] + scale * (bent - unit * jnp.mean(bent * unit, axis=1, keepdims=True))
    gi_out[...] = total.astype(BF)

    def half_block(col):
        offset = block_of(at.row, col) - 4 * at.row
        return gi_in.at[pl.ds(pl.multiple_of(offset * BLOCK, BLOCK), BLOCK), :]

    gi_keys = [
        net.send(gi_out.at[:, feat_lanes(col)], half_block(at.col), device)
        for device, col in peers
    ]
    half_block(at.col)[...] = gi_out[:, feat_lanes(at.col)]
    others = (
        (at.S, at.row, at.sib),
        (at.N1, 1 - at.row, at.col),
        (at.N1S, 1 - at.row, at.sib),
        (at.O, at.row, at.far),
        (at.OS, at.row, at.sibfar),
        (at.N2, 1 - at.row, at.far),
        (at.N2S, 1 - at.row, at.sibfar),
    )
    sums_in[at.row * 4 + at.col] = gain_sums[:, feat_lanes(at.col)]
    sums_keys = [
        net.send(gain_sums.at[:, feat_lanes(col)], sums_in.at[at.row * 4 + at.col], device)
        for device, row, col in others
    ]
    next(ring)
    held[1].wait()
    held[2].wait()
    project(0)
    for item in first:
        item.end()
    begin(last)
    next(ring)
    project(1)
    for key, (_, row, col) in zip(sums_keys, others, strict=True):
        net.take(key, sums_in.at[row * 4 + col])
    total = sums_in[0]
    for i in range(1, 8):
        total = total + sums_in[i]
    small_y[y, :, :FEAT] = total
    small_y[y, :, FEAT:] = bias_ref[...]
    small_keys = [net.send(small_y.at[y], small_y.at[y], d) for d in (at.YP, at.YM, at.Y2)]
    for item in last:
        item.middle()
    next(ring)
    project(2)
    for key, k in zip(small_keys, (y - 1, y + 1, y + 2), strict=True):
        net.take(key, small_y.at[lax.rem(k + 4, 4)])
    small_z[z] = (small_y[0] + small_y[1]) + (small_y[2] + small_y[3])
    small_keys = [net.send(small_z.at[z], small_z.at[z], d) for d in (at.ZP, at.ZM, at.Z2)]
    for item in last:
        item.end()
    after = ring_dp(
        net,
        at,
        (lambda zz, yy: [qkv_piece(zz * 4 + yy)], lambda zz, yy: [out_piece(zz * 4 + yy)]),
    )
    next(after)
    next(ring)
    project(3)
    next(after)
    for key, k in zip(small_keys, (z - 1, z + 1, z + 2), strict=True):
        net.take(key, small_z.at[lax.rem(k + 4, 4)])
    small_out[...] = (small_z[0] + small_z[1]) + (small_z[2] + small_z[3])
    for key, (_, col) in zip(gi_keys, peers, strict=True):
        net.take(key, half_block(col))
    for _ in ring:
        next(after, None)
    drain(after)
    out_ref[...] = outs.step(3)
    net.finish()


def run_sums(gu, qkv, out, *args):
    def shape(dims, dtype):
        return jax.ShapeDtypeStruct(dims, dtype)

    outs = (
        shape((2, FEAT, 4 * PART), BF),
        shape((FEAT, QKV), BF),
        shape((QCOLS, FEAT), BF),
        shape((8, FEAT + QKV), F32),
        shape((SEQ // 2, FEAT), F32),
        shape((SEQ // 2, FEAT), BF),
    )
    return pl.pallas_call(
        sums_kernel,
        out_shape=outs,
        in_specs=[vmem()] * len(args) + [anywhere()] * 3,
        out_specs=[anywhere()] + [vmem()] * 5,
        scratch_shapes=[pltpu.VMEM((4, 8, FEAT + QKV), F32)] * 2
        + [
            pltpu.VMEM((SEQ, PART), BF),
            pltpu.VMEM((PART, MODEL), BF),
            pltpu.VMEM((SEQ // 2, QCOLS), F32),
            pltpu.VMEM((MODEL, QKV), BF),
            pltpu.VMEM((BLOCK, MODEL), BF),
            pltpu.VMEM((BLOCK, MODEL), BF),
            pltpu.VMEM((BLOCK, MODEL), BF),
            pltpu.VMEM((8, MODEL), F32),
            pltpu.VMEM((8, 8, FEAT), F32),
        ]
        + reduce8_scratch(SEQ // 2, FEAT)
        + ring_scratch(SMALL_FIRST, SMALL_LAST)
        + [pltpu.SemaphoreType.DMA((128,)), pltpu.SemaphoreType.DMA((128,))]
        + [pltpu.SemaphoreType.DMA((4,))],
        compiler_params=pltpu.CompilerParams(
            collective_id=3, has_side_effects=True, vmem_limit_bytes=VMEM_LIMIT
        ),
        cost_estimate=pl.CostEstimate(
            flops=4 * 10**9, bytes_accessed=60 * 10**6, transcendentals=0
        ),
        name="sums_over_sequences",
    )(gu, qkv, out, *args)


def widen_kernel(
    gu,
    down,
    qkv,
    out,
    small,
    gi,
    lo,
    gate_out,
    up_out,
    down_out,
    lo_out,
    gi_out,
    query_out,
    key_out,
    value_out,
    proj_out,
    gain1_out,
    gain2_out,
    bq_out,
    bk_out,
    bv_out,
    gu_in,
    down_in,
    gate_buf,
    up_buf,
    down_buf,
    in_sems,
    out_sems,
):
    skip = 3 * PART

    def loads(n):
        rows = pl.ds(640 * (n % 2), 640)
        return [
            pltpu.make_async_copy(gu.at[:, pl.ds(n * 48, 48), :], gu_in.at[n], in_sems.at[n, 0]),
            pltpu.make_async_copy(down.at[n // 2, rows, :], down_in.at[n], in_sems.at[n, 1]),
        ]

    def stores(n):
        place, quarter, part = n % 2, n // 2, n % 2
        rows = pl.ds(n * 48, 48)
        drop = HEAD if quarter == 3 and part == 0 else 0
        start = PART * quarter + 576 * part - (HEAD if quarter == 3 and part == 1 else 0)
        return [
            pltpu.make_async_copy(gate_buf.at[place], gate_out.at[rows, :], out_sems.at[place, 0]),
            pltpu.make_async_copy(up_buf.at[place], up_out.at[rows, :], out_sems.at[place, 1]),
            pltpu.make_async_copy(
                down_buf.at[place, pl.ds(drop, 576 - drop), :],
                down_out.at[pl.ds(start, 576 - drop), :],
                out_sems.at[place, 2],
            ),
        ]

    def run(copies):
        for copy in copies:
            copy.start()
        return copies

    def wait(copies):
        for copy in copies:
            copy.wait()

    arriving = [run(loads(n)) for n in range(8)]
    lo_out[...] = lo[...]
    gi_out[...] = gi[...].astype(F32)
    query_out[...] = qkv[:, :QCOLS].astype(F32)
    key_out[...] = qkv[:, QCOLS : QCOLS + HEAD].astype(F32)
    value_out[...] = qkv[:, QCOLS + HEAD :].astype(F32)
    proj_out[...] = out[...].astype(F32)
    first = 0
    for ref, row, width in (
        (gain1_out, 0, FEAT),
        (bq_out, 0, QCOLS),
        (bk_out, 0, HEAD),
        (bv_out, 0, HEAD),
    ):
        ref[...] = small[row, first : first + width]
        first += width
    gain2_out[...] = small[1, :FEAT]
    leaving = {}
    for n in range(8):
        place = n % 2
        wait(arriving[n])
        if n > 1:
            wait(leaving[n - 2])
        for i, buf in enumerate((gate_buf, up_buf)):
            buf[place, :, :skip] = gu_in[n, i, :, :skip].astype(F32)
            buf[place, :, skip:] = gu_in[n, i, :, skip + HEAD :].astype(F32)
        for m in range(4):
            down_buf[place, pl.ds(144 * m, 80), :] = down_in[
                n, pl.ds(160 * m, 80), :
            ].astype(F32)
            down_buf[place, pl.ds(144 * m + 80, 64), :] = down_in[
                n, pl.ds(160 * m + 96, 64), :
            ].astype(F32)
        leaving[n] = run(stores(n))
    wait(leaving[6])
    wait(leaving[7])


def run_widen(gu, down, qkv, out, small, grad_input, layer_output):
    shapes = [(FEAT, UNITS)] * 2 + [(UNITS, FEAT)] + [(SEQ // 2, FEAT)] * 2
    shapes += [(FEAT, QCOLS), (FEAT, HEAD), (FEAT, HEAD), (QCOLS, FEAT)]
    shapes += [(FEAT,), (FEAT,), (QCOLS,), (HEAD,), (HEAD,)]
    return pl.pallas_call(
        widen_kernel,
        out_shape=[jax.ShapeDtypeStruct(dims, F32) for dims in shapes],
        in_specs=[anywhere()] * 2 + [vmem()] * 5,
        out_specs=[anywhere()] * 3 + [vmem()] * 11,
        scratch_shapes=[
            pltpu.VMEM((8, 2, 48, 4 * PART), BF),
            pltpu.VMEM((8, 640, FEAT), BF),
            pltpu.VMEM((2, 48, UNITS), F32),
            pltpu.VMEM((2, 48, UNITS), F32),
            pltpu.VMEM((2, 576, FEAT), F32),
            pltpu.SemaphoreType.DMA((8, 2)),
            pltpu.SemaphoreType.DMA((2, 3)),
        ],
        compiler_params=pltpu.CompilerParams(vmem_limit_bytes=VMEM_LIMIT),
        cost_estimate=pl.CostEstimate(
            flops=10**7, bytes_accessed=36 * 10**6, transcendentals=0
        ),
        name="widen",
    )(gu, down, qkv, out, small, grad_input, layer_output)


def rope_tables(count):
    places = np.arange(count, dtype=np.float32)
    inverse = (1.0 / THETA ** (np.arange(0, HEAD, 2) / HEAD)).astype(np.float32)
    angles = places[:, None] * inverse[None, :]
    cosine, sine = np.cos(angles), np.sin(angles)
    tables = np.concatenate([cosine, cosine], axis=-1), np.concatenate([-sine, sine], axis=-1)
    return tuple(jnp.asarray(table, F32) for table in tables)


def body(
    layer_input,
    gain_attn,
    w_query,
    w_key,
    w_value,
    b_query,
    b_key,
    b_value,
    w_out,
    gain_ffn,
    w_gate,
    w_up,
    w_down,
    out_grad,
):
    cosine, sine = rope_tables(SEQ)
    (
        xs,
        normed1_cols,
        grads_block,
        qkv_w,
        out_w,
        queries,
        key,
        value,
        lse,
        attn,
        mid,
        gains_all,
        dn2,
        hidden,
        down_w,
        grad_gu,
        grad_down,
    ) = run_forward(
        layer_input,
        out_grad,
        w_query,
        w_key,
        w_value,
        w_out,
        w_gate,
        w_up,
        w_down,
        cosine,
        sine,
        b_query,
        b_key,
        b_value,
        gain_attn,
        gain_ffn,
    )
    grad_out, grad_qkv, sums, d_mid, d_qkv, bias_sums, grad_gu, grad_down = run_backward(
        dn2,
        mid,
        grads_block,
        gains_all,
        normed1_cols,
        attn,
        queries,
        key,
        value,
        lse,
        cosine,
        sine,
        out_w,
        grad_gu.reshape(2, 4, 2, 4, 48, PART),
        grad_down,
    )
    grad_gu, grad_qkv, grad_out, small, layer_output, grad_input = run_sums(
        grad_gu,
        grad_qkv.reshape(2, 4, 48, QKV),
        grad_out.reshape(2, 2, 4, 48, FEAT),
        sums,
        d_mid,
        d_qkv,
        bias_sums,
        xs,
        gains_all,
        mid,
        hidden,
        down_w,
        qkv_w,
    )
    (
        grad_gate,
        grad_up,
        grad_down,
        layer_output,
        grad_input,
        grad_query,
        grad_key,
        grad_value,
        grad_out,
        *vectors,
    ) = run_widen(
        grad_gu, grad_down, grad_qkv, grad_out, small, grad_input, layer_output
    )
    gain1, gain2, bias_query, bias_key, bias_value = vectors
    return (
        layer_output,
        grad_input,
        gain1,
        grad_query,
        grad_key,
        grad_value,
        bias_query,
        bias_key,
        bias_value,
        grad_out,
        gain2,
        grad_gate,
        grad_up,
        grad_down,
    )


def solution(mesh):
    in_specs = (
        P(("dp", "row"), "col"),
        P("col"),
        P("col", "row"),
        P("col", "row"),
        P("col", "row"),
        P("row"),
        P("row"),
        P("row"),
        P("row", "col"),
        P("col"),
        P("col", "row"),
        P("col", "row"),
        P("row", "col"),
        P(("dp", "row"), "col"),
    )
    out_specs = (
        P(("dp", "row"), "col"),
        P(("dp", "row"), "col"),
        P("col"),
        P("col", "row"),
        P("col", "row"),
        P("col", "row"),
        P("row"),
        P("row"),
        P("row"),
        P("row", "col"),
        P("col"),
        P("col", "row"),
        P("col", "row"),
        P("row", "col"),
    )
    return jax.shard_map(body, mesh=mesh, in_specs=in_specs, out_specs=out_specs, check_vma=False)
```
